32 devices in a mesh: seq: 8 (over z, x), grp: 4 (over y, core).
Axes of the slice: x: 2, y: 2, z: 4, core: 2. Of those that a mesh axis runs over, the one named last changes fastest.
Arguments:
- tokens: bfloat16 [4, 1024, 2048], P('grp', 'seq'), may hold values from -6 to 6
- cotangent: bfloat16 [4, 1024, 2048], P('grp', 'seq'), may hold values from -6 to 6
- lengths: int32 [4, 4], replicated, may hold values from 16 to 912, as said below
- prenorm_gain: float32 [2048], replicated, may hold values from 0.1 to 1.9
- w_query: bfloat16 [2048, 2048], P('seq', 'grp'), may hold values from -0.125 to 0.125
- w_key: bfloat16 [2048, 2048], P('seq', 'grp'), may hold values from -0.125 to 0.125
- w_value: bfloat16 [2048, 2048], P('seq', 'grp'), may hold values from -0.125 to 0.125
- w_gate: bfloat16 [2048, 2048], P('seq', 'grp'), may hold values from -0.125 to 0.125
- rate_weight: bfloat16 [2048, 32], replicated, may hold values from -0.125 to 0.125
- rate_bias: float32 [32], replicated, may hold values from -4 to 4
- init_weight: float32 [32, 64, 64], replicated, may hold values from -0.75 to 0.75
- init_bias: float32 [32, 64], replicated, may hold values from -3 to 3
- inner_gain: float32 [32, 64], replicated, may hold values from 0.1 to 1.9
- inner_bias: float32 [32, 64], replicated, may hold values from -3 to 3
- post_gain: float32 [2048], replicated, may hold values from 0.1 to 1.9
- post_bias: float32 [2048], replicated, may hold values from -2 to 2
- w_out: bfloat16 [2048, 2048], P('grp', 'seq'), may hold values from -0.25 to 0.25
- feedforward_norm_gain: float32 [2048], replicated, may hold values from 0.1 to 1.9
- w_swish: bfloat16 [2048, 5504], P('seq', 'grp'), may hold values from -0.125 to 0.125
- w_up: bfloat16 [2048, 5504], P('seq', 'grp'), may hold values from -0.125 to 0.125
- w_down: bfloat16 [5504, 2048], P('grp', 'seq'), may hold values from -0.15625 to 0.15625
Outputs:
- out_tokens: bfloat16 [4, 1024, 2048], P('grp', 'seq')
- grad_tokens: float32 [4, 1024, 2048], P('grp', 'seq')
- grad_pre_gain: float32 [2048], replicated
- grad_query: float32 [2048, 2048], P('seq', 'grp')
- grad_key: float32 [2048, 2048], P('seq', 'grp')
- grad_value: float32 [2048, 2048], P('seq', 'grp')
- grad_gate: float32 [2048, 2048], P('seq', 'grp')
- grad_rate_weight: float32 [2048, 32], replicated
- grad_rate_bias: float32 [32], replicated
- grad_init_weight: float32 [32, 64, 64], replicated
- grad_init_bias: float32 [32, 64], replicated
- grad_inner_gain: float32 [32, 64], replicated
- grad_inner_bias: float32 [32, 64], replicated
- grad_post_gain: float32 [2048], replicated
- grad_post_bias: float32 [2048], replicated
- grad_out: float32 [2048, 2048], P('grp', 'seq')
- grad_ffn_gain: float32 [2048], replicated
- grad_swish: float32 [2048, 5504], P('seq', 'grp')
- grad_up: float32 [2048, 5504], P('seq', 'grp')
- grad_down: float32 [5504, 2048], P('grp', 'seq')
The draws below stay inside these ranges and needn't reach their ends.
Inputs may be any that keep to these rules, and one draw needn't show every extreme that they name: `lengths`: lengths are multiples of 16; in each group they leave a padding of at least 16 and under a tenth of 1024 positions at the end; one document of each group, at a place drawn from the seed, covers positions from the first 128 to the last 128 of the stream, and it is the longest.
All inputs are finite; a program needn't handle non-finite values.
Results may differ from the reference program's by a relative error of at most 0.025.
Values may be sent and summed in bfloat16 or wider, within the bound.
No kernel may reach another device: no remote copies, remote signals or barrier semaphores. Data moves between devices by JAX's collectives and lax.ppermute only.
A program may use at most 192 MiB of HBM per device.

```python
from functools import partial
import jax
import jax.numpy as jnp
from jax import lax

D = 2048
HEADS = 32
HEAD = 64
FF = 5504
MB = 16
DOCS = 4
TOK_DEV = 128
GROUPS = 4
STREAM = 1024


def draw_lengths(key, part):
    key = jax.random.fold_in(key, 7)
    units = TOK_DEV // MB
    quarter = units // 4
    keys_all = jax.random.split(key, 3)
    drawn = jax.random.randint(keys_all[0], (GROUPS, DOCS - 1), 1, quarter + 1)
    shorts = jnp.concatenate([jnp.ones((GROUPS, 1), jnp.int32), drawn[:, 1:]], 1)
    longest = STREAM // MB - ((DOCS - 1) * quarter + 1) + 0 * jnp.sum(shorts, 1, keepdims=True)
    placed = jax.random.randint(keys_all[2], (GROUPS, 1), 0, DOCS)
    slots = jnp.arange(DOCS)[None, :]
    before = jnp.concatenate([shorts, shorts[:, -1:]], 1)
    after = jnp.concatenate([shorts[:, :1], shorts], 1)
    picked = jnp.where(slots < placed, before, jnp.where(slots == placed, longest, after))
    return (picked * MB).astype(jnp.int32)


def block_levels(rng, dims, cuts, low, largest):
    loudness, own = 1.0, jax.random.fold_in(rng, 6)
    for dim, parts in cuts:
        steps = jnp.exp(jax.random.uniform(jax.random.fold_in(own, dim), (parts,), jnp.float32, low / len(cuts), largest / len(cuts)))
        loudness = loudness * jnp.repeat(steps, dims[dim] // parts).reshape([-1 if axis == dim else 1 for axis in range(len(dims))])
    return loudness


def scatter_about(key, dims, width, limit, cuts=(), dtype=jnp.bfloat16):
    factor_of = block_levels(key, dims, cuts, -0.22, 0.18) if cuts else 1.0
    values = jax.random.normal(key, dims, jnp.float32) * width * factor_of
    return jnp.minimum(jnp.maximum(values, -limit), limit).astype(dtype)


def setup_inputs(seed: int = 0) -> dict:
    arg_keys = jax.random.split(jax.random.key(seed), 22)
    tokens = scatter_about(arg_keys[0], (GROUPS, STREAM, D), 1.0, 6.0, ((0, 4), (1, 8)))
    cotangent = scatter_about(arg_keys[1], (GROUPS, STREAM, D), 1.0, 6.0, ((0, 4), (1, 8)))
    lengths = draw_lengths(jax.random.fold_in(arg_keys[21], 71), 0)
    prenorm_gain = jnp.clip(1.0 + 0.18 * jax.random.normal(arg_keys[3], (D,), jnp.float32), 0.1, 1.9)
    w_query = scatter_about(arg_keys[4], (D, D), D ** -0.5, 0.125, ((0, 8), (1, 4)))
    w_key = scatter_about(arg_keys[5], (D, D), D ** -0.5, 0.125, ((0, 8), (1, 4)))
    w_value = scatter_about(arg_keys[6], (D, D), D ** -0.5, 0.125, ((0, 8), (1, 4)))
    w_gate = scatter_about(arg_keys[7], (D, D), D ** -0.5, 0.125, ((0, 8), (1, 4)))
    rate_weight = scatter_about(arg_keys[8], (D, HEADS), D ** -0.5, 0.125)
    rate_bias = scatter_about(arg_keys[9], (HEADS,), 1.0, 4.0, (), jnp.float32)
    init_weight = scatter_about(arg_keys[10], (HEADS, HEAD, HEAD), HEAD ** -0.5, 0.75, (), jnp.float32)
    init_bias = scatter_about(arg_keys[11], (HEADS, HEAD), 0.5, 3.0, (), jnp.float32)
    inner_gain = jnp.clip(1.0 + 0.18 * jax.random.normal(arg_keys[12], (HEADS, HEAD), jnp.float32), 0.1, 1.9)
    inner_bias = scatter_about(arg_keys[13], (HEADS, HEAD), 0.5, 3.0, (), jnp.float32)
    post_gain = jnp.clip(1.0 + 0.18 * jax.random.normal(arg_keys[14], (D,), jnp.float32), 0.1, 1.9)
    post_bias = scatter_about(arg_keys[15], (D,), 0.3, 2.0, (), jnp.float32)
    w_out = scatter_about(arg_keys[16], (D, D), (D // 4) ** -0.5, 0.25, ((0, 4), (1, 8)))
    feedforward_norm_gain = jnp.clip(1.0 + 0.18 * jax.random.normal(arg_keys[17], (D,), jnp.float32), 0.1, 1.9)
    w_swish = scatter_about(arg_keys[18], (D, FF), D ** -0.5, 0.125, ((0, 8), (1, 4)))
    w_up = scatter_about(arg_keys[19], (D, FF), D ** -0.5, 0.125, ((0, 8), (1, 4)))
    w_down = scatter_about(arg_keys[20], (FF, D), (FF // 4) ** -0.5, 0.15625, ((0, 4), (1, 8)))
    return dict(tokens=tokens, cotangent=cotangent, lengths=lengths, prenorm_gain=prenorm_gain, w_query=w_query, w_key=w_key, w_value=w_value, w_gate=w_gate, rate_weight=rate_weight, rate_bias=rate_bias, init_weight=init_weight, init_bias=init_bias, inner_gain=inner_gain, inner_bias=inner_bias, post_gain=post_gain, post_bias=post_bias, w_out=w_out, feedforward_norm_gain=feedforward_norm_gain, w_swish=w_swish, w_up=w_up, w_down=w_down)


EPS = 1e-06
HIGH = lax.Precision.HIGHEST

@jax.custom_vjp
def low(v):
    return lax.optimization_barrier(v.astype(jnp.bfloat16)).astype(jnp.float32)

@jax.custom_vjp
def low_back(v):
    return v

def low_keep(v):
    return (low(v), None)

def low_pass(kept, grad):
    return (grad,)

def back_keep(v):
    return (v, None)

def back_low(kept, grad):
    return (low(grad),)
low.defvjp(low_keep, low_pass)
low_back.defvjp(back_keep, back_low)

def norm_parts(values):
    centred = values - lax.optimization_barrier(jnp.mean(values, -1, keepdims=True))
    return centred * lax.rsqrt(lax.optimization_barrier(jnp.mean(centred * centred, -1, keepdims=True)) + EPS)

def inner_step(params, carried, inputs):
    init_w, init_b, in_gain, in_shift = params
    state_w, state_b = carried
    queries, key_rows, val_rows, rates, starting = inputs
    state_w = jnp.where(starting[:, None, None, None], init_w[None], state_w)
    state_b = jnp.where(starting[:, None, None], init_b[None], state_b)
    hidden = jnp.einsum('gthf,ghfe->gthe', key_rows, state_w, precision=HIGH) + state_b[:, None]
    centred = hidden - lax.optimization_barrier(jnp.mean(hidden, -1, keepdims=True))
    inv_std = lax.rsqrt(lax.optimization_barrier(jnp.mean(centred * centred, -1, keepdims=True)) + EPS)
    normalized_rows = centred * inv_std
    err_grad = (normalized_rows * in_gain + in_shift - (val_rows - key_rows)) * in_gain
    grad_hidden = inv_std * (err_grad - lax.optimization_barrier(jnp.mean(err_grad, -1, keepdims=True)) - normalized_rows * lax.optimization_barrier(jnp.mean(err_grad * normalized_rows, -1, keepdims=True)))
    scaled = rates[..., None] * grad_hidden
    lower = (jnp.arange(MB)[:, None] >= jnp.arange(MB)[None, :]).astype(jnp.float32)
    scores = jnp.einsum('gthf,gshf->ghts', queries, key_rows, precision=HIGH)
    mixed = jnp.einsum('ghts,gshf->gthf', (scores + 1.0) * lower, scaled, precision=HIGH)
    updated = jnp.einsum('gthf,ghfe->gthe', queries, state_w, precision=HIGH) + state_b[:, None] - mixed
    result = queries + norm_parts(updated) * in_gain + in_shift
    new_w = state_w - jnp.einsum('gthf,gthe->ghfe', key_rows, scaled, precision=HIGH)
    new_b = state_b - lax.optimization_barrier(jnp.sum(scaled, 1))
    return ((new_w, new_b), result)

def run_span(state_pair, queries, key_rows, val_rows, rates, starting, params):
    groups = queries.shape[0]
    blocks = queries.shape[1] // MB

    def split_rows(array):
        return jnp.moveaxis(array.reshape((groups, blocks, MB) + array.shape[2:]), 1, 0)
    state_pair, outputs = lax.scan(jax.checkpoint(partial(inner_step, params)), state_pair, (split_rows(queries), split_rows(key_rows), split_rows(val_rows), split_rows(rates), jnp.moveaxis(starting, 1, 0)))
    return (state_pair, jnp.moveaxis(outputs, 0, 1).reshape(queries.shape))

def group_block(weights, tokens_g, lengths_g):
    prenorm_gain, w_query, w_key, w_value, w_gate, rate_weight, rate_bias, init_weight, init_bias, inner_gain, inner_bias, post_gain, post_bias, w_out, feedforward_norm_gain, w_swish, w_up, w_down = weights
    stream_len = tokens_g.shape[0]
    ends = jnp.cumsum(lengths_g)
    starts = ends - lengths_g
    live = (jnp.arange(stream_len) < ends[-1]).astype(jnp.float32)
    block_starts = jnp.arange(stream_len // MB) * MB
    starting = jnp.any(block_starts[:, None] == starts[None, :], -1)
    first_inverse_norm = lax.rsqrt(lax.optimization_barrier(jnp.mean(tokens_g * tokens_g, -1, keepdims=True)) + EPS)
    normalized_rows = low(tokens_g * first_inverse_norm * prenorm_gain)

    def project(matrix):
        return jnp.dot(normalized_rows, matrix, precision=HIGH)
    queries = low_back(low(project(w_query)))
    key_rows = low_back(low(project(w_key)))
    val_rows = low_back(low(project(w_value)))
    gate_pre = low_back(project(w_gate))
    logits = low_back(project(rate_weight) + rate_bias)
    rates = jax.nn.sigmoid(logits) / HEAD * live[:, None]
    shape_four = (1, stream_len, HEADS, HEAD)
    zero_state = (jnp.zeros((1, HEADS, HEAD, HEAD), jnp.float32), jnp.zeros((1, HEADS, HEAD), jnp.float32))
    _, inner = run_span(zero_state, queries.reshape(shape_four), key_rows.reshape(shape_four), val_rows.reshape(shape_four), rates.reshape(1, stream_len, HEADS), starting[None], (init_weight, init_bias, inner_gain, inner_bias))
    inner = inner.reshape(stream_len, D)
    mean_o = lax.optimization_barrier(jnp.mean(inner, -1, keepdims=True))
    var_o = lax.optimization_barrier(jnp.mean(inner * inner, -1, keepdims=True)) - mean_o * mean_o
    post = (inner - mean_o) * lax.rsqrt(var_o + EPS) * post_gain + post_bias
    gated = low(jax.nn.gelu(gate_pre) * post)
    mixing = low_back(jnp.dot(gated, w_out, precision=HIGH))
    residual_stream = tokens_g + mixing
    second_inverse_norm = lax.rsqrt(lax.optimization_barrier(jnp.mean(residual_stream * residual_stream, -1, keepdims=True)) + EPS)
    feedforward_input = low(residual_stream * second_inverse_norm * feedforward_norm_gain)
    act_a = low_back(jnp.dot(feedforward_input, w_swish, precision=HIGH))
    act_u = low_back(jnp.dot(feedforward_input, w_up, precision=HIGH))
    hidden = low(jax.nn.silu(act_a) * act_u)
    return residual_stream + low_back(jnp.dot(hidden, w_down, precision=HIGH))

def reference(tokens, cotangent, lengths, prenorm_gain, w_query, w_key, w_value, w_gate, rate_weight, rate_bias, init_weight, init_bias, inner_gain, inner_bias, post_gain, post_bias, w_out, feedforward_norm_gain, w_swish, w_up, w_down):
    weights = tuple((item.astype(jnp.float32) for item in (prenorm_gain, w_query, w_key, w_value, w_gate, rate_weight, rate_bias, init_weight, init_bias, inner_gain, inner_bias, post_gain, post_bias, w_out, feedforward_norm_gain, w_swish, w_up, w_down)))
    inputs_f = tokens.astype(jnp.float32)

    def forward(inputs_all, weight_set):
        block_fn = jax.checkpoint(partial(group_block, weight_set))

        def per_group(both_in):
            return block_fn(both_in[0], both_in[1])
        return lax.map(per_group, (inputs_all, lengths))
    output, pull_back = jax.vjp(forward, inputs_f, weights)
    grad_in, grad_w = pull_back(cotangent.astype(jnp.float32))
    return (output.astype(jnp.bfloat16), grad_in, grad_w[0], grad_w[1], grad_w[2], grad_w[3], grad_w[4], grad_w[5], grad_w[6], grad_w[7], grad_w[8], grad_w[9], grad_w[10], grad_w[11], grad_w[12], grad_w[13], grad_w[14], grad_w[15], grad_w[16], grad_w[17])
```

```python
from functools import partial

import jax
import jax.numpy as jnp
from jax import lax
from jax.experimental import pallas as pl
from jax.experimental.pallas import tpu as pltpu
from jax.sharding import PartitionSpec as P

MB = 16
EPS = 1e-06
F32 = jnp.float32
BF16 = jnp.bfloat16


def mm(left, right):
    return jnp.dot(left, right, preferred_element_type=F32)


def mm_nt(left, right):
    return lax.dot_general(left, right, (((1,), (1,)), ((), ())), preferred_element_type=F32)


def split_two(value):
    high = value.astype(BF16)
    return high, (value - high.astype(F32)).astype(BF16)


def mean_rows(value):
    return jnp.mean(value, axis=0, keepdims=True)


def chunk_rows(ref_value, heads, lanes):
    tokens = ref_value.shape[1]
    parts = [
        ref_value[h, m * MB : (m + 1) * MB, lanes[0] : lanes[1]]
        for m in range(tokens // MB)
        for h in range(heads)
    ]
    return jnp.concatenate(parts, axis=0)


def chunk_masks(info, heads, count):
    step = MB * heads
    row = lax.broadcasted_iota(jnp.int32, (count, count), 0)
    col = lax.broadcasted_iota(jnp.int32, (count, count), 1)
    columns = jnp.transpose(info)
    same = ((row % step) // MB == (col % step) // MB) & (columns[:, 1:2] == info[1:2, :])
    return row // step, col // step, row % MB, col % MB, same, columns


def augment(rows, heads, head_dim, wide):
    count = rows.shape[0]
    near = lax.broadcasted_iota(jnp.int32, (head_dim, wide), 0)
    far = lax.broadcasted_iota(jnp.int32, (head_dim, wide), 1)
    tile = (far % head_dim == near).astype(BF16)
    lane = lax.broadcasted_iota(jnp.int32, (count, wide), 1)
    own = (lax.broadcasted_iota(jnp.int32, (count, wide), 0) % (MB * heads)) // MB
    return jnp.where(lane // head_dim == own, mm(rows, tile), 0.0)


def one_hot_heads(count, heads):
    lane = lax.broadcasted_iota(jnp.int32, (count, 128), 1)
    own = (lax.broadcasted_iota(jnp.int32, (count, 128), 0) % (MB * heads)) // MB
    return (lane == own).astype(BF16)


def forward_kernel(
    heads, x_ref, info_ref, gb_ref, init_ref, out_ref, n_ref, r_ref, nb_ref, stat_ref, w_ref, state
):
    head_dim = gb_ref.shape[1]
    tokens = x_ref.shape[1]
    count = heads * tokens
    full = init_ref.shape[1]
    wide = full - 128

    @pl.when(pl.program_id(0) == 0)
    def _():
        state[...] = init_ref[...]

    carried = state[...]
    w_ref[0] = carried
    info = info_ref[...]
    x = x_ref[...]
    q_rows = chunk_rows(x, heads, (0, head_dim))
    k_rows = chunk_rows(x, heads, (head_dim, 2 * head_dim))
    v_rows = chunk_rows(x, heads, (2 * head_dim, 3 * head_dim))
    g_rows = chunk_rows(x, heads, (3 * head_dim, 4 * head_dim))
    q_t = jnp.transpose(q_rows.astype(F32))
    target_t = jnp.transpose(v_rows.astype(F32) - k_rows.astype(F32))
    mb_row, mb_col, t_row, t_col, same, columns = chunk_masks(info, heads, count)
    gram = jnp.where(same & (mb_row < mb_col), mm_nt(k_rows, k_rows) + 1.0, 0.0).astype(BF16)
    cross = jnp.where(
        same & ((mb_row < mb_col) | ((mb_row == mb_col) & (t_row <= t_col))),
        mm_nt(k_rows, q_rows) + 1.0,
        0.0,
    ).astype(BF16)
    hot = one_hot_heads(count, heads)
    k_aug = jnp.concatenate([augment(k_rows, heads, head_dim, wide).astype(BF16), hot], axis=1)
    q_aug = jnp.concatenate([augment(q_rows, heads, head_dim, wide).astype(BF16), hot], axis=1)
    init = init_ref[...]
    stacked = jnp.concatenate(split_two(carried) + split_two(init), axis=0)
    fresh = info[2:3, :] > 0.5

    def through_state(rows):
        both = mm_nt(stacked, rows)
        return jnp.where(
            fresh,
            both[2 * head_dim : 3 * head_dim] + both[3 * head_dim :],
            both[:head_dim] + both[head_dim : 2 * head_dim],
        )

    z_start = through_state(k_aug)
    gain = gb_ref[0]
    shift = gb_ref[1]
    repeats = count // 128
    inner = 128 // (MB * heads)
    done = []
    for p in range(repeats):
        cols = slice(p * 128, (p + 1) * 128)
        z_base = z_start[:, cols]
        if p:
            z_base = z_base - mm(jnp.concatenate(done, axis=1), gram[: p * 128, cols])
        target = target_t[:, cols]
        rate = info[0:1, cols]
        z = z_base
        for step in range(inner):
            if step:
                z = z_base - mm(scaled.astype(BF16), gram[cols, cols])
            centred = z - mean_rows(z)
            inv = lax.rsqrt(mean_rows(centred * centred) + EPS)
            n = centred * inv
            err = (n * gain + shift - target) * gain
            scaled = (rate * inv) * (err - mean_rows(err) - n * mean_rows(err * n))
        done.append(scaled.astype(BF16))
        n_ref[:, cols] = n
        r_ref[:, cols] = scaled
        stat_ref[0:1, cols] = inv
    r_bf = jnp.concatenate(done, axis=1)
    z_bar = through_state(q_aug) - mm(r_bf, cross)
    centred = z_bar - mean_rows(z_bar)
    inv = lax.rsqrt(mean_rows(centred * centred) + EPS)
    nb = centred * inv
    nb_ref[...] = nb
    stat_ref[1:2, :] = inv
    wide_gain = jnp.concatenate([gain] * repeats, axis=1)
    wide_shift = jnp.concatenate([shift] * repeats, axis=1)
    out_rows = jnp.transpose(q_t + nb * wide_gain + wide_shift)
    packed = jnp.concatenate([out_rows.astype(BF16), g_rows], axis=1)
    for m in range(tokens // MB):
        for h in range(heads):
            at = (m * heads + h) * MB
            out_ref[0, h, m * MB : (m + 1) * MB, :] = packed[at : at + MB]
    base = jnp.where(info[4:5, 0:1] > 0.5, init, carried)
    state[...] = base - mm((r_ref[...] * info[3:4, :]).astype(BF16), k_aug)


def backward_kernel(
    heads,
    x_ref,
    d_ref,
    info_ref,
    gb_ref,
    init_ref,
    n_ref,
    r_ref,
    nb_ref,
    stat_ref,
    w_ref,
    dx_ref,
    dr_ref,
    dgb_ref,
    dinit_ref,
    state,
):
    head_dim = gb_ref.shape[1]
    tokens = x_ref.shape[1]
    count = heads * tokens
    full = init_ref.shape[1]
    wide = full - 128

    @pl.when(pl.program_id(0) == 0)
    def _():
        state[...] = jnp.zeros_like(state)
        dgb_ref[...] = jnp.zeros_like(dgb_ref)
        dinit_ref[...] = jnp.zeros_like(dinit_ref)

    d_end = state[...]
    carried = w_ref[0]
    init = init_ref[...]
    info = info_ref[...]
    x = x_ref[...]
    d_in = d_ref[0]
    q_rows = chunk_rows(x, heads, (0, head_dim))
    k_rows = chunk_rows(x, heads, (head_dim, 2 * head_dim))
    v_rows = chunk_rows(x, heads, (2 * head_dim, 3 * head_dim))
    d_rows = chunk_rows(d_in, heads, (0, head_dim))
    dg_rows = chunk_rows(d_in, heads, (head_dim, 2 * head_dim))
    target_t = jnp.transpose(v_rows.astype(F32) - k_rows.astype(F32))
    d_t = jnp.transpose(d_rows.astype(F32))
    mb_row, mb_col, t_row, t_col, same, columns = chunk_masks(info, heads, count)
    earlier = same & (mb_row < mb_col)
    later = same & (mb_row > mb_col)
    up_to = same & ((mb_row < mb_col) | ((mb_row == mb_col) & (t_row <= t_col)))
    from_on = same & ((mb_row > mb_col) | ((mb_row == mb_col) & (t_row >= t_col)))
    gram = jnp.where(later, mm_nt(k_rows, k_rows) + 1.0, 0.0).astype(BF16)
    cross = jnp.where(from_on, mm_nt(q_rows, k_rows) + 1.0, 0.0).astype(BF16)
    hot = one_hot_heads(count, heads)
    k_aug = jnp.concatenate([augment(k_rows, heads, head_dim, wide).astype(BF16), hot], axis=1)
    q_aug = jnp.concatenate([augment(q_rows, heads, head_dim, wide).astype(BF16), hot], axis=1)
    gain = gb_ref[0]
    shift = gb_ref[1]
    repeats = count // 128
    inner = 128 // (MB * heads)
    wide_gain = jnp.concatenate([gain] * repeats, axis=1)
    nb = nb_ref[...]
    inv_b = stat_ref[1:2, :]
    d_nb = d_t * wide_gain
    d_zbar = inv_b * (d_nb - mean_rows(d_nb) - nb * mean_rows(d_nb * nb))
    scaled_t = r_ref[...]
    last = info[3:4, :]
    dr_base = -mm(d_zbar.astype(BF16), cross) - last * mm_nt(d_end.astype(BF16), k_aug)
    gain_sum = jnp.zeros((head_dim, 128), F32)
    shift_sum = jnp.zeros((head_dim, 128), F32)
    for p in range(repeats):
        cols = slice(p * 128, (p + 1) * 128)
        gain_sum = gain_sum + d_t[:, cols] * nb[:, cols]
        shift_sum = shift_sum + d_t[:, cols]
    done = []
    errs = []
    for p in reversed(range(repeats)):
        cols = slice(p * 128, (p + 1) * 128)
        base = dr_base[:, cols]
        if done:
            base = base - mm(jnp.concatenate(done, axis=1), gram[(p + 1) * 128 :, cols])
        n = n_ref[:, cols]
        inv = stat_ref[0:1, cols]
        rate = info[0:1, cols]
        miss = n * gain + shift - target_t[:, cols]
        err = miss * gain
        along = mean_rows(err * n)
        plain = inv * (err - mean_rows(err) - n * along)
        gain2 = gain * gain
        d_scaled = base
        for step in range(inner):
            if step:
                d_scaled = base - mm(d_z.astype(BF16), gram[cols, cols])
            g = rate * d_scaled
            g_n = mean_rows(g * n)
            d_err = inv * (g - mean_rows(g) - n * g_n)
            d_n = d_err * gain2 - inv * (g * along + err * g_n)
            d_z = inv * (d_n - mean_rows(d_n) - n * (mean_rows(d_n * n) + mean_rows(g * plain)))
        done.insert(0, d_z.astype(BF16))
        errs.insert(0, d_err * gain)
        dr_ref[0:1, cols] = jnp.sum(d_scaled * plain, axis=0, keepdims=True)
        gain_sum = gain_sum + d_err * (miss + gain * n)
        shift_sum = shift_sum + d_err * gain
    dgb_ref[0] += gain_sum
    dgb_ref[1] += shift_sum
    dz_bf = jnp.concatenate(done, axis=1)
    d_z = dz_bf.astype(F32)
    d_errg = jnp.concatenate(errs, axis=1)
    turned = jnp.transpose(jnp.concatenate([d_zbar, scaled_t, d_z, d_errg], axis=0))
    zb_rows = turned[:, :head_dim].astype(BF16)
    r_rows = turned[:, head_dim : 2 * head_dim].astype(BF16)
    z_rows = turned[:, 2 * head_dim : 3 * head_dim].astype(BF16)
    e_rows = turned[:, 3 * head_dim :]
    d_cross = jnp.where(from_on, -mm_nt(zb_rows, r_rows), 0.0).astype(BF16)
    d_cross_t = jnp.where(up_to, -mm_nt(r_rows, zb_rows), 0.0).astype(BF16)
    d_gram = (
        jnp.where(later, -mm_nt(z_rows, r_rows), 0.0)
        + jnp.where(earlier, -mm_nt(r_rows, z_rows), 0.0)
    ).astype(BF16)
    is_init = columns[:, 2:3] > 0.5
    is_last = columns[:, 3:4] > 0.5

    def stack_heads(weight):
        parts = [weight[:, h * head_dim : (h + 1) * head_dim] for h in range(heads)]
        pad = wide - heads * head_dim
        if pad:
            parts.append(jnp.zeros((pad, head_dim), F32))
        return jnp.concatenate(parts, axis=0).astype(BF16)

    w_both = jnp.concatenate([stack_heads(carried), stack_heads(init)], axis=0)
    d_stack = stack_heads(d_end)

    def by_state(rows):
        own = augment(rows, heads, head_dim, wide)
        return jnp.concatenate(
            [jnp.where(is_init, 0.0, own), jnp.where(is_init, own, 0.0)], axis=1
        ).astype(BF16)

    dq = d_rows.astype(F32) + mm(d_cross, k_rows) + mm(by_state(zb_rows), w_both)
    r_own = jnp.where(is_last, augment(r_rows, heads, head_dim, wide), 0.0).astype(BF16)
    dk = (
        e_rows
        + mm(d_gram, k_rows)
        + mm(d_cross_t, q_rows)
        + mm(by_state(z_rows), w_both)
        - mm(r_own, d_stack)
    )
    packed = jnp.concatenate(
        [dq.astype(BF16), dk.astype(BF16), (-e_rows).astype(BF16), dg_rows], axis=1
    )
    for m in range(tokens // MB):
        for h in range(heads):
            at = (m * heads + h) * MB
            dx_ref[h, m * MB : (m + 1) * MB, :] = packed[at : at + MB]
    row_init = info[2:3, :] > 0.5
    zb_two = jnp.concatenate(
        [jnp.where(row_init, 0.0, d_zbar), jnp.where(row_init, d_zbar, 0.0)], axis=0
    ).astype(BF16)
    z_two = jnp.concatenate(
        [jnp.where(row_init, 0.0, d_z), jnp.where(row_init, d_z, 0.0)], axis=0
    ).astype(BF16)
    d_both = mm(zb_two, q_aug) + mm(z_two, k_aug)
    fresh = info[4:5, 0:1] > 0.5
    state[...] = d_both[:head_dim] + jnp.where(fresh, 0.0, d_end)
    dinit_ref[...] += d_both[head_dim:] + jnp.where(fresh, d_end, 0.0)


def chain_specs(heads, tokens, head_dim, full, at):
    count = heads * tokens
    return dict(
        x=pl.BlockSpec((heads, tokens, 4 * head_dim), lambda i: (0, at(i), 0)),
        pair=pl.BlockSpec((1, heads, tokens, 2 * head_dim), lambda i: (at(i), 0, 0, 0)),
        info=pl.BlockSpec((8, count), lambda i: (0, at(i))),
        gb=pl.BlockSpec((2, head_dim, 128), lambda i: (0, 0, 0)),
        init=pl.BlockSpec((head_dim, full), lambda i: (0, 0)),
        tall=pl.BlockSpec((head_dim, count), lambda i: (0, at(i))),
        weight=pl.BlockSpec((1, head_dim, full), lambda i: (at(i), 0, 0)),
    )


def chain_forward(x4, info, gb, init, tokens):
    heads, total, packed = x4.shape
    head_dim = packed // 4
    chunks = total // tokens
    full = init.shape[1]
    s = chain_specs(heads, tokens, head_dim, full, lambda i: i)
    tall = jax.ShapeDtypeStruct((head_dim, heads * total), F32)
    return pl.pallas_call(
        partial(forward_kernel, heads),
        grid=(chunks,),
        in_specs=[s["x"], s["info"], s["gb"], s["init"]],
        out_specs=[s["pair"], s["tall"], s["tall"], s["tall"], s["info"], s["weight"]],
        out_shape=[
            jax.ShapeDtypeStruct((chunks, heads, tokens, 2 * head_dim), BF16),
            tall,
            tall,
            tall,
            jax.ShapeDtypeStruct((8, heads * total), F32),
            jax.ShapeDtypeStruct((chunks, head_dim, full), F32),
        ],
        scratch_shapes=[pltpu.VMEM((head_dim, full), F32)],
        compiler_params=pltpu.CompilerParams(
            dimension_semantics=("arbitrary",), vmem_limit_bytes=32 * 1024 * 1024
        ),
        cost_estimate=pl.CostEstimate(
            flops=40_000_000_000, bytes_accessed=16_000_000, transcendentals=0
        ),
        name="chain_forward",
    )(x4, info, gb, init)


def chain_backward(x4, d_pair, info, gb, init, kept, tokens):
    heads, total, packed = x4.shape
    head_dim = packed // 4
    chunks = total // tokens
    full = init.shape[1]
    s = chain_specs(heads, tokens, head_dim, full, lambda i: chunks - 1 - i)
    return pl.pallas_call(
        partial(backward_kernel, heads),
        grid=(chunks,),
        in_specs=[
            s["x"],
            s["pair"],
            s["info"],
            s["gb"],
            s["init"],
            s["tall"],
            s["tall"],
            s["tall"],
            s["info"],
            s["weight"],
        ],
        out_specs=[s["x"], s["info"], s["gb"], s["init"]],
        out_shape=[
            jax.ShapeDtypeStruct(x4.shape, BF16),
            jax.ShapeDtypeStruct((8, heads * total), F32),
            jax.ShapeDtypeStruct(gb.shape, F32),
            jax.ShapeDtypeStruct(init.shape, F32),
        ],
        scratch_shapes=[pltpu.VMEM((head_dim, full), F32)],
        compiler_params=pltpu.CompilerParams(
            dimension_semantics=("arbitrary",), vmem_limit_bytes=40 * 1024 * 1024
        ),
        cost_estimate=pl.CostEstimate(
            flops=80_000_000_000, bytes_accessed=20_000_000, transcendentals=0
        ),
        name="chain_backward",
    )(x4, d_pair, info, gb, init, *kept)


def chain_setup(starting, rates, init_weight, init_bias, inner_gain, inner_bias, blocks):
    heads, head_dim, _ = init_weight.shape
    count = starting.shape[0]
    doc = jnp.cumsum(starting.astype(jnp.int32))
    by_chunk = doc.reshape(-1, blocks)
    before = jnp.concatenate([jnp.zeros((1,), jnp.int32), by_chunk[:-1, -1]])
    use_init = by_chunk > before[:, None]
    in_last = by_chunk == by_chunk[:, -1:]
    fresh = jnp.broadcast_to(use_init[:, -1:], use_init.shape)
    spread = jnp.stack(
        [by_chunk, use_init.astype(jnp.int32), in_last.astype(jnp.int32), fresh.astype(jnp.int32)]
    ).astype(F32).reshape(4, count)
    spread = jnp.broadcast_to(spread[:, :, None], (4, count, heads * MB)).reshape(4, -1)
    rate_row = jnp.swapaxes(rates.reshape(count, MB, heads), 1, 2).reshape(1, -1)
    info = jnp.concatenate([rate_row, spread, jnp.zeros((3, rate_row.shape[1]), F32)], axis=0)
    reps = 128 // (MB * heads)

    def pattern(item):
        row = jnp.broadcast_to(item.T[:, None, :, None], (head_dim, reps, heads, MB))
        return row.reshape(head_dim, 128)

    gb = jnp.stack([pattern(inner_gain), pattern(inner_bias)])
    wide = max(128, heads * head_dim)
    w_t = jnp.transpose(init_weight, (2, 0, 1)).reshape(head_dim, heads * head_dim)
    init = jnp.concatenate(
        [
            jnp.pad(w_t, ((0, 0), (0, wide - heads * head_dim))),
            jnp.pad(init_bias.T, ((0, 0), (0, 128 - heads))),
        ],
        axis=1,
    )
    return info, gb, init


def chain_param_grads(dgb, dinit, heads):
    head_dim = dinit.shape[0]
    wide = dinit.shape[1] - 128
    d_w = dinit[:, : heads * head_dim].reshape(head_dim, heads, head_dim).transpose(1, 2, 0)
    d_b = dinit[:, wide : wide + heads].T
    both = jnp.sum(dgb.reshape(2, head_dim, -1, heads, MB), axis=(2, 4))
    return d_w, d_b, both[0].T, both[1].T


def trans_dot(left, right):
    return lax.dot_general(
        left, right, (((0,), (0,)), ((), ())), preferred_element_type=jnp.float32
    )


class HeadPlan:
    def __init__(self, heads, seq, grp):
        self.seq, self.grp, self.heads = seq, grp, heads
        self.local = heads // seq
        self.mixed = (heads // grp) % seq == 0
        self.each = (heads // grp) // seq if self.mixed else 0

    def pick(self, item, seq_index):
        rest = item.shape[1:]
        if self.mixed:
            item = item.reshape((self.grp, self.seq, self.each) + rest)
            item = lax.dynamic_index_in_dim(item, seq_index, 1, keepdims=False)
            return item.reshape((self.local,) + rest)
        return lax.dynamic_slice_in_dim(item, seq_index * self.local, self.local, 0)

    def order(self, item):
        rest = item.shape[2:]
        if self.mixed:
            item = item.reshape((self.seq, self.grp, self.each) + rest)
            item = jnp.swapaxes(item, 0, 1)
        return item.reshape((self.heads,) + rest)


def gather_heads(plan, mats, head_dim):
    rows = mats[0].shape[0]
    count = len(mats)
    if plan.mixed:
        block = jnp.stack(
            [m.reshape(rows, plan.seq, plan.each, head_dim) for m in mats], axis=3
        )
        block = block.transpose(1, 2, 0, 3, 4).reshape(plan.seq, plan.each, rows, -1)
        block = lax.all_to_all(block, "seq", 0, 0, tiled=True)
        block = jnp.swapaxes(block, 0, 1).reshape(plan.each, plan.seq * rows, -1)
        return lax.all_gather(block, "grp", axis=0, tiled=True)
    block = lax.all_gather(jnp.stack(mats), "grp", axis=2, tiled=True)
    block = block.reshape(count, rows, plan.seq, plan.local, head_dim)
    block = block.transpose(2, 3, 1, 0, 4).reshape(plan.seq, plan.local, rows, -1)
    block = lax.all_to_all(block, "seq", 0, 0, tiled=True)
    return jnp.swapaxes(block, 0, 1).reshape(plan.local, plan.seq * rows, -1)


def scatter_heads(plan, grads, count):
    local, all_rows, packed = grads.shape
    rows = all_rows // plan.seq
    head_dim = packed // count
    if plan.mixed:
        grads = lax.psum_scatter(grads, "grp", scatter_dimension=0, tiled=True)
        block = jnp.swapaxes(grads.reshape(plan.each, plan.seq, rows, packed), 0, 1)
        block = lax.all_to_all(block, "seq", 0, 0, tiled=True)
        block = block.reshape(plan.seq * plan.each, rows, count, head_dim)
        out = block.transpose(2, 1, 0, 3).reshape(count, rows, -1)
    else:
        block = jnp.swapaxes(grads.reshape(local, plan.seq, rows, packed), 0, 1)
        block = lax.all_to_all(block, "seq", 0, 0, tiled=True)
        block = block.reshape(plan.heads, rows, count, head_dim)
        block = block.transpose(2, 1, 0, 3).reshape(count, rows, -1)
        out = lax.psum_scatter(block, "grp", scatter_dimension=2, tiled=True)
    return out.astype(jnp.float32)


def to_owner(plan, pair):
    got = lax.all_to_all(pair, "seq", 0, 0, tiled=True)
    tokens, packed = got.shape[2:]
    got = plan.order(got.reshape(plan.seq, plan.local, tokens, 2, packed // 2))
    return got.transpose(2, 1, 0, 3).reshape(2, tokens, -1)


def from_owner(plan, first, second, head_dim):
    tokens = first.shape[0]
    both = jnp.stack([first, second], axis=1).reshape(tokens, 2, plan.heads, head_dim)
    both = both.transpose(2, 0, 1, 3).reshape(plan.heads, tokens, 2 * head_dim)
    if plan.mixed:
        both = both.reshape(plan.grp, plan.seq, plan.each, tokens, 2 * head_dim)
        both = jnp.swapaxes(both, 0, 1)
    both = both.reshape(plan.seq, plan.local, tokens, 2 * head_dim)
    return lax.all_to_all(both, "seq", 0, 0, tiled=True)


def body(
    tokens,
    cotangent,
    lengths,
    prenorm_gain,
    w_query,
    w_key,
    w_value,
    w_gate,
    rate_weight,
    rate_bias,
    init_weight,
    init_bias,
    inner_gain,
    inner_bias,
    post_gain,
    post_bias,
    w_out,
    feedforward_norm_gain,
    w_swish,
    w_up,
    w_down,
):
    seq_index = lax.axis_index("seq")
    grp_index = lax.axis_index("grp")
    groups = lax.axis_size("grp")
    seq = lax.axis_size("seq")
    rows_tok = tokens.shape[1]
    width = tokens.shape[2]
    heads, head_dim, _ = init_weight.shape
    plan = HeadPlan(heads, seq, groups)
    local = plan.local
    stream = rows_tok * seq
    all_rows = groups * rows_tok

    stream_rows = lax.all_gather(tokens[0], "seq", axis=0, tiled=True).astype(F32)
    w_heads = gather_heads(plan, (w_query, w_key, w_value, w_gate), head_dim)
    m_out = lax.all_gather(w_out, "seq", axis=1, tiled=True)
    m_swish = lax.all_gather(w_swish, "seq", axis=0, tiled=True)
    m_up = lax.all_gather(w_up, "seq", axis=0, tiled=True)
    m_down = lax.all_gather(w_down, "seq", axis=1, tiled=True)
    grad_own = cotangent[0]
    grad_rows = lax.all_gather(grad_own, "grp", axis=0, tiled=True)

    own_lengths = lax.dynamic_index_in_dim(lengths, grp_index, 0, keepdims=False)
    ends = jnp.cumsum(own_lengths)
    starts = ends - own_lengths
    live = (jnp.arange(stream, dtype=jnp.int32) < ends[-1]).astype(F32)[:, None]
    block_pos = jnp.arange(stream // MB, dtype=jnp.int32) * MB
    starting = jnp.any(block_pos[:, None] == starts[None, :], -1)

    inv_first = lax.rsqrt(jnp.mean(stream_rows * stream_rows, -1, keepdims=True) + EPS)
    unit_all = stream_rows * inv_first
    normed = (unit_all * prenorm_gain).astype(BF16)
    x4 = lax.dot_general(
        normed, w_heads, (((1,), (1,)), ((), ())), preferred_element_type=F32
    ).astype(BF16)
    x4 = x4.transpose(1, 0, 2)
    rate_cols = plan.pick(rate_weight.T, seq_index).T
    logits = mm(normed, rate_cols) + plan.pick(rate_bias, seq_index)
    rate_sig = jax.nn.sigmoid(logits)
    rates = rate_sig / head_dim * live
    own_params = [
        plan.pick(item, seq_index) for item in (init_weight, init_bias, inner_gain, inner_bias)
    ]
    info, gb, init = chain_setup(starting, rates, *own_params, rows_tok // MB)
    pair, *kept = chain_forward(x4, info, gb, init, rows_tok)
    inner, gate_pre = to_owner(plan, pair).astype(F32)

    mean_o = jnp.mean(inner, -1, keepdims=True)
    inv_o = lax.rsqrt(jnp.mean(inner * inner, -1, keepdims=True) - mean_o * mean_o + EPS)
    o_hat = (inner - mean_o) * inv_o
    post = o_hat * post_gain + post_bias
    gelu_val, gelu_pull = jax.vjp(jax.nn.gelu, gate_pre)
    gated_own = (gelu_val * post).astype(BF16)
    gated = lax.all_to_all(gated_own, "grp", 1, 0, tiled=True)
    mix_part = mm(gated, m_out).astype(BF16)
    mixing = lax.psum_scatter(mix_part, "grp", scatter_dimension=0, tiled=True).astype(F32)
    own_rows = tokens[0].astype(F32)
    resid = own_rows + mixing
    inv_second = lax.rsqrt(jnp.mean(resid * resid, -1, keepdims=True) + EPS)
    unit_second = resid * inv_second
    ffn_in = (unit_second * feedforward_norm_gain).astype(BF16)
    ffn_rows = lax.all_gather(ffn_in, "grp", axis=0, tiled=True)
    act_a = mm(ffn_rows, m_swish)
    act_u = mm(ffn_rows, m_up)
    sig_a = jax.nn.sigmoid(act_a)
    hidden = (act_a * sig_a * act_u).astype(BF16)
    ffn_out = lax.psum_scatter(
        mm(hidden, m_down).astype(BF16), "grp", scatter_dimension=0, tiled=True
    ).astype(F32)
    out_tokens = (resid + ffn_out).astype(BF16)[None]

    d_hidden = mm_nt(grad_rows, m_down)
    g_down = trans_dot(hidden, grad_rows).astype(BF16)
    d_a = (d_hidden * act_u * sig_a * (1.0 + act_a * (1.0 - sig_a))).astype(BF16)
    d_u = (d_hidden * act_a * sig_a).astype(BF16)
    d_ffn_part = (mm_nt(d_a, m_swish) + mm_nt(d_u, m_up)).astype(BF16)
    d_ffn = lax.psum_scatter(d_ffn_part, "grp", scatter_dimension=0, tiled=True).astype(F32)
    g_swish = trans_dot(ffn_rows, d_a).astype(BF16)
    g_up = trans_dot(ffn_rows, d_u).astype(BF16)
    second_scaled = d_ffn * feedforward_norm_gain
    g_ffn_gain = jnp.sum(d_ffn * unit_second, 0)
    d_resid = grad_own.astype(F32) + inv_second * (
        second_scaled - unit_second * jnp.mean(second_scaled * unit_second, -1, keepdims=True)
    )
    d_mix = lax.all_gather(d_resid.astype(BF16), "grp", axis=0, tiled=True)
    d_gated_cols = mm_nt(d_mix, m_out).astype(BF16)
    g_out = trans_dot(gated, d_mix).astype(BF16)
    d_gated = lax.all_to_all(d_gated_cols, "grp", 0, 1, tiled=True).astype(F32)
    d_post = d_gated * gelu_val
    d_gate_pre = gelu_pull(d_gated * post)[0].astype(BF16)
    g_post_gain = jnp.sum(d_post * o_hat, 0)
    g_post_bias = jnp.sum(d_post, 0)
    d_ohat = d_post * post_gain
    d_inner = inv_o * (
        d_ohat
        - jnp.mean(d_ohat, -1, keepdims=True)
        - o_hat * jnp.mean(d_ohat * o_hat, -1, keepdims=True)
    )
    d_pair = from_owner(plan, d_inner.astype(BF16), d_gate_pre, head_dim)
    d_x4, d_rate_rows, d_gb, d_init = chain_backward(x4, d_pair, info, gb, init, kept, rows_tok)
    d_rates = d_rate_rows[0].reshape(stream // MB, local, MB).swapaxes(1, 2).reshape(stream, local)
    d_logits = (d_rates * live * rate_sig * (1.0 - rate_sig) / head_dim).astype(BF16)
    d_normed_part = lax.dot_general(
        d_x4, w_heads, (((0, 2), (0, 2)), ((), ())), preferred_element_type=F32
    ) + mm_nt(d_logits, rate_cols)
    g_pre_gain = jnp.sum(d_normed_part * unit_all, 0)
    d_normed = lax.psum_scatter(
        d_normed_part.astype(BF16), "seq", scatter_dimension=0, tiled=True
    ).astype(F32)
    own_inv = lax.rsqrt(jnp.mean(own_rows * own_rows, -1, keepdims=True) + EPS)
    own_unit = own_rows * own_inv
    first_scaled = d_normed * prenorm_gain
    grad_tokens = (
        d_resid
        + own_inv
        * (first_scaled - own_unit * jnp.mean(first_scaled * own_unit, -1, keepdims=True))
    )[None]
    g_heads = lax.dot_general(
        normed, d_x4, (((0,), (1,)), ((), ())), preferred_element_type=F32
    ).astype(BF16)
    g_heads = scatter_heads(plan, g_heads.transpose(1, 0, 2), 4)
    g_rate_cols = trans_dot(normed, d_logits)
    g_rate_shift = jnp.sum(d_logits.astype(F32), 0)
    head_grads = chain_param_grads(d_gb, d_init, local)
    packed = jnp.concatenate(
        [item.reshape(local, -1) for item in head_grads]
        + [g_rate_cols.T, g_rate_shift[:, None]],
        axis=1,
    )
    packed = jnp.pad(packed, ((0, 0), (0, -packed.shape[1] % 128)))
    packed = plan.order(lax.all_gather(lax.psum(packed, "grp"), "seq", axis=0))
    sizes = (head_dim * head_dim, head_dim, head_dim, head_dim, width, 1)
    small = []
    offset = 0
    for size in sizes:
        small.append(packed[:, offset : offset + size])
        offset += size
    wide = lax.psum((g_post_gain, g_post_bias, g_ffn_gain), ("seq", "grp"))
    g_pre_gain = lax.psum(g_pre_gain, ("seq", "grp"))
    scatter = partial(lax.psum_scatter, axis_name="seq", tiled=True)
    return (
        out_tokens,
        grad_tokens,
        g_pre_gain,
        g_heads[0],
        g_heads[1],
        g_heads[2],
        g_heads[3],
        small[4].T,
        small[5][:, 0],
        small[0].reshape(heads, head_dim, head_dim),
        small[1],
        small[2],
        small[3],
        wide[0],
        wide[1],
        scatter(g_out, scatter_dimension=1).astype(F32),
        wide[2],
        scatter(g_swish, scatter_dimension=0).astype(F32),
        scatter(g_up, scatter_dimension=0).astype(F32),
        scatter(g_down, scatter_dimension=1).astype(F32),
    )


def solution(mesh):
    whole = P()
    rows = P("grp", "seq", None)
    wide = P("seq", "grp")
    tall = P("grp", "seq")
    return jax.shard_map(
        body,
        mesh=mesh,
        in_specs=(rows, rows, whole, whole, wide, wide, wide, wide)
        + (whole,) * 8
        + (tall, whole, wide, wide, tall),
        out_specs=(rows, rows, whole, wide, wide, wide, wide)
        + (whole,) * 8
        + (tall, whole, wide, wide, tall),
        check_vma=False,
    )
```

```python
from functools import partial

import jax
import jax.numpy as jnp
from jax import lax
from jax.experimental import pallas as pl
from jax.experimental.pallas import tpu as pltpu
from jax.sharding import PartitionSpec as P

MB = 16
EPS = 1e-06
F32 = jnp.float32
BF16 = jnp.bfloat16


def mm(left, right):
    return jnp.dot(left, right, preferred_element_type=F32)


def mm_nt(left, right):
    return lax.dot_general(left, right, (((1,), (1,)), ((), ())), preferred_element_type=F32)


def split_two(value):
    high = value.astype(BF16)
    return high, (value - high.astype(F32)).astype(BF16)


def mean_rows(value):
    return jnp.mean(value, axis=0, keepdims=True)


def chunk_rows(ref_value, heads, lanes):
    tokens = ref_value.shape[1]
    parts = [
        ref_value[h, m * MB : (m + 1) * MB, lanes[0] : lanes[1]]
        for m in range(tokens // MB)
        for h in range(heads)
    ]
    return jnp.concatenate(parts, axis=0)


def chunk_masks(info, heads, count):
    step = MB * heads
    row = lax.broadcasted_iota(jnp.int32, (count, count), 0)
    col = lax.broadcasted_iota(jnp.int32, (count, count), 1)
    columns = jnp.transpose(info)
    same = ((row % step) // MB == (col % step) // MB) & (columns[:, 1:2] == info[1:2, :])
    return row // step, col // step, row % MB, col % MB, same, columns


def augment(rows, heads, head_dim, wide):
    count = rows.shape[0]
    near = lax.broadcasted_iota(jnp.int32, (head_dim, wide), 0)
    far = lax.broadcasted_iota(jnp.int32, (head_dim, wide), 1)
    tile = (far % head_dim == near).astype(BF16)
    lane = lax.broadcasted_iota(jnp.int32, (count, wide), 1)
    own = (lax.broadcasted_iota(jnp.int32, (count, wide), 0) % (MB * heads)) // MB
    return jnp.where(lane // head_dim == own, mm(rows, tile), 0.0)


def one_hot_heads(count, heads):
    lane = lax.broadcasted_iota(jnp.int32, (count, 128), 1)
    own = (lax.broadcasted_iota(jnp.int32, (count, 128), 0) % (MB * heads)) // MB
    return (lane == own).astype(BF16)


def forward_kernel(
    heads, idx_ref, x_ref, info_ref, gb_ref, init_ref, out_ref, n_ref, r_ref, nb_ref, stat_ref, w_ref, state
):
    head_dim = gb_ref.shape[1]
    tokens = x_ref.shape[1]
    count = heads * tokens
    full = init_ref.shape[1]
    wide = full - 128

    @pl.when(pl.program_id(0) == 0)
    def _():
        state[...] = init_ref[...]

    carried = state[...]
    w_ref[0] = carried
    info = info_ref[...]
    x = x_ref[...]
    q_rows = chunk_rows(x, heads, (0, head_dim))
    k_rows = chunk_rows(x, heads, (head_dim, 2 * head_dim))
    v_rows = chunk_rows(x, heads, (2 * head_dim, 3 * head_dim))
    q_t = jnp.transpose(q_rows.astype(F32))
    target_t = jnp.transpose(v_rows.astype(F32) - k_rows.astype(F32))
    mb_row, mb_col, t_row, t_col, same, columns = chunk_masks(info, heads, count)
    gram = jnp.where(same & (mb_row < mb_col), mm_nt(k_rows, k_rows) + 1.0, 0.0).astype(BF16)
    cross = jnp.where(
        same & ((mb_row < mb_col) | ((mb_row == mb_col) & (t_row <= t_col))),
        mm_nt(k_rows, q_rows) + 1.0,
        0.0,
    ).astype(BF16)
    hot = one_hot_heads(count, heads)
    k_aug = jnp.concatenate([augment(k_rows, heads, head_dim, wide).astype(BF16), hot], axis=1)
    q_aug = jnp.concatenate([augment(q_rows, heads, head_dim, wide).astype(BF16), hot], axis=1)
    init = init_ref[...]
    stacked = jnp.concatenate(split_two(carried) + split_two(init), axis=0)
    fresh = info[2:3, :] > 0.5

    def through_state(rows):
        both = mm_nt(stacked, rows)
        return jnp.where(
            fresh,
            both[2 * head_dim : 3 * head_dim] + both[3 * head_dim :],
            both[:head_dim] + both[head_dim : 2 * head_dim],
        )

    z_start = through_state(k_aug)
    gain = gb_ref[0]
    shift = gb_ref[1]
    repeats = count // 128
    inner = 128 // (MB * heads)
    done = []
    for p in range(repeats):
        cols = slice(p * 128, (p + 1) * 128)
        z_base = z_start[:, cols]
        if p:
            z_base = z_base - mm(jnp.concatenate(done, axis=1), gram[: p * 128, cols])
        target = target_t[:, cols]
        rate = info[0:1, cols]
        z = z_base
        for step in range(inner):
            if step:
                z = z_base - mm(scaled.astype(BF16), gram[cols, cols])
            centred = z - mean_rows(z)
            inv = lax.rsqrt(mean_rows(centred * centred) + EPS)
            n = centred * inv
            err = (n * gain + shift - target) * gain
            scaled = (rate * inv) * (err - mean_rows(err) - n * mean_rows(err * n))
        done.append(scaled.astype(BF16))
        n_ref[:, cols] = n
        r_ref[:, cols] = scaled
        stat_ref[0:1, cols] = inv
    r_bf = jnp.concatenate(done, axis=1)
    z_bar = through_state(q_aug) - mm(r_bf, cross)
    centred = z_bar - mean_rows(z_bar)
    inv = lax.rsqrt(mean_rows(centred * centred) + EPS)
    nb = centred * inv
    nb_ref[...] = nb
    stat_ref[1:2, :] = inv
    wide_gain = jnp.concatenate([gain] * repeats, axis=1)
    wide_shift = jnp.concatenate([shift] * repeats, axis=1)
    out_rows = jnp.transpose(q_t + nb * wide_gain + wide_shift)
    for m in range(tokens // MB):
        for h in range(heads):
            at = (m * heads + h) * MB
            out_ref[m * MB : (m + 1) * MB, h * head_dim : (h + 1) * head_dim] = out_rows[
                at : at + MB
            ]
    base = jnp.where(info[4:5, 0:1] > 0.5, init, carried)
    state[...] = base - mm((r_ref[...] * info[3:4, :]).astype(BF16), k_aug)


def backward_kernel(
    heads,
    idx_ref,
    x_ref,
    d_ref,
    info_ref,
    gb_ref,
    init_ref,
    n_ref,
    r_ref,
    nb_ref,
    stat_ref,
    w_ref,
    dx_ref,
    dr_ref,
    dgb_ref,
    dinit_ref,
    state,
):
    head_dim = gb_ref.shape[1]
    tokens = x_ref.shape[1]
    count = heads * tokens
    full = init_ref.shape[1]
    wide = full - 128

    @pl.when(pl.program_id(0) == 0)
    def _():
        state[...] = jnp.zeros_like(state)
        dgb_ref[...] = jnp.zeros_like(dgb_ref)
        dinit_ref[...] = jnp.zeros_like(dinit_ref)

    d_end = state[...]
    carried = w_ref[0]
    init = init_ref[...]
    info = info_ref[...]
    x = x_ref[...]
    d_in = d_ref[...]
    q_rows = chunk_rows(x, heads, (0, head_dim))
    k_rows = chunk_rows(x, heads, (head_dim, 2 * head_dim))
    v_rows = chunk_rows(x, heads, (2 * head_dim, 3 * head_dim))
    d_heads = [d_in[:, h * head_dim : (h + 1) * head_dim] for h in range(heads)]
    d_rows = jnp.concatenate(
        [d_heads[h][m * MB : (m + 1) * MB] for m in range(tokens // MB) for h in range(heads)],
        axis=0,
    )
    target_t = jnp.transpose(v_rows.astype(F32) - k_rows.astype(F32))
    d_t = jnp.transpose(d_rows)
    mb_row, mb_col, t_row, t_col, same, columns = chunk_masks(info, heads, count)
    earlier = same & (mb_row < mb_col)
    later = same & (mb_row > mb_col)
    up_to = same & ((mb_row < mb_col) | ((mb_row == mb_col) & (t_row <= t_col)))
    from_on = same & ((mb_row > mb_col) | ((mb_row == mb_col) & (t_row >= t_col)))
    gram = jnp.where(later, mm_nt(k_rows, k_rows) + 1.0, 0.0).astype(BF16)
    cross = jnp.where(from_on, mm_nt(q_rows, k_rows) + 1.0, 0.0).astype(BF16)
    hot = one_hot_heads(count, heads)
    k_aug = jnp.concatenate([augment(k_rows, heads, head_dim, wide).astype(BF16), hot], axis=1)
    q_aug = jnp.concatenate([augment(q_rows, heads, head_dim, wide).astype(BF16), hot], axis=1)
    gain = gb_ref[0]
    shift = gb_ref[1]
    repeats = count // 128
    inner = 128 // (MB * heads)
    wide_gain = jnp.concatenate([gain] * repeats, axis=1)
    nb = nb_ref[...]
    inv_b = stat_ref[1:2, :]
    d_nb = d_t * wide_gain
    d_zbar = inv_b * (d_nb - mean_rows(d_nb) - nb * mean_rows(d_nb * nb))
    scaled_t = r_ref[...]
    last = info[3:4, :]
    dr_base = -mm(d_zbar.astype(BF16), cross) - last * mm_nt(d_end.astype(BF16), k_aug)
    gain_sum = jnp.zeros((head_dim, 128), F32)
    shift_sum = jnp.zeros((head_dim, 128), F32)
    for p in range(repeats):
        cols = slice(p * 128, (p + 1) * 128)
        gain_sum = gain_sum + d_t[:, cols] * nb[:, cols]
        shift_sum = shift_sum + d_t[:, cols]
    done = []
    errs = []
    for p in reversed(range(repeats)):
        cols = slice(p * 128, (p + 1) * 128)
        base = dr_base[:, cols]
        if done:
            base = base - mm(jnp.concatenate(done, axis=1), gram[(p + 1) * 128 :, cols])
        n = n_ref[:, cols]
        inv = stat_ref[0:1, cols]
        rate = info[0:1, cols]
        miss = n * gain + shift - target_t[:, cols]
        err = miss * gain
        along = mean_rows(err * n)
        plain = inv * (err - mean_rows(err) - n * along)
        gain2 = gain * gain
        d_scaled = base
        for step in range(inner):
            if step:
                d_scaled = base - mm(d_z.astype(BF16), gram[cols, cols])
            g = rate * d_scaled
            g_n = mean_rows(g * n)
            d_err = inv * (g - mean_rows(g) - n * g_n)
            d_n = d_err * gain2 - inv * (g * along + err * g_n)
            d_z = inv * (d_n - mean_rows(d_n) - n * (mean_rows(d_n * n) + mean_rows(g * plain)))
        done.insert(0, d_z.astype(BF16))
        errs.insert(0, d_err * gain)
        dr_ref[0:1, cols] = jnp.sum(d_scaled * plain, axis=0, keepdims=True)
        gain_sum = gain_sum + d_err * (miss + gain * n)
        shift_sum = shift_sum + d_err * gain
    dgb_ref[0] += gain_sum
    dgb_ref[1] += shift_sum
    dz_bf = jnp.concatenate(done, axis=1)
    d_z = dz_bf.astype(F32)
    d_errg = jnp.concatenate(errs, axis=1)
    turned = jnp.transpose(jnp.concatenate([d_zbar, scaled_t, d_z, d_errg], axis=0))
    zb_rows = turned[:, :head_dim].astype(BF16)
    r_rows = turned[:, head_dim : 2 * head_dim].astype(BF16)
    z_rows = turned[:, 2 * head_dim : 3 * head_dim].astype(BF16)
    e_rows = turned[:, 3 * head_dim :]
    d_cross = jnp.where(from_on, -mm_nt(zb_rows, r_rows), 0.0).astype(BF16)
    d_cross_t = jnp.where(up_to, -mm_nt(r_rows, zb_rows), 0.0).astype(BF16)
    d_gram = (
        jnp.where(later, -mm_nt(z_rows, r_rows), 0.0)
        + jnp.where(earlier, -mm_nt(r_rows, z_rows), 0.0)
    ).astype(BF16)
    is_init = columns[:, 2:3] > 0.5
    is_last = columns[:, 3:4] > 0.5

    def stack_heads(weight):
        parts = [weight[:, h * head_dim : (h + 1) * head_dim] for h in range(heads)]
        pad = wide - heads * head_dim
        if pad:
            parts.append(jnp.zeros((pad, head_dim), F32))
        return jnp.concatenate(parts, axis=0).astype(BF16)

    w_both = jnp.concatenate([stack_heads(carried), stack_heads(init)], axis=0)
    d_stack = stack_heads(d_end)

    def by_state(rows):
        own = augment(rows, heads, head_dim, wide)
        return jnp.concatenate(
            [jnp.where(is_init, 0.0, own), jnp.where(is_init, own, 0.0)], axis=1
        ).astype(BF16)

    dq = d_rows + mm(d_cross, k_rows) + mm(by_state(zb_rows), w_both)
    r_own = jnp.where(is_last, augment(r_rows, heads, head_dim, wide), 0.0).astype(BF16)
    dk = (
        e_rows
        + mm(d_gram, k_rows)
        + mm(d_cross_t, q_rows)
        + mm(by_state(z_rows), w_both)
        - mm(r_own, d_stack)
    )
    packed = jnp.concatenate([dq.astype(BF16), dk.astype(BF16), (-e_rows).astype(BF16)], axis=1)
    for m in range(tokens // MB):
        for h in range(heads):
            at = (m * heads + h) * MB
            dx_ref[h, m * MB : (m + 1) * MB, :] = packed[at : at + MB]
    row_init = info[2:3, :] > 0.5
    zb_two = jnp.concatenate(
        [jnp.where(row_init, 0.0, d_zbar), jnp.where(row_init, d_zbar, 0.0)], axis=0
    ).astype(BF16)
    z_two = jnp.concatenate(
        [jnp.where(row_init, 0.0, d_z), jnp.where(row_init, d_z, 0.0)], axis=0
    ).astype(BF16)
    d_both = mm(zb_two, q_aug) + mm(z_two, k_aug)
    fresh = info[4:5, 0:1] > 0.5
    state[...] = d_both[:head_dim] + jnp.where(fresh, 0.0, d_end)
    dinit_ref[...] += d_both[head_dim:] + jnp.where(fresh, d_end, 0.0)


def chain_specs(heads, tokens, head_dim, full, at):
    count = heads * tokens
    return dict(
        x=pl.BlockSpec((heads, tokens, 3 * head_dim), lambda i, idx: (0, idx[at(i)], 0)),
        rows=pl.BlockSpec((tokens, heads * head_dim), lambda i, idx: (idx[at(i)], 0)),
        info=pl.BlockSpec((8, count), lambda i, idx: (0, idx[at(i)])),
        gb=pl.BlockSpec((2, head_dim, 128), lambda i, idx: (0, 0, 0)),
        init=pl.BlockSpec((head_dim, full), lambda i, idx: (0, 0)),
        tall=pl.BlockSpec((head_dim, count), lambda i, idx: (0, at(i))),
        stat=pl.BlockSpec((8, count), lambda i, idx: (0, at(i))),
        weight=pl.BlockSpec((1, head_dim, full), lambda i, idx: (at(i), 0, 0)),
    )


def chain_forward(idx, x3, info, gb, init, tokens):
    heads, total, packed = x3.shape
    head_dim = packed // 3
    chunks = total // tokens
    full = init.shape[1]
    s = chain_specs(heads, tokens, head_dim, full, lambda i: i)
    tall = jax.ShapeDtypeStruct((head_dim, heads * total), F32)
    return pl.pallas_call(
        partial(forward_kernel, heads),
        grid_spec=pltpu.PrefetchScalarGridSpec(
            num_scalar_prefetch=1,
            grid=(chunks,),
            in_specs=[s["x"], s["info"], s["gb"], s["init"]],
            out_specs=[s["rows"], s["tall"], s["tall"], s["tall"], s["stat"], s["weight"]],
            scratch_shapes=[pltpu.VMEM((head_dim, full), F32)],
        ),
        out_shape=[
            jax.ShapeDtypeStruct((total, heads * head_dim), F32),
            tall,
            tall,
            tall,
            jax.ShapeDtypeStruct((8, heads * total), F32),
            jax.ShapeDtypeStruct((chunks, head_dim, full), F32),
        ],
        compiler_params=pltpu.CompilerParams(
            dimension_semantics=("arbitrary",), vmem_limit_bytes=32 * 1024 * 1024
        ),
        cost_estimate=pl.CostEstimate(
            flops=20_000_000_000, bytes_accessed=16_000_000, transcendentals=0
        ),
        name="chain_forward",
    )(idx, x3, info, gb, init)


def chain_backward(idx, x3, d_inner, info, gb, init, kept, tokens):
    heads, total, packed = x3.shape
    head_dim = packed // 3
    chunks = total // tokens
    full = init.shape[1]
    s = chain_specs(heads, tokens, head_dim, full, lambda i: chunks - 1 - i)
    return pl.pallas_call(
        partial(backward_kernel, heads),
        grid_spec=pltpu.PrefetchScalarGridSpec(
            num_scalar_prefetch=1,
            grid=(chunks,),
            in_specs=[
                s["x"],
                s["rows"],
                s["info"],
                s["gb"],
                s["init"],
                s["tall"],
                s["tall"],
                s["tall"],
                s["stat"],
                s["weight"],
            ],
            out_specs=[s["x"], s["info"], s["gb"], s["init"]],
            scratch_shapes=[pltpu.VMEM((head_dim, full), F32)],
        ),
        out_shape=[
            jax.ShapeDtypeStruct(x3.shape, BF16),
            jax.ShapeDtypeStruct((8, heads * total), F32),
            jax.ShapeDtypeStruct(gb.shape, F32),
            jax.ShapeDtypeStruct(init.shape, F32),
        ],
        compiler_params=pltpu.CompilerParams(
            dimension_semantics=("arbitrary",), vmem_limit_bytes=40 * 1024 * 1024
        ),
        cost_estimate=pl.CostEstimate(
            flops=30_000_000_000, bytes_accessed=20_000_000, transcendentals=0
        ),
        name="chain_backward",
    )(idx, x3, d_inner, info, gb, init, *kept)


def chain_info(starts, chunk_start, rates, heads, tokens):
    blocks = tokens // MB
    chunks = chunk_start.shape[0]

    def begun(limit):
        return jnp.sum((starts < limit[..., None]).astype(jnp.int32), -1)

    at = chunk_start[:, None] + jnp.arange(blocks, dtype=jnp.int32) * MB
    doc = begun(at + 1)
    before = begun(chunk_start)[:, None]
    end = begun(chunk_start + tokens)[:, None]
    fresh = jnp.broadcast_to(end > before, doc.shape)
    spread = jnp.stack(
        [item.astype(F32) for item in (doc, doc > before, doc == end, fresh)]
    ).reshape(4, chunks * blocks, 1)
    spread = jnp.broadcast_to(spread, (4, chunks * blocks, heads * MB)).reshape(4, -1)
    rate_row = jnp.swapaxes(rates.reshape(-1, MB, heads), 1, 2).reshape(1, -1)
    return jnp.concatenate([rate_row, spread, jnp.zeros((3, rate_row.shape[1]), F32)], axis=0)


def chain_params(init_weight, init_bias, inner_gain, inner_bias):
    heads, head_dim, _ = init_weight.shape
    reps = 128 // (MB * heads)

    def pattern(item):
        row = jnp.broadcast_to(item.T[:, None, :, None], (head_dim, reps, heads, MB))
        return row.reshape(head_dim, 128)

    gb = jnp.stack([pattern(inner_gain), pattern(inner_bias)])
    wide = max(128, heads * head_dim)
    w_t = jnp.transpose(init_weight, (2, 0, 1)).reshape(head_dim, heads * head_dim)
    init = jnp.concatenate(
        [
            jnp.pad(w_t, ((0, 0), (0, wide - heads * head_dim))),
            jnp.pad(init_bias.T, ((0, 0), (0, 128 - heads))),
        ],
        axis=1,
    )
    return gb, init


def chain_param_grads(dgb, dinit, heads):
    head_dim = dinit.shape[0]
    wide = dinit.shape[1] - 128
    d_w = dinit[:, : heads * head_dim].reshape(head_dim, heads, head_dim).transpose(1, 2, 0)
    d_b = dinit[:, wide : wide + heads].T
    both = jnp.sum(dgb.reshape(2, head_dim, -1, heads, MB), axis=(2, 4))
    return d_w, d_b, both[0].T, both[1].T


def trans_dot(left, right):
    return lax.dot_general(
        left, right, (((0,), (0,)), ((), ())), preferred_element_type=jnp.float32
    )


def tie(*values):
    return lax.optimization_barrier(values)


def ring_pairs(size, step):
    order = list(range(0, size, 2)) + list(range(size - 1, 0, -2))
    return [(order[i], order[(i + step) % size]) for i in range(size)]


def ring_place(size, index):
    return jnp.where(index % 2 == 0, index // 2, size - (index + 1) // 2)


def ring_member(size, place):
    return jnp.where(place < size // 2, 2 * place, 2 * (size - place) - 1)


def slot_steps(size):
    steps = [0]
    for s in range(1, size // 2):
        steps += [-s, s]
    return steps + [-(size // 2)]


def ring_gather(block, size):
    arrived = [(block,)]
    ahead = back = block
    for s in range(1, size // 2 + 1):
        ahead = lax.ppermute(ahead, "seq", ring_pairs(size, 1))
        if s < size // 2:
            back = lax.ppermute(back, "seq", ring_pairs(size, -1))
            ahead, back = tie(ahead, back)
            arrived.append((ahead, back))
        else:
            arrived.append((ahead,))
    return arrived


def ring_scatter(part, size):
    half = size // 2
    ahead, back = part(half).astype(BF16), part(1 - half).astype(BF16)
    for s in range(1, half + 1):
        ahead, back = tie(ahead, back)
        ahead = lax.ppermute(ahead, "seq", ring_pairs(size, 1)).astype(F32)
        if s < half:
            back = lax.ppermute(back, "seq", ring_pairs(size, -1)).astype(F32)
            ahead = (ahead + part(half - s)).astype(BF16)
            if s < half - 1:
                back = (back + part(1 - half + s)).astype(BF16)
    return part(0) + ahead + back


def pairwise_sum(value, axis, size):
    bit = 1
    while bit < size:
        value = value + lax.ppermute(value, axis, [(i, i ^ bit) for i in range(size)])
        bit *= 2
    return value


def swap(value, bit):
    return lax.ppermute(value, "grp", [(i, i ^ bit) for i in range(4)])


def grp_gather(value):
    if lax.axis_size("grp") != 4:
        return lax.all_gather(value, "grp", axis=0)
    index = lax.axis_index("grp")
    across = swap(value, 2)
    beside = swap(value, 1)
    corner = swap(across, 1)
    out = jnp.zeros((4,) + value.shape, value.dtype)
    for k, block in enumerate((value, beside, across, corner)):
        out = lax.dynamic_update_index_in_dim(out, block, index ^ k, 0)
    return out


def grp_scatter(value):
    if lax.axis_size("grp") != 4:
        return lax.psum_scatter(value.astype(BF16), "grp", scatter_dimension=0, tiled=False)
    index = lax.axis_index("grp")

    def block(k):
        return lax.dynamic_index_in_dim(value, index ^ k, 0, keepdims=False)

    corner = swap(block(3).astype(BF16), 1).astype(F32)
    across = swap((corner + block(2)).astype(BF16), 2).astype(F32)
    beside = swap(block(1).astype(BF16), 1).astype(F32)
    return (block(0) + beside + across).astype(BF16)


class HeadPlan:
    def __init__(self, heads, seq, grp):
        self.seq, self.grp, self.heads = seq, grp, heads
        self.local = heads // seq
        self.mixed = (heads // grp) % seq == 0
        self.each = (heads // grp) // seq if self.mixed else 0

    def pick(self, item, seq_index):
        rest = item.shape[1:]
        if self.mixed:
            item = item.reshape((self.grp, self.seq, self.each) + rest)
            item = lax.dynamic_index_in_dim(item, seq_index, 1, keepdims=False)
            return item.reshape((self.local,) + rest)
        return lax.dynamic_slice_in_dim(item, seq_index * self.local, self.local, 0)

    def order(self, item):
        rest = item.shape[2:]
        if self.mixed:
            item = item.reshape((self.seq, self.grp, self.each) + rest)
            item = jnp.swapaxes(item, 0, 1)
        return item.reshape((self.heads,) + rest)


def exchange(block):
    return lax.all_to_all(block, "seq", 0, 0, tiled=True)


def gather_heads(plan, mats, head_dim, gather):
    cols = mats[0].shape[1]
    count = len(mats)
    seq = plan.seq
    if plan.mixed:
        block = jnp.stack([m.reshape(seq, plan.each, head_dim, cols) for m in mats], axis=2)
        block = exchange(block.reshape(seq, -1, cols))
        block = block.transpose(1, 0, 2).reshape(plan.each, count * head_dim, seq * cols)
        return gather(block).reshape(plan.local, count * head_dim, seq * cols)
    block = lax.all_gather(jnp.stack(mats), "grp", axis=1, tiled=True)
    block = block.reshape(count, seq, plan.local, head_dim, cols).transpose(1, 2, 0, 3, 4)
    block = exchange(block.reshape(seq, -1, cols))
    return block.transpose(1, 0, 2).reshape(plan.local, count * head_dim, seq * cols)


def scatter_heads(plan, grads, count, scatter):
    local, packed, width = grads.shape
    seq = plan.seq
    cols = width // seq
    head_dim = packed // count
    if plan.mixed:
        block = scatter(grads.reshape(plan.grp, plan.each * packed, width))
        block = block.reshape(-1, seq, cols).transpose(1, 0, 2)
        block = exchange(block).reshape(seq, plan.each, count, head_dim, cols)
        return block.transpose(2, 0, 1, 3, 4).reshape(count, -1, cols).astype(F32)
    block = grads.astype(BF16).reshape(local * packed, seq, cols).transpose(1, 0, 2)
    block = exchange(block).reshape(seq, local, count, head_dim, cols)
    block = block.transpose(2, 0, 1, 3, 4).reshape(count, -1, cols)
    return lax.psum_scatter(block, "grp", scatter_dimension=1, tiled=True).astype(F32)


def body(
    tokens,
    cotangent,
    lengths,
    prenorm_gain,
    w_query,
    w_key,
    w_value,
    w_gate,
    rate_weight,
    rate_bias,
    init_weight,
    init_bias,
    inner_gain,
    inner_bias,
    post_gain,
    post_bias,
    w_out,
    feedforward_norm_gain,
    w_swish,
    w_up,
    w_down,
):
    seq_index = lax.axis_index("seq")
    grp_index = lax.axis_index("grp")
    groups = lax.axis_size("grp")
    seq = lax.axis_size("seq")
    rows_tok = tokens.shape[1]
    width = tokens.shape[2]
    heads, head_dim, _ = init_weight.shape
    plan = HeadPlan(heads, seq, groups)
    local = plan.local
    features = local * head_dim
    stream = rows_tok * seq
    far = partial(lax.all_gather, axis_name="grp", axis=0)
    steps = slot_steps(seq)
    place = ring_place(seq, seq_index)
    member_of_slot = ring_member(seq, (place + jnp.array(steps, jnp.int32)) % seq)
    apart = (ring_place(seq, jnp.arange(seq, dtype=jnp.int32)) - place) % seq
    slot_of_member = jnp.where(apart >= seq // 2, 2 * (seq - apart) - 1, 2 * apart)
    slot_of_member = jnp.where(apart == 0, 0, slot_of_member)
    to_slots = (member_of_slot[:, None] == jnp.arange(seq)[None, :]).astype(F32)

    def in_slots(stat):
        cut = stat.reshape(-1, seq, rows_tok)
        out = jnp.einsum("sm,kmt->kst", to_slots, cut, precision=lax.Precision.HIGHEST)
        return out.reshape(-1, stream)

    def in_order(stat):
        cut = stat.reshape(-1, seq, rows_tok)
        out = jnp.einsum("sm,kst->kmt", to_slots, cut, precision=lax.Precision.HIGHEST)
        return out.reshape(-1, stream)

    def by_distance(rows):
        cut = rows.reshape(seq, rows_tok, width)
        return lambda k: cut[steps.index(k if k < seq // 2 else k - seq)]

    w_proj = gather_heads(plan, (w_query.T, w_key.T, w_value.T), head_dim, grp_gather)
    token_steps = ring_gather(tokens[0], seq)
    stream_rows = jnp.concatenate(sum(token_steps, ()), axis=0).astype(F32)
    w_side = gather_heads(plan, (w_gate.T, w_out), head_dim, grp_gather)
    grad_own, _ = tie(cotangent[0], token_steps[-1][0])
    grad_steps = ring_gather(grad_own, seq)
    share = w_down.shape[0] // seq
    padded = share + -share % MB

    def cut_hidden(mat):
        cut = mat.reshape(seq, share, mat.shape[1])
        return jnp.pad(cut, ((0, 0), (0, padded - share), (0, 0)))

    ffn_block = jnp.concatenate([cut_hidden(m) for m in (w_swish.T, w_up.T, w_down)], axis=1)
    ffn_block, _ = tie(ffn_block, token_steps[-1][0])
    ffn_block = exchange(ffn_block).transpose(1, 0, 2).reshape(3 * padded, width)
    ffn_all = far(ffn_block).reshape(groups, 3, padded, width)
    m_swish, m_up, m_down = (ffn_all[:, i].reshape(groups * padded, width) for i in range(3))
    m_gate = w_side[:, :head_dim].reshape(features, width)
    m_out = w_side[:, head_dim:].reshape(features, width)

    own_lengths = lax.dynamic_index_in_dim(lengths, grp_index, 0, keepdims=False)
    ends = jnp.cumsum(own_lengths)
    starts = ends - own_lengths
    chunk_start = member_of_slot * rows_tok
    positions = (chunk_start[:, None] + jnp.arange(rows_tok, dtype=jnp.int32)).reshape(stream, 1)
    live = (positions < ends[-1]).astype(F32)

    inv_first = lax.rsqrt(jnp.mean(stream_rows * stream_rows, -1, keepdims=True) + EPS)
    unit_all = stream_rows * inv_first
    normed = (unit_all * prenorm_gain).astype(BF16)
    x3 = jnp.stack([mm_nt(normed, w_proj[h]).astype(BF16) for h in range(local)])
    gate_pre = mm_nt(normed, m_gate)
    rate_rows = plan.pick(rate_weight.T, seq_index)
    logits = mm_nt(normed, rate_rows) + plan.pick(rate_bias, seq_index)
    rate_sig = jax.nn.sigmoid(logits)
    rates = rate_sig / head_dim * live
    gb, init = chain_params(
        *(plan.pick(item, seq_index) for item in (init_weight, init_bias, inner_gain, inner_bias))
    )
    info = chain_info(starts, chunk_start, rates, local, rows_tok)
    inner, *kept = chain_forward(slot_of_member, x3, info, gb, init, rows_tok)

    sums = jnp.stack([jnp.sum(inner, -1), jnp.sum(inner * inner, -1)])
    sums = in_slots(pairwise_sum(in_order(sums), "seq", seq)) / width
    mean_o = sums[0][:, None]
    inv_o = lax.rsqrt(sums[1][:, None] - mean_o * mean_o + EPS)
    o_hat = (inner - mean_o) * inv_o
    post_g = plan.pick(post_gain.reshape(heads, head_dim), seq_index).reshape(features)
    post_b = plan.pick(post_bias.reshape(heads, head_dim), seq_index).reshape(features)
    post = o_hat * post_g + post_b
    gelu_val, gelu_pull = jax.vjp(jax.nn.gelu, gate_pre)
    gated = (gelu_val * post).astype(BF16)
    mixing = ring_scatter(by_distance(mm(gated, m_out)), seq)
    own_rows = tokens[0].astype(F32)
    resid = own_rows + mixing
    inv_second = lax.rsqrt(jnp.mean(resid * resid, -1, keepdims=True) + EPS)
    unit_second = resid * inv_second
    ffn_in = (unit_second * feedforward_norm_gain).astype(BF16)

    kept_ffn = []
    for arrived, grads in zip(ring_gather(ffn_in, seq), grad_steps):
        rows = jnp.concatenate(arrived, axis=0)
        grad = jnp.concatenate(grads, axis=0)
        act_a = mm_nt(rows, m_swish)
        act_u = mm_nt(rows, m_up)
        sig_a = jax.nn.sigmoid(act_a)
        hidden = (act_a * sig_a * act_u).astype(BF16)
        d_hidden = mm_nt(grad, m_down)
        d_a = (d_hidden * act_u * sig_a * (1.0 + act_a * (1.0 - sig_a))).astype(BF16)
        d_u = (d_hidden * act_a * sig_a).astype(BF16)
        d_in = mm(d_a, m_swish) + mm(d_u, m_up)
        kept_ffn.append((rows, grad, hidden, d_a, d_u, d_in))
    ffn_rows, grad_rows, hidden, d_a, d_u, d_in = (
        jnp.concatenate(items, axis=0) for items in zip(*kept_ffn)
    )
    d_ffn = ring_scatter(by_distance(d_in), seq)
    g_ffn = jnp.stack(
        [
            trans_dot(left, right).astype(BF16).reshape(groups, padded, width)
            for left, right in ((d_a, ffn_rows), (d_u, ffn_rows), (hidden, grad_rows))
        ],
        axis=1,
    ).reshape(groups, 3 * padded, width)
    g_ffn = lax.psum_scatter(g_ffn, "grp", scatter_dimension=0, tiled=False)
    g_ffn = exchange(g_ffn.reshape(3 * padded, seq, -1).transpose(1, 0, 2))
    g_ffn = g_ffn.reshape(seq, 3, padded, -1)[:, :, :share].transpose(1, 0, 2, 3)
    g_ffn = g_ffn.reshape(3, seq * share, -1).astype(F32)
    ffn_part = mm(hidden, m_down).astype(BF16).reshape(seq, rows_tok, width)
    ffn_part = jnp.take(ffn_part, slot_of_member, axis=0)
    ffn_out = lax.psum_scatter(ffn_part, "seq", scatter_dimension=0, tiled=False).astype(F32)
    out_tokens = (resid + ffn_out).astype(BF16)[None]

    second_scaled = d_ffn * feedforward_norm_gain
    g_ffn_gain = jnp.sum(d_ffn * unit_second, 0)
    d_resid = grad_own.astype(F32) + inv_second * (
        second_scaled - unit_second * jnp.mean(second_scaled * unit_second, -1, keepdims=True)
    )
    mix_steps = ring_gather(d_resid.astype(BF16), seq)
    d_mix = jnp.concatenate(sum(mix_steps, ()), axis=0)
    d_gated = jnp.concatenate(
        [mm_nt(jnp.concatenate(arrived, axis=0), m_out) for arrived in mix_steps], axis=0
    )
    d_post = d_gated * gelu_val
    d_gate_pre = gelu_pull(d_gated * post)[0].astype(BF16)
    g_post_gain = jnp.sum(d_post * o_hat, 0)
    g_post_bias = jnp.sum(d_post, 0)
    d_ohat = d_post * post_g
    sums = jnp.stack([jnp.sum(d_ohat, -1), jnp.sum(d_ohat * o_hat, -1)])
    sums = in_slots(pairwise_sum(in_order(sums), "seq", seq)) / width
    d_inner = inv_o * (d_ohat - sums[0][:, None] - o_hat * sums[1][:, None])
    g_side = jnp.concatenate(
        [
            trans_dot(d_gate_pre, normed).astype(BF16).reshape(local, head_dim, width),
            trans_dot(gated, d_mix).astype(BF16).reshape(local, head_dim, width),
        ],
        axis=1,
    )
    far_sum = partial(lax.psum_scatter, axis_name="grp", scatter_dimension=0, tiled=False)
    g_side = scatter_heads(plan, g_side, 2, far_sum)
    d_x3, d_rate_rows, d_gb, d_init = chain_backward(
        slot_of_member, x3, d_inner, info, gb, init, kept, rows_tok
    )
    d_rates = d_rate_rows[0].reshape(stream // MB, local, MB).swapaxes(1, 2).reshape(stream, local)
    d_logits = (d_rates * live * rate_sig * (1.0 - rate_sig) / head_dim).astype(BF16)
    d_normed_part = mm(d_gate_pre, m_gate) + mm(d_logits, rate_rows)
    for h in range(local):
        d_normed_part = d_normed_part + mm(d_x3[h], w_proj[h])
    d_normed = ring_scatter(by_distance(d_normed_part), seq)
    g_pre_gain = jnp.sum(d_normed_part * unit_all, 0)
    g_proj = jnp.stack([trans_dot(d_x3[h], normed) for h in range(local)])
    g_proj = scatter_heads(plan, g_proj, 3, grp_scatter)
    own_inv = lax.rsqrt(jnp.mean(own_rows * own_rows, -1, keepdims=True) + EPS)
    own_unit = own_rows * own_inv
    first_scaled = d_normed * prenorm_gain
    grad_tokens = (
        d_resid
        + own_inv
        * (first_scaled - own_unit * jnp.mean(first_scaled * own_unit, -1, keepdims=True))
    )[None]

    g_rate_cols = trans_dot(d_logits, normed)
    g_rate_shift = jnp.sum(d_logits.astype(F32), 0)
    parts = [item.reshape(local, -1) for item in chain_param_grads(d_gb, d_init, local)]
    parts += [item.reshape(local, head_dim) for item in (g_post_gain, g_post_bias)]
    parts += [g_rate_cols, g_rate_shift[:, None]]
    sizes = [item.shape[1] for item in parts]
    packed = jnp.concatenate(parts, axis=1)
    packed = jnp.pad(packed, ((0, 0), (0, -packed.shape[1] % 1024)))
    flat = jnp.concatenate([packed.reshape(-1), g_pre_gain, g_ffn_gain]).reshape(-1, 1024)
    flat = pairwise_sum(flat, "grp", groups)
    count = packed.size // 1024
    gains = pairwise_sum(flat[count:], "seq", seq).reshape(2, width)
    blocks = jnp.stack(sum(ring_gather(flat[:count], seq), ()))
    blocks = jnp.take(blocks, slot_of_member, axis=0)
    packed = plan.order(blocks.reshape(seq, local, -1))
    small = []
    offset = 0
    for size in sizes:
        small.append(packed[:, offset : offset + size])
        offset += size
    return (
        out_tokens,
        grad_tokens,
        gains[0],
        g_proj[0].T,
        g_proj[1].T,
        g_proj[2].T,
        g_side[0].T,
        small[6].T,
        small[7][:, 0],
        small[0].reshape(heads, head_dim, head_dim),
        small[1],
        small[2],
        small[3],
        small[4].reshape(width),
        small[5].reshape(width),
        g_side[1],
        gains[1],
        g_ffn[0].T,
        g_ffn[1].T,
        g_ffn[2],
    )


def solution(mesh):
    whole = P()
    rows = P("grp", "seq", None)
    wide = P("seq", "grp")
    tall = P("grp", "seq")
    return jax.shard_map(
        body,
        mesh=mesh,
        in_specs=(rows, rows, whole, whole, wide, wide, wide, wide)
        + (whole,) * 8
        + (tall, whole, wide, wide, tall),
        out_specs=(rows, rows, whole, wide, wide, wide, wide)
        + (whole,) * 8
        + (tall, whole, wide, wide, tall),
        check_vma=False,
    )
```

```python
from functools import partial

import jax
import jax.numpy as jnp
from jax import lax
from jax.experimental import pallas as pl
from jax.experimental.pallas import tpu as pltpu
from jax.sharding import PartitionSpec as P

MB = 16
EPS = 1e-06
F32 = jnp.float32
BF16 = jnp.bfloat16


def mm(left, right):
    return jnp.dot(left, right, preferred_element_type=F32)


def mm_nt(left, right):
    return lax.dot_general(left, right, (((1,), (1,)), ((), ())), preferred_element_type=F32)


def split_two(value):
    high = value.astype(BF16)
    return high, (value - high.astype(F32)).astype(BF16)


def mean_rows(value):
    return jnp.mean(value, axis=0, keepdims=True)


def chunk_rows(value, heads, start, lanes, size):
    tokens = value.shape[0]
    cuts = [value[:, lanes * h + start : lanes * h + start + size] for h in range(heads)]
    parts = [cut[m * MB : (m + 1) * MB] for m in range(tokens // MB) for cut in cuts]
    return jnp.concatenate(parts, axis=0)


def head_rows(rows, heads, h):
    step = MB * heads
    parts = [rows[m * step + h * MB : m * step + (h + 1) * MB] for m in range(rows.shape[0] // step)]
    return jnp.concatenate(parts, axis=0)


def chunk_masks(info, heads, count):
    step = MB * heads
    row = lax.broadcasted_iota(jnp.int32, (count, count), 0)
    col = lax.broadcasted_iota(jnp.int32, (count, count), 1)
    columns = jnp.transpose(info)
    same = ((row % step) // MB == (col % step) // MB) & (columns[:, 1:2] == info[1:2, :])
    return row // step, col // step, row % MB, col % MB, same, columns


def augment(rows, heads, head_dim, wide):
    count = rows.shape[0]
    near = lax.broadcasted_iota(jnp.int32, (head_dim, wide), 0)
    far = lax.broadcasted_iota(jnp.int32, (head_dim, wide), 1)
    tile = (far % head_dim == near).astype(BF16)
    lane = lax.broadcasted_iota(jnp.int32, (count, wide), 1)
    own = (lax.broadcasted_iota(jnp.int32, (count, wide), 0) % (MB * heads)) // MB
    return jnp.where(lane // head_dim == own, mm(rows, tile), 0.0)


def one_hot_heads(count, heads):
    lane = lax.broadcasted_iota(jnp.int32, (count, 128), 1)
    own = (lax.broadcasted_iota(jnp.int32, (count, 128), 0) % (MB * heads)) // MB
    return (lane == own).astype(BF16)


def forward_kernel(
    heads, idx_ref, x_ref, info_ref, gb_ref, init_ref, out_ref, n_ref, r_ref, nb_ref, stat_ref, w_ref, state
):
    head_dim = gb_ref.shape[1]
    tokens = x_ref.shape[0]
    count = heads * tokens
    full = init_ref.shape[1]
    wide = full - 128

    @pl.when(pl.program_id(0) == 0)
    def _():
        state[...] = init_ref[...]

    carried = state[...]
    w_ref[0] = carried
    info = info_ref[...]
    x = x_ref[...]
    q_rows = chunk_rows(x, heads, 0, 3 * head_dim, head_dim)
    k_rows = chunk_rows(x, heads, head_dim, 3 * head_dim, head_dim)
    v_rows = chunk_rows(x, heads, 2 * head_dim, 3 * head_dim, head_dim)
    q_t = jnp.transpose(q_rows.astype(F32))
    target_t = jnp.transpose(v_rows.astype(F32) - k_rows.astype(F32))
    mb_row, mb_col, t_row, t_col, same, columns = chunk_masks(info, heads, count)
    gram = jnp.where(same & (mb_row < mb_col), mm_nt(k_rows, k_rows) + 1.0, 0.0).astype(BF16)
    cross = jnp.where(
        same & ((mb_row < mb_col) | ((mb_row == mb_col) & (t_row <= t_col))),
        mm_nt(k_rows, q_rows) + 1.0,
        0.0,
    ).astype(BF16)
    hot = one_hot_heads(count, heads)
    k_aug = jnp.concatenate([augment(k_rows, heads, head_dim, wide).astype(BF16), hot], axis=1)
    q_aug = jnp.concatenate([augment(q_rows, heads, head_dim, wide).astype(BF16), hot], axis=1)
    init = init_ref[...]
    stacked = jnp.concatenate(split_two(carried) + split_two(init), axis=0)
    fresh = info[2:3, :] > 0.5

    def through_state(rows):
        both = mm_nt(stacked, rows)
        return jnp.where(
            fresh,
            both[2 * head_dim : 3 * head_dim] + both[3 * head_dim :],
            both[:head_dim] + both[head_dim : 2 * head_dim],
        )

    z_start = through_state(k_aug)
    gain = gb_ref[0]
    shift = gb_ref[1]
    repeats = count // 128
    inner = 128 // (MB * heads)
    done = []
    for p in range(repeats):
        cols = slice(p * 128, (p + 1) * 128)
        z_base = z_start[:, cols]
        if p:
            z_base = z_base - mm(jnp.concatenate(done, axis=1), gram[: p * 128, cols])
        target = target_t[:, cols]
        rate = info[0:1, cols]
        z = z_base
        for step in range(inner):
            if step:
                z = z_base - mm(scaled.astype(BF16), gram[cols, cols])
            centred = z - mean_rows(z)
            inv = lax.rsqrt(mean_rows(centred * centred) + EPS)
            n = centred * inv
            err = (n * gain + shift - target) * gain
            scaled = (rate * inv) * (err - mean_rows(err) - n * mean_rows(err * n))
        done.append(scaled.astype(BF16))
        n_ref[:, cols] = n
        r_ref[:, cols] = scaled
        stat_ref[0:1, cols] = inv
    r_bf = jnp.concatenate(done, axis=1)
    z_bar = through_state(q_aug) - mm(r_bf, cross)
    centred = z_bar - mean_rows(z_bar)
    inv = lax.rsqrt(mean_rows(centred * centred) + EPS)
    nb = centred * inv
    nb_ref[...] = nb
    stat_ref[1:2, :] = inv
    wide_gain = jnp.concatenate([gain] * repeats, axis=1)
    wide_shift = jnp.concatenate([shift] * repeats, axis=1)
    out_t = q_t + nb * wide_gain + wide_shift
    stat_ref[2:3, :] = jnp.sum(out_t, axis=0, keepdims=True)
    stat_ref[3:4, :] = jnp.sum(out_t * out_t, axis=0, keepdims=True)
    out_rows = jnp.transpose(out_t)
    for h in range(heads):
        out_ref[:, h * head_dim : (h + 1) * head_dim] = head_rows(out_rows, heads, h)
    base = jnp.where(info[4:5, 0:1] > 0.5, init, carried)
    state[...] = base - mm((r_ref[...] * info[3:4, :]).astype(BF16), k_aug)


def backward_kernel(
    heads,
    idx_ref,
    x_ref,
    d_ref,
    gate_ref,
    info_ref,
    gb_ref,
    init_ref,
    n_ref,
    r_ref,
    nb_ref,
    stat_ref,
    w_ref,
    dx_ref,
    dgb_ref,
    dinit_ref,
    state,
):
    head_dim = gb_ref.shape[1]
    tokens = x_ref.shape[0]
    count = heads * tokens
    full = init_ref.shape[1]
    wide = full - 128

    @pl.when(pl.program_id(0) == 0)
    def _():
        state[...] = jnp.zeros_like(state)
        dgb_ref[...] = jnp.zeros_like(dgb_ref)
        dinit_ref[...] = jnp.zeros_like(dinit_ref)

    d_end = state[...]
    carried = w_ref[0]
    init = init_ref[...]
    info = info_ref[...]
    x = x_ref[...]
    q_rows = chunk_rows(x, heads, 0, 3 * head_dim, head_dim)
    k_rows = chunk_rows(x, heads, head_dim, 3 * head_dim, head_dim)
    v_rows = chunk_rows(x, heads, 2 * head_dim, 3 * head_dim, head_dim)
    d_rows = chunk_rows(d_ref[...], heads, 0, head_dim, head_dim)
    target_t = jnp.transpose(v_rows.astype(F32) - k_rows.astype(F32))
    d_t = jnp.transpose(d_rows)
    mb_row, mb_col, t_row, t_col, same, columns = chunk_masks(info, heads, count)
    earlier = same & (mb_row < mb_col)
    later = same & (mb_row > mb_col)
    up_to = same & ((mb_row < mb_col) | ((mb_row == mb_col) & (t_row <= t_col)))
    from_on = same & ((mb_row > mb_col) | ((mb_row == mb_col) & (t_row >= t_col)))
    gram = jnp.where(later, mm_nt(k_rows, k_rows) + 1.0, 0.0).astype(BF16)
    cross = jnp.where(from_on, mm_nt(q_rows, k_rows) + 1.0, 0.0).astype(BF16)
    hot = one_hot_heads(count, heads)
    k_aug = jnp.concatenate([augment(k_rows, heads, head_dim, wide).astype(BF16), hot], axis=1)
    q_aug = jnp.concatenate([augment(q_rows, heads, head_dim, wide).astype(BF16), hot], axis=1)
    gain = gb_ref[0]
    shift = gb_ref[1]
    repeats = count // 128
    inner = 128 // (MB * heads)
    wide_gain = jnp.concatenate([gain] * repeats, axis=1)
    nb = nb_ref[...]
    inv_b = stat_ref[1:2, :]
    d_nb = d_t * wide_gain
    d_zbar = inv_b * (d_nb - mean_rows(d_nb) - nb * mean_rows(d_nb * nb))
    scaled_t = r_ref[...]
    last = info[3:4, :]
    dr_base = -mm(d_zbar.astype(BF16), cross) - last * mm_nt(d_end.astype(BF16), k_aug)
    gain_sum = jnp.zeros((head_dim, 128), F32)
    shift_sum = jnp.zeros((head_dim, 128), F32)
    for p in range(repeats):
        cols = slice(p * 128, (p + 1) * 128)
        gain_sum = gain_sum + d_t[:, cols] * nb[:, cols]
        shift_sum = shift_sum + d_t[:, cols]
    done = []
    errs = []
    d_rates = []
    for p in reversed(range(repeats)):
        cols = slice(p * 128, (p + 1) * 128)
        base = dr_base[:, cols]
        if done:
            base = base - mm(jnp.concatenate(done, axis=1), gram[(p + 1) * 128 :, cols])
        n = n_ref[:, cols]
        inv = stat_ref[0:1, cols]
        rate = info[0:1, cols]
        miss = n * gain + shift - target_t[:, cols]
        err = miss * gain
        along = mean_rows(err * n)
        plain = inv * (err - mean_rows(err) - n * along)
        gain2 = gain * gain
        d_scaled = base
        for step in range(inner):
            if step:
                d_scaled = base - mm(d_z.astype(BF16), gram[cols, cols])
            g = rate * d_scaled
            g_n = mean_rows(g * n)
            d_err = inv * (g - mean_rows(g) - n * g_n)
            d_n = d_err * gain2 - inv * (g * along + err * g_n)
            d_z = inv * (d_n - mean_rows(d_n) - n * (mean_rows(d_n * n) + mean_rows(g * plain)))
        done.insert(0, d_z.astype(BF16))
        errs.insert(0, d_err * gain)
        d_rates.insert(0, jnp.sum(d_scaled * plain, axis=0, keepdims=True))
        gain_sum = gain_sum + d_err * (miss + gain * n)
        shift_sum = shift_sum + d_err * gain
    dgb_ref[0] += gain_sum
    dgb_ref[1] += shift_sum
    dz_bf = jnp.concatenate(done, axis=1)
    d_z = dz_bf.astype(F32)
    d_errg = jnp.concatenate(errs, axis=1)
    turned = jnp.transpose(jnp.concatenate([d_zbar, scaled_t, d_z, d_errg], axis=0))
    zb_rows = turned[:, :head_dim].astype(BF16)
    r_rows = turned[:, head_dim : 2 * head_dim].astype(BF16)
    z_rows = turned[:, 2 * head_dim : 3 * head_dim].astype(BF16)
    e_rows = turned[:, 3 * head_dim :]
    d_cross = jnp.where(from_on, -mm_nt(zb_rows, r_rows), 0.0).astype(BF16)
    d_cross_t = jnp.where(up_to, -mm_nt(r_rows, zb_rows), 0.0).astype(BF16)
    d_gram = (
        jnp.where(later, -mm_nt(z_rows, r_rows), 0.0)
        + jnp.where(earlier, -mm_nt(r_rows, z_rows), 0.0)
    ).astype(BF16)
    is_init = columns[:, 2:3] > 0.5
    is_last = columns[:, 3:4] > 0.5

    def stack_heads(weight):
        parts = [weight[:, h * head_dim : (h + 1) * head_dim] for h in range(heads)]
        pad = wide - heads * head_dim
        if pad:
            parts.append(jnp.zeros((pad, head_dim), F32))
        return jnp.concatenate(parts, axis=0).astype(BF16)

    w_both = jnp.concatenate([stack_heads(carried), stack_heads(init)], axis=0)
    d_stack = stack_heads(d_end)

    def by_state(rows):
        own = augment(rows, heads, head_dim, wide)
        return jnp.concatenate(
            [jnp.where(is_init, 0.0, own), jnp.where(is_init, own, 0.0)], axis=1
        ).astype(BF16)

    dq = d_rows + mm(d_cross, k_rows) + mm(by_state(zb_rows), w_both)
    r_own = jnp.where(is_last, augment(r_rows, heads, head_dim, wide), 0.0).astype(BF16)
    dk = (
        e_rows
        + mm(d_gram, k_rows)
        + mm(d_cross_t, q_rows)
        + mm(by_state(z_rows), w_both)
        - mm(r_own, d_stack)
    )
    packed = jnp.concatenate([dq.astype(BF16), dk.astype(BF16), (-e_rows).astype(BF16)], axis=1)
    each = 3 * head_dim
    d_logits = jnp.concatenate(d_rates, axis=1) * info[5:6, :]
    turned = jnp.transpose(jnp.concatenate([d_logits, jnp.zeros((7, count), F32)], axis=0))
    lane = lax.broadcasted_iota(jnp.int32, (tokens, 128), 1)
    logit_rows = jnp.zeros((tokens, 128), F32)
    for h in range(heads):
        dx_ref[:, h * each : (h + 1) * each] = head_rows(packed, heads, h)
        logit_rows = jnp.where(lane == h, head_rows(turned, heads, h)[:, 0:1], logit_rows)
    dx_ref[:, heads * each : heads * each + 128] = logit_rows.astype(BF16)
    dx_ref[:, heads * each + 128 :] = gate_ref[...]
    row_init = info[2:3, :] > 0.5
    zb_two = jnp.concatenate(
        [jnp.where(row_init, 0.0, d_zbar), jnp.where(row_init, d_zbar, 0.0)], axis=0
    ).astype(BF16)
    z_two = jnp.concatenate(
        [jnp.where(row_init, 0.0, d_z), jnp.where(row_init, d_z, 0.0)], axis=0
    ).astype(BF16)
    d_both = mm(zb_two, q_aug) + mm(z_two, k_aug)
    fresh = info[4:5, 0:1] > 0.5
    state[...] = d_both[:head_dim] + jnp.where(fresh, 0.0, d_end)
    dinit_ref[...] += d_both[head_dim:] + jnp.where(fresh, d_end, 0.0)


def chain_specs(heads, tokens, head_dim, full, at):
    count = heads * tokens
    return dict(
        x=pl.BlockSpec((tokens, heads * 3 * head_dim), lambda i, idx: (idx[at(i)], 0)),
        dx=pl.BlockSpec((tokens, heads * 4 * head_dim + 128), lambda i, idx: (idx[at(i)], 0)),
        rows=pl.BlockSpec((tokens, heads * head_dim), lambda i, idx: (idx[at(i)], 0)),
        info=pl.BlockSpec((8, count), lambda i, idx: (0, idx[at(i)])),
        gb=pl.BlockSpec((2, head_dim, 128), lambda i, idx: (0, 0, 0)),
        init=pl.BlockSpec((head_dim, full), lambda i, idx: (0, 0)),
        tall=pl.BlockSpec((head_dim, count), lambda i, idx: (0, at(i))),
        stat=pl.BlockSpec((8, count), lambda i, idx: (0, at(i))),
        weight=pl.BlockSpec((1, head_dim, full), lambda i, idx: (at(i), 0, 0)),
    )


def chain_forward(idx, x3, info, gb, init, tokens):
    total = x3.shape[0]
    head_dim = gb.shape[1]
    heads = x3.shape[1] // (3 * head_dim)
    chunks = total // tokens
    full = init.shape[1]
    s = chain_specs(heads, tokens, head_dim, full, lambda i: i)
    tall = jax.ShapeDtypeStruct((head_dim, heads * total), F32)
    return pl.pallas_call(
        partial(forward_kernel, heads),
        grid_spec=pltpu.PrefetchScalarGridSpec(
            num_scalar_prefetch=1,
            grid=(chunks,),
            in_specs=[s["x"], s["info"], s["gb"], s["init"]],
            out_specs=[s["rows"], s["tall"], s["tall"], s["tall"], s["stat"], s["weight"]],
            scratch_shapes=[pltpu.VMEM((head_dim, full), F32)],
        ),
        out_shape=[
            jax.ShapeDtypeStruct((total, heads * head_dim), F32),
            tall,
            tall,
            tall,
            jax.ShapeDtypeStruct((8, heads * total), F32),
            jax.ShapeDtypeStruct((chunks, head_dim, full), F32),
        ],
        compiler_params=pltpu.CompilerParams(
            dimension_semantics=("arbitrary",), vmem_limit_bytes=32 * 1024 * 1024
        ),
        cost_estimate=pl.CostEstimate(
            flops=1, bytes_accessed=1, transcendentals=0
        ),
        name="chain_forward",
    )(idx, x3, info, gb, init)


def chain_backward(idx, x3, d_inner, d_gate, info, gb, init, kept, tokens):
    total = x3.shape[0]
    head_dim = gb.shape[1]
    heads = x3.shape[1] // (3 * head_dim)
    chunks = total // tokens
    full = init.shape[1]
    s = chain_specs(heads, tokens, head_dim, full, lambda i: chunks - 1 - i)
    return pl.pallas_call(
        partial(backward_kernel, heads),
        grid_spec=pltpu.PrefetchScalarGridSpec(
            num_scalar_prefetch=1,
            grid=(chunks,),
            in_specs=[
                s["x"],
                s["rows"],
                s["rows"],
                s["info"],
                s["gb"],
                s["init"],
                s["tall"],
                s["tall"],
                s["tall"],
                s["stat"],
                s["weight"],
            ],
            out_specs=[s["dx"], s["gb"], s["init"]],
            scratch_shapes=[pltpu.VMEM((head_dim, full), F32)],
        ),
        out_shape=[
            jax.ShapeDtypeStruct((total, heads * 4 * head_dim + 128), BF16),
            jax.ShapeDtypeStruct(gb.shape, F32),
            jax.ShapeDtypeStruct(init.shape, F32),
        ],
        compiler_params=pltpu.CompilerParams(
            dimension_semantics=("arbitrary",), vmem_limit_bytes=40 * 1024 * 1024
        ),
        cost_estimate=pl.CostEstimate(
            flops=1, bytes_accessed=1, transcendentals=0
        ),
        name="chain_backward",
    )(idx, x3, d_inner, d_gate, info, gb, init, *kept)


def chain_info(starts, chunk_start, rates, factors, heads, tokens):
    blocks = tokens // MB
    chunks = chunk_start.shape[0]

    def begun(limit):
        return jnp.sum((starts < limit[..., None]).astype(jnp.int32), -1)

    at = chunk_start[:, None] + jnp.arange(blocks, dtype=jnp.int32) * MB
    doc = begun(at + 1)
    before = begun(chunk_start)[:, None]
    end = begun(chunk_start + tokens)[:, None]
    fresh = jnp.broadcast_to(end > before, doc.shape)
    spread = jnp.stack(
        [item.astype(F32) for item in (doc, doc > before, doc == end, fresh)]
    ).reshape(4, chunks * blocks, 1)
    spread = jnp.broadcast_to(spread, (4, chunks * blocks, heads * MB)).reshape(4, -1)

    def as_row(item):
        return jnp.swapaxes(item.reshape(-1, MB, heads), 1, 2).reshape(1, -1)

    rows = [as_row(rates), spread, as_row(factors)]
    return jnp.concatenate(rows + [jnp.zeros((2, spread.shape[1]), F32)], axis=0)


def chain_params(init_weight, init_bias, inner_gain, inner_bias):
    heads, head_dim, _ = init_weight.shape
    reps = 128 // (MB * heads)

    def pattern(item):
        row = jnp.broadcast_to(item.T[:, None, :, None], (head_dim, reps, heads, MB))
        return row.reshape(head_dim, 128)

    gb = jnp.stack([pattern(inner_gain), pattern(inner_bias)])
    wide = max(128, heads * head_dim)
    w_t = jnp.transpose(init_weight, (2, 0, 1)).reshape(head_dim, heads * head_dim)
    init = jnp.concatenate(
        [
            jnp.pad(w_t, ((0, 0), (0, wide - heads * head_dim))),
            jnp.pad(init_bias.T, ((0, 0), (0, 128 - heads))),
        ],
        axis=1,
    )
    return gb, init


def chain_param_grads(dgb, dinit, heads):
    head_dim = dinit.shape[0]
    wide = dinit.shape[1] - 128
    d_w = dinit[:, : heads * head_dim].reshape(head_dim, heads, head_dim).transpose(1, 2, 0)
    d_b = dinit[:, wide : wide + heads].T
    both = jnp.sum(dgb.reshape(2, head_dim, -1, heads, MB), axis=(2, 4))
    return d_w, d_b, both[0].T, both[1].T


def cut_kernel(turned, share, padded, *refs):
    mats, out_ref, held = refs[: len(turned)], refs[-2], refs[-1]
    for i, mat in enumerate(mats):
        value = mat[...].astype(F32)
        held[...] = jnp.transpose(value) if turned[i] else value
        for s in range(out_ref.shape[0]):
            out_ref[s, i * padded : i * padded + share] = held[
                s * share : (s + 1) * share
            ].astype(BF16)
            if padded > share:
                out_ref[s, i * padded + share : (i + 1) * padded] = jnp.zeros(
                    (padded - share, out_ref.shape[2]), BF16
                )


def cut_features(seq, mats, turned):
    features = mats[0].shape[1] if turned[0] else mats[0].shape[0]
    cols = mats[0].shape[0] if turned[0] else mats[0].shape[1]
    share = features // seq
    padded = share + -share % MB
    return pl.pallas_call(
        partial(cut_kernel, turned, share, padded),
        out_shape=jax.ShapeDtypeStruct((seq, len(mats) * padded, cols), BF16),
        scratch_shapes=[pltpu.VMEM((features, cols), F32)],
        compiler_params=pltpu.CompilerParams(vmem_limit_bytes=24 * 1024 * 1024),
        cost_estimate=pl.CostEstimate(flops=1, bytes_accessed=1, transcendentals=0),
        name="cut_features",
    )(*mats)


def join_kernel(turned, share, padded, in_ref, *refs):
    outs, held = refs[:-1], refs[-1]
    for i, out in enumerate(outs):
        for s in range(in_ref.shape[0]):
            held[s * share : (s + 1) * share] = in_ref[
                s, i * padded : i * padded + share
            ].astype(F32)
        out[...] = jnp.transpose(held[...]) if turned[i] else held[...]


def join_features(block, features, turned):
    seq, rows, cols = block.shape
    shapes = [(cols, features) if turn else (features, cols) for turn in turned]
    return pl.pallas_call(
        partial(join_kernel, turned, features // seq, rows // len(turned)),
        out_shape=[jax.ShapeDtypeStruct(shape, F32) for shape in shapes],
        scratch_shapes=[pltpu.VMEM((features, cols), F32)],
        compiler_params=pltpu.CompilerParams(vmem_limit_bytes=24 * 1024 * 1024),
        cost_estimate=pl.CostEstimate(flops=1, bytes_accessed=1, transcendentals=0),
        name="join_features",
    )(block)


def ffn_kernel(count, parts, kept, member_ref, *refs):
    rows_refs = refs[:count]
    grad_refs = refs[count : 2 * count]
    weights = refs[2 * count : 2 * count + parts]
    outs = refs[2 * count + parts + kept :]
    (x_ref, g_ref, at_ref, ut_ref, ht_ref, y_ref, d_ref, a_t, u_t, h_t, y_all, d_all) = outs
    step = pl.program_id(0)
    size = rows_refs[0].shape[0]

    @pl.when(step == 0)
    def _():
        padded = weights[0].shape[0] // 3
        swish, up, down = (
            jnp.concatenate([w[i * padded : (i + 1) * padded] for w in weights], axis=0)
            for i in range(3)
        )
        rows = jnp.concatenate([ref[...] for ref in rows_refs], axis=0)
        grad = jnp.concatenate([ref[0] for ref in grad_refs], axis=0)
        act_a = mm_nt(rows, swish)
        act_u = mm_nt(rows, up)
        d_hidden = mm_nt(grad, down)
        sig = jax.nn.sigmoid(act_a)
        gate = act_a * sig
        hidden = gate * act_u
        d_a = d_hidden * act_u * sig * (1.0 + act_a * (1.0 - sig))
        d_u = d_hidden * gate
        d_all[...] = (mm(d_a.astype(BF16), swish) + mm(d_u.astype(BF16), up)).astype(BF16)
        y_all[...] = mm(hidden.astype(BF16), down).astype(BF16)
        fill = -hidden.shape[1] % 128
        for out, value in ((a_t, d_a), (u_t, d_u), (h_t, hidden)):
            if fill:
                value = jnp.concatenate([value, jnp.zeros((value.shape[0], fill), F32)], axis=1)
            out[...] = jnp.transpose(value)[: out.shape[0]].astype(BF16)

    for i in range(count):

        @pl.when(step == i)
        def _(i=i):
            part = slice(i * size, (i + 1) * size)
            x_ref[...] = rows_refs[i][...]
            g_ref[...] = grad_refs[i][0]
            at_ref[...] = a_t[:, part]
            ut_ref[...] = u_t[:, part]
            ht_ref[...] = h_t[:, part]
            y_ref[0] = y_all[part]
            d_ref[...] = d_all[part]


def ffn_step(members, slot, rows, grad_all, weights, kept):
    count = len(rows)
    size, width = rows[0].shape
    seq = grad_all.shape[0]
    total = seq * size
    features = sum(w.shape[0] for w in weights) // 3
    whole = pl.BlockSpec(memory_space=pltpu.VMEM)

    def grad_spec(i):
        return pl.BlockSpec((1, size, width), lambda s, member: (member[i], 0, 0))

    row_spec = pl.BlockSpec((size, width), lambda s, member: (slot + s, 0))
    turned_spec = pl.BlockSpec((features, size), lambda s, member: (0, slot + s))
    turned = jax.ShapeDtypeStruct((features, total), BF16)
    tall = jax.ShapeDtypeStruct((total, width), BF16)
    first = 1 + 2 * count + len(weights)
    out = pl.pallas_call(
        partial(ffn_kernel, count, len(weights), len(kept)),
        grid_spec=pltpu.PrefetchScalarGridSpec(
            num_scalar_prefetch=1,
            grid=(count,),
            in_specs=[whole] * count
            + [grad_spec(i) for i in range(count)]
            + [whole] * len(weights)
            + [pl.BlockSpec(memory_space=pl.ANY)] * len(kept),
            out_specs=[row_spec, row_spec]
            + [turned_spec] * 3
            + [
                pl.BlockSpec((1, size, width), lambda s, member: (member[s], 0, 0)),
                pl.BlockSpec((size, width), lambda s, member: (s, 0)),
            ],
            scratch_shapes=[pltpu.VMEM((features, count * size), BF16)] * 3
            + [pltpu.VMEM((count * size, width), BF16)] * 2,
        ),
        out_shape=[tall, tall, turned, turned, turned]
        + [
            jax.ShapeDtypeStruct((seq, size, width), BF16),
            jax.ShapeDtypeStruct((count * size, width), BF16),
        ],
        input_output_aliases={first + i: i for i in range(len(kept))},
        compiler_params=pltpu.CompilerParams(
            dimension_semantics=("arbitrary",), vmem_limit_bytes=48 * 1024 * 1024
        ),
        cost_estimate=pl.CostEstimate(
            flops=12_000_000_000, bytes_accessed=1, transcendentals=0
        ),
        name="ffn_step",
    )(members, *rows, *([grad_all] * count), *weights, *kept)
    return out[:-1], out[-1]


def ffn_grad_kernel(parts, at_ref, ut_ref, ht_ref, x_ref, g_ref, *outs):
    x = x_ref[...]
    g = g_ref[...]
    padded = at_ref.shape[0] // parts
    for i, out in enumerate(outs):
        own = slice(i * padded, (i + 1) * padded)
        out[:padded] = mm(at_ref[own], x).astype(BF16)
        out[padded : 2 * padded] = mm(ut_ref[own], x).astype(BF16)
        out[2 * padded :] = mm(ht_ref[own], g).astype(BF16)


def ffn_grads(parts, kept):
    x, g, a_t, u_t, h_t = kept
    total, width = x.shape
    features = a_t.shape[0]
    wide = pl.BlockSpec((total, 256), lambda i: (0, i))
    whole = pl.BlockSpec((features, total), lambda i: (0, 0))
    rows = 3 * features // parts
    return pl.pallas_call(
        partial(ffn_grad_kernel, parts),
        grid=(width // 256,),
        in_specs=[whole] * 3 + [wide] * 2,
        out_specs=[pl.BlockSpec((rows, 256), lambda i: (0, i))] * parts,
        out_shape=[jax.ShapeDtypeStruct((rows, width), BF16)] * parts,
        compiler_params=pltpu.CompilerParams(
            dimension_semantics=("arbitrary",), vmem_limit_bytes=40 * 1024 * 1024
        ),
        cost_estimate=pl.CostEstimate(
            flops=12_000_000_000, bytes_accessed=1, transcendentals=0
        ),
        name="ffn_grads",
    )(a_t, u_t, h_t, x, g)


def proj_grad_kernel(heads, head_dim, d_ref, x_ref, w_ref, *refs):
    outs, rate_ref, gain_ref, turned = refs[:heads], refs[heads], refs[heads + 1], refs[heads + 2]
    each = 3 * head_dim

    @pl.when(pl.program_id(0) == 0)
    def _():
        turned[...] = jnp.transpose(d_ref[...].astype(F32)).astype(BF16)

    grad = mm(turned[...], x_ref[...])
    gain_ref[...] = jnp.broadcast_to(
        jnp.sum(grad * w_ref[...].astype(F32), axis=0, keepdims=True), gain_ref.shape
    )
    gate = heads * each + 128
    for h, out in enumerate(outs):
        out[:each] = grad[h * each : (h + 1) * each].astype(BF16)
        out[each:] = grad[gate + h * head_dim : gate + (h + 1) * head_dim].astype(BF16)
    rate_ref[...] = grad[heads * each : heads * each + 8]


def proj_grads(d_x, normed, weight, heads, head_dim):
    total, packed = d_x.shape
    width = normed.shape[1]

    def wide(rows):
        return pl.BlockSpec((rows, 256), lambda i: (0, i))

    return pl.pallas_call(
        partial(proj_grad_kernel, heads, head_dim),
        grid=(width // 256,),
        in_specs=[pl.BlockSpec((total, packed), lambda i: (0, 0)), wide(total), wide(packed)],
        out_specs=[wide(4 * head_dim)] * heads + [wide(8)] * 2,
        out_shape=[jax.ShapeDtypeStruct((4 * head_dim, width), BF16)] * heads
        + [jax.ShapeDtypeStruct((8, width), F32)] * 2,
        scratch_shapes=[pltpu.VMEM((packed, total), BF16)],
        compiler_params=pltpu.CompilerParams(
            dimension_semantics=("arbitrary",), vmem_limit_bytes=40 * 1024 * 1024
        ),
        cost_estimate=pl.CostEstimate(
            flops=9_000_000_000, bytes_accessed=1, transcendentals=0
        ),
        name="proj_grads",
    )(d_x, normed, weight)


def trans_dot(left, right):
    return lax.dot_general(
        left, right, (((0,), (0,)), ((), ())), preferred_element_type=jnp.float32
    )


def after(value, *first):
    anywhere = pl.BlockSpec(memory_space=pl.ANY)
    return pl.pallas_call(
        lambda *refs: None,
        out_shape=jax.ShapeDtypeStruct(value.shape, value.dtype),
        in_specs=[anywhere] * (1 + len(first)),
        out_specs=anywhere,
        input_output_aliases={0: 0},
        name="after",
    )(value, *first)


def ring_pairs(size, step):
    order = list(range(0, size, 2)) + list(range(size - 1, 0, -2))
    return [(order[i], order[(i + step) % size]) for i in range(size)]


def ring_place(size, index):
    return jnp.where(index % 2 == 0, index // 2, size - (index + 1) // 2)


def ring_member(size, place):
    return jnp.where(place < size // 2, 2 * place, 2 * (size - place) - 1)


def slot_steps(size):
    steps = [0, -(size // 2)]
    for s in range(1, size // 2):
        steps += [-s, s]
    return steps


def by_slots(arrived):
    return [arrived[0], arrived[-1]] + list(arrived[1:-1])


def ring_gather(block, size, work=None):
    arrived = [(block,)]
    ahead = back = block
    for s in range(1, size // 2 + 1):
        done = work(s - 1, arrived[-1]) if work else []
        ahead = lax.ppermute(ahead, "seq", ring_pairs(size, 1))
        if done:
            ahead = after(ahead, *done)
        if s < size // 2:
            back = lax.ppermute(back, "seq", ring_pairs(size, -1))
            arrived.append((ahead, back))
        else:
            arrived.append((ahead,))
    if work:
        work(size // 2, arrived[-1])
    return arrived


def ring_scatter(part, size, work=()):
    half = size // 2
    ahead, back = part(half).astype(BF16), part(1 - half).astype(BF16)
    for s in range(1, half + 1):
        done = work[s - 1](ahead) if s <= len(work) else []
        ahead = lax.ppermute(ahead, "seq", ring_pairs(size, 1))
        if s < half:
            back = lax.ppermute(back, "seq", ring_pairs(size, -1))
        if done:
            ahead = after(ahead, *done)
        ahead = ahead.astype(F32)
        if s < half:
            ahead = (ahead + part(half - s)).astype(BF16)
            if s < half - 1:
                back = (back.astype(F32) + part(1 - half + s)).astype(BF16)
    return part(0).astype(F32) + ahead + back.astype(F32)


def pairwise_sum(value, axis, size):
    bit = 1
    while bit < size:
        value = value + lax.ppermute(value, axis, [(i, i ^ bit) for i in range(size)])
        bit *= 2
    return value


def swap(value, bit):
    return lax.ppermute(value, "grp", [(i, i ^ bit) for i in range(4)])


def near(index, k):
    return index ^ k if lax.axis_size("grp") == 4 else k


def start_gather(value):
    if lax.axis_size("grp") != 4:
        whole = lax.all_gather(value, "grp", axis=0)
        return [whole[k] for k in range(whole.shape[0])]
    return [value, swap(value, 1), swap(value, 2)]


def end_gather(parts):
    if lax.axis_size("grp") != 4:
        return parts
    return parts + [swap(parts[2], 1)]


def start_scatter(block):
    if lax.axis_size("grp") != 4:
        whole = jnp.stack([block(k) for k in range(lax.axis_size("grp"))]).astype(BF16)
        return lax.psum_scatter(whole, "grp", scatter_dimension=0, tiled=False)
    return swap(block(3).astype(BF16), 1)


def cross_scatter(block, corner):
    if lax.axis_size("grp") != 4:
        return corner
    return swap((corner.astype(F32) + block(2)).astype(BF16), 2)


def end_scatter(block, across):
    if lax.axis_size("grp") != 4:
        return across
    beside = swap(block(1).astype(BF16), 1).astype(F32)
    return (block(0) + beside + across.astype(F32)).astype(BF16)


def in_turn(blocks, order):
    picked = [lax.dynamic_index_in_dim(blocks, order[i], 0) for i in range(blocks.shape[0])]
    return jnp.concatenate(picked, axis=0)


class HeadPlan:
    def __init__(self, heads, seq, grp):
        self.seq, self.grp, self.heads = seq, grp, heads
        self.local = heads // seq
        self.mixed = (heads // grp) % seq == 0
        self.each = (heads // grp) // seq if self.mixed else 0

    def pick(self, item, seq_index, grp_index):
        rest = item.shape[1:]
        if self.mixed:
            item = item.reshape((self.grp, self.seq, self.each) + rest)
            item = lax.dynamic_index_in_dim(item, seq_index, 1, keepdims=False)
            return self.turn(item.reshape((self.local,) + rest), grp_index)
        return lax.dynamic_slice_in_dim(item, seq_index * self.local, self.local, 0)

    def turn(self, item, grp_index):
        if not self.mixed:
            return item
        item = item.reshape((self.grp, self.each) + item.shape[1:])
        parts = [
            lax.dynamic_index_in_dim(item, near(grp_index, k), 0, keepdims=False)
            for k in range(self.grp)
        ]
        return jnp.concatenate(parts, axis=0)

    def order(self, item):
        rest = item.shape[2:]
        if self.mixed:
            item = item.reshape((self.seq, self.grp, self.each) + rest)
            item = jnp.swapaxes(item, 0, 1)
        return item.reshape((self.heads,) + rest)


def exchange(block):
    return lax.all_to_all(block, "seq", 0, 0, tiled=True)


def cut_heads(plan, mats, turned, head_dim):
    count = len(mats)
    seq = plan.seq
    if plan.each == 1:
        return cut_features(seq, mats, turned)
    mats = [m.T if turn else m for m, turn in zip(mats, turned)]
    cols = mats[0].shape[1]
    if plan.mixed:
        block = jnp.stack([m.reshape(seq, plan.each, head_dim, cols) for m in mats], axis=2)
    else:
        block = lax.all_gather(jnp.stack(mats), "grp", axis=1, tiled=True)
        block = block.reshape(count, seq, plan.local, head_dim, cols).transpose(1, 2, 0, 3, 4)
    return block.reshape(seq, -1, cols)


def gather_heads(plan, block, count, head_dim):
    seq, _, cols = block.shape
    block = block.transpose(1, 0, 2).reshape(-1, seq * cols)
    parts = end_gather(start_gather(block)) if plan.mixed else [block]
    size = count * head_dim
    return [part[i : i + size] for part in parts for i in range(0, part.shape[0], size)]


def heads_block(plan, grads):
    each = plan.each
    return lambda k: jnp.concatenate(grads[k * each : (k + 1) * each], axis=0)


def scatter_heads(plan, grads, block, count):
    packed, width = grads[0].shape
    seq = plan.seq
    cols = width // seq
    head_dim = packed // count
    if plan.mixed:
        each = plan.each
        block = exchange(block.reshape(-1, seq, cols).transpose(1, 0, 2))
        if each == 1:
            return join_features(block, seq * head_dim, (True,) * count)
        block = block.reshape(seq, each, count, head_dim, cols)
        block = block.transpose(2, 0, 1, 3, 4).reshape(count, -1, cols).astype(F32)
        return [part.T for part in block]
    block = jnp.concatenate(grads, axis=0).astype(BF16)
    block = block.reshape(-1, seq, cols).transpose(1, 0, 2)
    block = exchange(block).reshape(seq, plan.local, count, head_dim, cols)
    block = block.transpose(2, 0, 1, 3, 4).reshape(count, -1, cols)
    block = lax.psum_scatter(block, "grp", scatter_dimension=1, tiled=True).astype(F32)
    return [part.T for part in block]


def body(
    tokens,
    cotangent,
    lengths,
    prenorm_gain,
    w_query,
    w_key,
    w_value,
    w_gate,
    rate_weight,
    rate_bias,
    init_weight,
    init_bias,
    inner_gain,
    inner_bias,
    post_gain,
    post_bias,
    w_out,
    feedforward_norm_gain,
    w_swish,
    w_up,
    w_down,
):
    seq_index = lax.axis_index("seq")
    grp_index = lax.axis_index("grp")
    groups = lax.axis_size("grp")
    seq = lax.axis_size("seq")
    rows_tok = tokens.shape[1]
    width = tokens.shape[2]
    heads, head_dim, _ = init_weight.shape
    plan = HeadPlan(heads, seq, groups)
    local = plan.local
    features = local * head_dim
    stream = rows_tok * seq
    steps = slot_steps(seq)
    place = ring_place(seq, seq_index)
    member_of_slot = ring_member(seq, (place + jnp.array(steps, jnp.int32)) % seq)
    apart = (ring_place(seq, jnp.arange(seq, dtype=jnp.int32)) - place) % seq
    slot_of_member = jnp.where(apart > seq // 2, 2 * (seq - apart), 2 * apart + 1)
    slot_of_member = jnp.where(apart == 0, 0, jnp.where(apart == seq // 2, 1, slot_of_member))
    to_slots = (member_of_slot[:, None] == jnp.arange(seq)[None, :]).astype(F32)

    def in_slots(stat):
        cut = stat.reshape(-1, seq, rows_tok)
        out = jnp.einsum("sm,kmt->kst", to_slots, cut, precision=lax.Precision.HIGHEST)
        return out.reshape(-1, stream)

    def in_order(stat):
        cut = stat.reshape(-1, seq, rows_tok)
        out = jnp.einsum("sm,kst->kmt", to_slots, cut, precision=lax.Precision.HIGHEST)
        return out.reshape(-1, stream)

    def pick(item):
        return plan.pick(item, seq_index, grp_index)

    def by_distance(rows):
        return lambda k: lax.slice_in_dim(
            rows, at_slot(k) * rows_tok, (at_slot(k) + 1) * rows_tok, axis=0
        )

    def at_slot(k):
        return steps.index(k if k < seq // 2 else k - seq)

    own_lengths = lax.dynamic_index_in_dim(lengths, grp_index, 0, keepdims=False)
    ends = jnp.cumsum(own_lengths)
    starts = ends - own_lengths
    chunk_start = member_of_slot * rows_tok
    positions = (chunk_start[:, None] + jnp.arange(rows_tok, dtype=jnp.int32)).reshape(stream, 1)
    live = (positions < ends[-1]).astype(F32)

    proj_block = exchange(
        cut_heads(plan, (w_query, w_key, w_value), (True, True, True), head_dim)
    )
    padded = w_down.shape[0] // seq
    padded += -padded % MB
    token_steps = ring_gather(tokens[0], seq)
    last_tokens = token_steps[-1][0]
    rate_rows = jnp.pad(pick(rate_weight.T), ((0, 128 - local), (0, 0)))
    w_proj = jnp.concatenate(gather_heads(plan, proj_block, 3, head_dim) + [rate_rows], axis=0)
    packed = w_proj.shape[0] - 128
    side_block = cut_heads(plan, (w_gate, w_out), (True, False), head_dim)
    side_block = exchange(after(side_block, last_tokens))
    ffn_block = cut_features(seq, (w_swish, w_up, w_down), (True, True, False))
    ffn_block = exchange(after(ffn_block, last_tokens))
    grad_own = cotangent[0]
    grad_all = lax.all_gather(after(grad_own, ffn_block), "seq", axis=0)

    kept_first = []
    for arrived in token_steps:
        rows = jnp.concatenate(arrived, axis=0).astype(F32)
        inv = lax.rsqrt(jnp.mean(rows * rows, -1, keepdims=True) + EPS)
        unit_gain = (rows * inv * prenorm_gain).astype(BF16)
        out = mm_nt(unit_gain, w_proj)
        kept_first.append((unit_gain, out[:, :packed].astype(BF16), out[:, packed:]))
    normed, x3, logits = (
        jnp.concatenate(items, axis=0) for items in zip(*by_slots(kept_first))
    )
    logits = logits[:, :local] + pick(rate_bias)
    rate_sig = jax.nn.sigmoid(logits)
    rates = rate_sig / head_dim * live
    factors = live * rate_sig * (1.0 - rate_sig) / head_dim
    gb, init = chain_params(*(pick(i) for i in (init_weight, init_bias, inner_gain, inner_bias)))
    info = chain_info(starts, chunk_start, rates, factors, local, rows_tok)
    inner, *kept = chain_forward(slot_of_member, x3, info, gb, init, rows_tok)
    kept_stat = after(kept[3], side_block, ffn_block)

    sides = gather_heads(plan, side_block, 2, head_dim)
    m_gate = jnp.concatenate([side[:head_dim] for side in sides], axis=0)
    m_out = jnp.concatenate([side[head_dim:] for side in sides], axis=0)
    gate_pre = mm_nt(normed, m_gate)
    ffn_block = ffn_block.transpose(1, 0, 2).reshape(3 * padded, width)
    ffn_parts = start_gather(ffn_block)

    sums = jnp.sum(kept_stat[2:4].reshape(2, stream // MB, local, MB), axis=2).reshape(2, stream)
    sums = in_slots(pairwise_sum(sums, "seq", seq)) / width
    mean_o = sums[0][:, None]
    inv_o = lax.rsqrt(sums[1][:, None] - mean_o * mean_o + EPS)
    o_hat = (inner - mean_o) * inv_o
    post_g = pick(post_gain.reshape(heads, head_dim)).reshape(features)
    post_b = pick(post_bias.reshape(heads, head_dim)).reshape(features)
    post = o_hat * post_g + post_b
    gelu_val, gelu_pull = jax.vjp(jax.nn.gelu, gate_pre)
    gated = (gelu_val * post).astype(BF16)
    ffn = {}

    mixing = ring_scatter(
        by_distance(mm(gated, m_out).astype(BF16)),
        seq,
        [lambda since: [], lambda since: [], lambda since: [], lambda since: ffn_parts[2:3]],
    )
    ffn["parts"] = end_gather(ffn_parts)
    own_rows = tokens[0].astype(F32)
    resid = own_rows + mixing
    inv_second = lax.rsqrt(jnp.mean(resid * resid, -1, keepdims=True) + EPS)
    unit_second = resid * inv_second
    ffn_in = (unit_second * feedforward_norm_gain).astype(BF16)

    got = {"kept": ()}
    d_parts = {}

    def step_work(s, arrived):
        slot = 2 * s if s < seq // 2 else 1
        members = lax.slice_in_dim(member_of_slot, slot, slot + len(arrived))
        got["kept"], d_in = ffn_step(
            members, slot, arrived, grad_all, ffn["parts"], got["kept"]
        )
        for i in range(len(arrived)):
            d_parts[steps[slot + i]] = d_in[i * rows_tok : (i + 1) * rows_tok]
        return [d_in]

    ring_gather(ffn_in, seq, step_work)
    kept_ffn = got["kept"]

    def ffn_work(since):
        rows, *others = kept_ffn[:5]
        got["ffn"] = ffn_grads(groups, [after(rows, since)] + others)
        return got["ffn"][:1]

    def ffn_corner(since):
        got["corner"] = start_scatter(ffn_grad)
        got["across"] = cross_scatter(ffn_grad, got["corner"])
        return [got["corner"]]

    def ffn_grad(k):
        return got["ffn"][k]

    d_ffn = ring_scatter(
        lambda k: d_parts[k if k < seq // 2 else k - seq], seq, [ffn_work, ffn_corner]
    )
    ffn_out = lax.psum_scatter(
        after(kept_ffn[5], d_ffn), "seq", scatter_dimension=0, tiled=False
    )
    out_tokens = (resid + ffn_out.astype(F32)).astype(BF16)[None]
    second_scaled = d_ffn * feedforward_norm_gain
    g_ffn_gain = jnp.sum(d_ffn * unit_second, 0)
    d_resid = grad_own.astype(F32) + inv_second * (
        second_scaled - unit_second * jnp.mean(second_scaled * unit_second, -1, keepdims=True)
    )
    mix_steps = ring_gather(d_resid.astype(BF16), seq)
    g_ffn = end_scatter(ffn_grad, got["across"])
    g_ffn = after(g_ffn.reshape(3 * padded, seq, -1).transpose(1, 0, 2), mix_steps[-1][0])
    d_gated = []
    g_out = 0.0
    for s, arrived in enumerate(mix_steps):
        rows = jnp.concatenate(arrived, axis=0)
        first = (2 * s if s < seq // 2 else 1) * rows_tok
        d_gated.append(mm_nt(rows, m_out))
        g_out = g_out + trans_dot(gated[first : first + rows.shape[0]], rows)
    d_gated = jnp.concatenate(by_slots(d_gated), axis=0)
    d_post = d_gated * gelu_val
    d_gate_pre = gelu_pull(d_gated * post)[0].astype(BF16)
    g_post_gain = jnp.sum(d_post * o_hat, 0)
    g_post_bias = jnp.sum(d_post, 0)
    d_ohat = d_post * post_g
    sums = jnp.stack([jnp.sum(d_ohat, -1), jnp.sum(d_ohat * o_hat, -1)])
    sums = in_slots(pairwise_sum(in_order(sums), "seq", seq)) / width
    g_ffn = exchange(after(g_ffn, sums))
    d_inner = inv_o * (d_ohat - sums[0][:, None] - o_hat * sums[1][:, None])
    g_out = g_out.astype(BF16).reshape(local, head_dim, width)
    if plan.mixed:
        g_out = plan.turn(g_out, grp_index).reshape(groups, plan.each * head_dim, width)
        g_out = lax.psum_scatter(g_out, "grp", scatter_dimension=0, tiled=False)
        g_out = g_out.reshape(plan.each, head_dim, width)
    d_x, d_gb, d_init = chain_backward(
        slot_of_member, x3, d_inner, d_gate_pre, info, gb, init, kept, rows_tok
    )
    w_all = jnp.concatenate([w_proj, m_gate], axis=0)
    d_normed_part = after(mm(d_x, w_all).astype(BF16), g_ffn, ffn_out)

    def proj_work(since):
        *got["heads"], got["rates"], got["gain"] = proj_grads(
            d_x, after(normed, since), w_all, local, head_dim
        )
        return got["heads"][:1]

    def heads_work(since):
        if not plan.mixed:
            return []
        block = heads_block(plan, got["heads"])
        got["corner"] = start_scatter(block)
        got["across"] = cross_scatter(block, got["corner"])
        return [got["corner"]]

    d_normed = ring_scatter(by_distance(d_normed_part), seq, [proj_work, heads_work])
    summed = end_scatter(heads_block(plan, got["heads"]), got["across"]) if plan.mixed else None
    g_heads = scatter_heads(plan, got["heads"], summed, 4)
    g_out = exchange(after(g_out, d_normed_part).reshape(-1, seq, width // seq).transpose(1, 0, 2))
    g_out = g_out.reshape(-1, width // seq)
    if not plan.mixed:
        g_out = lax.psum_scatter(g_out, "grp", scatter_dimension=0, tiled=True)
    own_inv = lax.rsqrt(jnp.mean(own_rows * own_rows, -1, keepdims=True) + EPS)
    own_unit = own_rows * own_inv
    first_scaled = d_normed * prenorm_gain
    grad_tokens = (
        d_resid
        + own_inv
        * (first_scaled - own_unit * jnp.mean(first_scaled * own_unit, -1, keepdims=True))
    )[None]

    d_logits = d_x[:, packed : packed + local].astype(F32)
    parts = [item.reshape(local, -1) for item in chain_param_grads(d_gb, d_init, local)]
    parts += [item.reshape(local, head_dim) for item in (g_post_gain, g_post_bias)]
    parts += [got["rates"][:local], jnp.sum(d_logits, 0)[:, None]]
    sizes = [item.shape[1] for item in parts]
    flat = jnp.concatenate(parts, axis=1)
    flat = plan.turn(jnp.pad(flat, ((0, 0), (0, -flat.shape[1] % 1024))), grp_index)
    count = flat.size
    flat = jnp.concatenate([flat.reshape(-1), got["gain"][0] / prenorm_gain, g_ffn_gain])
    flat = pairwise_sum(flat.reshape(-1, 1024), "grp", groups)
    flat = lax.all_gather(flat, "seq", axis=0).reshape(seq, -1)
    gains = jnp.sum(flat[:, count:], 0).reshape(2, width)
    flat = plan.order(flat[:, :count].reshape(seq, local, -1))
    small = []
    offset = 0
    for size in sizes:
        small.append(flat[:, offset : offset + size])
        offset += size
    g_ffn = join_features(g_ffn, w_down.shape[0], (True, True, False))
    return (
        out_tokens,
        grad_tokens,
        gains[0],
        g_heads[0],
        g_heads[1],
        g_heads[2],
        g_heads[3],
        small[6].T,
        small[7][:, 0],
        small[0].reshape(heads, head_dim, head_dim),
        small[1],
        small[2],
        small[3],
        small[4].reshape(width),
        small[5].reshape(width),
        g_out.astype(F32),
        gains[1],
        g_ffn[0],
        g_ffn[1],
        g_ffn[2],
    )


def solution(mesh):
    whole = P()
    rows = P("grp", "seq", None)
    wide = P("seq", "grp")
    tall = P("grp", "seq")
    return jax.shard_map(
        body,
        mesh=mesh,
        in_specs=(rows, rows, whole, whole, wide, wide, wide, wide)
        + (whole,) * 8
        + (tall, whole, wide, wide, tall),
        out_specs=(rows, rows, whole, wide, wide, wide, wide)
        + (whole,) * 8
        + (tall, whole, wide, wide, tall),
        check_vma=False,
    )
```

```python
from functools import partial

import jax
import jax.numpy as jnp
from jax import lax
from jax.experimental import pallas as pl
from jax.experimental.pallas import tpu as pltpu
from jax.sharding import PartitionSpec as P

MB = 16
EPS = 1e-06
F32 = jnp.float32
VMEM_ASKED = 58 * 1024 * 1024
BF16 = jnp.bfloat16


def mm(left, right):
    return jnp.dot(left, right, preferred_element_type=F32)


def mm_nt(left, right):
    return lax.dot_general(left, right, (((1,), (1,)), ((), ())), preferred_element_type=F32)


def split_two(value):
    high = value.astype(BF16)
    return high, (value - high.astype(F32)).astype(BF16)


def mean_rows(value):
    return jnp.mean(value, axis=0, keepdims=True)


def chunk_rows(value, heads, start, lanes, size):
    tokens = value.shape[0]
    cuts = [value[:, lanes * h + start : lanes * h + start + size] for h in range(heads)]
    parts = [cut[m * MB : (m + 1) * MB] for m in range(tokens // MB) for cut in cuts]
    return jnp.concatenate(parts, axis=0)


def head_rows(rows, heads, h):
    step = MB * heads
    parts = [rows[m * step + h * MB : m * step + (h + 1) * MB] for m in range(rows.shape[0] // step)]
    return jnp.concatenate(parts, axis=0)


def chunk_masks(info, heads, count):
    step = MB * heads
    row = lax.broadcasted_iota(jnp.int32, (count, count), 0)
    col = lax.broadcasted_iota(jnp.int32, (count, count), 1)
    columns = jnp.transpose(info)
    same = ((row % step) // MB == (col % step) // MB) & (columns[:, 1:2] == info[1:2, :])
    return row // step, col // step, row % MB, col % MB, same, columns


def chunk_info(docs_ref, logits, heads, head_dim, chunk):
    tokens = logits.shape[0]
    count = heads * tokens
    step = MB * heads
    docs = docs_ref.shape[0] - 1
    pieces = [logits[m * MB : (m + 1) * MB] for m in range(tokens // MB) for _ in range(heads)]
    spread = jnp.concatenate(pieces, axis=0)
    lane = lax.broadcasted_iota(jnp.int32, spread.shape, 1)
    own = (lax.broadcasted_iota(jnp.int32, spread.shape, 0) % step) // MB
    logit = jnp.sum(jnp.transpose(jnp.where(lane == own, spread, 0.0)), axis=0, keepdims=True)
    start = chunk * tokens
    col = lax.broadcasted_iota(jnp.int32, (1, count), 1)
    block_at = start + (col // step) * MB
    doc = jnp.zeros((1, count), jnp.int32)
    before = end = jnp.int32(0)
    for d in range(docs):
        doc = doc + (block_at >= docs_ref[d]).astype(jnp.int32)
        before = before + (docs_ref[d] < start).astype(jnp.int32)
        end = end + (docs_ref[d] < start + tokens).astype(jnp.int32)
    live = (block_at + col % MB < docs_ref[docs]).astype(F32)
    sig = jax.nn.sigmoid(logit)
    zero = jnp.zeros((1, count), F32)
    return jnp.concatenate(
        [
            sig / head_dim * live,
            doc.astype(F32),
            (doc > before).astype(F32),
            (doc == end).astype(F32),
            zero + (end > before).astype(F32),
            live * sig * (1.0 - sig) / head_dim,
            zero,
            zero,
        ],
        axis=0,
    )


def augment(rows, heads, head_dim, wide):
    count = rows.shape[0]
    near = lax.broadcasted_iota(jnp.int32, (head_dim, wide), 0)
    far = lax.broadcasted_iota(jnp.int32, (head_dim, wide), 1)
    tile = (far % head_dim == near).astype(BF16)
    lane = lax.broadcasted_iota(jnp.int32, (count, wide), 1)
    own = (lax.broadcasted_iota(jnp.int32, (count, wide), 0) % (MB * heads)) // MB
    return jnp.where(lane // head_dim == own, mm(rows, tile), 0.0)


def one_hot_heads(count, heads):
    lane = lax.broadcasted_iota(jnp.int32, (count, 128), 1)
    own = (lax.broadcasted_iota(jnp.int32, (count, 128), 0) % (MB * heads)) // MB
    return (lane == own).astype(BF16)


def forward_kernel(
    heads, idx_ref, docs_ref, x_ref, logit_ref, gb_ref, init_ref, out_ref, n_ref, r_ref, nb_ref, stat_ref, w_ref, state
):
    head_dim = gb_ref.shape[1]
    tokens = x_ref.shape[0]
    count = heads * tokens
    full = init_ref.shape[1]
    wide = full - 128

    @pl.when(pl.program_id(0) == 0)
    def _():
        state[...] = init_ref[...]

    carried = state[...]
    w_ref[0] = carried
    info = chunk_info(docs_ref, logit_ref[...], heads, head_dim, pl.program_id(0))
    x = x_ref[...]
    q_rows = chunk_rows(x, heads, 0, 3 * head_dim, head_dim)
    k_rows = chunk_rows(x, heads, head_dim, 3 * head_dim, head_dim)
    v_rows = chunk_rows(x, heads, 2 * head_dim, 3 * head_dim, head_dim)
    q_t = jnp.transpose(q_rows.astype(F32))
    target_t = jnp.transpose(v_rows.astype(F32) - k_rows.astype(F32))
    mb_row, mb_col, t_row, t_col, same, columns = chunk_masks(info, heads, count)
    gram = jnp.where(same & (mb_row < mb_col), mm_nt(k_rows, k_rows) + 1.0, 0.0).astype(BF16)
    cross = jnp.where(
        same & ((mb_row < mb_col) | ((mb_row == mb_col) & (t_row <= t_col))),
        mm_nt(k_rows, q_rows) + 1.0,
        0.0,
    ).astype(BF16)
    hot = one_hot_heads(count, heads)
    k_aug = jnp.concatenate([augment(k_rows, heads, head_dim, wide).astype(BF16), hot], axis=1)
    q_aug = jnp.concatenate([augment(q_rows, heads, head_dim, wide).astype(BF16), hot], axis=1)
    init = init_ref[...]
    stacked = jnp.concatenate(split_two(carried) + split_two(init), axis=0)
    fresh = info[2:3, :] > 0.5

    def through_state(rows):
        both = mm_nt(stacked, rows)
        return jnp.where(
            fresh,
            both[2 * head_dim : 3 * head_dim] + both[3 * head_dim :],
            both[:head_dim] + both[head_dim : 2 * head_dim],
        )

    z_start = through_state(k_aug)
    gain = gb_ref[0]
    shift = gb_ref[1]
    repeats = count // 128
    inner = 128 // (MB * heads)
    done = []
    for p in range(repeats):
        cols = slice(p * 128, (p + 1) * 128)
        z_base = z_start[:, cols]
        if p:
            z_base = z_base - mm(jnp.concatenate(done, axis=1), gram[: p * 128, cols])
        target = target_t[:, cols]
        rate = info[0:1, cols]
        z = z_base
        for step in range(inner):
            if step:
                z = z_base - mm(scaled.astype(BF16), gram[cols, cols])
            centred = z - mean_rows(z)
            inv = lax.rsqrt(mean_rows(centred * centred) + EPS)
            n = centred * inv
            err = (n * gain + shift - target) * gain
            scaled = (rate * inv) * (err - mean_rows(err) - n * mean_rows(err * n))
        done.append(scaled.astype(BF16))
        n_ref[:, cols] = n
        r_ref[:, cols] = scaled
        stat_ref[0:1, cols] = inv
    r_bf = jnp.concatenate(done, axis=1)
    z_bar = through_state(q_aug) - mm(r_bf, cross)
    centred = z_bar - mean_rows(z_bar)
    inv = lax.rsqrt(mean_rows(centred * centred) + EPS)
    nb = centred * inv
    nb_ref[...] = nb
    stat_ref[1:2, :] = inv
    wide_gain = jnp.concatenate([gain] * repeats, axis=1)
    wide_shift = jnp.concatenate([shift] * repeats, axis=1)
    out_t = q_t + nb * wide_gain + wide_shift
    stat_ref[2:3, :] = jnp.sum(out_t, axis=0, keepdims=True)
    stat_ref[3:4, :] = jnp.sum(out_t * out_t, axis=0, keepdims=True)
    out_rows = jnp.transpose(out_t)
    for h in range(heads):
        out_ref[:, h * head_dim : (h + 1) * head_dim] = head_rows(out_rows, heads, h)
    base = jnp.where(info[4:5, 0:1] > 0.5, init, carried)
    state[...] = base - mm((r_ref[...] * info[3:4, :]).astype(BF16), k_aug)


def backward_kernel(
    heads,
    idx_ref,
    docs_ref,
    x_ref,
    d_ref,
    gate_ref,
    logit_ref,
    gb_ref,
    init_ref,
    n_ref,
    r_ref,
    nb_ref,
    stat_ref,
    w_ref,
    dx_ref,
    dgb_ref,
    dinit_ref,
    state,
):
    head_dim = gb_ref.shape[1]
    tokens = x_ref.shape[0]
    count = heads * tokens
    full = init_ref.shape[1]
    wide = full - 128

    @pl.when(pl.program_id(0) == 0)
    def _():
        state[...] = jnp.zeros_like(state)
        dgb_ref[...] = jnp.zeros_like(dgb_ref)
        dinit_ref[...] = jnp.zeros_like(dinit_ref)

    d_end = state[...]
    carried = w_ref[0]
    init = init_ref[...]
    chunk = pl.num_programs(0) - 1 - pl.program_id(0)
    info = chunk_info(docs_ref, logit_ref[...], heads, head_dim, chunk)
    x = x_ref[...]
    q_rows = chunk_rows(x, heads, 0, 3 * head_dim, head_dim)
    k_rows = chunk_rows(x, heads, head_dim, 3 * head_dim, head_dim)
    v_rows = chunk_rows(x, heads, 2 * head_dim, 3 * head_dim, head_dim)
    d_rows = chunk_rows(d_ref[...], heads, 0, head_dim, head_dim)
    target_t = jnp.transpose(v_rows.astype(F32) - k_rows.astype(F32))
    d_t = jnp.transpose(d_rows)
    mb_row, mb_col, t_row, t_col, same, columns = chunk_masks(info, heads, count)
    earlier = same & (mb_row < mb_col)
    later = same & (mb_row > mb_col)
    up_to = same & ((mb_row < mb_col) | ((mb_row == mb_col) & (t_row <= t_col)))
    from_on = same & ((mb_row > mb_col) | ((mb_row == mb_col) & (t_row >= t_col)))
    gram = jnp.where(later, mm_nt(k_rows, k_rows) + 1.0, 0.0).astype(BF16)
    cross = jnp.where(from_on, mm_nt(q_rows, k_rows) + 1.0, 0.0).astype(BF16)
    hot = one_hot_heads(count, heads)
    k_aug = jnp.concatenate([augment(k_rows, heads, head_dim, wide).astype(BF16), hot], axis=1)
    q_aug = jnp.concatenate([augment(q_rows, heads, head_dim, wide).astype(BF16), hot], axis=1)
    gain = gb_ref[0]
    shift = gb_ref[1]
    repeats = count // 128
    inner = 128 // (MB * heads)
    wide_gain = jnp.concatenate([gain] * repeats, axis=1)
    nb = nb_ref[...]
    inv_b = stat_ref[1:2, :]
    d_nb = d_t * wide_gain
    d_zbar = inv_b * (d_nb - mean_rows(d_nb) - nb * mean_rows(d_nb * nb))
    scaled_t = r_ref[...]
    last = info[3:4, :]
    dr_base = -mm(d_zbar.astype(BF16), cross) - last * mm_nt(d_end.astype(BF16), k_aug)
    gain_sum = jnp.zeros((head_dim, 128), F32)
    shift_sum = jnp.zeros((head_dim, 128), F32)
    for p in range(repeats):
        cols = slice(p * 128, (p + 1) * 128)
        gain_sum = gain_sum + d_t[:, cols] * nb[:, cols]
        shift_sum = shift_sum + d_t[:, cols]
    done = []
    errs = []
    d_rates = []
    for p in reversed(range(repeats)):
        cols = slice(p * 128, (p + 1) * 128)
        base = dr_base[:, cols]
        if done:
            base = base - mm(jnp.concatenate(done, axis=1), gram[(p + 1) * 128 :, cols])
        n = n_ref[:, cols]
        inv = stat_ref[0:1, cols]
        rate = info[0:1, cols]
        miss = n * gain + shift - target_t[:, cols]
        err = miss * gain
        along = mean_rows(err * n)
        plain = inv * (err - mean_rows(err) - n * along)
        gain2 = gain * gain
        d_scaled = base
        for step in range(inner):
            if step:
                d_scaled = base - mm(d_z.astype(BF16), gram[cols, cols])
            g = rate * d_scaled
            g_n = mean_rows(g * n)
            d_err = inv * (g - mean_rows(g) - n * g_n)
            d_n = d_err * gain2 - inv * (g * along + err * g_n)
            d_z = inv * (d_n - mean_rows(d_n) - n * (mean_rows(d_n * n) + mean_rows(g * plain)))
        done.insert(0, d_z.astype(BF16))
        errs.insert(0, d_err * gain)
        d_rates.insert(0, jnp.sum(d_scaled * plain, axis=0, keepdims=True))
        gain_sum = gain_sum + d_err * (miss + gain * n)
        shift_sum = shift_sum + d_err * gain
    dgb_ref[0] += gain_sum
    dgb_ref[1] += shift_sum
    dz_bf = jnp.concatenate(done, axis=1)
    d_z = dz_bf.astype(F32)
    d_errg = jnp.concatenate(errs, axis=1)
    turned = jnp.transpose(jnp.concatenate([d_zbar, scaled_t, d_z, d_errg], axis=0))
    zb_rows = turned[:, :head_dim].astype(BF16)
    r_rows = turned[:, head_dim : 2 * head_dim].astype(BF16)
    z_rows = turned[:, 2 * head_dim : 3 * head_dim].astype(BF16)
    e_rows = turned[:, 3 * head_dim :]
    d_cross = jnp.where(from_on, -mm_nt(zb_rows, r_rows), 0.0).astype(BF16)
    d_cross_t = jnp.where(up_to, -mm_nt(r_rows, zb_rows), 0.0).astype(BF16)
    d_gram = (
        jnp.where(later, -mm_nt(z_rows, r_rows), 0.0)
        + jnp.where(earlier, -mm_nt(r_rows, z_rows), 0.0)
    ).astype(BF16)
    is_init = columns[:, 2:3] > 0.5
    is_last = columns[:, 3:4] > 0.5

    def stack_heads(weight):
        parts = [weight[:, h * head_dim : (h + 1) * head_dim] for h in range(heads)]
        pad = wide - heads * head_dim
        if pad:
            parts.append(jnp.zeros((pad, head_dim), F32))
        return jnp.concatenate(parts, axis=0).astype(BF16)

    w_both = jnp.concatenate([stack_heads(carried), stack_heads(init)], axis=0)
    d_stack = stack_heads(d_end)

    def by_state(rows):
        own = augment(rows, heads, head_dim, wide)
        return jnp.concatenate(
            [jnp.where(is_init, 0.0, own), jnp.where(is_init, own, 0.0)], axis=1
        ).astype(BF16)

    dq = d_rows + mm(d_cross, k_rows) + mm(by_state(zb_rows), w_both)
    r_own = jnp.where(is_last, augment(r_rows, heads, head_dim, wide), 0.0).astype(BF16)
    dk = (
        e_rows
        + mm(d_gram, k_rows)
        + mm(d_cross_t, q_rows)
        + mm(by_state(z_rows), w_both)
        - mm(r_own, d_stack)
    )
    packed = jnp.concatenate([dq.astype(BF16), dk.astype(BF16), (-e_rows).astype(BF16)], axis=1)
    each = 3 * head_dim
    d_logits = jnp.concatenate(d_rates, axis=1) * info[5:6, :]
    turned = jnp.transpose(jnp.concatenate([d_logits, jnp.zeros((7, count), F32)], axis=0))
    lane = lax.broadcasted_iota(jnp.int32, (tokens, 128), 1)
    logit_rows = jnp.zeros((tokens, 128), F32)
    for h in range(heads):
        dx_ref[:, h * each : (h + 1) * each] = head_rows(packed, heads, h)
        logit_rows = jnp.where(lane == h, head_rows(turned, heads, h)[:, 0:1], logit_rows)
    dx_ref[:, heads * each : heads * each + 128] = logit_rows.astype(BF16)
    dx_ref[:, heads * each + 128 :] = gate_ref[...]
    row_init = info[2:3, :] > 0.5
    zb_two = jnp.concatenate(
        [jnp.where(row_init, 0.0, d_zbar), jnp.where(row_init, d_zbar, 0.0)], axis=0
    ).astype(BF16)
    z_two = jnp.concatenate(
        [jnp.where(row_init, 0.0, d_z), jnp.where(row_init, d_z, 0.0)], axis=0
    ).astype(BF16)
    d_both = mm(zb_two, q_aug) + mm(z_two, k_aug)
    fresh = info[4:5, 0:1] > 0.5
    state[...] = d_both[:head_dim] + jnp.where(fresh, 0.0, d_end)
    dinit_ref[...] += d_both[head_dim:] + jnp.where(fresh, d_end, 0.0)


def chain_specs(heads, tokens, head_dim, full, at):
    count = heads * tokens
    return dict(
        x=pl.BlockSpec((tokens, heads * 3 * head_dim), lambda i, idx, docs: (idx[at(i)], 0)),
        dx=pl.BlockSpec((tokens, heads * 4 * head_dim + 128), lambda i, idx, docs: (idx[at(i)], 0)),
        rows=pl.BlockSpec((tokens, heads * head_dim), lambda i, idx, docs: (idx[at(i)], 0)),
        logit=pl.BlockSpec((tokens, 128), lambda i, idx, docs: (idx[at(i)], 0)),
        gb=pl.BlockSpec((2, head_dim, 128), lambda i, idx, docs: (0, 0, 0)),
        init=pl.BlockSpec((head_dim, full), lambda i, idx, docs: (0, 0)),
        tall=pl.BlockSpec((head_dim, count), lambda i, idx, docs: (0, at(i))),
        stat=pl.BlockSpec((8, count), lambda i, idx, docs: (0, at(i))),
        weight=pl.BlockSpec((1, head_dim, full), lambda i, idx, docs: (at(i), 0, 0)),
    )


def chain_forward(idx, docs, x3, logits, gb, init, tokens):
    total = x3.shape[0]
    head_dim = gb.shape[1]
    heads = x3.shape[1] // (3 * head_dim)
    chunks = total // tokens
    full = init.shape[1]
    s = chain_specs(heads, tokens, head_dim, full, lambda i: i)
    tall = jax.ShapeDtypeStruct((head_dim, heads * total), F32)
    return pl.pallas_call(
        partial(forward_kernel, heads),
        grid_spec=pltpu.PrefetchScalarGridSpec(
            num_scalar_prefetch=2,
            grid=(chunks,),
            in_specs=[s["x"], s["logit"], s["gb"], s["init"]],
            out_specs=[s["rows"], s["tall"], s["tall"], s["tall"], s["stat"], s["weight"]],
            scratch_shapes=[pltpu.VMEM((head_dim, full), F32)],
        ),
        out_shape=[
            jax.ShapeDtypeStruct((total, heads * head_dim), F32),
            tall,
            tall,
            tall,
            jax.ShapeDtypeStruct((8, heads * total), F32),
            jax.ShapeDtypeStruct((chunks, head_dim, full), F32),
        ],
        compiler_params=pltpu.CompilerParams(
            dimension_semantics=("arbitrary",), vmem_limit_bytes=VMEM_ASKED
        ),
        cost_estimate=pl.CostEstimate(flops=1, bytes_accessed=1, transcendentals=0),
        name="chain_forward",
    )(idx, docs, x3, logits, gb, init)


def chain_backward(idx, docs, x3, d_inner, d_gate, logits, gb, init, kept, tokens):
    total = x3.shape[0]
    head_dim = gb.shape[1]
    heads = x3.shape[1] // (3 * head_dim)
    chunks = total // tokens
    full = init.shape[1]
    s = chain_specs(heads, tokens, head_dim, full, lambda i: chunks - 1 - i)
    return pl.pallas_call(
        partial(backward_kernel, heads),
        grid_spec=pltpu.PrefetchScalarGridSpec(
            num_scalar_prefetch=2,
            grid=(chunks,),
            in_specs=[
                s["x"],
                s["rows"],
                s["rows"],
                s["logit"],
                s["gb"],
                s["init"],
                s["tall"],
                s["tall"],
                s["tall"],
                s["stat"],
                s["weight"],
            ],
            out_specs=[s["dx"], s["gb"], s["init"]],
            scratch_shapes=[pltpu.VMEM((head_dim, full), F32)],
        ),
        out_shape=[
            jax.ShapeDtypeStruct((total, heads * 4 * head_dim + 128), BF16),
            jax.ShapeDtypeStruct(gb.shape, F32),
            jax.ShapeDtypeStruct(init.shape, F32),
        ],
        compiler_params=pltpu.CompilerParams(
            dimension_semantics=("arbitrary",), vmem_limit_bytes=VMEM_ASKED
        ),
        cost_estimate=pl.CostEstimate(flops=1, bytes_accessed=1, transcendentals=0),
        name="chain_backward",
    )(idx, docs, x3, d_inner, d_gate, logits, gb, init, *kept)


def chain_params(init_weight, init_bias, inner_gain, inner_bias):
    heads, head_dim, _ = init_weight.shape
    reps = 128 // (MB * heads)

    def pattern(item):
        row = jnp.broadcast_to(item.T[:, None, :, None], (head_dim, reps, heads, MB))
        return row.reshape(head_dim, 128)

    gb = jnp.stack([pattern(inner_gain), pattern(inner_bias)])
    wide = max(128, heads * head_dim)
    w_t = jnp.transpose(init_weight, (2, 0, 1)).reshape(head_dim, heads * head_dim)
    init = jnp.concatenate(
        [
            jnp.pad(w_t, ((0, 0), (0, wide - heads * head_dim))),
            jnp.pad(init_bias.T, ((0, 0), (0, 128 - heads))),
        ],
        axis=1,
    )
    return gb, init


def chain_param_grads(dgb, dinit, heads):
    head_dim = dinit.shape[0]
    wide = dinit.shape[1] - 128
    d_w = dinit[:, : heads * head_dim].reshape(head_dim, heads, head_dim).transpose(1, 2, 0)
    d_b = dinit[:, wide : wide + heads].T
    both = jnp.sum(dgb.reshape(2, head_dim, -1, heads, MB), axis=(2, 4))
    return d_w, d_b, both[0].T, both[1].T


def cut_kernel(turned, shares, *refs):
    mats, out_ref, held = refs[: len(turned)], refs[-2], refs[-1]
    at = 0
    for mat, turn, share in zip(mats, turned, shares):
        padded = share + -share % MB
        value = mat[...].astype(F32)
        held[: value.shape[1] if turn else value.shape[0]] = jnp.transpose(value) if turn else value
        for s in range(out_ref.shape[0]):
            out_ref[s, at : at + share] = held[s * share : (s + 1) * share].astype(BF16)
            if padded > share:
                out_ref[s, at + share : at + padded] = jnp.zeros(
                    (padded - share, out_ref.shape[2]), BF16
                )
        at += padded


def cut_features(seq, mats, turned):
    features = [m.shape[1] if turn else m.shape[0] for m, turn in zip(mats, turned)]
    cols = mats[0].shape[0] if turned[0] else mats[0].shape[1]
    shares = [count // seq for count in features]
    rows = sum(share + -share % MB for share in shares)
    return pl.pallas_call(
        partial(cut_kernel, turned, shares),
        out_shape=jax.ShapeDtypeStruct((seq, rows, cols), BF16),
        scratch_shapes=[pltpu.VMEM((max(features), cols), F32)],
        compiler_params=pltpu.CompilerParams(vmem_limit_bytes=VMEM_ASKED),
        cost_estimate=pl.CostEstimate(flops=1, bytes_accessed=1, transcendentals=0),
        name="cut_features",
    )(*mats)


def join_kernel(turned, share, padded, in_ref, *refs):
    outs, held = refs[:-1], refs[-1]
    for i, out in enumerate(outs):
        for s in range(in_ref.shape[0]):
            held[s * share : (s + 1) * share] = in_ref[
                s, i * padded : i * padded + share
            ].astype(F32)
        out[...] = jnp.transpose(held[...]) if turned[i] else held[...]


def join_features(block, features, turned):
    seq, rows, cols = block.shape
    shapes = [(cols, features) if turn else (features, cols) for turn in turned]
    return pl.pallas_call(
        partial(join_kernel, turned, features // seq, rows // len(turned)),
        out_shape=[jax.ShapeDtypeStruct(shape, F32) for shape in shapes],
        scratch_shapes=[pltpu.VMEM((features, cols), F32)],
        compiler_params=pltpu.CompilerParams(vmem_limit_bytes=VMEM_ASKED),
        cost_estimate=pl.CostEstimate(flops=1, bytes_accessed=1, transcendentals=0),
        name="join_features",
    )(block)


def ffn_kernel(count, parts, kept, member_ref, *refs):
    rows_refs = refs[:count]
    grad_refs = refs[count : 2 * count]
    weights = refs[2 * count : 2 * count + parts]
    outs = refs[2 * count + parts + kept :]
    (at_ref, ut_ref, ht_ref, y_ref, d_ref, a_t, u_t, h_t, y_all, d_all) = outs
    step = pl.program_id(0)
    size = rows_refs[0].shape[0]

    @pl.when(step == 0)
    def _():
        padded = weights[0].shape[0] // 3
        swish, up, down = (
            jnp.concatenate([w[i * padded : (i + 1) * padded] for w in weights], axis=0)
            for i in range(3)
        )
        rows = jnp.concatenate([ref[...] for ref in rows_refs], axis=0)
        grad = jnp.concatenate([ref[...] for ref in grad_refs], axis=0)
        act_a = mm_nt(rows, swish)
        act_u = mm_nt(rows, up)
        d_hidden = mm_nt(grad, down)
        sig = jax.nn.sigmoid(act_a)
        gate = act_a * sig
        hidden = gate * act_u
        d_a = d_hidden * act_u * sig * (1.0 + act_a * (1.0 - sig))
        d_u = d_hidden * gate
        d_all[...] = (mm(d_a.astype(BF16), swish) + mm(d_u.astype(BF16), up)).astype(BF16)
        y_all[...] = mm(hidden.astype(BF16), down).astype(BF16)
        fill = -hidden.shape[1] % 128
        for out, value in ((a_t, d_a), (u_t, d_u), (h_t, hidden)):
            if fill:
                value = jnp.concatenate([value, jnp.zeros((value.shape[0], fill), F32)], axis=1)
            out[...] = jnp.transpose(value)[: out.shape[0]].astype(BF16)

    for i in range(count):

        @pl.when(step == i)
        def _(i=i):
            part = slice(i * size, (i + 1) * size)
            at_ref[...] = a_t[:, part]
            ut_ref[...] = u_t[:, part]
            ht_ref[...] = h_t[:, part]
            y_ref[0] = y_all[part]
            d_ref[...] = d_all[part]


def ffn_step(members, seq, slot, rows, grads, weights, kept):
    count = len(rows)
    size, width = rows[0].shape
    total = seq * size
    features = sum(w.shape[0] for w in weights) // 3
    whole = pl.BlockSpec(memory_space=pltpu.VMEM)

    turned_spec = pl.BlockSpec((features, size), lambda s, member: (0, slot + s))
    turned = jax.ShapeDtypeStruct((features, total), BF16)
    first = 1 + 2 * count + len(weights)
    out = pl.pallas_call(
        partial(ffn_kernel, count, len(weights), len(kept)),
        grid_spec=pltpu.PrefetchScalarGridSpec(
            num_scalar_prefetch=1,
            grid=(count,),
            in_specs=[whole] * (2 * count + len(weights))
            + [pl.BlockSpec(memory_space=pl.ANY)] * len(kept),
            out_specs=[turned_spec] * 3
            + [
                pl.BlockSpec((1, size, width), lambda s, member: (member[s], 0, 0)),
                pl.BlockSpec((size, width), lambda s, member: (s, 0)),
            ],
            scratch_shapes=[pltpu.VMEM((features, count * size), BF16)] * 3
            + [pltpu.VMEM((count * size, width), BF16)] * 2,
        ),
        out_shape=[turned] * 3
        + [
            jax.ShapeDtypeStruct((seq, size, width), BF16),
            jax.ShapeDtypeStruct((count * size, width), BF16),
        ],
        input_output_aliases={first + i: i for i in range(len(kept))},
        compiler_params=pltpu.CompilerParams(
            dimension_semantics=("arbitrary",), vmem_limit_bytes=VMEM_ASKED
        ),
        cost_estimate=pl.CostEstimate(flops=1, bytes_accessed=1, transcendentals=0),
        name="ffn_step",
    )(members, *rows, *grads, *weights, *kept)
    return out[:-1], out[-1]


def ffn_grad_kernel(parts, count, at_ref, ut_ref, ht_ref, *refs):
    x = jnp.concatenate([ref[...] for ref in refs[:count]], axis=0)
    g = jnp.concatenate([ref[...] for ref in refs[count : 2 * count]], axis=0)
    padded = at_ref.shape[0] // parts
    for i, out in enumerate(refs[2 * count :]):
        own = slice(i * padded, (i + 1) * padded)
        out[:padded] = mm(at_ref[own], x).astype(BF16)
        out[padded : 2 * padded] = mm(ut_ref[own], x).astype(BF16)
        out[2 * padded :] = mm(ht_ref[own], g).astype(BF16)


def ffn_grads(parts, turned, rows, grads):
    size, width = rows[0].shape
    count = len(rows)
    features = turned[0].shape[0]
    wide = pl.BlockSpec((size, 256), lambda i: (0, i))
    whole = pl.BlockSpec((features, count * size), lambda i: (0, 0))
    each = 3 * features // parts
    return pl.pallas_call(
        partial(ffn_grad_kernel, parts, count),
        grid=(width // 256,),
        in_specs=[whole] * 3 + [wide] * (2 * count),
        out_specs=[pl.BlockSpec((each, 256), lambda i: (0, i))] * parts,
        out_shape=[jax.ShapeDtypeStruct((each, width), BF16)] * parts,
        compiler_params=pltpu.CompilerParams(
            dimension_semantics=("arbitrary",), vmem_limit_bytes=VMEM_ASKED
        ),
        cost_estimate=pl.CostEstimate(flops=1, bytes_accessed=1, transcendentals=0),
        name="ffn_grads",
    )(*turned, *rows, *grads)


def proj_grad_kernel(heads, head_dim, d_ref, x_ref, w_ref, gated_ref, *refs):
    count = len(refs) - heads - 4
    mix = refs[:count]
    outs, rate_ref, gain_ref = refs[count : count + heads], refs[-4], refs[-3]
    turned, gated_turned = refs[-2:]
    each = 3 * head_dim

    @pl.when(pl.program_id(0) == 0)
    def _():
        turned[...] = jnp.transpose(d_ref[...].astype(F32)).astype(BF16)
        gated_turned[...] = jnp.transpose(gated_ref[...].astype(F32)).astype(BF16)

    grad = mm(turned[...], x_ref[...])
    grad_out = mm(gated_turned[...], jnp.concatenate([ref[...] for ref in mix], axis=0))
    gain_ref[...] = jnp.broadcast_to(
        jnp.sum(grad * w_ref[...].astype(F32), axis=0, keepdims=True), gain_ref.shape
    )
    gate = heads * each + 128
    for h, out in enumerate(outs):
        own = slice(h * head_dim, (h + 1) * head_dim)
        out[:each] = grad[h * each : (h + 1) * each].astype(BF16)
        out[each : each + head_dim] = grad[gate + h * head_dim : gate + (h + 1) * head_dim].astype(
            BF16
        )
        out[each + head_dim :] = grad_out[own].astype(BF16)
    rate_ref[...] = grad[heads * each : heads * each + 8]


def proj_grads(d_x, normed, weight, gated, mix, heads, head_dim):
    total, packed = d_x.shape
    width = normed.shape[1]

    def wide(rows):
        return pl.BlockSpec((rows, 256), lambda i: (0, i))

    def whole(array):
        return pl.BlockSpec(array.shape, lambda i: (0, 0))

    return pl.pallas_call(
        partial(proj_grad_kernel, heads, head_dim),
        grid=(width // 256,),
        in_specs=[whole(d_x), wide(total), wide(packed), whole(gated)]
        + [wide(block.shape[0]) for block in mix],
        out_specs=[wide(5 * head_dim)] * heads + [wide(8)] * 2,
        out_shape=[jax.ShapeDtypeStruct((5 * head_dim, width), BF16)] * heads
        + [jax.ShapeDtypeStruct((8, width), F32)] * 2,
        scratch_shapes=[pltpu.VMEM((packed, total), BF16), pltpu.VMEM(gated.shape[::-1], BF16)],
        compiler_params=pltpu.CompilerParams(
            dimension_semantics=("arbitrary",), vmem_limit_bytes=VMEM_ASKED
        ),
        cost_estimate=pl.CostEstimate(flops=1, bytes_accessed=1, transcendentals=0),
        name="proj_grads",
    )(d_x, normed, weight, gated, *mix)


def project_kernel(count, parts, *refs):
    blocks = refs[:count]
    weights = refs[count : count + parts]
    rate_ref, bias_ref, gain_ref, normed_ref, x_ref, logit_ref = refs[count + parts :]
    size = blocks[0].shape[0]
    packed = x_ref.shape[1]
    for i in range(0, count, 2):

        @pl.when(pl.program_id(0) == i // 2)
        def _(i=i):
            rows = jnp.concatenate([ref[...] for ref in blocks[i : i + 2]], axis=0).astype(F32)
            inv = lax.rsqrt(jnp.mean(rows * rows, -1, keepdims=True) + EPS)
            normed = (rows * inv * gain_ref[...]).astype(BF16)
            normed_ref[...] = normed
            weight = jnp.concatenate([ref[...] for ref in weights] + [rate_ref[...]], axis=0)
            out = mm_nt(normed, weight)
            x_ref[...] = out[:, :packed].astype(BF16)
            logit_ref[...] = out[:, packed:] + bias_ref[...]


def project(blocks, weights, rate_rows, bias, gain):
    size, width = blocks[0].shape
    count = len(blocks)
    total = count * size
    packed = sum(w.shape[0] for w in weights)

    def rows(lanes):
        return pl.BlockSpec((2 * size, lanes), lambda i: (i, 0))

    return pl.pallas_call(
        partial(project_kernel, count, len(weights)),
        grid=(count // 2,),
        in_specs=[pl.BlockSpec(memory_space=pltpu.VMEM)] * (count + len(weights) + 3),
        out_specs=[rows(width), rows(packed), rows(128)],
        out_shape=[
            jax.ShapeDtypeStruct((total, width), BF16),
            jax.ShapeDtypeStruct((total, packed), BF16),
            jax.ShapeDtypeStruct((total, 128), F32),
        ],
        compiler_params=pltpu.CompilerParams(
            dimension_semantics=("arbitrary",), vmem_limit_bytes=VMEM_ASKED
        ),
        cost_estimate=pl.CostEstimate(flops=1, bytes_accessed=1, transcendentals=0),
        name="project",
    )(*blocks, *weights, rate_rows, bias, gain)


def trans_dot(left, right):
    return lax.dot_general(
        left, right, (((0,), (0,)), ((), ())), preferred_element_type=jnp.float32
    )


def after(value, *first):
    anywhere = pl.BlockSpec(memory_space=pl.ANY)
    return pl.pallas_call(
        lambda *refs: None,
        out_shape=jax.ShapeDtypeStruct(value.shape, value.dtype),
        in_specs=[anywhere] * (1 + len(first)),
        out_specs=anywhere,
        input_output_aliases={0: 0},
        name="after",
    )(value, *first)


def ring_pairs(size, step):
    order = list(range(0, size, 2)) + list(range(size - 1, 0, -2))
    return [(order[i], order[(i + step) % size]) for i in range(size)]


def ring_place(size, index):
    return jnp.where(index % 2 == 0, index // 2, size - (index + 1) // 2)


def ring_member(size, place):
    return jnp.where(place < size // 2, 2 * place, 2 * (size - place) - 1)


def slot_steps(size):
    steps = [0, -(size // 2)]
    for s in range(1, size // 2):
        steps += [-s, s]
    return steps


def by_slots(arrived):
    return [arrived[0], arrived[-1]] + list(arrived[1:-1])


def ring_gather(block, size, work=None, beside=None):
    arrived = [(block,)]
    others = [(beside,)]
    ahead = back = block
    ahead_too = back_too = beside

    def move(value, step):
        return None if value is None else lax.ppermute(value, "seq", ring_pairs(size, step))

    def do_work(s):
        if not work:
            return []
        return list(work(s, arrived[s], others[s]) if beside is not None else work(s, arrived[s]))

    for s in range(1, size // 2 + 1):
        last = s == size // 2
        done = do_work(s - 1)
        ahead, ahead_too = move(ahead, 1), move(ahead_too, 1)
        if not last:
            back, back_too = move(back, -1), move(back_too, -1)
            done += [back, back_too]
        done = [item for item in done + [ahead_too] if item is not None]
        if done:
            ahead = after(ahead, *done)
        arrived.append((ahead,) if last else (ahead, back))
        others.append((ahead_too,) if last else (ahead_too, back_too))
    do_work(size // 2)
    return arrived


def ring_scatter(part, size, work=()):
    half = size // 2
    ahead, back = part(half).astype(BF16), part(1 - half).astype(BF16)
    for s in range(1, half + 1):
        done = work[s - 1](ahead) if s <= len(work) else []
        ahead = lax.ppermute(ahead, "seq", ring_pairs(size, 1))
        if s < half:
            back = lax.ppermute(back, "seq", ring_pairs(size, -1))
            done = list(done) + [back]
        if done:
            ahead = after(ahead, *done)
        if s < half:
            back = after(back, ahead)
        ahead = ahead.astype(F32)
        if s < half:
            ahead = (ahead + part(half - s)).astype(BF16)
            if s < half - 1:
                back = (back.astype(F32) + part(1 - half + s)).astype(BF16)
    return part(0).astype(F32) + ahead + back.astype(F32)


def pairwise_sum(value, axis, size):
    bit = 1
    while bit < size:
        value = value + lax.ppermute(value, axis, [(i, i ^ bit) for i in range(size)])
        bit *= 2
    return value


def swap(value, bit):
    return lax.ppermute(value, "grp", [(i, i ^ bit) for i in range(4)])


def near(index, k):
    return index ^ k if lax.axis_size("grp") == 4 else k


def start_gather(value):
    if lax.axis_size("grp") != 4:
        whole = lax.all_gather(value, "grp", axis=0)
        return [whole[k] for k in range(whole.shape[0])]
    return [value, swap(value, 1), swap(value, 2)]


def end_gather(parts):
    if lax.axis_size("grp") != 4:
        return parts
    return parts + [swap(parts[2], 1)]


def start_scatter(block):
    if lax.axis_size("grp") != 4:
        whole = jnp.stack([block(k) for k in range(lax.axis_size("grp"))]).astype(BF16)
        return lax.psum_scatter(whole, "grp", scatter_dimension=0, tiled=False)
    return swap(block(3).astype(BF16), 1)


def cross_scatter(block, corner):
    if lax.axis_size("grp") != 4:
        return corner
    return swap((corner.astype(F32) + block(2)).astype(BF16), 2)


def end_scatter(block, across):
    if lax.axis_size("grp") != 4:
        return across
    beside = swap(block(1).astype(BF16), 1).astype(F32)
    return (block(0) + beside + across.astype(F32)).astype(BF16)


def in_turn(blocks, order):
    picked = [lax.dynamic_index_in_dim(blocks, order[i], 0) for i in range(blocks.shape[0])]
    return jnp.concatenate(picked, axis=0)


class HeadPlan:
    def __init__(self, heads, seq, grp):
        self.seq, self.grp, self.heads = seq, grp, heads
        self.local = heads // seq
        self.mixed = (heads // grp) % seq == 0
        self.each = (heads // grp) // seq if self.mixed else 0

    def pick(self, item, seq_index, grp_index):
        rest = item.shape[1:]
        if self.mixed:
            item = item.reshape((self.grp, self.seq, self.each) + rest)
            item = lax.dynamic_index_in_dim(item, seq_index, 1, keepdims=False)
            return self.turn(item.reshape((self.local,) + rest), grp_index)
        return lax.dynamic_slice_in_dim(item, seq_index * self.local, self.local, 0)

    def turn(self, item, grp_index):
        if not self.mixed:
            return item
        item = item.reshape((self.grp, self.each) + item.shape[1:])
        parts = [
            lax.dynamic_index_in_dim(item, near(grp_index, k), 0, keepdims=False)
            for k in range(self.grp)
        ]
        return jnp.concatenate(parts, axis=0)

    def order(self, item):
        rest = item.shape[2:]
        if self.mixed:
            item = item.reshape((self.seq, self.grp, self.each) + rest)
            item = jnp.swapaxes(item, 0, 1)
        return item.reshape((self.heads,) + rest)


def exchange(block):
    return lax.all_to_all(block, "seq", 0, 0, tiled=True)


def cut_heads(plan, mats, turned, head_dim):
    count = len(mats)
    seq = plan.seq
    if plan.each == 1:
        return cut_features(seq, mats, turned)
    mats = [m.T if turn else m for m, turn in zip(mats, turned)]
    cols = mats[0].shape[1]
    if plan.mixed:
        block = jnp.stack([m.reshape(seq, plan.each, head_dim, cols) for m in mats], axis=2)
    else:
        block = lax.all_gather(jnp.stack(mats), "grp", axis=1, tiled=True)
        block = block.reshape(count, seq, plan.local, head_dim, cols).transpose(1, 2, 0, 3, 4)
    return block.reshape(seq, -1, cols)


def start_heads(plan, block):
    seq, _, cols = block.shape
    block = block.transpose(1, 0, 2).reshape(-1, seq * cols)
    return start_gather(block) if plan.mixed else [block]


def end_heads(plan, parts, count, head_dim):
    parts = end_gather(parts) if plan.mixed else parts
    size = count * head_dim
    return [part[i : i + size] for part in parts for i in range(0, part.shape[0], size)]


def heads_block(plan, grads):
    each = plan.each
    return lambda k: jnp.concatenate(grads[k * each : (k + 1) * each], axis=0)


def scatter_heads(plan, grads, block, turned):
    packed, width = grads[0].shape
    count = len(turned)
    seq = plan.seq
    cols = width // seq
    head_dim = packed // count
    if plan.mixed:
        each = plan.each
        block = exchange(block.reshape(-1, seq, cols).transpose(1, 0, 2))
        if each == 1:
            return join_features(block, seq * head_dim, turned)
        block = block.reshape(seq, each, count, head_dim, cols)
        block = block.transpose(2, 0, 1, 3, 4).reshape(count, -1, cols).astype(F32)
        return [part.T if turn else part for part, turn in zip(block, turned)]
    block = jnp.concatenate(grads, axis=0).astype(BF16)
    block = block.reshape(-1, seq, cols).transpose(1, 0, 2)
    block = exchange(block).reshape(seq, plan.local, count, head_dim, cols)
    block = block.transpose(2, 0, 1, 3, 4).reshape(count, -1, cols)
    block = lax.psum_scatter(block, "grp", scatter_dimension=1, tiled=True).astype(F32)
    return [part.T if turn else part for part, turn in zip(block, turned)]


def body(
    tokens,
    cotangent,
    lengths,
    prenorm_gain,
    w_query,
    w_key,
    w_value,
    w_gate,
    rate_weight,
    rate_bias,
    init_weight,
    init_bias,
    inner_gain,
    inner_bias,
    post_gain,
    post_bias,
    w_out,
    feedforward_norm_gain,
    w_swish,
    w_up,
    w_down,
):
    seq_index = lax.axis_index("seq")
    grp_index = lax.axis_index("grp")
    groups = lax.axis_size("grp")
    seq = lax.axis_size("seq")
    rows_tok = tokens.shape[1]
    width = tokens.shape[2]
    heads, head_dim, _ = init_weight.shape
    plan = HeadPlan(heads, seq, groups)
    local = plan.local
    features = local * head_dim
    stream = rows_tok * seq
    steps = slot_steps(seq)
    place = ring_place(seq, seq_index)
    member_of_slot = ring_member(seq, (place + jnp.array(steps, jnp.int32)) % seq)
    apart = (ring_place(seq, jnp.arange(seq, dtype=jnp.int32)) - place) % seq
    slot_of_member = jnp.where(apart > seq // 2, 2 * (seq - apart), 2 * apart + 1)
    slot_of_member = jnp.where(apart == 0, 0, jnp.where(apart == seq // 2, 1, slot_of_member))
    to_slots = (member_of_slot[:, None] == jnp.arange(seq)[None, :]).astype(F32)

    def in_slots(stat):
        cut = stat.reshape(-1, seq, rows_tok)
        out = jnp.einsum("sm,kmt->kst", to_slots, cut, precision=lax.Precision.HIGHEST)
        return out.reshape(-1, stream)

    def in_order(stat):
        cut = stat.reshape(-1, seq, rows_tok)
        out = jnp.einsum("sm,kst->kmt", to_slots, cut, precision=lax.Precision.HIGHEST)
        return out.reshape(-1, stream)

    def pick(item):
        return plan.pick(item, seq_index, grp_index)

    def by_distance(rows):
        return lambda k: lax.slice_in_dim(
            rows, at_slot(k) * rows_tok, (at_slot(k) + 1) * rows_tok, axis=0
        )

    def at_slot(k):
        return steps.index(k if k < seq // 2 else k - seq)

    own_lengths = lax.dynamic_index_in_dim(lengths, grp_index, 0, keepdims=False)
    ends = jnp.cumsum(own_lengths)
    starts = ends - own_lengths
    docs = jnp.concatenate([starts, ends[-1:]])

    proj_block = exchange(
        cut_heads(plan, (w_query, w_key, w_value), (True, True, True), head_dim)
    )
    padded = w_down.shape[0] // seq
    padded += -padded % MB
    rate_rows = jnp.pad(pick(rate_weight.T), ((0, 128 - local), (0, 0)))
    gb, init = chain_params(*(pick(i) for i in (init_weight, init_bias, inner_gain, inner_bias)))
    own = {}

    bias = jnp.pad(pick(rate_bias), (0, 128 - local))[None]

    def token_work(s, arrived):
        if s == 1:
            own["parts"] = start_heads(plan, after(proj_block, arrived[0]))
            return [gb, init]
        if s == seq // 2 - 2:
            mats = (w_swish.T, w_up.T, w_down)
            if plan.each == 1:
                turned = (True, False, False, False, False)
                own["rest"] = cut_features(seq, (w_gate, w_out) + mats, turned)
            else:
                side = cut_heads(plan, (w_gate, w_out), (True, False), head_dim)
                own["rest"] = jnp.concatenate(
                    [side, cut_features(seq, mats, (False,) * 3)], axis=1
                )
            return [own["rest"]]
        if s == seq // 2 - 1:
            own["parts"] = end_heads(plan, own["parts"], 3, head_dim)
            return own["parts"][-1:]
        return []

    token_steps = ring_gather(tokens[0], seq, token_work)
    normed, x3, logits = project(
        sum(by_slots(token_steps), ()), own["parts"], rate_rows, bias, prenorm_gain[None]
    )
    rest_block = exchange(after(own["rest"], logits))
    grad_own = cotangent[0]

    inner, *kept = chain_forward(slot_of_member, docs, x3, logits, gb, init, rows_tok)
    kept_stat = after(kept[3], rest_block)
    side_rows = rest_block.shape[1] - 3 * padded
    side_block, ffn_block = rest_block[:, :side_rows], rest_block[:, side_rows:]

    sides = end_heads(plan, start_heads(plan, side_block), 2, head_dim)
    m_gate = jnp.concatenate([side[:head_dim] for side in sides], axis=0)
    m_out = jnp.concatenate([side[head_dim:] for side in sides], axis=0)
    gate_pre = mm_nt(normed, m_gate)
    ffn_block = ffn_block.transpose(1, 0, 2).reshape(3 * padded, width)
    ffn_parts = start_gather(ffn_block)

    sums = jnp.sum(kept_stat[2:4].reshape(2, stream // MB, local, MB), axis=2).reshape(2, stream)
    sums = in_slots(pairwise_sum(sums, "seq", seq)) / width
    mean_o = sums[0][:, None]
    inv_o = lax.rsqrt(sums[1][:, None] - mean_o * mean_o + EPS)
    o_hat = (inner - mean_o) * inv_o
    post_g = pick(post_gain.reshape(heads, head_dim)).reshape(features)
    post_b = pick(post_bias.reshape(heads, head_dim)).reshape(features)
    post = o_hat * post_g + post_b
    gelu_val, gelu_pull = jax.vjp(jax.nn.gelu, gate_pre)
    gated = (gelu_val * post).astype(BF16)
    ffn = {}


    def ffn_corner(since):
        ffn["parts"] = end_gather(ffn_parts)
        return ffn["parts"][-1:]

    mixing = ring_scatter(
        by_distance(mm(gated, m_out).astype(BF16)),
        seq,
        [lambda since: [], lambda since: [], lambda since: [], ffn_corner],
    )
    own_rows = tokens[0].astype(F32)
    resid = own_rows + mixing
    inv_second = lax.rsqrt(jnp.mean(resid * resid, -1, keepdims=True) + EPS)
    unit_second = resid * inv_second
    ffn_in = (unit_second * feedforward_norm_gain).astype(BF16)

    got = {"kept": (), "rows": [], "grads": []}
    d_parts = {}

    def step_work(s, arrived, grads):
        slot = 2 * s if s < seq // 2 else 1
        members = lax.slice_in_dim(member_of_slot, slot, slot + len(arrived))
        got["kept"], d_in = ffn_step(
            members, seq, slot, arrived, grads, ffn["parts"], got["kept"]
        )
        got["rows"].append(arrived)
        got["grads"].append(grads)
        for i in range(len(arrived)):
            d_parts[steps[slot + i]] = d_in[i * rows_tok : (i + 1) * rows_tok]
        return [d_in]

    ring_gather(ffn_in, seq, step_work, grad_own)
    kept_ffn = got["kept"]

    def ffn_work(since):
        first, *others = kept_ffn[:3]
        got["ffn"] = ffn_grads(
            groups,
            [after(first, since)] + others,
            sum(by_slots(got["rows"]), ()),
            sum(by_slots(got["grads"]), ()),
        )
        return got["ffn"][:1]

    def ffn_corner_work(since):
        got["corner"] = start_scatter(lambda k: after(got["ffn"][k], since))
        got["across"] = cross_scatter(ffn_grad, got["corner"])
        return [got["corner"]]

    def ffn_grad(k):
        return got["ffn"][k]

    d_ffn = ring_scatter(
        lambda k: d_parts[k if k < seq // 2 else k - seq], seq, [ffn_work, ffn_corner_work]
    )
    second_scaled = d_ffn * feedforward_norm_gain
    g_ffn_gain = jnp.sum(d_ffn * unit_second, 0)
    d_resid = grad_own.astype(F32) + inv_second * (
        second_scaled - unit_second * jnp.mean(second_scaled * unit_second, -1, keepdims=True)
    )

    def mix_work(s, arrived):
        return [got["across"]] if s == seq // 2 - 2 else []

    mix_steps = ring_gather(d_resid.astype(BF16), seq, mix_work)
    ffn_out = lax.psum_scatter(
        after(kept_ffn[3], d_ffn), "seq", scatter_dimension=0, tiled=False
    )
    out_tokens = (resid + ffn_out.astype(F32)).astype(BF16)[None]
    g_ffn = end_scatter(ffn_grad, got["across"])
    g_ffn = after(g_ffn.reshape(3 * padded, seq, -1).transpose(1, 0, 2), mix_steps[-1][0])
    d_gated = [mm_nt(jnp.concatenate(arrived, axis=0), m_out) for arrived in mix_steps]
    d_gated = jnp.concatenate(by_slots(d_gated), axis=0)
    d_post = d_gated * gelu_val
    d_gate_pre = gelu_pull(d_gated * post)[0].astype(BF16)
    g_post_gain = jnp.sum(d_post * o_hat, 0)
    g_post_bias = jnp.sum(d_post, 0)
    d_ohat = d_post * post_g
    sums = jnp.stack([jnp.sum(d_ohat, -1), jnp.sum(d_ohat * o_hat, -1)])
    sums = in_slots(pairwise_sum(in_order(sums), "seq", seq)) / width
    g_ffn = exchange(after(g_ffn, sums))
    d_inner = inv_o * (d_ohat - sums[0][:, None] - o_hat * sums[1][:, None])
    d_x, d_gb, d_init = chain_backward(
        slot_of_member, docs, x3, d_inner, d_gate_pre, logits, gb, init, kept, rows_tok
    )
    w_all = jnp.concatenate(own["parts"] + [rate_rows, m_gate], axis=0)
    d_x = after(d_x, g_ffn, ffn_out)
    *head_rows_grads, g_rates, g_gain = proj_grads(
        d_x, normed, w_all, gated, sum(by_slots(mix_steps), ()), local, head_dim
    )
    d_logits = d_x[:, 3 * features : 3 * features + local].astype(F32)
    parts = [item.reshape(local, -1) for item in chain_param_grads(d_gb, d_init, local)]
    parts += [item.reshape(local, head_dim) for item in (g_post_gain, g_post_bias)]
    parts += [g_rates[:local], jnp.sum(d_logits, 0)[:, None]]
    sizes = [item.shape[1] for item in parts]
    flat = jnp.concatenate(parts, axis=1)
    flat = plan.turn(jnp.pad(flat, ((0, 0), (0, -flat.shape[1] % 1024))), grp_index)
    count = flat.size
    flat = jnp.concatenate([flat.reshape(-1), g_gain[0] / prenorm_gain, g_ffn_gain])
    flat = pairwise_sum(flat.reshape(-1, 1024), "grp", groups)
    flat_all = lax.all_gather(flat, "seq", axis=0)
    d_x = after(d_x, g_gain)
    d_normed_part = mm(d_x, w_all).astype(BF16)

    def corner_work(since):
        if not plan.mixed:
            return []
        block = heads_block(plan, head_rows_grads)
        got["corner"] = start_scatter(block)
        got["across"] = cross_scatter(block, after(got["corner"], flat))
        return [got["corner"]]

    def join_work(since):
        got["join"] = join_features(after(g_ffn, since), w_down.shape[0], (False,) * 3)
        return got["join"][:1]

    def across_work(since):
        return [got["across"]] if plan.mixed else []

    d_normed = ring_scatter(
        by_distance(d_normed_part), seq, [corner_work, join_work, across_work]
    )
    summed = end_scatter(heads_block(plan, head_rows_grads), got["across"]) if plan.mixed else None
    g_heads = scatter_heads(plan, head_rows_grads, summed, (True,) * 4 + (False,))
    own_inv = lax.rsqrt(jnp.mean(own_rows * own_rows, -1, keepdims=True) + EPS)
    own_unit = own_rows * own_inv
    first_scaled = d_normed * prenorm_gain
    grad_tokens = (
        d_resid
        + own_inv
        * (first_scaled - own_unit * jnp.mean(first_scaled * own_unit, -1, keepdims=True))
    )[None]

    flat = after(flat_all, d_normed).reshape(seq, -1)
    gains = jnp.sum(flat[:, count:], 0).reshape(2, width)
    flat = plan.order(flat[:, :count].reshape(seq, local, -1))
    small = []
    offset = 0
    for size in sizes:
        small.append(flat[:, offset : offset + size])
        offset += size
    g_ffn = got["join"]
    return (
        out_tokens,
        grad_tokens,
        gains[0],
        g_heads[0],
        g_heads[1],
        g_heads[2],
        g_heads[3],
        small[6].T,
        small[7][:, 0],
        small[0].reshape(heads, head_dim, head_dim),
        small[1],
        small[2],
        small[3],
        small[4].reshape(width),
        small[5].reshape(width),
        g_heads[4],
        gains[1],
        g_ffn[0].T,
        g_ffn[1].T,
        g_ffn[2],
    )


def solution(mesh):
    whole = P()
    rows = P("grp", "seq", None)
    wide = P("seq", "grp")
    tall = P("grp", "seq")
    return jax.shard_map(
        body,
        mesh=mesh,
        in_specs=(rows, rows, whole, whole, wide, wide, wide, wide)
        + (whole,) * 8
        + (tall, whole, wide, wide, tall),
        out_specs=(rows, rows, whole, wide, wide, wide, wide)
        + (whole,) * 8
        + (tall, whole, wide, wide, tall),
        check_vma=False,
    )
```

```python
from functools import partial

import jax
import jax.numpy as jnp
from jax import lax
from jax.experimental import pallas as pl
from jax.experimental.pallas import tpu as pltpu
from jax.sharding import PartitionSpec as P

MB = 16
EPS = 1e-06
F32 = jnp.float32
VMEM_ASKED = 58 * 1024 * 1024
BF16 = jnp.bfloat16


def mm(left, right):
    return jnp.dot(left, right, preferred_element_type=F32)


def mm_nt(left, right):
    return lax.dot_general(left, right, (((1,), (1,)), ((), ())), preferred_element_type=F32)


def split_two(value):
    high = value.astype(BF16)
    return high, (value - high.astype(F32)).astype(BF16)


def mean_rows(value):
    return jnp.mean(value, axis=0, keepdims=True)


def chunk_rows(value, heads, start, lanes, size):
    tokens = value.shape[0]
    cuts = [value[:, lanes * h + start : lanes * h + start + size] for h in range(heads)]
    parts = [cut[m * MB : (m + 1) * MB] for m in range(tokens // MB) for cut in cuts]
    return jnp.concatenate(parts, axis=0)


def head_rows(rows, heads, h):
    step = MB * heads
    parts = [rows[m * step + h * MB : m * step + (h + 1) * MB] for m in range(rows.shape[0] // step)]
    return jnp.concatenate(parts, axis=0)


def chunk_masks(info, heads, count):
    step = MB * heads
    row = lax.broadcasted_iota(jnp.int32, (count, count), 0)
    col = lax.broadcasted_iota(jnp.int32, (count, count), 1)
    columns = jnp.transpose(info)
    same = ((row % step) // MB == (col % step) // MB) & (columns[:, 1:2] == info[1:2, :])
    return row // step, col // step, row % MB, col % MB, same, columns


def chunk_info(docs_ref, logits, heads, head_dim, chunk):
    tokens = logits.shape[0]
    count = heads * tokens
    step = MB * heads
    docs = docs_ref.shape[0] - 1
    pieces = [logits[m * MB : (m + 1) * MB] for m in range(tokens // MB) for _ in range(heads)]
    spread = jnp.concatenate(pieces, axis=0)
    lane = lax.broadcasted_iota(jnp.int32, spread.shape, 1)
    own = (lax.broadcasted_iota(jnp.int32, spread.shape, 0) % step) // MB
    logit = jnp.sum(jnp.transpose(jnp.where(lane == own, spread, 0.0)), axis=0, keepdims=True)
    start = chunk * tokens
    col = lax.broadcasted_iota(jnp.int32, (1, count), 1)
    block_at = start + (col // step) * MB
    doc = jnp.zeros((1, count), jnp.int32)
    before = end = jnp.int32(0)
    for d in range(docs):
        doc = doc + (block_at >= docs_ref[d]).astype(jnp.int32)
        before = before + (docs_ref[d] < start).astype(jnp.int32)
        end = end + (docs_ref[d] < start + tokens).astype(jnp.int32)
    live = (block_at + col % MB < docs_ref[docs]).astype(F32)
    sig = jax.nn.sigmoid(logit)
    zero = jnp.zeros((1, count), F32)
    return jnp.concatenate(
        [
            sig / head_dim * live,
            doc.astype(F32),
            (doc > before).astype(F32),
            (doc == end).astype(F32),
            zero + (end > before).astype(F32),
            live * sig * (1.0 - sig) / head_dim,
            zero,
            zero,
        ],
        axis=0,
    )


def augment(rows, heads, head_dim, wide):
    count = rows.shape[0]
    near = lax.broadcasted_iota(jnp.int32, (head_dim, wide), 0)
    far = lax.broadcasted_iota(jnp.int32, (head_dim, wide), 1)
    tile = (far % head_dim == near).astype(BF16)
    lane = lax.broadcasted_iota(jnp.int32, (count, wide), 1)
    own = (lax.broadcasted_iota(jnp.int32, (count, wide), 0) % (MB * heads)) // MB
    return jnp.where(lane // head_dim == own, mm(rows, tile), 0.0)


def one_hot_heads(count, heads):
    lane = lax.broadcasted_iota(jnp.int32, (count, 128), 1)
    own = (lax.broadcasted_iota(jnp.int32, (count, 128), 0) % (MB * heads)) // MB
    return (lane == own).astype(BF16)


def forward_kernel(
    heads, idx_ref, docs_ref, x_ref, logit_ref, gb_ref, init_ref, out_ref, n_ref, r_ref, nb_ref, stat_ref, w_ref, state
):
    head_dim = gb_ref.shape[1]
    tokens = x_ref.shape[0]
    count = heads * tokens
    full = init_ref.shape[1]
    wide = full - 128

    @pl.when(pl.program_id(0) == 0)
    def _():
        state[...] = init_ref[...]

    carried = state[...]
    w_ref[0] = carried
    info = chunk_info(docs_ref, logit_ref[...], heads, head_dim, pl.program_id(0))
    x = x_ref[...]
    q_rows = chunk_rows(x, heads, 0, 3 * head_dim, head_dim)
    k_rows = chunk_rows(x, heads, head_dim, 3 * head_dim, head_dim)
    v_rows = chunk_rows(x, heads, 2 * head_dim, 3 * head_dim, head_dim)
    q_t = jnp.transpose(q_rows.astype(F32))
    target_t = jnp.transpose(v_rows.astype(F32) - k_rows.astype(F32))
    mb_row, mb_col, t_row, t_col, same, columns = chunk_masks(info, heads, count)
    gram = jnp.where(same & (mb_row < mb_col), mm_nt(k_rows, k_rows) + 1.0, 0.0).astype(BF16)
    cross = jnp.where(
        same & ((mb_row < mb_col) | ((mb_row == mb_col) & (t_row <= t_col))),
        mm_nt(k_rows, q_rows) + 1.0,
        0.0,
    ).astype(BF16)
    hot = one_hot_heads(count, heads)
    k_aug = jnp.concatenate([augment(k_rows, heads, head_dim, wide).astype(BF16), hot], axis=1)
    q_aug = jnp.concatenate([augment(q_rows, heads, head_dim, wide).astype(BF16), hot], axis=1)
    init = init_ref[...]
    stacked = jnp.concatenate(split_two(carried) + split_two(init), axis=0)
    fresh = info[2:3, :] > 0.5

    def through_state(rows):
        both = mm_nt(stacked, rows)
        return jnp.where(
            fresh,
            both[2 * head_dim : 3 * head_dim] + both[3 * head_dim :],
            both[:head_dim] + both[head_dim : 2 * head_dim],
        )

    z_start = through_state(k_aug)
    gain = gb_ref[0]
    shift = gb_ref[1]
    repeats = count // 128
    inner = 128 // (MB * heads)
    done = []
    for p in range(repeats):
        cols = slice(p * 128, (p + 1) * 128)
        z_base = z_start[:, cols]
        if p:
            z_base = z_base - mm(jnp.concatenate(done, axis=1), gram[: p * 128, cols])
        target = target_t[:, cols]
        rate = info[0:1, cols]
        z = z_base
        for step in range(inner):
            if step:
                z = z_base - mm(scaled.astype(BF16), gram[cols, cols])
            centred = z - mean_rows(z)
            inv = lax.rsqrt(mean_rows(centred * centred) + EPS)
            n = centred * inv
            err = (n * gain + shift - target) * gain
            scaled = (rate * inv) * (err - mean_rows(err) - n * mean_rows(err * n))
        done.append(scaled.astype(BF16))
        n_ref[:, cols] = n
        r_ref[:, cols] = scaled
        stat_ref[0:1, cols] = inv
    r_bf = jnp.concatenate(done, axis=1)
    z_bar = through_state(q_aug) - mm(r_bf, cross)
    centred = z_bar - mean_rows(z_bar)
    inv = lax.rsqrt(mean_rows(centred * centred) + EPS)
    nb = centred * inv
    nb_ref[...] = nb
    stat_ref[1:2, :] = inv
    wide_gain = jnp.concatenate([gain] * repeats, axis=1)
    wide_shift = jnp.concatenate([shift] * repeats, axis=1)
    out_t = q_t + nb * wide_gain + wide_shift
    stat_ref[2:3, :] = jnp.sum(out_t, axis=0, keepdims=True)
    stat_ref[3:4, :] = jnp.sum(out_t * out_t, axis=0, keepdims=True)
    out_rows = jnp.transpose(out_t)
    for h in range(heads):
        out_ref[:, h * head_dim : (h + 1) * head_dim] = head_rows(out_rows, heads, h)
    base = jnp.where(info[4:5, 0:1] > 0.5, init, carried)
    state[...] = base - mm((r_ref[...] * info[3:4, :]).astype(BF16), k_aug)


def backward_kernel(
    heads,
    idx_ref,
    docs_ref,
    x_ref,
    d_ref,
    gate_ref,
    logit_ref,
    gb_ref,
    init_ref,
    n_ref,
    r_ref,
    nb_ref,
    stat_ref,
    w_ref,
    dx_ref,
    dgb_ref,
    dinit_ref,
    state,
):
    head_dim = gb_ref.shape[1]
    tokens = x_ref.shape[0]
    count = heads * tokens
    full = init_ref.shape[1]
    wide = full - 128

    @pl.when(pl.program_id(0) == 0)
    def _():
        state[...] = jnp.zeros_like(state)
        dgb_ref[...] = jnp.zeros_like(dgb_ref)
        dinit_ref[...] = jnp.zeros_like(dinit_ref)

    d_end = state[...]
    carried = w_ref[0]
    init = init_ref[...]
    chunk = pl.num_programs(0) - 1 - pl.program_id(0)
    info = chunk_info(docs_ref, logit_ref[...], heads, head_dim, chunk)
    x = x_ref[...]
    q_rows = chunk_rows(x, heads, 0, 3 * head_dim, head_dim)
    k_rows = chunk_rows(x, heads, head_dim, 3 * head_dim, head_dim)
    v_rows = chunk_rows(x, heads, 2 * head_dim, 3 * head_dim, head_dim)
    d_rows = chunk_rows(d_ref[...], heads, 0, head_dim, head_dim)
    target_t = jnp.transpose(v_rows.astype(F32) - k_rows.astype(F32))
    d_t = jnp.transpose(d_rows)
    mb_row, mb_col, t_row, t_col, same, columns = chunk_masks(info, heads, count)
    earlier = same & (mb_row < mb_col)
    later = same & (mb_row > mb_col)
    up_to = same & ((mb_row < mb_col) | ((mb_row == mb_col) & (t_row <= t_col)))
    from_on = same & ((mb_row > mb_col) | ((mb_row == mb_col) & (t_row >= t_col)))
    gram = jnp.where(later, mm_nt(k_rows, k_rows) + 1.0, 0.0).astype(BF16)
    cross = jnp.where(from_on, mm_nt(q_rows, k_rows) + 1.0, 0.0).astype(BF16)
    hot = one_hot_heads(count, heads)
    k_aug = jnp.concatenate([augment(k_rows, heads, head_dim, wide).astype(BF16), hot], axis=1)
    q_aug = jnp.concatenate([augment(q_rows, heads, head_dim, wide).astype(BF16), hot], axis=1)
    gain = gb_ref[0]
    shift = gb_ref[1]
    repeats = count // 128
    inner = 128 // (MB * heads)
    wide_gain = jnp.concatenate([gain] * repeats, axis=1)
    nb = nb_ref[...]
    inv_b = stat_ref[1:2, :]
    d_nb = d_t * wide_gain
    d_zbar = inv_b * (d_nb - mean_rows(d_nb) - nb * mean_rows(d_nb * nb))
    scaled_t = r_ref[...]
    last = info[3:4, :]
    dr_base = -mm(d_zbar.astype(BF16), cross) - last * mm_nt(d_end.astype(BF16), k_aug)
    gain_sum = jnp.zeros((head_dim, 128), F32)
    shift_sum = jnp.zeros((head_dim, 128), F32)
    for p in range(repeats):
        cols = slice(p * 128, (p + 1) * 128)
        gain_sum = gain_sum + d_t[:, cols] * nb[:, cols]
        shift_sum = shift_sum + d_t[:, cols]
    done = []
    errs = []
    d_rates = []
    for p in reversed(range(repeats)):
        cols = slice(p * 128, (p + 1) * 128)
        base = dr_base[:, cols]
        if done:
            base = base - mm(jnp.concatenate(done, axis=1), gram[(p + 1) * 128 :, cols])
        n = n_ref[:, cols]
        inv = stat_ref[0:1, cols]
        rate = info[0:1, cols]
        miss = n * gain + shift - target_t[:, cols]
        err = miss * gain
        along = mean_rows(err * n)
        plain = inv * (err - mean_rows(err) - n * along)
        gain2 = gain * gain
        d_scaled = base
        for step in range(inner):
            if step:
                d_scaled = base - mm(d_z.astype(BF16), gram[cols, cols])
            g = rate * d_scaled
            g_n = mean_rows(g * n)
            d_err = inv * (g - mean_rows(g) - n * g_n)
            d_n = d_err * gain2 - inv * (g * along + err * g_n)
            d_z = inv * (d_n - mean_rows(d_n) - n * (mean_rows(d_n * n) + mean_rows(g * plain)))
        done.insert(0, d_z.astype(BF16))
        errs.insert(0, d_err * gain)
        d_rates.insert(0, jnp.sum(d_scaled * plain, axis=0, keepdims=True))
        gain_sum = gain_sum + d_err * (miss + gain * n)
        shift_sum = shift_sum + d_err * gain
    dgb_ref[0] += gain_sum
    dgb_ref[1] += shift_sum
    dz_bf = jnp.concatenate(done, axis=1)
    d_z = dz_bf.astype(F32)
    d_errg = jnp.concatenate(errs, axis=1)
    turned = jnp.transpose(jnp.concatenate([d_zbar, scaled_t, d_z, d_errg], axis=0))
    zb_rows = turned[:, :head_dim].astype(BF16)
    r_rows = turned[:, head_dim : 2 * head_dim].astype(BF16)
    z_rows = turned[:, 2 * head_dim : 3 * head_dim].astype(BF16)
    e_rows = turned[:, 3 * head_dim :]
    d_cross = jnp.where(from_on, -mm_nt(zb_rows, r_rows), 0.0).astype(BF16)
    d_cross_t = jnp.where(up_to, -mm_nt(r_rows, zb_rows), 0.0).astype(BF16)
    d_gram = (
        jnp.where(later, -mm_nt(z_rows, r_rows), 0.0)
        + jnp.where(earlier, -mm_nt(r_rows, z_rows), 0.0)
    ).astype(BF16)
    is_init = columns[:, 2:3] > 0.5
    is_last = columns[:, 3:4] > 0.5

    def stack_heads(weight):
        parts = [weight[:, h * head_dim : (h + 1) * head_dim] for h in range(heads)]
        pad = wide - heads * head_dim
        if pad:
            parts.append(jnp.zeros((pad, head_dim), F32))
        return jnp.concatenate(parts, axis=0).astype(BF16)

    w_both = jnp.concatenate([stack_heads(carried), stack_heads(init)], axis=0)
    d_stack = stack_heads(d_end)

    def by_state(rows):
        own = augment(rows, heads, head_dim, wide)
        return jnp.concatenate(
            [jnp.where(is_init, 0.0, own), jnp.where(is_init, own, 0.0)], axis=1
        ).astype(BF16)

    dq = d_rows + mm(d_cross, k_rows) + mm(by_state(zb_rows), w_both)
    r_own = jnp.where(is_last, augment(r_rows, heads, head_dim, wide), 0.0).astype(BF16)
    dk = (
        e_rows
        + mm(d_gram, k_rows)
        + mm(d_cross_t, q_rows)
        + mm(by_state(z_rows), w_both)
        - mm(r_own, d_stack)
    )
    packed = jnp.concatenate([dq.astype(BF16), dk.astype(BF16), (-e_rows).astype(BF16)], axis=1)
    each = 3 * head_dim
    d_logits = jnp.concatenate(d_rates, axis=1) * info[5:6, :]
    turned = jnp.transpose(jnp.concatenate([d_logits, jnp.zeros((7, count), F32)], axis=0))
    lane = lax.broadcasted_iota(jnp.int32, (tokens, 128), 1)
    logit_rows = jnp.zeros((tokens, 128), F32)
    for h in range(heads):
        dx_ref[:, h * each : (h + 1) * each] = head_rows(packed, heads, h)
        logit_rows = jnp.where(lane == h, head_rows(turned, heads, h)[:, 0:1], logit_rows)
    dx_ref[:, heads * each : heads * each + 128] = logit_rows.astype(BF16)
    dx_ref[:, heads * each + 128 :] = gate_ref[...]
    row_init = info[2:3, :] > 0.5
    zb_two = jnp.concatenate(
        [jnp.where(row_init, 0.0, d_zbar), jnp.where(row_init, d_zbar, 0.0)], axis=0
    ).astype(BF16)
    z_two = jnp.concatenate(
        [jnp.where(row_init, 0.0, d_z), jnp.where(row_init, d_z, 0.0)], axis=0
    ).astype(BF16)
    d_both = mm(zb_two, q_aug) + mm(z_two, k_aug)
    fresh = info[4:5, 0:1] > 0.5
    state[...] = d_both[:head_dim] + jnp.where(fresh, 0.0, d_end)
    dinit_ref[...] += d_both[head_dim:] + jnp.where(fresh, d_end, 0.0)


def chain_specs(heads, tokens, head_dim, full, at):
    count = heads * tokens
    return dict(
        x=pl.BlockSpec((tokens, heads * 3 * head_dim), lambda i, idx, docs: (idx[at(i)], 0)),
        dx=pl.BlockSpec((tokens, heads * 4 * head_dim + 128), lambda i, idx, docs: (idx[at(i)], 0)),
        rows=pl.BlockSpec((tokens, heads * head_dim), lambda i, idx, docs: (idx[at(i)], 0)),
        logit=pl.BlockSpec((tokens, 128), lambda i, idx, docs: (idx[at(i)], 0)),
        gb=pl.BlockSpec((2, head_dim, 128), lambda i, idx, docs: (0, 0, 0)),
        init=pl.BlockSpec((head_dim, full), lambda i, idx, docs: (0, 0)),
        tall=pl.BlockSpec((head_dim, count), lambda i, idx, docs: (0, at(i))),
        stat=pl.BlockSpec((8, count), lambda i, idx, docs: (0, at(i))),
        weight=pl.BlockSpec((1, head_dim, full), lambda i, idx, docs: (at(i), 0, 0)),
    )


def chain_forward(idx, docs, x3, logits, gb, init, tokens):
    total = x3.shape[0]
    head_dim = gb.shape[1]
    heads = x3.shape[1] // (3 * head_dim)
    chunks = total // tokens
    full = init.shape[1]
    s = chain_specs(heads, tokens, head_dim, full, lambda i: i)
    tall = jax.ShapeDtypeStruct((head_dim, heads * total), F32)
    return pl.pallas_call(
        partial(forward_kernel, heads),
        grid_spec=pltpu.PrefetchScalarGridSpec(
            num_scalar_prefetch=2,
            grid=(chunks,),
            in_specs=[s["x"], s["logit"], s["gb"], s["init"]],
            out_specs=[s["rows"], s["tall"], s["tall"], s["tall"], s["stat"], s["weight"]],
            scratch_shapes=[pltpu.VMEM((head_dim, full), F32)],
        ),
        out_shape=[
            jax.ShapeDtypeStruct((total, heads * head_dim), F32),
            tall,
            tall,
            tall,
            jax.ShapeDtypeStruct((8, heads * total), F32),
            jax.ShapeDtypeStruct((chunks, head_dim, full), F32),
        ],
        compiler_params=pltpu.CompilerParams(
            dimension_semantics=("arbitrary",), vmem_limit_bytes=VMEM_ASKED
        ),
        cost_estimate=pl.CostEstimate(flops=1, bytes_accessed=1, transcendentals=0),
        name="chain_forward",
    )(idx, docs, x3, logits, gb, init)


def chain_backward(idx, docs, x3, d_inner, d_gate, logits, gb, init, kept, tokens):
    total = x3.shape[0]
    head_dim = gb.shape[1]
    heads = x3.shape[1] // (3 * head_dim)
    chunks = total // tokens
    full = init.shape[1]
    s = chain_specs(heads, tokens, head_dim, full, lambda i: chunks - 1 - i)
    return pl.pallas_call(
        partial(backward_kernel, heads),
        grid_spec=pltpu.PrefetchScalarGridSpec(
            num_scalar_prefetch=2,
            grid=(chunks,),
            in_specs=[
                s["x"],
                s["rows"],
                s["rows"],
                s["logit"],
                s["gb"],
                s["init"],
                s["tall"],
                s["tall"],
                s["tall"],
                s["stat"],
                s["weight"],
            ],
            out_specs=[s["dx"], s["gb"], s["init"]],
            scratch_shapes=[pltpu.VMEM((head_dim, full), F32)],
        ),
        out_shape=[
            jax.ShapeDtypeStruct((total, heads * 4 * head_dim + 128), BF16),
            jax.ShapeDtypeStruct(gb.shape, F32),
            jax.ShapeDtypeStruct(init.shape, F32),
        ],
        compiler_params=pltpu.CompilerParams(
            dimension_semantics=("arbitrary",), vmem_limit_bytes=VMEM_ASKED
        ),
        cost_estimate=pl.CostEstimate(flops=1, bytes_accessed=1, transcendentals=0),
        name="chain_backward",
    )(idx, docs, x3, d_inner, d_gate, logits, gb, init, *kept)


def chain_params(init_weight, init_bias, inner_gain, inner_bias):
    heads, head_dim, _ = init_weight.shape
    reps = 128 // (MB * heads)

    def pattern(item):
        row = jnp.broadcast_to(item.T[:, None, :, None], (head_dim, reps, heads, MB))
        return row.reshape(head_dim, 128)

    gb = jnp.stack([pattern(inner_gain), pattern(inner_bias)])
    wide = max(128, heads * head_dim)
    w_t = jnp.transpose(init_weight, (2, 0, 1)).reshape(head_dim, heads * head_dim)
    init = jnp.concatenate(
        [
            jnp.pad(w_t, ((0, 0), (0, wide - heads * head_dim))),
            jnp.pad(init_bias.T, ((0, 0), (0, 128 - heads))),
        ],
        axis=1,
    )
    return gb, init


def chain_param_grads(dgb, dinit, heads):
    head_dim = dinit.shape[0]
    wide = dinit.shape[1] - 128
    d_w = dinit[:, : heads * head_dim].reshape(head_dim, heads, head_dim).transpose(1, 2, 0)
    d_b = dinit[:, wide : wide + heads].T
    both = jnp.sum(dgb.reshape(2, head_dim, -1, heads, MB), axis=(2, 4))
    return d_w, d_b, both[0].T, both[1].T


def cut_kernel(turned, shares, *refs):
    mats, out_ref, held = refs[: len(turned)], refs[-2], refs[-1]
    at = 0
    for mat, turn, share in zip(mats, turned, shares):
        padded = share + -share % MB
        value = mat[...].astype(F32)
        held[: value.shape[1] if turn else value.shape[0]] = jnp.transpose(value) if turn else value
        for s in range(out_ref.shape[0]):
            out_ref[s, at : at + share] = held[s * share : (s + 1) * share].astype(BF16)
            if padded > share:
                out_ref[s, at + share : at + padded] = jnp.zeros(
                    (padded - share, out_ref.shape[2]), BF16
                )
        at += padded


def cut_features(seq, mats, turned):
    features = [m.shape[1] if turn else m.shape[0] for m, turn in zip(mats, turned)]
    cols = mats[0].shape[0] if turned[0] else mats[0].shape[1]
    shares = [count // seq for count in features]
    rows = sum(share + -share % MB for share in shares)
    return pl.pallas_call(
        partial(cut_kernel, turned, shares),
        out_shape=jax.ShapeDtypeStruct((seq, rows, cols), BF16),
        scratch_shapes=[pltpu.VMEM((max(features), cols), F32)],
        compiler_params=pltpu.CompilerParams(vmem_limit_bytes=VMEM_ASKED),
        cost_estimate=pl.CostEstimate(flops=1, bytes_accessed=1, transcendentals=0),
        name="cut_features",
    )(*mats)


def join_kernel(turned, share, padded, in_ref, *refs):
    outs, held = refs[:-1], refs[-1]
    for i, out in enumerate(outs):
        for s in range(in_ref.shape[0]):
            held[s * share : (s + 1) * share] = in_ref[
                s, i * padded : i * padded + share
            ].astype(F32)
        out[...] = jnp.transpose(held[...]) if turned[i] else held[...]


def join_features(block, features, turned):
    seq, rows, cols = block.shape
    shapes = [(cols, features) if turn else (features, cols) for turn in turned]
    return pl.pallas_call(
        partial(join_kernel, turned, features // seq, rows // len(turned)),
        out_shape=[jax.ShapeDtypeStruct(shape, F32) for shape in shapes],
        scratch_shapes=[pltpu.VMEM((features, cols), F32)],
        compiler_params=pltpu.CompilerParams(vmem_limit_bytes=VMEM_ASKED),
        cost_estimate=pl.CostEstimate(flops=1, bytes_accessed=1, transcendentals=0),
        name="join_features",
    )(block)


def ffn_kernel(count, parts, kept, member_ref, *refs):
    rows_refs = refs[:count]
    grad_refs = refs[count : 2 * count]
    weights = refs[2 * count : 2 * count + parts]
    outs = refs[2 * count + parts + kept :]
    (at_ref, ut_ref, ht_ref, y_ref, d_ref, a_t, u_t, h_t, y_all, d_all) = outs
    step = pl.program_id(0)
    size = rows_refs[0].shape[0]

    @pl.when(step == 0)
    def _():
        padded = weights[0].shape[0] // 3
        swish, up, down = (
            jnp.concatenate([w[i * padded : (i + 1) * padded] for w in weights], axis=0)
            for i in range(3)
        )
        rows = jnp.concatenate([ref[...] for ref in rows_refs], axis=0)
        grad = jnp.concatenate([ref[...] for ref in grad_refs], axis=0)
        act_a = mm_nt(rows, swish)
        act_u = mm_nt(rows, up)
        d_hidden = mm_nt(grad, down)
        sig = jax.nn.sigmoid(act_a)
        gate = act_a * sig
        hidden = gate * act_u
        d_a = d_hidden * act_u * sig * (1.0 + act_a * (1.0 - sig))
        d_u = d_hidden * gate
        d_all[...] = (mm(d_a.astype(BF16), swish) + mm(d_u.astype(BF16), up)).astype(BF16)
        y_all[...] = mm(hidden.astype(BF16), down).astype(BF16)
        fill = -hidden.shape[1] % 128
        for out, value in ((a_t, d_a), (u_t, d_u), (h_t, hidden)):
            if fill:
                value = jnp.concatenate([value, jnp.zeros((value.shape[0], fill), F32)], axis=1)
            out[...] = jnp.transpose(value)[: out.shape[0]].astype(BF16)

    for i in range(count):

        @pl.when(step == i)
        def _(i=i):
            part = slice(i * size, (i + 1) * size)
            at_ref[...] = a_t[:, part]
            ut_ref[...] = u_t[:, part]
            ht_ref[...] = h_t[:, part]
            y_ref[0] = y_all[part]
            d_ref[...] = d_all[part]


def ffn_step(members, seq, slot, rows, grads, weights, kept):
    count = len(rows)
    size, width = rows[0].shape
    total = seq * size
    features = sum(w.shape[0] for w in weights) // 3
    whole = pl.BlockSpec(memory_space=pltpu.VMEM)

    turned_spec = pl.BlockSpec((features, size), lambda s, member: (0, slot + s))
    turned = jax.ShapeDtypeStruct((features, total), BF16)
    first = 1 + 2 * count + len(weights)
    out = pl.pallas_call(
        partial(ffn_kernel, count, len(weights), len(kept)),
        grid_spec=pltpu.PrefetchScalarGridSpec(
            num_scalar_prefetch=1,
            grid=(count,),
            in_specs=[whole] * (2 * count + len(weights))
            + [pl.BlockSpec(memory_space=pl.ANY)] * len(kept),
            out_specs=[turned_spec] * 3
            + [
                pl.BlockSpec((1, size, width), lambda s, member: (member[s], 0, 0)),
                pl.BlockSpec((size, width), lambda s, member: (s, 0)),
            ],
            scratch_shapes=[pltpu.VMEM((features, count * size), BF16)] * 3
            + [pltpu.VMEM((count * size, width), BF16)] * 2,
        ),
        out_shape=[turned] * 3
        + [
            jax.ShapeDtypeStruct((seq, size, width), BF16),
            jax.ShapeDtypeStruct((count * size, width), BF16),
        ],
        input_output_aliases={first + i: i for i in range(len(kept))},
        compiler_params=pltpu.CompilerParams(
            dimension_semantics=("arbitrary",), vmem_limit_bytes=VMEM_ASKED
        ),
        cost_estimate=pl.CostEstimate(flops=1, bytes_accessed=1, transcendentals=0),
        name="ffn_step",
    )(members, *rows, *grads, *weights, *kept)
    return out[:-1], out[-1]


def ffn_grad_kernel(parts, count, at_ref, ut_ref, ht_ref, *refs):
    x = jnp.concatenate([ref[...] for ref in refs[:count]], axis=0)
    g = jnp.concatenate([ref[...] for ref in refs[count : 2 * count]], axis=0)
    padded = at_ref.shape[0] // parts
    for i, out in enumerate(refs[2 * count :]):
        own = slice(i * padded, (i + 1) * padded)
        out[:padded] = mm(at_ref[own], x).astype(BF16)
        out[padded : 2 * padded] = mm(ut_ref[own], x).astype(BF16)
        out[2 * padded :] = mm(ht_ref[own], g).astype(BF16)


def ffn_grads(parts, turned, rows, grads):
    size, width = rows[0].shape
    count = len(rows)
    features = turned[0].shape[0]
    wide = pl.BlockSpec((size, 256), lambda i: (0, i))
    whole = pl.BlockSpec((features, count * size), lambda i: (0, 0))
    each = 3 * features // parts
    return pl.pallas_call(
        partial(ffn_grad_kernel, parts, count),
        grid=(width // 256,),
        in_specs=[whole] * 3 + [wide] * (2 * count),
        out_specs=[pl.BlockSpec((each, 256), lambda i: (0, i))] * parts,
        out_shape=[jax.ShapeDtypeStruct((each, width), BF16)] * parts,
        compiler_params=pltpu.CompilerParams(
            dimension_semantics=("arbitrary",), vmem_limit_bytes=VMEM_ASKED
        ),
        cost_estimate=pl.CostEstimate(flops=1, bytes_accessed=1, transcendentals=0),
        name="ffn_grads",
    )(*turned, *rows, *grads)


def proj_grad_kernel(heads, head_dim, d_ref, x_ref, w_ref, gated_ref, *refs):
    count = len(refs) - heads - 4
    mix = refs[:count]
    outs, rate_ref, gain_ref = refs[count : count + heads], refs[-4], refs[-3]
    turned, gated_turned = refs[-2:]
    each = 3 * head_dim

    @pl.when(pl.program_id(0) == 0)
    def _():
        turned[...] = jnp.transpose(d_ref[...].astype(F32)).astype(BF16)
        gated_turned[...] = jnp.transpose(gated_ref[...].astype(F32)).astype(BF16)

    grad = mm(turned[...], x_ref[...])
    grad_out = mm(gated_turned[...], jnp.concatenate([ref[...] for ref in mix], axis=0))
    gain_ref[...] = jnp.broadcast_to(
        jnp.sum(grad * w_ref[...].astype(F32), axis=0, keepdims=True), gain_ref.shape
    )
    gate = heads * each + 128
    for h, out in enumerate(outs):
        own = slice(h * head_dim, (h + 1) * head_dim)
        out[:each] = grad[h * each : (h + 1) * each].astype(BF16)
        out[each : each + head_dim] = grad[gate + h * head_dim : gate + (h + 1) * head_dim].astype(
            BF16
        )
        out[each + head_dim :] = grad_out[own].astype(BF16)
    rate_ref[...] = grad[heads * each : heads * each + 8]


def proj_grads(d_x, normed, weight, gated, mix, heads, head_dim):
    total, packed = d_x.shape
    width = normed.shape[1]

    def wide(rows):
        return pl.BlockSpec((rows, 256), lambda i: (0, i))

    def whole(array):
        return pl.BlockSpec(array.shape, lambda i: (0, 0))

    return pl.pallas_call(
        partial(proj_grad_kernel, heads, head_dim),
        grid=(width // 256,),
        in_specs=[whole(d_x), wide(total), wide(packed), whole(gated)]
        + [wide(block.shape[0]) for block in mix],
        out_specs=[wide(5 * head_dim)] * heads + [wide(8)] * 2,
        out_shape=[jax.ShapeDtypeStruct((5 * head_dim, width), BF16)] * heads
        + [jax.ShapeDtypeStruct((8, width), F32)] * 2,
        scratch_shapes=[pltpu.VMEM((packed, total), BF16), pltpu.VMEM(gated.shape[::-1], BF16)],
        compiler_params=pltpu.CompilerParams(
            dimension_semantics=("arbitrary",), vmem_limit_bytes=VMEM_ASKED
        ),
        cost_estimate=pl.CostEstimate(flops=1, bytes_accessed=1, transcendentals=0),
        name="proj_grads",
    )(d_x, normed, weight, gated, *mix)


def project_kernel(count, parts, *refs):
    blocks = refs[:count]
    weights = refs[count : count + parts]
    rate_ref, bias_ref, gain_ref, normed_ref, x_ref, logit_ref = refs[count + parts :]
    size = blocks[0].shape[0]
    packed = x_ref.shape[1]
    for i in range(0, count, 2):

        @pl.when(pl.program_id(0) == i // 2)
        def _(i=i):
            rows = jnp.concatenate([ref[...] for ref in blocks[i : i + 2]], axis=0).astype(F32)
            inv = lax.rsqrt(jnp.mean(rows * rows, -1, keepdims=True) + EPS)
            normed = (rows * inv * gain_ref[...]).astype(BF16)
            normed_ref[...] = normed
            weight = jnp.concatenate([ref[...] for ref in weights] + [rate_ref[...]], axis=0)
            out = mm_nt(normed, weight)
            x_ref[...] = out[:, :packed].astype(BF16)
            logit_ref[...] = out[:, packed:] + bias_ref[...]


def project(blocks, weights, rate_rows, bias, gain):
    size, width = blocks[0].shape
    count = len(blocks)
    total = count * size
    packed = sum(w.shape[0] for w in weights)

    def rows(lanes):
        return pl.BlockSpec((2 * size, lanes), lambda i: (i, 0))

    return pl.pallas_call(
        partial(project_kernel, count, len(weights)),
        grid=(count // 2,),
        in_specs=[pl.BlockSpec(memory_space=pltpu.VMEM)] * (count + len(weights) + 3),
        out_specs=[rows(width), rows(packed), rows(128)],
        out_shape=[
            jax.ShapeDtypeStruct((total, width), BF16),
            jax.ShapeDtypeStruct((total, packed), BF16),
            jax.ShapeDtypeStruct((total, 128), F32),
        ],
        compiler_params=pltpu.CompilerParams(
            dimension_semantics=("arbitrary",), vmem_limit_bytes=VMEM_ASKED
        ),
        cost_estimate=pl.CostEstimate(flops=1, bytes_accessed=1, transcendentals=0),
        name="project",
    )(*blocks, *weights, rate_rows, bias, gain)


def trans_dot(left, right):
    return lax.dot_general(
        left, right, (((0,), (0,)), ((), ())), preferred_element_type=jnp.float32
    )


def after(value, *first):
    anywhere = pl.BlockSpec(memory_space=pl.ANY)
    return pl.pallas_call(
        lambda *refs: None,
        out_shape=jax.ShapeDtypeStruct(value.shape, value.dtype),
        in_specs=[anywhere] * (1 + len(first)),
        out_specs=anywhere,
        input_output_aliases={0: 0},
        name="after",
    )(value, *first)


def ring_pairs(size, step):
    order = list(range(0, size, 2)) + list(range(size - 1, 0, -2))
    return [(order[i], order[(i + step) % size]) for i in range(size)]


def ring_place(size, index):
    return jnp.where(index % 2 == 0, index // 2, size - (index + 1) // 2)


def ring_member(size, place):
    return jnp.where(place < size // 2, 2 * place, 2 * (size - place) - 1)


def slot_steps(size):
    steps = [0, -(size // 2)]
    for s in range(1, size // 2):
        steps += [-s, s]
    return steps


def by_slots(arrived):
    return [arrived[0], arrived[-1]] + list(arrived[1:-1])


def ring_gather(block, size, work=None, beside=None):
    arrived = [(block,)]
    others = [(beside,)]
    ahead = back = block
    ahead_too = back_too = beside

    def move(value, step):
        return None if value is None else lax.ppermute(value, "seq", ring_pairs(size, step))

    def do_work(s):
        if not work:
            return []
        return list(work(s, arrived[s], others[s]) if beside is not None else work(s, arrived[s]))

    for s in range(1, size // 2 + 1):
        last = s == size // 2
        done = do_work(s - 1)
        ahead, ahead_too = move(ahead, 1), move(ahead_too, 1)
        if not last:
            back, back_too = move(back, -1), move(back_too, -1)
            done += [back, back_too]
        done = [item for item in done + [ahead_too] if item is not None]
        if done:
            ahead = after(ahead, *done)
        arrived.append((ahead,) if last else (ahead, back))
        others.append((ahead_too,) if last else (ahead_too, back_too))
    do_work(size // 2)
    return arrived


def ring_scatter(part, size, work=()):
    half = size // 2
    ahead, back = part(half).astype(BF16), part(1 - half).astype(BF16)
    for s in range(1, half + 1):
        done = work[s - 1](ahead) if s <= len(work) else []
        ahead = lax.ppermute(ahead, "seq", ring_pairs(size, 1))
        if s < half:
            back = lax.ppermute(back, "seq", ring_pairs(size, -1))
            done = list(done) + [back]
        if done:
            ahead = after(ahead, *done)
        if s < half:
            back = after(back, ahead)
        ahead = ahead.astype(F32)
        if s < half:
            ahead = (ahead + part(half - s)).astype(BF16)
            if s < half - 1:
                back = (back.astype(F32) + part(1 - half + s)).astype(BF16)
    return part(0).astype(F32) + ahead + back.astype(F32)


def pairwise_sum(value, axis, size):
    bit = 1
    while bit < size:
        value = value + lax.ppermute(value, axis, [(i, i ^ bit) for i in range(size)])
        bit *= 2
    return value


def swap(value, bit):
    return lax.ppermute(value, "grp", [(i, i ^ bit) for i in range(4)])


def near(index, k):
    return index ^ k if lax.axis_size("grp") == 4 else k


def start_gather(value):
    if lax.axis_size("grp") != 4:
        whole = lax.all_gather(value, "grp", axis=0)
        return [whole[k] for k in range(whole.shape[0])]
    return [value, swap(value, 1), swap(value, 2)]


def end_gather(parts):
    if lax.axis_size("grp") != 4:
        return parts
    return parts + [swap(parts[2], 1)]


def start_scatter(block):
    if lax.axis_size("grp") != 4:
        whole = jnp.stack([block(k) for k in range(lax.axis_size("grp"))]).astype(BF16)
        return lax.psum_scatter(whole, "grp", scatter_dimension=0, tiled=False)
    return swap(block(3).astype(BF16), 1)


def cross_scatter(block, corner):
    if lax.axis_size("grp") != 4:
        return corner
    return swap((corner.astype(F32) + block(2)).astype(BF16), 2)


def end_scatter(block, across):
    if lax.axis_size("grp") != 4:
        return across
    beside = swap(block(1).astype(BF16), 1).astype(F32)
    return (block(0) + beside + across.astype(F32)).astype(BF16)


def in_turn(blocks, order):
    picked = [lax.dynamic_index_in_dim(blocks, order[i], 0) for i in range(blocks.shape[0])]
    return jnp.concatenate(picked, axis=0)


class HeadPlan:
    def __init__(self, heads, seq, grp):
        self.seq, self.grp, self.heads = seq, grp, heads
        self.local = heads // seq
        self.mixed = (heads // grp) % seq == 0
        self.each = (heads // grp) // seq if self.mixed else 0

    def pick(self, item, seq_index, grp_index):
        rest = item.shape[1:]
        if self.mixed:
            item = item.reshape((self.grp, self.seq, self.each) + rest)
            item = lax.dynamic_index_in_dim(item, seq_index, 1, keepdims=False)
            return self.turn(item.reshape((self.local,) + rest), grp_index)
        return lax.dynamic_slice_in_dim(item, seq_index * self.local, self.local, 0)

    def turn(self, item, grp_index):
        if not self.mixed:
            return item
        item = item.reshape((self.grp, self.each) + item.shape[1:])
        parts = [
            lax.dynamic_index_in_dim(item, near(grp_index, k), 0, keepdims=False)
            for k in range(self.grp)
        ]
        return jnp.concatenate(parts, axis=0)

    def order(self, item):
        rest = item.shape[2:]
        if self.mixed:
            item = item.reshape((self.seq, self.grp, self.each) + rest)
            item = jnp.swapaxes(item, 0, 1)
        return item.reshape((self.heads,) + rest)


def exchange(block):
    return lax.all_to_all(block, "seq", 0, 0, tiled=True)


def cut_heads(plan, mats, turned, head_dim):
    count = len(mats)
    seq = plan.seq
    if plan.each == 1:
        return cut_features(seq, mats, turned)
    mats = [m.T if turn else m for m, turn in zip(mats, turned)]
    cols = mats[0].shape[1]
    if plan.mixed:
        block = jnp.stack([m.reshape(seq, plan.each, head_dim, cols) for m in mats], axis=2)
    else:
        block = lax.all_gather(jnp.stack(mats), "grp", axis=1, tiled=True)
        block = block.reshape(count, seq, plan.local, head_dim, cols).transpose(1, 2, 0, 3, 4)
    return block.reshape(seq, -1, cols)


def start_heads(plan, block):
    seq, _, cols = block.shape
    block = block.transpose(1, 0, 2).reshape(-1, seq * cols)
    return start_gather(block) if plan.mixed else [block]


def end_heads(plan, parts, count, head_dim):
    parts = end_gather(parts) if plan.mixed else parts
    size = count * head_dim
    return [part[i : i + size] for part in parts for i in range(0, part.shape[0], size)]


def heads_block(plan, grads):
    each = plan.each
    return lambda k: jnp.concatenate(grads[k * each : (k + 1) * each], axis=0)


def scatter_heads(plan, grads, block, turned):
    packed, width = grads[0].shape
    count = len(turned)
    seq = plan.seq
    cols = width // seq
    head_dim = packed // count
    if plan.mixed:
        each = plan.each
        block = exchange(block.reshape(-1, seq, cols).transpose(1, 0, 2))
        if each == 1:
            return join_features(block, seq * head_dim, turned)
        block = block.reshape(seq, each, count, head_dim, cols)
        block = block.transpose(2, 0, 1, 3, 4).reshape(count, -1, cols).astype(F32)
        return [part.T if turn else part for part, turn in zip(block, turned)]
    block = jnp.concatenate(grads, axis=0).astype(BF16)
    block = block.reshape(-1, seq, cols).transpose(1, 0, 2)
    block = exchange(block).reshape(seq, plan.local, count, head_dim, cols)
    block = block.transpose(2, 0, 1, 3, 4).reshape(count, -1, cols)
    block = lax.psum_scatter(block, "grp", scatter_dimension=1, tiled=True).astype(F32)
    return [part.T if turn else part for part, turn in zip(block, turned)]


def body(
    tokens,
    cotangent,
    lengths,
    prenorm_gain,
    w_query,
    w_key,
    w_value,
    w_gate,
    rate_weight,
    rate_bias,
    init_weight,
    init_bias,
    inner_gain,
    inner_bias,
    post_gain,
    post_bias,
    w_out,
    feedforward_norm_gain,
    w_swish,
    w_up,
    w_down,
):
    seq_index = lax.axis_index("seq")
    grp_index = lax.axis_index("grp")
    groups = lax.axis_size("grp")
    seq = lax.axis_size("seq")
    rows_tok = tokens.shape[1]
    width = tokens.shape[2]
    heads, head_dim, _ = init_weight.shape
    plan = HeadPlan(heads, seq, groups)
    local = plan.local
    features = local * head_dim
    stream = rows_tok * seq
    steps = slot_steps(seq)
    place = ring_place(seq, seq_index)
    member_of_slot = ring_member(seq, (place + jnp.array(steps, jnp.int32)) % seq)
    apart = (ring_place(seq, jnp.arange(seq, dtype=jnp.int32)) - place) % seq
    slot_of_member = jnp.where(apart > seq // 2, 2 * (seq - apart), 2 * apart + 1)
    slot_of_member = jnp.where(apart == 0, 0, jnp.where(apart == seq // 2, 1, slot_of_member))
    to_slots = (member_of_slot[:, None] == jnp.arange(seq)[None, :]).astype(F32)

    def in_slots(stat):
        cut = stat.reshape(-1, seq, rows_tok)
        out = jnp.einsum("sm,kmt->kst", to_slots, cut, precision=lax.Precision.HIGHEST)
        return out.reshape(-1, stream)

    def in_order(stat):
        cut = stat.reshape(-1, seq, rows_tok)
        out = jnp.einsum("sm,kst->kmt", to_slots, cut, precision=lax.Precision.HIGHEST)
        return out.reshape(-1, stream)

    def pick(item):
        return plan.pick(item, seq_index, grp_index)

    def by_distance(rows):
        return lambda k: lax.slice_in_dim(
            rows, at_slot(k) * rows_tok, (at_slot(k) + 1) * rows_tok, axis=0
        )

    def at_slot(k):
        return steps.index(k if k < seq // 2 else k - seq)

    own_lengths = lax.dynamic_index_in_dim(lengths, grp_index, 0, keepdims=False)
    ends = jnp.cumsum(own_lengths)
    starts = ends - own_lengths
    docs = jnp.concatenate([starts, ends[-1:]])

    proj_block = exchange(
        cut_heads(plan, (w_query, w_key, w_value), (True, True, True), head_dim)
    )
    padded = w_down.shape[0] // seq
    padded += -padded % MB
    rate_rows = jnp.pad(pick(rate_weight.T), ((0, 128 - local), (0, 0)))
    gb, init = chain_params(*(pick(i) for i in (init_weight, init_bias, inner_gain, inner_bias)))
    own = {}

    bias = jnp.pad(pick(rate_bias), (0, 128 - local))[None]

    def token_work(s, arrived):
        if s == 1:
            own["parts"] = start_heads(plan, after(proj_block, arrived[0]))
            return [gb, init]
        if s == seq // 2 - 2:
            mats = (w_swish.T, w_up.T, w_down)
            if plan.each == 1:
                turned = (True, False, False, False, False)
                own["rest"] = cut_features(seq, (w_gate, w_out) + mats, turned)
            else:
                side = cut_heads(plan, (w_gate, w_out), (True, False), head_dim)
                own["rest"] = jnp.concatenate(
                    [side, cut_features(seq, mats, (False,) * 3)], axis=1
                )
            return [own["rest"]]
        if s == seq // 2 - 1:
            own["parts"] = end_heads(plan, own["parts"], 3, head_dim)
            return own["parts"][-1:]
        return []

    token_steps = ring_gather(tokens[0], seq, token_work)
    normed, x3, logits = project(
        sum(by_slots(token_steps), ()), own["parts"], rate_rows, bias, prenorm_gain[None]
    )
    rest_block = exchange(after(own["rest"], token_steps[-1][0]))
    grad_own = cotangent[0]

    inner, *kept = chain_forward(slot_of_member, docs, x3, logits, gb, init, rows_tok)
    kept_stat = after(kept[3], rest_block)
    side_rows = rest_block.shape[1] - 3 * padded
    side_block, ffn_block = rest_block[:, :side_rows], rest_block[:, side_rows:]

    sides = end_heads(plan, start_heads(plan, side_block), 2, head_dim)
    m_gate = jnp.concatenate([side[:head_dim] for side in sides], axis=0)
    m_out = jnp.concatenate([side[head_dim:] for side in sides], axis=0)
    gate_pre = mm_nt(normed, m_gate)
    ffn_block = ffn_block.transpose(1, 0, 2).reshape(3 * padded, width)
    ffn_parts = start_gather(ffn_block)

    sums = jnp.sum(kept_stat[2:4].reshape(2, stream // MB, local, MB), axis=2).reshape(2, stream)
    sums = in_slots(pairwise_sum(sums, "seq", seq)) / width
    mean_o = sums[0][:, None]
    inv_o = lax.rsqrt(sums[1][:, None] - mean_o * mean_o + EPS)
    o_hat = (inner - mean_o) * inv_o
    post_g = pick(post_gain.reshape(heads, head_dim)).reshape(features)
    post_b = pick(post_bias.reshape(heads, head_dim)).reshape(features)
    post = o_hat * post_g + post_b
    gelu_val, gelu_pull = jax.vjp(jax.nn.gelu, gate_pre)
    gated = (gelu_val * post).astype(BF16)
    ffn = {}


    def ffn_corner(since):
        ffn["parts"] = end_gather(ffn_parts[:-1] + [after(ffn_parts[-1], since)])
        return ffn["parts"][-1:]

    mixing = ring_scatter(
        by_distance(mm(gated, m_out).astype(BF16)),
        seq,
        [lambda since: [], lambda since: [], lambda since: [], ffn_corner],
    )
    own_rows = tokens[0].astype(F32)
    resid = own_rows + mixing
    inv_second = lax.rsqrt(jnp.mean(resid * resid, -1, keepdims=True) + EPS)
    unit_second = resid * inv_second
    ffn_in = (unit_second * feedforward_norm_gain).astype(BF16)

    got = {"kept": (), "rows": [], "grads": []}
    d_parts = {}

    def step_work(s, arrived, grads):
        slot = 2 * s if s < seq // 2 else 1
        members = lax.slice_in_dim(member_of_slot, slot, slot + len(arrived))
        got["kept"], d_in = ffn_step(
            members, seq, slot, arrived, grads, ffn["parts"], got["kept"]
        )
        got["rows"].append(arrived)
        got["grads"].append(grads)
        for i in range(len(arrived)):
            d_parts[steps[slot + i]] = d_in[i * rows_tok : (i + 1) * rows_tok]
        return [d_in]

    ring_gather(ffn_in, seq, step_work, grad_own)
    kept_ffn = got["kept"]

    def ffn_work(since):
        first, *others = kept_ffn[:3]
        got["ffn"] = ffn_grads(
            groups,
            [after(first, since)] + others,
            sum(by_slots(got["rows"]), ()),
            sum(by_slots(got["grads"]), ()),
        )
        return got["ffn"][:1]

    def ffn_corner_work(since):
        got["corner"] = start_scatter(lambda k: after(got["ffn"][k], since))
        got["across"] = cross_scatter(ffn_grad, got["corner"])
        return [got["corner"]]

    def ffn_grad(k):
        return got["ffn"][k]

    d_ffn = ring_scatter(
        lambda k: d_parts[k if k < seq // 2 else k - seq], seq, [ffn_work, ffn_corner_work]
    )
    second_scaled = d_ffn * feedforward_norm_gain
    g_ffn_gain = jnp.sum(d_ffn * unit_second, 0)
    d_resid = grad_own.astype(F32) + inv_second * (
        second_scaled - unit_second * jnp.mean(second_scaled * unit_second, -1, keepdims=True)
    )

    def mix_work(s, arrived):
        if s == seq // 2 - 2:
            return [got["across"]]
        if s == seq // 2 - 1:
            summed = end_scatter(ffn_grad, after(got["across"], arrived[0]))
            got["summed"] = summed.reshape(3 * padded, seq, -1).transpose(1, 0, 2)
            return [got["summed"]]
        return []

    mix_steps = ring_gather(d_resid.astype(BF16), seq, mix_work)
    ffn_out = lax.psum_scatter(
        after(kept_ffn[3], mix_steps[seq // 2 - 2][0]), "seq", scatter_dimension=0, tiled=False
    )
    out_tokens = (resid + ffn_out.astype(F32)).astype(BF16)[None]
    d_gated = [mm_nt(jnp.concatenate(arrived, axis=0), m_out) for arrived in mix_steps]
    d_gated = jnp.concatenate(by_slots(d_gated), axis=0)
    d_post = d_gated * gelu_val
    d_gate_pre = gelu_pull(d_gated * post)[0].astype(BF16)
    g_post_gain = jnp.sum(d_post * o_hat, 0)
    g_post_bias = jnp.sum(d_post, 0)
    d_ohat = d_post * post_g
    sums = jnp.stack([jnp.sum(d_ohat, -1), jnp.sum(d_ohat * o_hat, -1)])
    sums = in_slots(pairwise_sum(in_order(sums), "seq", seq)) / width
    g_ffn = exchange(after(got["summed"], sums))
    d_inner = inv_o * (d_ohat - sums[0][:, None] - o_hat * sums[1][:, None])
    d_x, d_gb, d_init = chain_backward(
        slot_of_member, docs, x3, d_inner, d_gate_pre, logits, gb, init, kept, rows_tok
    )
    w_all = jnp.concatenate(own["parts"] + [rate_rows, m_gate], axis=0)
    *head_rows_grads, g_rates, g_gain = proj_grads(
        d_x, normed, w_all, gated, sum(by_slots(mix_steps), ()), local, head_dim
    )
    d_logits = d_x[:, 3 * features : 3 * features + local].astype(F32)
    parts = [item.reshape(local, -1) for item in chain_param_grads(d_gb, d_init, local)]
    parts += [item.reshape(local, head_dim) for item in (g_post_gain, g_post_bias)]
    parts += [g_rates[:local], jnp.sum(d_logits, 0)[:, None]]
    sizes = [item.shape[1] for item in parts]
    flat = jnp.concatenate(parts, axis=1)
    flat = plan.turn(jnp.pad(flat, ((0, 0), (0, -flat.shape[1] % 1024))), grp_index)
    count = flat.size
    flat = jnp.concatenate([flat.reshape(-1), g_gain[0] / prenorm_gain, g_ffn_gain])
    flat = pairwise_sum(flat.reshape(-1, 1024), "grp", groups)
    flat_all = lax.all_gather(flat, "seq", axis=0)
    d_x = after(d_x, g_gain, g_ffn)
    d_normed_part = mm(d_x, w_all).astype(BF16)

    def corner_work(since):
        if not plan.mixed:
            return []
        block = heads_block(plan, head_rows_grads)
        got["corner"] = start_scatter(block)
        got["across"] = cross_scatter(block, after(got["corner"], flat))
        return [got["corner"]]

    def join_work(since):
        got["join"] = join_features(after(g_ffn, since), w_down.shape[0], (False,) * 3)
        return got["join"][:1]

    def across_work(since):
        return [ffn_out] + ([got["across"]] if plan.mixed else [])

    d_normed = ring_scatter(
        by_distance(d_normed_part), seq, [corner_work, join_work, across_work]
    )
    summed = end_scatter(heads_block(plan, head_rows_grads), got["across"]) if plan.mixed else None
    g_heads = scatter_heads(plan, head_rows_grads, summed, (True,) * 4 + (False,))
    own_inv = lax.rsqrt(jnp.mean(own_rows * own_rows, -1, keepdims=True) + EPS)
    own_unit = own_rows * own_inv
    first_scaled = d_normed * prenorm_gain
    grad_tokens = (
        d_resid
        + own_inv
        * (first_scaled - own_unit * jnp.mean(first_scaled * own_unit, -1, keepdims=True))
    )[None]

    flat = after(flat_all, d_normed).reshape(seq, -1)
    gains = jnp.sum(flat[:, count:], 0).reshape(2, width)
    flat = plan.order(flat[:, :count].reshape(seq, local, -1))
    small = []
    offset = 0
    for size in sizes:
        small.append(flat[:, offset : offset + size])
        offset += size
    g_ffn = got["join"]
    return (
        out_tokens,
        grad_tokens,
        gains[0],
        g_heads[0],
        g_heads[1],
        g_heads[2],
        g_heads[3],
        small[6].T,
        small[7][:, 0],
        small[0].reshape(heads, head_dim, head_dim),
        small[1],
        small[2],
        small[3],
        small[4].reshape(width),
        small[5].reshape(width),
        g_heads[4],
        gains[1],
        g_ffn[0].T,
        g_ffn[1].T,
        g_ffn[2],
    )


def solution(mesh):
    whole = P()
    rows = P("grp", "seq", None)
    wide = P("seq", "grp")
    tall = P("grp", "seq")
    return jax.shard_map(
        body,
        mesh=mesh,
        in_specs=(rows, rows, whole, whole, wide, wide, wide, wide)
        + (whole,) * 8
        + (tall, whole, wide, wide, tall),
        out_specs=(rows, rows, whole, wide, wide, wide, wide)
        + (whole,) * 8
        + (tall, whole, wide, wide, tall),
        check_vma=False,
    )
```

```python
from functools import partial

import jax
import jax.numpy as jnp
from jax import lax
from jax.experimental import pallas as pl
from jax.experimental.pallas import tpu as pltpu
from jax.sharding import PartitionSpec as P

MB = 16
EPS = 1e-06
F32 = jnp.float32
VMEM_ASKED = 58 * 1024 * 1024
BF16 = jnp.bfloat16


def mm(left, right):
    return jnp.dot(left, right, preferred_element_type=F32)


def mm_nt(left, right):
    return lax.dot_general(left, right, (((1,), (1,)), ((), ())), preferred_element_type=F32)


def split_two(value):
    high = value.astype(BF16)
    return high, (value - high.astype(F32)).astype(BF16)


def mean_rows(value):
    return jnp.mean(value, axis=0, keepdims=True)


def chunk_rows(value, heads, start, lanes, size):
    tokens = value.shape[0]
    cuts = [value[:, lanes * h + start : lanes * h + start + size] for h in range(heads)]
    parts = [cut[m * MB : (m + 1) * MB] for m in range(tokens // MB) for cut in cuts]
    return jnp.concatenate(parts, axis=0)


def head_rows(rows, heads, h):
    step = MB * heads
    parts = [rows[m * step + h * MB : m * step + (h + 1) * MB] for m in range(rows.shape[0] // step)]
    return jnp.concatenate(parts, axis=0)


def chunk_masks(info, heads, count):
    step = MB * heads
    row = lax.broadcasted_iota(jnp.int32, (count, count), 0)
    col = lax.broadcasted_iota(jnp.int32, (count, count), 1)
    columns = jnp.transpose(info)
    same = ((row % step) // MB == (col % step) // MB) & (columns[:, 1:2] == info[1:2, :])
    return row // step, col // step, row % MB, col % MB, same, columns


def chunk_info(docs_ref, logits, heads, head_dim, chunk):
    tokens = logits.shape[0]
    count = heads * tokens
    step = MB * heads
    docs = docs_ref.shape[0] - 1
    pieces = [logits[m * MB : (m + 1) * MB] for m in range(tokens // MB) for _ in range(heads)]
    spread = jnp.concatenate(pieces, axis=0)
    lane = lax.broadcasted_iota(jnp.int32, spread.shape, 1)
    own = (lax.broadcasted_iota(jnp.int32, spread.shape, 0) % step) // MB
    logit = jnp.sum(jnp.transpose(jnp.where(lane == own, spread, 0.0)), axis=0, keepdims=True)
    start = chunk * tokens
    col = lax.broadcasted_iota(jnp.int32, (1, count), 1)
    block_at = start + (col // step) * MB
    doc = jnp.zeros((1, count), jnp.int32)
    before = end = jnp.int32(0)
    for d in range(docs):
        doc = doc + (block_at >= docs_ref[d]).astype(jnp.int32)
        before = before + (docs_ref[d] < start).astype(jnp.int32)
        end = end + (docs_ref[d] < start + tokens).astype(jnp.int32)
    live = (block_at + col % MB < docs_ref[docs]).astype(F32)
    sig = jax.nn.sigmoid(logit)
    zero = jnp.zeros((1, count), F32)
    return jnp.concatenate(
        [
            sig / head_dim * live,
            doc.astype(F32),
            (doc > before).astype(F32),
            (doc == end).astype(F32),
            zero + (end > before).astype(F32),
            live * sig * (1.0 - sig) / head_dim,
            zero,
            zero,
        ],
        axis=0,
    )


def augment(rows, heads, head_dim, wide):
    count = rows.shape[0]
    near = lax.broadcasted_iota(jnp.int32, (head_dim, wide), 0)
    far = lax.broadcasted_iota(jnp.int32, (head_dim, wide), 1)
    tile = (far % head_dim == near).astype(BF16)
    lane = lax.broadcasted_iota(jnp.int32, (count, wide), 1)
    own = (lax.broadcasted_iota(jnp.int32, (count, wide), 0) % (MB * heads)) // MB
    return jnp.where(lane // head_dim == own, mm(rows, tile), 0.0)


def one_hot_heads(count, heads):
    lane = lax.broadcasted_iota(jnp.int32, (count, 128), 1)
    own = (lax.broadcasted_iota(jnp.int32, (count, 128), 0) % (MB * heads)) // MB
    return (lane == own).astype(BF16)


def forward_kernel(
    heads, idx_ref, docs_ref, x_ref, logit_ref, gb_ref, init_ref, out_ref, n_ref, r_ref, nb_ref, stat_ref, w_ref, state
):
    head_dim = gb_ref.shape[1]
    tokens = x_ref.shape[0]
    count = heads * tokens
    full = init_ref.shape[1]
    wide = full - 128

    @pl.when(pl.program_id(0) == 0)
    def _():
        state[...] = init_ref[...]

    carried = state[...]
    w_ref[0] = carried
    info = chunk_info(docs_ref, logit_ref[...], heads, head_dim, pl.program_id(0))
    x = x_ref[...]
    q_rows = chunk_rows(x, heads, 0, 3 * head_dim, head_dim)
    k_rows = chunk_rows(x, heads, head_dim, 3 * head_dim, head_dim)
    v_rows = chunk_rows(x, heads, 2 * head_dim, 3 * head_dim, head_dim)
    q_t = jnp.transpose(q_rows.astype(F32))
    target_t = jnp.transpose(v_rows.astype(F32) - k_rows.astype(F32))
    mb_row, mb_col, t_row, t_col, same, columns = chunk_masks(info, heads, count)
    gram = jnp.where(same & (mb_row < mb_col), mm_nt(k_rows, k_rows) + 1.0, 0.0).astype(BF16)
    cross = jnp.where(
        same & ((mb_row < mb_col) | ((mb_row == mb_col) & (t_row <= t_col))),
        mm_nt(k_rows, q_rows) + 1.0,
        0.0,
    ).astype(BF16)
    hot = one_hot_heads(count, heads)
    k_aug = jnp.concatenate([augment(k_rows, heads, head_dim, wide).astype(BF16), hot], axis=1)
    q_aug = jnp.concatenate([augment(q_rows, heads, head_dim, wide).astype(BF16), hot], axis=1)
    init = init_ref[...]
    stacked = jnp.concatenate(split_two(carried) + split_two(init), axis=0)
    fresh = info[2:3, :] > 0.5

    def through_state(rows):
        both = mm_nt(stacked, rows)
        return jnp.where(
            fresh,
            both[2 * head_dim : 3 * head_dim] + both[3 * head_dim :],
            both[:head_dim] + both[head_dim : 2 * head_dim],
        )

    z_start = through_state(k_aug)
    gain = gb_ref[0]
    shift = gb_ref[1]
    repeats = count // 128
    inner = 128 // (MB * heads)
    done = []
    for p in range(repeats):
        cols = slice(p * 128, (p + 1) * 128)
        z_base = z_start[:, cols]
        if p:
            z_base = z_base - mm(jnp.concatenate(done, axis=1), gram[: p * 128, cols])
        target = target_t[:, cols]
        rate = info[0:1, cols]
        z = z_base
        for step in range(inner):
            if step:
                z = z_base - mm(scaled.astype(BF16), gram[cols, cols])
            centred = z - mean_rows(z)
            inv = lax.rsqrt(mean_rows(centred * centred) + EPS)
            n = centred * inv
            err = (n * gain + shift - target) * gain
            scaled = (rate * inv) * (err - mean_rows(err) - n * mean_rows(err * n))
        done.append(scaled.astype(BF16))
        n_ref[:, cols] = n
        r_ref[:, cols] = scaled
        stat_ref[0:1, cols] = inv
    r_bf = jnp.concatenate(done, axis=1)
    z_bar = through_state(q_aug) - mm(r_bf, cross)
    centred = z_bar - mean_rows(z_bar)
    inv = lax.rsqrt(mean_rows(centred * centred) + EPS)
    nb = centred * inv
    nb_ref[...] = nb
    stat_ref[1:2, :] = inv
    wide_gain = jnp.concatenate([gain] * repeats, axis=1)
    wide_shift = jnp.concatenate([shift] * repeats, axis=1)
    out_t = q_t + nb * wide_gain + wide_shift
    stat_ref[2:3, :] = jnp.sum(out_t, axis=0, keepdims=True)
    stat_ref[3:4, :] = jnp.sum(out_t * out_t, axis=0, keepdims=True)
    out_rows = jnp.transpose(out_t)
    for h in range(heads):
        out_ref[:, h * head_dim : (h + 1) * head_dim] = head_rows(out_rows, heads, h)
    base = jnp.where(info[4:5, 0:1] > 0.5, init, carried)
    state[...] = base - mm((r_ref[...] * info[3:4, :]).astype(BF16), k_aug)


def backward_kernel(
    heads,
    idx_ref,
    docs_ref,
    x_ref,
    d_ref,
    gate_ref,
    logit_ref,
    gb_ref,
    init_ref,
    n_ref,
    r_ref,
    nb_ref,
    stat_ref,
    w_ref,
    dx_ref,
    dgb_ref,
    dinit_ref,
    state,
):
    head_dim = gb_ref.shape[1]
    tokens = x_ref.shape[0]
    count = heads * tokens
    full = init_ref.shape[1]
    wide = full - 128

    @pl.when(pl.program_id(0) == 0)
    def _():
        state[...] = jnp.zeros_like(state)
        dgb_ref[...] = jnp.zeros_like(dgb_ref)
        dinit_ref[...] = jnp.zeros_like(dinit_ref)

    d_end = state[...]
    carried = w_ref[0]
    init = init_ref[...]
    chunk = pl.num_programs(0) - 1 - pl.program_id(0)
    info = chunk_info(docs_ref, logit_ref[...], heads, head_dim, chunk)
    x = x_ref[...]
    q_rows = chunk_rows(x, heads, 0, 3 * head_dim, head_dim)
    k_rows = chunk_rows(x, heads, head_dim, 3 * head_dim, head_dim)
    v_rows = chunk_rows(x, heads, 2 * head_dim, 3 * head_dim, head_dim)
    d_rows = chunk_rows(d_ref[...], heads, 0, head_dim, head_dim)
    target_t = jnp.transpose(v_rows.astype(F32) - k_rows.astype(F32))
    d_t = jnp.transpose(d_rows)
    mb_row, mb_col, t_row, t_col, same, columns = chunk_masks(info, heads, count)
    earlier = same & (mb_row < mb_col)
    later = same & (mb_row > mb_col)
    up_to = same & ((mb_row < mb_col) | ((mb_row == mb_col) & (t_row <= t_col)))
    from_on = same & ((mb_row > mb_col) | ((mb_row == mb_col) & (t_row >= t_col)))
    gram = jnp.where(later, mm_nt(k_rows, k_rows) + 1.0, 0.0).astype(BF16)
    cross = jnp.where(from_on, mm_nt(q_rows, k_rows) + 1.0, 0.0).astype(BF16)
    hot = one_hot_heads(count, heads)
    k_aug = jnp.concatenate([augment(k_rows, heads, head_dim, wide).astype(BF16), hot], axis=1)
    q_aug = jnp.concatenate([augment(q_rows, heads, head_dim, wide).astype(BF16), hot], axis=1)
    gain = gb_ref[0]
    shift = gb_ref[1]
    repeats = count // 128
    inner = 128 // (MB * heads)
    wide_gain = jnp.concatenate([gain] * repeats, axis=1)
    nb = nb_ref[...]
    inv_b = stat_ref[1:2, :]
    d_nb = d_t * wide_gain
    d_zbar = inv_b * (d_nb - mean_rows(d_nb) - nb * mean_rows(d_nb * nb))
    scaled_t = r_ref[...]
    last = info[3:4, :]
    dr_base = -mm(d_zbar.astype(BF16), cross) - last * mm_nt(d_end.astype(BF16), k_aug)
    gain_sum = jnp.zeros((head_dim, 128), F32)
    shift_sum = jnp.zeros((head_dim, 128), F32)
    for p in range(repeats):
        cols = slice(p * 128, (p + 1) * 128)
        gain_sum = gain_sum + d_t[:, cols] * nb[:, cols]
        shift_sum = shift_sum + d_t[:, cols]
    done = []
    errs = []
    d_rates = []
    for p in reversed(range(repeats)):
        cols = slice(p * 128, (p + 1) * 128)
        base = dr_base[:, cols]
        if done:
            base = base - mm(jnp.concatenate(done, axis=1), gram[(p + 1) * 128 :, cols])
        n = n_ref[:, cols]
        inv = stat_ref[0:1, cols]
        rate = info[0:1, cols]
        miss = n * gain + shift - target_t[:, cols]
        err = miss * gain
        along = mean_rows(err * n)
        plain = inv * (err - mean_rows(err) - n * along)
        gain2 = gain * gain
        d_scaled = base
        for step in range(inner):
            if step:
                d_scaled = base - mm(d_z.astype(BF16), gram[cols, cols])
            g = rate * d_scaled
            g_n = mean_rows(g * n)
            d_err = inv * (g - mean_rows(g) - n * g_n)
            d_n = d_err * gain2 - inv * (g * along + err * g_n)
            d_z = inv * (d_n - mean_rows(d_n) - n * (mean_rows(d_n * n) + mean_rows(g * plain)))
        done.insert(0, d_z.astype(BF16))
        errs.insert(0, d_err * gain)
        d_rates.insert(0, jnp.sum(d_scaled * plain, axis=0, keepdims=True))
        gain_sum = gain_sum + d_err * (miss + gain * n)
        shift_sum = shift_sum + d_err * gain
    dgb_ref[0] += gain_sum
    dgb_ref[1] += shift_sum
    dz_bf = jnp.concatenate(done, axis=1)
    d_z = dz_bf.astype(F32)
    d_errg = jnp.concatenate(errs, axis=1)
    turned = jnp.transpose(jnp.concatenate([d_zbar, scaled_t, d_z, d_errg], axis=0))
    zb_rows = turned[:, :head_dim].astype(BF16)
    r_rows = turned[:, head_dim : 2 * head_dim].astype(BF16)
    z_rows = turned[:, 2 * head_dim : 3 * head_dim].astype(BF16)
    e_rows = turned[:, 3 * head_dim :]
    d_cross = jnp.where(from_on, -mm_nt(zb_rows, r_rows), 0.0).astype(BF16)
    d_cross_t = jnp.where(up_to, -mm_nt(r_rows, zb_rows), 0.0).astype(BF16)
    d_gram = (
        jnp.where(later, -mm_nt(z_rows, r_rows), 0.0)
        + jnp.where(earlier, -mm_nt(r_rows, z_rows), 0.0)
    ).astype(BF16)
    is_init = columns[:, 2:3] > 0.5
    is_last = columns[:, 3:4] > 0.5

    def stack_heads(weight):
        parts = [weight[:, h * head_dim : (h + 1) * head_dim] for h in range(heads)]
        pad = wide - heads * head_dim
        if pad:
            parts.append(jnp.zeros((pad, head_dim), F32))
        return jnp.concatenate(parts, axis=0).astype(BF16)

    w_both = jnp.concatenate([stack_heads(carried), stack_heads(init)], axis=0)
    d_stack = stack_heads(d_end)

    def by_state(rows):
        own = augment(rows, heads, head_dim, wide)
        return jnp.concatenate(
            [jnp.where(is_init, 0.0, own), jnp.where(is_init, own, 0.0)], axis=1
        ).astype(BF16)

    dq = d_rows + mm(d_cross, k_rows) + mm(by_state(zb_rows), w_both)
    r_own = jnp.where(is_last, augment(r_rows, heads, head_dim, wide), 0.0).astype(BF16)
    dk = (
        e_rows
        + mm(d_gram, k_rows)
        + mm(d_cross_t, q_rows)
        + mm(by_state(z_rows), w_both)
        - mm(r_own, d_stack)
    )
    packed = jnp.concatenate([dq.astype(BF16), dk.astype(BF16), (-e_rows).astype(BF16)], axis=1)
    each = 3 * head_dim
    d_logits = jnp.concatenate(d_rates, axis=1) * info[5:6, :]
    turned = jnp.transpose(jnp.concatenate([d_logits, jnp.zeros((7, count), F32)], axis=0))
    lane = lax.broadcasted_iota(jnp.int32, (tokens, 128), 1)
    logit_rows = jnp.zeros((tokens, 128), F32)
    for h in range(heads):
        dx_ref[:, h * each : (h + 1) * each] = head_rows(packed, heads, h)
        logit_rows = jnp.where(lane == h, head_rows(turned, heads, h)[:, 0:1], logit_rows)
    dx_ref[:, heads * each : heads * each + 128] = logit_rows.astype(BF16)
    dx_ref[:, heads * each + 128 :] = gate_ref[...]
    row_init = info[2:3, :] > 0.5
    zb_two = jnp.concatenate(
        [jnp.where(row_init, 0.0, d_zbar), jnp.where(row_init, d_zbar, 0.0)], axis=0
    ).astype(BF16)
    z_two = jnp.concatenate(
        [jnp.where(row_init, 0.0, d_z), jnp.where(row_init, d_z, 0.0)], axis=0
    ).astype(BF16)
    d_both = mm(zb_two, q_aug) + mm(z_two, k_aug)
    fresh = info[4:5, 0:1] > 0.5
    state[...] = d_both[:head_dim] + jnp.where(fresh, 0.0, d_end)
    dinit_ref[...] += d_both[head_dim:] + jnp.where(fresh, d_end, 0.0)


def chain_specs(heads, tokens, head_dim, full, at):
    count = heads * tokens
    return dict(
        x=pl.BlockSpec((tokens, heads * 3 * head_dim), lambda i, idx, docs: (idx[at(i)], 0)),
        dx=pl.BlockSpec((tokens, heads * 4 * head_dim + 128), lambda i, idx, docs: (idx[at(i)], 0)),
        rows=pl.BlockSpec((tokens, heads * head_dim), lambda i, idx, docs: (idx[at(i)], 0)),
        logit=pl.BlockSpec((tokens, 128), lambda i, idx, docs: (idx[at(i)], 0)),
        gb=pl.BlockSpec((2, head_dim, 128), lambda i, idx, docs: (0, 0, 0)),
        init=pl.BlockSpec((head_dim, full), lambda i, idx, docs: (0, 0)),
        tall=pl.BlockSpec((head_dim, count), lambda i, idx, docs: (0, at(i))),
        stat=pl.BlockSpec((8, count), lambda i, idx, docs: (0, at(i))),
        weight=pl.BlockSpec((1, head_dim, full), lambda i, idx, docs: (at(i), 0, 0)),
    )


def chain_forward(idx, docs, x3, logits, gb, init, tokens):
    total = x3.shape[0]
    head_dim = gb.shape[1]
    heads = x3.shape[1] // (3 * head_dim)
    chunks = total // tokens
    full = init.shape[1]
    s = chain_specs(heads, tokens, head_dim, full, lambda i: i)
    tall = jax.ShapeDtypeStruct((head_dim, heads * total), F32)
    return pl.pallas_call(
        partial(forward_kernel, heads),
        grid_spec=pltpu.PrefetchScalarGridSpec(
            num_scalar_prefetch=2,
            grid=(chunks,),
            in_specs=[s["x"], s["logit"], s["gb"], s["init"]],
            out_specs=[s["rows"], s["tall"], s["tall"], s["tall"], s["stat"], s["weight"]],
            scratch_shapes=[pltpu.VMEM((head_dim, full), F32)],
        ),
        out_shape=[
            jax.ShapeDtypeStruct((total, heads * head_dim), F32),
            tall,
            tall,
            tall,
            jax.ShapeDtypeStruct((8, heads * total), F32),
            jax.ShapeDtypeStruct((chunks, head_dim, full), F32),
        ],
        compiler_params=pltpu.CompilerParams(
            dimension_semantics=("arbitrary",), vmem_limit_bytes=VMEM_ASKED
        ),
        cost_estimate=pl.CostEstimate(flops=1, bytes_accessed=1, transcendentals=0),
        name="chain_forward",
    )(idx, docs, x3, logits, gb, init)


def chain_backward(idx, docs, x3, d_inner, d_gate, logits, gb, init, kept, tokens):
    total = x3.shape[0]
    head_dim = gb.shape[1]
    heads = x3.shape[1] // (3 * head_dim)
    chunks = total // tokens
    full = init.shape[1]
    s = chain_specs(heads, tokens, head_dim, full, lambda i: chunks - 1 - i)
    return pl.pallas_call(
        partial(backward_kernel, heads),
        grid_spec=pltpu.PrefetchScalarGridSpec(
            num_scalar_prefetch=2,
            grid=(chunks,),
            in_specs=[
                s["x"],
                s["rows"],
                s["rows"],
                s["logit"],
                s["gb"],
                s["init"],
                s["tall"],
                s["tall"],
                s["tall"],
                s["stat"],
                s["weight"],
            ],
            out_specs=[s["dx"], s["gb"], s["init"]],
            scratch_shapes=[pltpu.VMEM((head_dim, full), F32)],
        ),
        out_shape=[
            jax.ShapeDtypeStruct((total, heads * 4 * head_dim + 128), BF16),
            jax.ShapeDtypeStruct(gb.shape, F32),
            jax.ShapeDtypeStruct(init.shape, F32),
        ],
        compiler_params=pltpu.CompilerParams(
            dimension_semantics=("arbitrary",), vmem_limit_bytes=VMEM_ASKED
        ),
        cost_estimate=pl.CostEstimate(flops=1, bytes_accessed=1, transcendentals=0),
        name="chain_backward",
    )(idx, docs, x3, d_inner, d_gate, logits, gb, init, *kept)


def chain_params(init_weight, init_bias, inner_gain, inner_bias):
    heads, head_dim, _ = init_weight.shape
    reps = 128 // (MB * heads)

    def pattern(item):
        row = jnp.broadcast_to(item.T[:, None, :, None], (head_dim, reps, heads, MB))
        return row.reshape(head_dim, 128)

    gb = jnp.stack([pattern(inner_gain), pattern(inner_bias)])
    wide = max(128, heads * head_dim)
    w_t = jnp.transpose(init_weight, (2, 0, 1)).reshape(head_dim, heads * head_dim)
    init = jnp.concatenate(
        [
            jnp.pad(w_t, ((0, 0), (0, wide - heads * head_dim))),
            jnp.pad(init_bias.T, ((0, 0), (0, 128 - heads))),
        ],
        axis=1,
    )
    return gb, init


def chain_param_grads(dgb, dinit, heads):
    head_dim = dinit.shape[0]
    wide = dinit.shape[1] - 128
    d_w = dinit[:, : heads * head_dim].reshape(head_dim, heads, head_dim).transpose(1, 2, 0)
    d_b = dinit[:, wide : wide + heads].T
    both = jnp.sum(dgb.reshape(2, head_dim, -1, heads, MB), axis=(2, 4))
    return d_w, d_b, both[0].T, both[1].T


def cut_kernel(turned, shares, *refs):
    mats, out_ref, held = refs[: len(turned)], refs[-2], refs[-1]
    at = 0
    for mat, turn, share in zip(mats, turned, shares):
        padded = share + -share % MB
        value = mat[...].astype(F32)
        held[: value.shape[1] if turn else value.shape[0]] = jnp.transpose(value) if turn else value
        for s in range(out_ref.shape[0]):
            out_ref[s, at : at + share] = held[s * share : (s + 1) * share].astype(BF16)
            if padded > share:
                out_ref[s, at + share : at + padded] = jnp.zeros(
                    (padded - share, out_ref.shape[2]), BF16
                )
        at += padded


def cut_features(seq, mats, turned):
    features = [m.shape[1] if turn else m.shape[0] for m, turn in zip(mats, turned)]
    cols = mats[0].shape[0] if turned[0] else mats[0].shape[1]
    shares = [count // seq for count in features]
    rows = sum(share + -share % MB for share in shares)
    return pl.pallas_call(
        partial(cut_kernel, turned, shares),
        out_shape=jax.ShapeDtypeStruct((seq, rows, cols), BF16),
        scratch_shapes=[pltpu.VMEM((max(features), cols), F32)],
        compiler_params=pltpu.CompilerParams(vmem_limit_bytes=VMEM_ASKED),
        cost_estimate=pl.CostEstimate(flops=1, bytes_accessed=1, transcendentals=0),
        name="cut_features",
    )(*mats)


def join_kernel(turned, share, padded, in_ref, *refs):
    outs, held = refs[:-1], refs[-1]
    for i, out in enumerate(outs):
        for s in range(in_ref.shape[0]):
            held[s * share : (s + 1) * share] = in_ref[
                s, i * padded : i * padded + share
            ].astype(F32)
        out[...] = jnp.transpose(held[...]) if turned[i] else held[...]


def join_features(block, features, turned):
    seq, rows, cols = block.shape
    shapes = [(cols, features) if turn else (features, cols) for turn in turned]
    return pl.pallas_call(
        partial(join_kernel, turned, features // seq, rows // len(turned)),
        out_shape=[jax.ShapeDtypeStruct(shape, F32) for shape in shapes],
        scratch_shapes=[pltpu.VMEM((features, cols), F32)],
        compiler_params=pltpu.CompilerParams(vmem_limit_bytes=VMEM_ASKED),
        cost_estimate=pl.CostEstimate(flops=1, bytes_accessed=1, transcendentals=0),
        name="join_features",
    )(block)


def ffn_kernel(count, parts, kept, member_ref, *refs):
    rows_refs = refs[:count]
    grad_refs = refs[count : 2 * count]
    weights = refs[2 * count : 2 * count + parts]
    outs = refs[2 * count + parts + kept :]
    (at_ref, ut_ref, ht_ref, y_ref, d_ref, a_t, u_t, h_t, y_all, d_all) = outs
    step = pl.program_id(0)
    size = rows_refs[0].shape[0]

    @pl.when(step == 0)
    def _():
        padded = weights[0].shape[0] // 3
        swish, up, down = (
            jnp.concatenate([w[i * padded : (i + 1) * padded] for w in weights], axis=0)
            for i in range(3)
        )
        rows = jnp.concatenate([ref[...] for ref in rows_refs], axis=0)
        grad = jnp.concatenate([ref[...] for ref in grad_refs], axis=0)
        act_a = mm_nt(rows, swish)
        act_u = mm_nt(rows, up)
        d_hidden = mm_nt(grad, down)
        sig = jax.nn.sigmoid(act_a)
        gate = act_a * sig
        hidden = gate * act_u
        d_a = d_hidden * act_u * sig * (1.0 + act_a * (1.0 - sig))
        d_u = d_hidden * gate
        d_all[...] = (mm(d_a.astype(BF16), swish) + mm(d_u.astype(BF16), up)).astype(BF16)
        y_all[...] = mm(hidden.astype(BF16), down).astype(BF16)
        fill = -hidden.shape[1] % 128
        for out, value in ((a_t, d_a), (u_t, d_u), (h_t, hidden)):
            if fill:
                value = jnp.concatenate([value, jnp.zeros((value.shape[0], fill), F32)], axis=1)
            out[...] = jnp.transpose(value)[: out.shape[0]].astype(BF16)

    for i in range(count):

        @pl.when(step == i)
        def _(i=i):
            part = slice(i * size, (i + 1) * size)
            at_ref[...] = a_t[:, part]
            ut_ref[...] = u_t[:, part]
            ht_ref[...] = h_t[:, part]
            y_ref[0] = y_all[part]
            d_ref[...] = d_all[part]


def ffn_step(members, seq, slot, rows, grads, weights, kept):
    count = len(rows)
    size, width = rows[0].shape
    total = seq * size
    features = sum(w.shape[0] for w in weights) // 3
    whole = pl.BlockSpec(memory_space=pltpu.VMEM)

    turned_spec = pl.BlockSpec((features, size), lambda s, member: (0, slot + s))
    turned = jax.ShapeDtypeStruct((features, total), BF16)
    first = 1 + 2 * count + len(weights)
    out = pl.pallas_call(
        partial(ffn_kernel, count, len(weights), len(kept)),
        grid_spec=pltpu.PrefetchScalarGridSpec(
            num_scalar_prefetch=1,
            grid=(count,),
            in_specs=[whole] * (2 * count + len(weights))
            + [pl.BlockSpec(memory_space=pl.ANY)] * len(kept),
            out_specs=[turned_spec] * 3
            + [
                pl.BlockSpec((1, size, width), lambda s, member: (member[s], 0, 0)),
                pl.BlockSpec((size, width), lambda s, member: (s, 0)),
            ],
            scratch_shapes=[pltpu.VMEM((features, count * size), BF16)] * 3
            + [pltpu.VMEM((count * size, width), BF16)] * 2,
        ),
        out_shape=[turned] * 3
        + [
            jax.ShapeDtypeStruct((seq, size, width), BF16),
            jax.ShapeDtypeStruct((count * size, width), BF16),
        ],
        input_output_aliases={first + i: i for i in range(len(kept))},
        compiler_params=pltpu.CompilerParams(
            dimension_semantics=("arbitrary",), vmem_limit_bytes=VMEM_ASKED
        ),
        cost_estimate=pl.CostEstimate(flops=1, bytes_accessed=1, transcendentals=0),
        name="ffn_step",
    )(members, *rows, *grads, *weights, *kept)
    return out[:-1], out[-1]


def ffn_grad_kernel(parts, count, at_ref, ut_ref, ht_ref, *refs):
    x = jnp.concatenate([ref[...] for ref in refs[:count]], axis=0)
    g = jnp.concatenate([ref[...] for ref in refs[count : 2 * count]], axis=0)
    padded = at_ref.shape[0] // parts
    for i, out in enumerate(refs[2 * count :]):
        own = slice(i * padded, (i + 1) * padded)
        out[:padded] = mm(at_ref[own], x).astype(BF16)
        out[padded : 2 * padded] = mm(ut_ref[own], x).astype(BF16)
        out[2 * padded :] = mm(ht_ref[own], g).astype(BF16)


def ffn_grads(parts, turned, rows, grads):
    size, width = rows[0].shape
    count = len(rows)
    features = turned[0].shape[0]
    wide = pl.BlockSpec((size, 256), lambda i: (0, i))
    whole = pl.BlockSpec((features, count * size), lambda i: (0, 0))
    each = 3 * features // parts
    return pl.pallas_call(
        partial(ffn_grad_kernel, parts, count),
        grid=(width // 256,),
        in_specs=[whole] * 3 + [wide] * (2 * count),
        out_specs=[pl.BlockSpec((each, 256), lambda i: (0, i))] * parts,
        out_shape=[jax.ShapeDtypeStruct((each, width), BF16)] * parts,
        compiler_params=pltpu.CompilerParams(
            dimension_semantics=("arbitrary",), vmem_limit_bytes=VMEM_ASKED
        ),
        cost_estimate=pl.CostEstimate(flops=1, bytes_accessed=1, transcendentals=0),
        name="ffn_grads",
    )(*turned, *rows, *grads)


def proj_grad_kernel(heads, head_dim, d_ref, x_ref, w_ref, gated_ref, *refs):
    count = len(refs) - heads - 4
    mix = refs[:count]
    outs, rate_ref, gain_ref = refs[count : count + heads], refs[-4], refs[-3]
    turned, gated_turned = refs[-2:]
    each = 3 * head_dim

    @pl.when(pl.program_id(0) == 0)
    def _():
        turned[...] = jnp.transpose(d_ref[...].astype(F32)).astype(BF16)
        gated_turned[...] = jnp.transpose(gated_ref[...].astype(F32)).astype(BF16)

    grad = mm(turned[...], x_ref[...])
    grad_out = mm(gated_turned[...], jnp.concatenate([ref[...] for ref in mix], axis=0))
    gain_ref[...] = jnp.broadcast_to(
        jnp.sum(grad * w_ref[...].astype(F32), axis=0, keepdims=True), gain_ref.shape
    )
    gate = heads * each + 128
    for h, out in enumerate(outs):
        own = slice(h * head_dim, (h + 1) * head_dim)
        out[:each] = grad[h * each : (h + 1) * each].astype(BF16)
        out[each : each + head_dim] = grad[gate + h * head_dim : gate + (h + 1) * head_dim].astype(
            BF16
        )
        out[each + head_dim :] = grad_out[own].astype(BF16)
    rate_ref[...] = grad[heads * each : heads * each + 8]


def proj_grads(d_x, normed, weight, gated, mix, heads, head_dim):
    total, packed = d_x.shape
    width = normed.shape[1]

    def wide(rows):
        return pl.BlockSpec((rows, 256), lambda i: (0, i))

    def whole(array):
        return pl.BlockSpec(array.shape, lambda i: (0, 0))

    return pl.pallas_call(
        partial(proj_grad_kernel, heads, head_dim),
        grid=(width // 256,),
        in_specs=[whole(d_x), wide(total), wide(packed), whole(gated)]
        + [wide(block.shape[0]) for block in mix],
        out_specs=[wide(5 * head_dim)] * heads + [wide(8)] * 2,
        out_shape=[jax.ShapeDtypeStruct((5 * head_dim, width), BF16)] * heads
        + [jax.ShapeDtypeStruct((8, width), F32)] * 2,
        scratch_shapes=[pltpu.VMEM((packed, total), BF16), pltpu.VMEM(gated.shape[::-1], BF16)],
        compiler_params=pltpu.CompilerParams(
            dimension_semantics=("arbitrary",), vmem_limit_bytes=VMEM_ASKED
        ),
        cost_estimate=pl.CostEstimate(flops=1, bytes_accessed=1, transcendentals=0),
        name="proj_grads",
    )(d_x, normed, weight, gated, *mix)


def project_kernel(count, parts, *refs):
    blocks = refs[:count]
    weights = refs[count : count + parts]
    rate_ref, bias_ref, gain_ref, normed_ref, x_ref, logit_ref = refs[count + parts :]
    size = blocks[0].shape[0]
    packed = x_ref.shape[1]
    for i in range(0, count, 2):

        @pl.when(pl.program_id(0) == i // 2)
        def _(i=i):
            rows = jnp.concatenate([ref[...] for ref in blocks[i : i + 2]], axis=0).astype(F32)
            inv = lax.rsqrt(jnp.mean(rows * rows, -1, keepdims=True) + EPS)
            normed = (rows * inv * gain_ref[...]).astype(BF16)
            normed_ref[...] = normed
            weight = jnp.concatenate([ref[...] for ref in weights] + [rate_ref[...]], axis=0)
            out = mm_nt(normed, weight)
            x_ref[...] = out[:, :packed].astype(BF16)
            logit_ref[...] = out[:, packed:] + bias_ref[...]


def project(blocks, weights, rate_rows, bias, gain):
    size, width = blocks[0].shape
    count = len(blocks)
    total = count * size
    packed = sum(w.shape[0] for w in weights)

    def rows(lanes):
        return pl.BlockSpec((2 * size, lanes), lambda i: (i, 0))

    return pl.pallas_call(
        partial(project_kernel, count, len(weights)),
        grid=(count // 2,),
        in_specs=[pl.BlockSpec(memory_space=pltpu.VMEM)] * (count + len(weights) + 3),
        out_specs=[rows(width), rows(packed), rows(128)],
        out_shape=[
            jax.ShapeDtypeStruct((total, width), BF16),
            jax.ShapeDtypeStruct((total, packed), BF16),
            jax.ShapeDtypeStruct((total, 128), F32),
        ],
        compiler_params=pltpu.CompilerParams(
            dimension_semantics=("arbitrary",), vmem_limit_bytes=VMEM_ASKED
        ),
        cost_estimate=pl.CostEstimate(flops=1, bytes_accessed=1, transcendentals=0),
        name="project",
    )(*blocks, *weights, rate_rows, bias, gain)


def trans_dot(left, right):
    return lax.dot_general(
        left, right, (((0,), (0,)), ((), ())), preferred_element_type=jnp.float32
    )


def after(value, *first):
    anywhere = pl.BlockSpec(memory_space=pl.ANY)
    return pl.pallas_call(
        lambda *refs: None,
        out_shape=jax.ShapeDtypeStruct(value.shape, value.dtype),
        in_specs=[anywhere] * (1 + len(first)),
        out_specs=anywhere,
        input_output_aliases={0: 0},
        name="after",
    )(value, *first)


def ring_pairs(size, step):
    order = list(range(0, size, 2)) + list(range(size - 1, 0, -2))
    return [(order[i], order[(i + step) % size]) for i in range(size)]


def ring_place(size, index):
    return jnp.where(index % 2 == 0, index // 2, size - (index + 1) // 2)


def ring_member(size, place):
    return jnp.where(place < size // 2, 2 * place, 2 * (size - place) - 1)


def slot_steps(size):
    steps = [0, -(size // 2)]
    for s in range(1, size // 2):
        steps += [-s, s]
    return steps


def by_slots(arrived):
    return [arrived[0], arrived[-1]] + list(arrived[1:-1])


def ring_gather(block, size, work=None, beside=None):
    arrived = [(block,)]
    others = [(beside,)]
    ahead = back = block
    ahead_too = back_too = beside

    def move(value, step):
        return None if value is None else lax.ppermute(value, "seq", ring_pairs(size, step))

    def do_work(s):
        if not work:
            return []
        return list(work(s, arrived[s], others[s]) if beside is not None else work(s, arrived[s]))

    for s in range(1, size // 2 + 1):
        last = s == size // 2
        done = do_work(s - 1)
        ahead, ahead_too = move(ahead, 1), move(ahead_too, 1)
        if not last:
            back, back_too = move(back, -1), move(back_too, -1)
            done += [back, back_too]
        done = [item for item in done + [ahead_too] if item is not None]
        if done:
            ahead = after(ahead, *done)
        arrived.append((ahead,) if last else (ahead, back))
        others.append((ahead_too,) if last else (ahead_too, back_too))
    do_work(size // 2)
    return arrived


def ring_scatter(part, size, work=()):
    half = size // 2
    ahead, back = part(half).astype(BF16), part(1 - half).astype(BF16)
    for s in range(1, half + 1):
        done = work[s - 1](ahead) if s <= len(work) else []
        ahead = lax.ppermute(ahead, "seq", ring_pairs(size, 1))
        if s < half:
            back = lax.ppermute(back, "seq", ring_pairs(size, -1))
            done = list(done) + [back]
        if done:
            ahead = after(ahead, *done)
        if s < half:
            back = after(back, ahead)
        ahead = ahead.astype(F32)
        if s < half:
            ahead = (ahead + part(half - s)).astype(BF16)
            if s < half - 1:
                back = (back.astype(F32) + part(1 - half + s)).astype(BF16)
    return part(0).astype(F32) + ahead + back.astype(F32)


def pairwise_sum(value, axis, size):
    bit = 1
    while bit < size:
        value = value + lax.ppermute(value, axis, [(i, i ^ bit) for i in range(size)])
        bit *= 2
    return value


def swap(value, bit):
    return lax.ppermute(value, "grp", [(i, i ^ bit) for i in range(4)])


def near(index, k):
    return index ^ k if lax.axis_size("grp") == 4 else k


def start_gather(value):
    if lax.axis_size("grp") != 4:
        whole = lax.all_gather(value, "grp", axis=0)
        return [whole[k] for k in range(whole.shape[0])]
    return [value, swap(value, 1), swap(value, 2)]


def end_gather(parts):
    if lax.axis_size("grp") != 4:
        return parts
    return parts + [swap(parts[2], 1)]


def start_scatter(block):
    if lax.axis_size("grp") != 4:
        whole = jnp.stack([block(k) for k in range(lax.axis_size("grp"))]).astype(BF16)
        return lax.psum_scatter(whole, "grp", scatter_dimension=0, tiled=False)
    return swap(block(3).astype(BF16), 1)


def cross_scatter(block, corner):
    if lax.axis_size("grp") != 4:
        return corner
    return swap((corner.astype(F32) + block(2)).astype(BF16), 2)


def end_scatter(block, across):
    if lax.axis_size("grp") != 4:
        return across
    beside = swap(block(1).astype(BF16), 1).astype(F32)
    return (block(0) + beside + across.astype(F32)).astype(BF16)


def in_turn(blocks, order):
    picked = [lax.dynamic_index_in_dim(blocks, order[i], 0) for i in range(blocks.shape[0])]
    return jnp.concatenate(picked, axis=0)


class HeadPlan:
    def __init__(self, heads, seq, grp):
        self.seq, self.grp, self.heads = seq, grp, heads
        self.local = heads // seq
        self.mixed = (heads // grp) % seq == 0
        self.each = (heads // grp) // seq if self.mixed else 0

    def pick(self, item, seq_index, grp_index):
        rest = item.shape[1:]
        if self.mixed:
            item = item.reshape((self.grp, self.seq, self.each) + rest)
            item = lax.dynamic_index_in_dim(item, seq_index, 1, keepdims=False)
            return self.turn(item.reshape((self.local,) + rest), grp_index)
        return lax.dynamic_slice_in_dim(item, seq_index * self.local, self.local, 0)

    def turn(self, item, grp_index):
        if not self.mixed:
            return item
        item = item.reshape((self.grp, self.each) + item.shape[1:])
        parts = [
            lax.dynamic_index_in_dim(item, near(grp_index, k), 0, keepdims=False)
            for k in range(self.grp)
        ]
        return jnp.concatenate(parts, axis=0)

    def order(self, item):
        rest = item.shape[2:]
        if self.mixed:
            item = item.reshape((self.seq, self.grp, self.each) + rest)
            item = jnp.swapaxes(item, 0, 1)
        return item.reshape((self.heads,) + rest)


def exchange(block):
    return lax.all_to_all(block, "seq", 0, 0, tiled=True)


def cut_heads(plan, mats, turned, head_dim):
    count = len(mats)
    seq = plan.seq
    if plan.each == 1:
        return cut_features(seq, mats, turned)
    mats = [m.T if turn else m for m, turn in zip(mats, turned)]
    cols = mats[0].shape[1]
    if plan.mixed:
        block = jnp.stack([m.reshape(seq, plan.each, head_dim, cols) for m in mats], axis=2)
    else:
        block = lax.all_gather(jnp.stack(mats), "grp", axis=1, tiled=True)
        block = block.reshape(count, seq, plan.local, head_dim, cols).transpose(1, 2, 0, 3, 4)
    return block.reshape(seq, -1, cols)


def start_heads(plan, block):
    seq, _, cols = block.shape
    block = block.transpose(1, 0, 2).reshape(-1, seq * cols)
    return start_gather(block) if plan.mixed else [block]


def end_heads(plan, parts, count, head_dim):
    parts = end_gather(parts) if plan.mixed else parts
    size = count * head_dim
    return [part[i : i + size] for part in parts for i in range(0, part.shape[0], size)]


def heads_block(plan, grads):
    each = plan.each
    return lambda k: jnp.concatenate(grads[k * each : (k + 1) * each], axis=0)


def scatter_heads(plan, grads, block, turned):
    packed, width = grads[0].shape
    count = len(turned)
    seq = plan.seq
    cols = width // seq
    head_dim = packed // count
    if plan.mixed:
        each = plan.each
        block = exchange(block.reshape(-1, seq, cols).transpose(1, 0, 2))
        if each == 1:
            return join_features(block, seq * head_dim, turned)
        block = block.reshape(seq, each, count, head_dim, cols)
        block = block.transpose(2, 0, 1, 3, 4).reshape(count, -1, cols).astype(F32)
        return [part.T if turn else part for part, turn in zip(block, turned)]
    block = jnp.concatenate(grads, axis=0).astype(BF16)
    block = block.reshape(-1, seq, cols).transpose(1, 0, 2)
    block = exchange(block).reshape(seq, plan.local, count, head_dim, cols)
    block = block.transpose(2, 0, 1, 3, 4).reshape(count, -1, cols)
    block = lax.psum_scatter(block, "grp", scatter_dimension=1, tiled=True).astype(F32)
    return [part.T if turn else part for part, turn in zip(block, turned)]


def body(
    tokens,
    cotangent,
    lengths,
    prenorm_gain,
    w_query,
    w_key,
    w_value,
    w_gate,
    rate_weight,
    rate_bias,
    init_weight,
    init_bias,
    inner_gain,
    inner_bias,
    post_gain,
    post_bias,
    w_out,
    feedforward_norm_gain,
    w_swish,
    w_up,
    w_down,
):
    seq_index = lax.axis_index("seq")
    grp_index = lax.axis_index("grp")
    groups = lax.axis_size("grp")
    seq = lax.axis_size("seq")
    rows_tok = tokens.shape[1]
    width = tokens.shape[2]
    heads, head_dim, _ = init_weight.shape
    plan = HeadPlan(heads, seq, groups)
    local = plan.local
    features = local * head_dim
    stream = rows_tok * seq
    steps = slot_steps(seq)
    place = ring_place(seq, seq_index)
    member_of_slot = ring_member(seq, (place + jnp.array(steps, jnp.int32)) % seq)
    apart = (ring_place(seq, jnp.arange(seq, dtype=jnp.int32)) - place) % seq
    slot_of_member = jnp.where(apart > seq // 2, 2 * (seq - apart), 2 * apart + 1)
    slot_of_member = jnp.where(apart == 0, 0, jnp.where(apart == seq // 2, 1, slot_of_member))
    to_slots = (member_of_slot[:, None] == jnp.arange(seq)[None, :]).astype(F32)

    def in_slots(stat):
        cut = stat.reshape(-1, seq, rows_tok)
        out = jnp.einsum("sm,kmt->kst", to_slots, cut, precision=lax.Precision.HIGHEST)
        return out.reshape(-1, stream)

    def in_order(stat):
        cut = stat.reshape(-1, seq, rows_tok)
        out = jnp.einsum("sm,kst->kmt", to_slots, cut, precision=lax.Precision.HIGHEST)
        return out.reshape(-1, stream)

    def pick(item):
        return plan.pick(item, seq_index, grp_index)

    def by_distance(rows):
        return lambda k: lax.slice_in_dim(
            rows, at_slot(k) * rows_tok, (at_slot(k) + 1) * rows_tok, axis=0
        )

    def at_slot(k):
        return steps.index(k if k < seq // 2 else k - seq)

    own_lengths = lax.dynamic_index_in_dim(lengths, grp_index, 0, keepdims=False)
    ends = jnp.cumsum(own_lengths)
    starts = ends - own_lengths
    docs = jnp.concatenate([starts, ends[-1:]])

    proj_block = exchange(
        cut_heads(plan, (w_query, w_key, w_value), (True, True, True), head_dim)
    )
    padded = w_down.shape[0] // seq
    padded += -padded % MB
    rate_rows = jnp.pad(pick(rate_weight.T), ((0, 128 - local), (0, 0)))
    gb, init = chain_params(*(pick(i) for i in (init_weight, init_bias, inner_gain, inner_bias)))
    own = {}

    bias = jnp.pad(pick(rate_bias), (0, 128 - local))[None]

    def token_work(s, arrived):
        if s == 1:
            own["parts"] = start_heads(plan, after(proj_block, arrived[0]))
            return [gb, init, rate_rows, bias, docs, slot_of_member, member_of_slot]
        if s == seq // 2 - 2:
            mats = (w_swish.T, w_up.T, w_down)
            if plan.each == 1:
                turned = (True, False, False, False, False)
                own["rest"] = cut_features(seq, (w_gate, w_out) + mats, turned)
            else:
                side = cut_heads(plan, (w_gate, w_out), (True, False), head_dim)
                own["rest"] = jnp.concatenate(
                    [side, cut_features(seq, mats, (False,) * 3)], axis=1
                )
            return [own["rest"]]
        if s == seq // 2 - 1:
            own["parts"] = end_heads(plan, own["parts"], 3, head_dim)
            return own["parts"][-1:]
        return []

    token_steps = ring_gather(tokens[0], seq, token_work)
    normed, x3, logits = project(
        sum(by_slots(token_steps), ()), own["parts"], rate_rows, bias, prenorm_gain[None]
    )
    rest_block = exchange(after(own["rest"], token_steps[-1][0]))
    grad_own = cotangent[0]

    inner, *kept = chain_forward(slot_of_member, docs, x3, logits, gb, init, rows_tok)
    side_rows = rest_block.shape[1] - 3 * padded
    side_block, ffn_block = rest_block[:, :side_rows], rest_block[:, side_rows:]

    sides = end_heads(plan, start_heads(plan, side_block), 2, head_dim)
    m_gate = jnp.concatenate([side[:head_dim] for side in sides], axis=0)
    m_out = jnp.concatenate([side[head_dim:] for side in sides], axis=0)
    gate_pre = mm_nt(normed, m_gate)
    ffn_block = ffn_block.transpose(1, 0, 2).reshape(3 * padded, width)
    ffn_parts = start_gather(ffn_block)

    sums = jnp.sum(kept[3][2:4].reshape(2, stream // MB, local, MB), axis=2).reshape(2, stream)
    sums = after(pairwise_sum(sums, "seq", seq), rest_block)
    sums = in_slots(sums) / width
    mean_o = sums[0][:, None]
    inv_o = lax.rsqrt(sums[1][:, None] - mean_o * mean_o + EPS)
    o_hat = (inner - mean_o) * inv_o
    post_g = pick(post_gain.reshape(heads, head_dim)).reshape(features)
    post_b = pick(post_bias.reshape(heads, head_dim)).reshape(features)
    post = o_hat * post_g + post_b
    gelu_val, gelu_pull = jax.vjp(jax.nn.gelu, gate_pre)
    gated = (gelu_val * post).astype(BF16)
    ffn = {}


    def ffn_corner(since):
        ffn["parts"] = end_gather(ffn_parts[:-1] + [after(ffn_parts[-1], since)])
        return ffn["parts"][-1:]

    mixing = ring_scatter(
        by_distance(mm(gated, m_out).astype(BF16)),
        seq,
        [lambda since: [], lambda since: [], lambda since: [], ffn_corner],
    )
    own_rows = tokens[0].astype(F32)
    resid = own_rows + mixing
    inv_second = lax.rsqrt(jnp.mean(resid * resid, -1, keepdims=True) + EPS)
    unit_second = resid * inv_second
    ffn_in = (unit_second * feedforward_norm_gain).astype(BF16)

    got = {"kept": (), "rows": [], "grads": []}
    d_parts = {}

    def step_work(s, arrived, grads):
        slot = 2 * s if s < seq // 2 else 1
        members = lax.slice_in_dim(member_of_slot, slot, slot + len(arrived))
        got["kept"], d_in = ffn_step(
            members, seq, slot, arrived, grads, ffn["parts"], got["kept"]
        )
        got["rows"].append(arrived)
        got["grads"].append(grads)
        for i in range(len(arrived)):
            d_parts[steps[slot + i]] = d_in[i * rows_tok : (i + 1) * rows_tok]
        return [d_in]

    ring_gather(ffn_in, seq, step_work, grad_own)
    kept_ffn = got["kept"]

    def ffn_work(since):
        first, *others = kept_ffn[:3]
        got["ffn"] = ffn_grads(
            groups,
            [after(first, since)] + others,
            sum(by_slots(got["rows"]), ()),
            sum(by_slots(got["grads"]), ()),
        )
        return got["ffn"][:1]

    def ffn_corner_work(since):
        got["corner"] = start_scatter(lambda k: after(got["ffn"][k], since))
        got["across"] = cross_scatter(ffn_grad, got["corner"])
        return [got["corner"]]

    def ffn_grad(k):
        return got["ffn"][k]

    d_ffn = ring_scatter(
        lambda k: d_parts[k if k < seq // 2 else k - seq], seq, [ffn_work, ffn_corner_work]
    )
    second_scaled = d_ffn * feedforward_norm_gain
    g_ffn_gain = jnp.sum(d_ffn * unit_second, 0)
    d_resid = grad_own.astype(F32) + inv_second * (
        second_scaled - unit_second * jnp.mean(second_scaled * unit_second, -1, keepdims=True)
    )

    def mix_work(s, arrived):
        if s == 0:
            late = [after(own["parts"][0], arrived[0])] + own["parts"][1:]
            got["w_all"] = jnp.concatenate(late + [rate_rows, m_gate], axis=0)
            return [got["w_all"]]
        if s == seq // 2 - 2:
            return [got["across"]]
        if s == seq // 2 - 1:
            summed = end_scatter(ffn_grad, after(got["across"], arrived[0]))
            got["summed"] = summed.reshape(3 * padded, seq, -1).transpose(1, 0, 2)
            return [got["summed"]]
        return []

    mix_steps = ring_gather(d_resid.astype(BF16), seq, mix_work)
    ffn_out = lax.psum_scatter(
        after(kept_ffn[3], mix_steps[seq // 2 - 2][0]), "seq", scatter_dimension=0, tiled=False
    )
    out_tokens = (resid + ffn_out.astype(F32)).astype(BF16)[None]
    d_gated = [mm_nt(jnp.concatenate(arrived, axis=0), m_out) for arrived in mix_steps]
    d_gated = jnp.concatenate(by_slots(d_gated), axis=0)
    d_post = d_gated * gelu_val
    d_gate_pre = gelu_pull(d_gated * post)[0].astype(BF16)
    g_post_gain = jnp.sum(d_post * o_hat, 0)
    g_post_bias = jnp.sum(d_post, 0)
    d_ohat = d_post * post_g
    sums = jnp.stack([jnp.sum(d_ohat, -1), jnp.sum(d_ohat * o_hat, -1)])
    sums = in_slots(pairwise_sum(in_order(sums), "seq", seq)) / width
    g_ffn = exchange(after(got["summed"], sums))
    d_inner = inv_o * (d_ohat - sums[0][:, None] - o_hat * sums[1][:, None])
    d_x, d_gb, d_init = chain_backward(
        slot_of_member, docs, x3, d_inner, d_gate_pre, logits, gb, init, kept, rows_tok
    )
    *head_rows_grads, g_rates, g_gain = proj_grads(
        d_x, normed, got["w_all"], gated, sum(by_slots(mix_steps), ()), local, head_dim
    )
    d_logits = d_x[:, 3 * features : 3 * features + local].astype(F32)
    parts = [item.reshape(local, -1) for item in chain_param_grads(d_gb, d_init, local)]
    parts += [item.reshape(local, head_dim) for item in (g_post_gain, g_post_bias)]
    parts += [g_rates[:local], jnp.sum(d_logits, 0)[:, None]]
    sizes = [item.shape[1] for item in parts]
    flat = jnp.concatenate(parts, axis=1)
    flat = plan.turn(jnp.pad(flat, ((0, 0), (0, -flat.shape[1] % 1024))), grp_index)
    count = flat.size
    flat = jnp.concatenate([flat.reshape(-1), g_gain[0] / prenorm_gain, g_ffn_gain])
    flat = pairwise_sum(flat.reshape(-1, 1024), "grp", groups)
    flat_all = lax.all_gather(flat, "seq", axis=0)
    d_x = after(d_x, g_gain, g_ffn)
    d_normed_part = mm(d_x, got["w_all"]).astype(BF16)

    def corner_work(since):
        if not plan.mixed:
            return []
        block = heads_block(plan, head_rows_grads)
        got["corner"] = start_scatter(block)
        got["across"] = cross_scatter(block, after(got["corner"], flat))
        return [got["corner"]]

    def join_work(since):
        got["join"] = join_features(after(g_ffn, since), w_down.shape[0], (False,) * 3)
        return got["join"][:1]

    def across_work(since):
        return [ffn_out] + ([got["across"]] if plan.mixed else [])

    d_normed = ring_scatter(
        by_distance(d_normed_part), seq, [corner_work, join_work, across_work]
    )
    summed = end_scatter(heads_block(plan, head_rows_grads), got["across"]) if plan.mixed else None
    g_heads = scatter_heads(plan, head_rows_grads, summed, (True,) * 4 + (False,))
    own_inv = lax.rsqrt(jnp.mean(own_rows * own_rows, -1, keepdims=True) + EPS)
    own_unit = own_rows * own_inv
    first_scaled = d_normed * prenorm_gain
    grad_tokens = (
        d_resid
        + own_inv
        * (first_scaled - own_unit * jnp.mean(first_scaled * own_unit, -1, keepdims=True))
    )[None]

    flat = after(flat_all, d_normed).reshape(seq, -1)
    gains = jnp.sum(flat[:, count:], 0).reshape(2, width)
    flat = plan.order(flat[:, :count].reshape(seq, local, -1))
    small = []
    offset = 0
    for size in sizes:
        small.append(flat[:, offset : offset + size])
        offset += size
    g_ffn = got["join"]
    return (
        out_tokens,
        grad_tokens,
        gains[0],
        g_heads[0],
        g_heads[1],
        g_heads[2],
        g_heads[3],
        small[6].T,
        small[7][:, 0],
        small[0].reshape(heads, head_dim, head_dim),
        small[1],
        small[2],
        small[3],
        small[4].reshape(width),
        small[5].reshape(width),
        g_heads[4],
        gains[1],
        g_ffn[0].T,
        g_ffn[1].T,
        g_ffn[2],
    )


def solution(mesh):
    whole = P()
    rows = P("grp", "seq", None)
    wide = P("seq", "grp")
    tall = P("grp", "seq")
    return jax.shard_map(
        body,
        mesh=mesh,
        in_specs=(rows, rows, whole, whole, wide, wide, wide, wide)
        + (whole,) * 8
        + (tall, whole, wide, wide, tall),
        out_specs=(rows, rows, whole, wide, wide, wide, wide)
        + (whole,) * 8
        + (tall, whole, wide, wide, tall),
        check_vma=False,
    )
```

```python
from functools import partial

import jax
import jax.numpy as jnp
from jax import lax
from jax.experimental import pallas as pl
from jax.experimental.pallas import tpu as pltpu
from jax.sharding import PartitionSpec as P

MB = 16
EPS = 1e-06
F32 = jnp.float32
VMEM_ASKED = 58 * 1024 * 1024
BF16 = jnp.bfloat16


def mm(left, right):
    return jnp.dot(left, right, preferred_element_type=F32)


def mm_nt(left, right):
    return lax.dot_general(left, right, (((1,), (1,)), ((), ())), preferred_element_type=F32)


def split_two(value):
    high = value.astype(BF16)
    return high, (value - high.astype(F32)).astype(BF16)


def mean_rows(value):
    return jnp.mean(value, axis=0, keepdims=True)


def chunk_rows(value, heads, start, lanes, size):
    tokens = value.shape[0]
    cuts = [value[:, lanes * h + start : lanes * h + start + size] for h in range(heads)]
    parts = [cut[m * MB : (m + 1) * MB] for m in range(tokens // MB) for cut in cuts]
    return jnp.concatenate(parts, axis=0)


def head_rows(rows, heads, h):
    step = MB * heads
    parts = [rows[m * step + h * MB : m * step + (h + 1) * MB] for m in range(rows.shape[0] // step)]
    return jnp.concatenate(parts, axis=0)


def chunk_masks(info, heads, count):
    step = MB * heads
    row = lax.broadcasted_iota(jnp.int32, (count, count), 0)
    col = lax.broadcasted_iota(jnp.int32, (count, count), 1)
    columns = jnp.transpose(info)
    same = ((row % step) // MB == (col % step) // MB) & (columns[:, 1:2] == info[1:2, :])
    return row // step, col // step, row % MB, col % MB, same, columns


def chunk_info(docs_ref, logits, heads, head_dim, chunk):
    tokens = logits.shape[0]
    count = heads * tokens
    step = MB * heads
    docs = docs_ref.shape[0] - 1
    pieces = [logits[m * MB : (m + 1) * MB] for m in range(tokens // MB) for _ in range(heads)]
    spread = jnp.concatenate(pieces, axis=0)
    lane = lax.broadcasted_iota(jnp.int32, spread.shape, 1)
    own = (lax.broadcasted_iota(jnp.int32, spread.shape, 0) % step) // MB
    logit = jnp.sum(jnp.transpose(jnp.where(lane == own, spread, 0.0)), axis=0, keepdims=True)
    start = chunk * tokens
    col = lax.broadcasted_iota(jnp.int32, (1, count), 1)
    block_at = start + (col // step) * MB
    doc = jnp.zeros((1, count), jnp.int32)
    before = end = jnp.int32(0)
    for d in range(docs):
        doc = doc + (block_at >= docs_ref[d]).astype(jnp.int32)
        before = before + (docs_ref[d] < start).astype(jnp.int32)
        end = end + (docs_ref[d] < start + tokens).astype(jnp.int32)
    live = (block_at + col % MB < docs_ref[docs]).astype(F32)
    sig = jax.nn.sigmoid(logit)
    zero = jnp.zeros((1, count), F32)
    return jnp.concatenate(
        [
            sig / head_dim * live,
            doc.astype(F32),
            (doc > before).astype(F32),
            (doc == end).astype(F32),
            zero + (end > before).astype(F32),
            live * sig * (1.0 - sig) / head_dim,
            zero,
            zero,
        ],
        axis=0,
    )


def augment(rows, heads, head_dim, wide):
    count = rows.shape[0]
    near = lax.broadcasted_iota(jnp.int32, (head_dim, wide), 0)
    far = lax.broadcasted_iota(jnp.int32, (head_dim, wide), 1)
    tile = (far % head_dim == near).astype(BF16)
    lane = lax.broadcasted_iota(jnp.int32, (count, wide), 1)
    own = (lax.broadcasted_iota(jnp.int32, (count, wide), 0) % (MB * heads)) // MB
    return jnp.where(lane // head_dim == own, mm(rows, tile), 0.0)


def one_hot_heads(count, heads):
    lane = lax.broadcasted_iota(jnp.int32, (count, 128), 1)
    own = (lax.broadcasted_iota(jnp.int32, (count, 128), 0) % (MB * heads)) // MB
    return (lane == own).astype(BF16)


def forward_kernel(
    heads, idx_ref, docs_ref, x_ref, logit_ref, gb_ref, init_ref, out_ref, n_ref, r_ref, nb_ref, stat_ref, w_ref, state
):
    head_dim = gb_ref.shape[1]
    tokens = x_ref.shape[0]
    count = heads * tokens
    full = init_ref.shape[1]
    wide = full - 128

    @pl.when(pl.program_id(0) == 0)
    def _():
        state[...] = init_ref[...]

    carried = state[...]
    w_ref[0] = carried
    info = chunk_info(docs_ref, logit_ref[...], heads, head_dim, pl.program_id(0))
    x = x_ref[...]
    q_rows = chunk_rows(x, heads, 0, 3 * head_dim, head_dim)
    k_rows = chunk_rows(x, heads, head_dim, 3 * head_dim, head_dim)
    v_rows = chunk_rows(x, heads, 2 * head_dim, 3 * head_dim, head_dim)
    q_t = jnp.transpose(q_rows.astype(F32))
    target_t = jnp.transpose(v_rows.astype(F32) - k_rows.astype(F32))
    mb_row, mb_col, t_row, t_col, same, columns = chunk_masks(info, heads, count)
    gram = jnp.where(same & (mb_row < mb_col), mm_nt(k_rows, k_rows) + 1.0, 0.0).astype(BF16)
    cross = jnp.where(
        same & ((mb_row < mb_col) | ((mb_row == mb_col) & (t_row <= t_col))),
        mm_nt(k_rows, q_rows) + 1.0,
        0.0,
    ).astype(BF16)
    hot = one_hot_heads(count, heads)
    k_aug = jnp.concatenate([augment(k_rows, heads, head_dim, wide).astype(BF16), hot], axis=1)
    q_aug = jnp.concatenate([augment(q_rows, heads, head_dim, wide).astype(BF16), hot], axis=1)
    init = init_ref[...]
    stacked = jnp.concatenate(split_two(carried) + split_two(init), axis=0)
    fresh = info[2:3, :] > 0.5

    def through_state(rows):
        both = mm_nt(stacked, rows)
        return jnp.where(
            fresh,
            both[2 * head_dim : 3 * head_dim] + both[3 * head_dim :],
            both[:head_dim] + both[head_dim : 2 * head_dim],
        )

    z_start = through_state(k_aug)
    gain = gb_ref[0]
    shift = gb_ref[1]
    repeats = count // 128
    inner = 128 // (MB * heads)
    done = []
    for p in range(repeats):
        cols = slice(p * 128, (p + 1) * 128)
        z_base = z_start[:, cols]
        if p:
            z_base = z_base - mm(jnp.concatenate(done, axis=1), gram[: p * 128, cols])
        target = target_t[:, cols]
        rate = info[0:1, cols]
        z = z_base
        for step in range(inner):
            if step:
                z = z_base - mm(scaled.astype(BF16), gram[cols, cols])
            centred = z - mean_rows(z)
            inv = lax.rsqrt(mean_rows(centred * centred) + EPS)
            n = centred * inv
            err = (n * gain + shift - target) * gain
            scaled = (rate * inv) * (err - mean_rows(err) - n * mean_rows(err * n))
        done.append(scaled.astype(BF16))
        n_ref[:, cols] = n
        r_ref[:, cols] = scaled
        stat_ref[0:1, cols] = inv
    r_bf = jnp.concatenate(done, axis=1)
    z_bar = through_state(q_aug) - mm(r_bf, cross)
    centred = z_bar - mean_rows(z_bar)
    inv = lax.rsqrt(mean_rows(centred * centred) + EPS)
    nb = centred * inv
    nb_ref[...] = nb
    stat_ref[1:2, :] = inv
    wide_gain = jnp.concatenate([gain] * repeats, axis=1)
    wide_shift = jnp.concatenate([shift] * repeats, axis=1)
    out_t = q_t + nb * wide_gain + wide_shift
    stat_ref[2:3, :] = jnp.sum(out_t, axis=0, keepdims=True)
    stat_ref[3:4, :] = jnp.sum(out_t * out_t, axis=0, keepdims=True)
    out_rows = jnp.transpose(out_t)
    for h in range(heads):
        out_ref[:, h * head_dim : (h + 1) * head_dim] = head_rows(out_rows, heads, h)
    base = jnp.where(info[4:5, 0:1] > 0.5, init, carried)
    state[...] = base - mm((r_ref[...] * info[3:4, :]).astype(BF16), k_aug)


def backward_kernel(
    heads,
    idx_ref,
    docs_ref,
    x_ref,
    d_ref,
    gate_ref,
    logit_ref,
    gb_ref,
    init_ref,
    n_ref,
    r_ref,
    nb_ref,
    stat_ref,
    w_ref,
    dx_ref,
    dgb_ref,
    dinit_ref,
    state,
):
    head_dim = gb_ref.shape[1]
    tokens = x_ref.shape[0]
    count = heads * tokens
    full = init_ref.shape[1]
    wide = full - 128

    @pl.when(pl.program_id(0) == 0)
    def _():
        state[...] = jnp.zeros_like(state)
        dgb_ref[...] = jnp.zeros_like(dgb_ref)
        dinit_ref[...] = jnp.zeros_like(dinit_ref)

    d_end = state[...]
    carried = w_ref[0]
    init = init_ref[...]
    chunk = pl.num_programs(0) - 1 - pl.program_id(0)
    info = chunk_info(docs_ref, logit_ref[...], heads, head_dim, chunk)
    x = x_ref[...]
    q_rows = chunk_rows(x, heads, 0, 3 * head_dim, head_dim)
    k_rows = chunk_rows(x, heads, head_dim, 3 * head_dim, head_dim)
    v_rows = chunk_rows(x, heads, 2 * head_dim, 3 * head_dim, head_dim)
    d_rows = chunk_rows(d_ref[...], heads, 0, head_dim, head_dim)
    target_t = jnp.transpose(v_rows.astype(F32) - k_rows.astype(F32))
    d_t = jnp.transpose(d_rows)
    mb_row, mb_col, t_row, t_col, same, columns = chunk_masks(info, heads, count)
    earlier = same & (mb_row < mb_col)
    later = same & (mb_row > mb_col)
    up_to = same & ((mb_row < mb_col) | ((mb_row == mb_col) & (t_row <= t_col)))
    from_on = same & ((mb_row > mb_col) | ((mb_row == mb_col) & (t_row >= t_col)))
    gram = jnp.where(later, mm_nt(k_rows, k_rows) + 1.0, 0.0).astype(BF16)
    cross = jnp.where(from_on, mm_nt(q_rows, k_rows) + 1.0, 0.0).astype(BF16)
    hot = one_hot_heads(count, heads)
    k_aug = jnp.concatenate([augment(k_rows, heads, head_dim, wide).astype(BF16), hot], axis=1)
    q_aug = jnp.concatenate([augment(q_rows, heads, head_dim, wide).astype(BF16), hot], axis=1)
    gain = gb_ref[0]
    shift = gb_ref[1]
    repeats = count // 128
    inner = 128 // (MB * heads)
    wide_gain = jnp.concatenate([gain] * repeats, axis=1)
    nb = nb_ref[...]
    inv_b = stat_ref[1:2, :]
    d_nb = d_t * wide_gain
    d_zbar = inv_b * (d_nb - mean_rows(d_nb) - nb * mean_rows(d_nb * nb))
    scaled_t = r_ref[...]
    last = info[3:4, :]
    dr_base = -mm(d_zbar.astype(BF16), cross) - last * mm_nt(d_end.astype(BF16), k_aug)
    gain_sum = jnp.zeros((head_dim, 128), F32)
    shift_sum = jnp.zeros((head_dim, 128), F32)
    for p in range(repeats):
        cols = slice(p * 128, (p + 1) * 128)
        gain_sum = gain_sum + d_t[:, cols] * nb[:, cols]
        shift_sum = shift_sum + d_t[:, cols]
    done = []
    errs = []
    d_rates = []
    for p in reversed(range(repeats)):
        cols = slice(p * 128, (p + 1) * 128)
        base = dr_base[:, cols]
        if done:
            base = base - mm(jnp.concatenate(done, axis=1), gram[(p + 1) * 128 :, cols])
        n = n_ref[:, cols]
        inv = stat_ref[0:1, cols]
        rate = info[0:1, cols]
        miss = n * gain + shift - target_t[:, cols]
        err = miss * gain
        along = mean_rows(err * n)
        plain = inv * (err - mean_rows(err) - n * along)
        gain2 = gain * gain
        d_scaled = base
        for step in range(inner):
            if step:
                d_scaled = base - mm(d_z.astype(BF16), gram[cols, cols])
            g = rate * d_scaled
            g_n = mean_rows(g * n)
            d_err = inv * (g - mean_rows(g) - n * g_n)
            d_n = d_err * gain2 - inv * (g * along + err * g_n)
            d_z = inv * (d_n - mean_rows(d_n) - n * (mean_rows(d_n * n) + mean_rows(g * plain)))
        done.insert(0, d_z.astype(BF16))
        errs.insert(0, d_err * gain)
        d_rates.insert(0, jnp.sum(d_scaled * plain, axis=0, keepdims=True))
        gain_sum = gain_sum + d_err * (miss + gain * n)
        shift_sum = shift_sum + d_err * gain
    dgb_ref[0] += gain_sum
    dgb_ref[1] += shift_sum
    dz_bf = jnp.concatenate(done, axis=1)
    d_z = dz_bf.astype(F32)
    d_errg = jnp.concatenate(errs, axis=1)
    turned = jnp.transpose(jnp.concatenate([d_zbar, scaled_t, d_z, d_errg], axis=0))
    zb_rows = turned[:, :head_dim].astype(BF16)
    r_rows = turned[:, head_dim : 2 * head_dim].astype(BF16)
    z_rows = turned[:, 2 * head_dim : 3 * head_dim].astype(BF16)
    e_rows = turned[:, 3 * head_dim :]
    d_cross = jnp.where(from_on, -mm_nt(zb_rows, r_rows), 0.0).astype(BF16)
    d_cross_t = jnp.where(up_to, -mm_nt(r_rows, zb_rows), 0.0).astype(BF16)
    d_gram = (
        jnp.where(later, -mm_nt(z_rows, r_rows), 0.0)
        + jnp.where(earlier, -mm_nt(r_rows, z_rows), 0.0)
    ).astype(BF16)
    is_init = columns[:, 2:3] > 0.5
    is_last = columns[:, 3:4] > 0.5

    def stack_heads(weight):
        parts = [weight[:, h * head_dim : (h + 1) * head_dim] for h in range(heads)]
        pad = wide - heads * head_dim
        if pad:
            parts.append(jnp.zeros((pad, head_dim), F32))
        return jnp.concatenate(parts, axis=0).astype(BF16)

    w_both = jnp.concatenate([stack_heads(carried), stack_heads(init)], axis=0)
    d_stack = stack_heads(d_end)

    def by_state(rows):
        own = augment(rows, heads, head_dim, wide)
        return jnp.concatenate(
            [jnp.where(is_init, 0.0, own), jnp.where(is_init, own, 0.0)], axis=1
        ).astype(BF16)

    dq = d_rows + mm(d_cross, k_rows) + mm(by_state(zb_rows), w_both)
    r_own = jnp.where(is_last, augment(r_rows, heads, head_dim, wide), 0.0).astype(BF16)
    dk = (
        e_rows
        + mm(d_gram, k_rows)
        + mm(d_cross_t, q_rows)
        + mm(by_state(z_rows), w_both)
        - mm(r_own, d_stack)
    )
    packed = jnp.concatenate([dq.astype(BF16), dk.astype(BF16), (-e_rows).astype(BF16)], axis=1)
    each = 3 * head_dim
    d_logits = jnp.concatenate(d_rates, axis=1) * info[5:6, :]
    turned = jnp.transpose(jnp.concatenate([d_logits, jnp.zeros((7, count), F32)], axis=0))
    lane = lax.broadcasted_iota(jnp.int32, (tokens, 128), 1)
    logit_rows = jnp.zeros((tokens, 128), F32)
    for h in range(heads):
        dx_ref[:, h * each : (h + 1) * each] = head_rows(packed, heads, h)
        logit_rows = jnp.where(lane == h, head_rows(turned, heads, h)[:, 0:1], logit_rows)
    dx_ref[:, heads * each : heads * each + 128] = logit_rows.astype(BF16)
    dx_ref[:, heads * each + 128 :] = gate_ref[...]
    row_init = info[2:3, :] > 0.5
    zb_two = jnp.concatenate(
        [jnp.where(row_init, 0.0, d_zbar), jnp.where(row_init, d_zbar, 0.0)], axis=0
    ).astype(BF16)
    z_two = jnp.concatenate(
        [jnp.where(row_init, 0.0, d_z), jnp.where(row_init, d_z, 0.0)], axis=0
    ).astype(BF16)
    d_both = mm(zb_two, q_aug) + mm(z_two, k_aug)
    fresh = info[4:5, 0:1] > 0.5
    state[...] = d_both[:head_dim] + jnp.where(fresh, 0.0, d_end)
    dinit_ref[...] += d_both[head_dim:] + jnp.where(fresh, d_end, 0.0)


def chain_specs(heads, tokens, head_dim, full, at):
    count = heads * tokens
    return dict(
        x=pl.BlockSpec((tokens, heads * 3 * head_dim), lambda i, idx, docs: (idx[at(i)], 0)),
        dx=pl.BlockSpec((tokens, heads * 4 * head_dim + 128), lambda i, idx, docs: (idx[at(i)], 0)),
        rows=pl.BlockSpec((tokens, heads * head_dim), lambda i, idx, docs: (idx[at(i)], 0)),
        logit=pl.BlockSpec((tokens, 128), lambda i, idx, docs: (idx[at(i)], 0)),
        gb=pl.BlockSpec((2, head_dim, 128), lambda i, idx, docs: (0, 0, 0)),
        init=pl.BlockSpec((head_dim, full), lambda i, idx, docs: (0, 0)),
        tall=pl.BlockSpec((head_dim, count), lambda i, idx, docs: (0, at(i))),
        stat=pl.BlockSpec((8, count), lambda i, idx, docs: (0, at(i))),
        weight=pl.BlockSpec((1, head_dim, full), lambda i, idx, docs: (at(i), 0, 0)),
    )


def chain_forward(idx, docs, x3, logits, gb, init, tokens):
    total = x3.shape[0]
    head_dim = gb.shape[1]
    heads = x3.shape[1] // (3 * head_dim)
    chunks = total // tokens
    full = init.shape[1]
    s = chain_specs(heads, tokens, head_dim, full, lambda i: i)
    tall = jax.ShapeDtypeStruct((head_dim, heads * total), F32)
    return pl.pallas_call(
        partial(forward_kernel, heads),
        grid_spec=pltpu.PrefetchScalarGridSpec(
            num_scalar_prefetch=2,
            grid=(chunks,),
            in_specs=[s["x"], s["logit"], s["gb"], s["init"]],
            out_specs=[s["rows"], s["tall"], s["tall"], s["tall"], s["stat"], s["weight"]],
            scratch_shapes=[pltpu.VMEM((head_dim, full), F32)],
        ),
        out_shape=[
            jax.ShapeDtypeStruct((total, heads * head_dim), F32),
            tall,
            tall,
            tall,
            jax.ShapeDtypeStruct((8, heads * total), F32),
            jax.ShapeDtypeStruct((chunks, head_dim, full), F32),
        ],
        compiler_params=pltpu.CompilerParams(
            dimension_semantics=("arbitrary",), vmem_limit_bytes=VMEM_ASKED
        ),
        cost_estimate=pl.CostEstimate(flops=1, bytes_accessed=1, transcendentals=0),
        name="chain_forward",
    )(idx, docs, x3, logits, gb, init)


def chain_backward(idx, docs, x3, d_inner, d_gate, logits, gb, init, kept, tokens):
    total = x3.shape[0]
    head_dim = gb.shape[1]
    heads = x3.shape[1] // (3 * head_dim)
    chunks = total // tokens
    full = init.shape[1]
    s = chain_specs(heads, tokens, head_dim, full, lambda i: chunks - 1 - i)
    return pl.pallas_call(
        partial(backward_kernel, heads),
        grid_spec=pltpu.PrefetchScalarGridSpec(
            num_scalar_prefetch=2,
            grid=(chunks,),
            in_specs=[
                s["x"],
                s["rows"],
                s["rows"],
                s["logit"],
                s["gb"],
                s["init"],
                s["tall"],
                s["tall"],
                s["tall"],
                s["stat"],
                s["weight"],
            ],
            out_specs=[s["dx"], s["gb"], s["init"]],
            scratch_shapes=[pltpu.VMEM((head_dim, full), F32)],
        ),
        out_shape=[
            jax.ShapeDtypeStruct((total, heads * 4 * head_dim + 128), BF16),
            jax.ShapeDtypeStruct(gb.shape, F32),
            jax.ShapeDtypeStruct(init.shape, F32),
        ],
        compiler_params=pltpu.CompilerParams(
            dimension_semantics=("arbitrary",), vmem_limit_bytes=VMEM_ASKED
        ),
        cost_estimate=pl.CostEstimate(flops=1, bytes_accessed=1, transcendentals=0),
        name="chain_backward",
    )(idx, docs, x3, d_inner, d_gate, logits, gb, init, *kept)


def chain_params(init_weight, init_bias, inner_gain, inner_bias):
    heads, head_dim, _ = init_weight.shape
    reps = 128 // (MB * heads)

    def pattern(item):
        row = jnp.broadcast_to(item.T[:, None, :, None], (head_dim, reps, heads, MB))
        return row.reshape(head_dim, 128)

    gb = jnp.stack([pattern(inner_gain), pattern(inner_bias)])
    wide = max(128, heads * head_dim)
    w_t = jnp.transpose(init_weight, (2, 0, 1)).reshape(head_dim, heads * head_dim)
    init = jnp.concatenate(
        [
            jnp.pad(w_t, ((0, 0), (0, wide - heads * head_dim))),
            jnp.pad(init_bias.T, ((0, 0), (0, 128 - heads))),
        ],
        axis=1,
    )
    return gb, init


def chain_param_grads(dgb, dinit, heads):
    head_dim = dinit.shape[0]
    wide = dinit.shape[1] - 128
    d_w = dinit[:, : heads * head_dim].reshape(head_dim, heads, head_dim).transpose(1, 2, 0)
    d_b = dinit[:, wide : wide + heads].T
    both = jnp.sum(dgb.reshape(2, head_dim, -1, heads, MB), axis=(2, 4))
    return d_w, d_b, both[0].T, both[1].T


def cut_kernel(turned, shares, *refs):
    mats, out_ref, held = refs[: len(turned)], refs[-2], refs[-1]
    at = 0
    for mat, turn, share in zip(mats, turned, shares):
        padded = share + -share % MB
        value = mat[...].astype(F32)
        held[: value.shape[1] if turn else value.shape[0]] = jnp.transpose(value) if turn else value
        for s in range(out_ref.shape[0]):
            out_ref[s, at : at + share] = held[s * share : (s + 1) * share].astype(BF16)
            if padded > share:
                out_ref[s, at + share : at + padded] = jnp.zeros(
                    (padded - share, out_ref.shape[2]), BF16
                )
        at += padded


def cut_features(seq, mats, turned):
    features = [m.shape[1] if turn else m.shape[0] for m, turn in zip(mats, turned)]
    cols = mats[0].shape[0] if turned[0] else mats[0].shape[1]
    shares = [count // seq for count in features]
    rows = sum(share + -share % MB for share in shares)
    return pl.pallas_call(
        partial(cut_kernel, turned, shares),
        out_shape=jax.ShapeDtypeStruct((seq, rows, cols), BF16),
        scratch_shapes=[pltpu.VMEM((max(features), cols), F32)],
        compiler_params=pltpu.CompilerParams(vmem_limit_bytes=VMEM_ASKED),
        cost_estimate=pl.CostEstimate(flops=1, bytes_accessed=1, transcendentals=0),
        name="cut_features",
    )(*mats)


def join_kernel(turned, share, padded, in_ref, *refs):
    outs, held = refs[:-1], refs[-1]
    for i, out in enumerate(outs):
        for s in range(in_ref.shape[0]):
            held[s * share : (s + 1) * share] = in_ref[
                s, i * padded : i * padded + share
            ].astype(F32)
        out[...] = jnp.transpose(held[...]) if turned[i] else held[...]


def join_features(block, features, turned):
    seq, rows, cols = block.shape
    shapes = [(cols, features) if turn else (features, cols) for turn in turned]
    return pl.pallas_call(
        partial(join_kernel, turned, features // seq, rows // len(turned)),
        out_shape=[jax.ShapeDtypeStruct(shape, F32) for shape in shapes],
        scratch_shapes=[pltpu.VMEM((features, cols), F32)],
        compiler_params=pltpu.CompilerParams(vmem_limit_bytes=VMEM_ASKED),
        cost_estimate=pl.CostEstimate(flops=1, bytes_accessed=1, transcendentals=0),
        name="join_features",
    )(block)


def ffn_kernel(count, parts, kept, member_ref, *refs):
    rows_refs = refs[:count]
    grad_refs = refs[count : 2 * count]
    weights = refs[2 * count : 2 * count + parts]
    outs = refs[2 * count + parts + kept :]
    (at_ref, ut_ref, ht_ref, y_ref, d_ref, a_t, u_t, h_t, y_all, d_all) = outs
    step = pl.program_id(0)
    size = rows_refs[0].shape[0]

    @pl.when(step == 0)
    def _():
        padded = weights[0].shape[0] // 3
        swish, up, down = (
            jnp.concatenate([w[i * padded : (i + 1) * padded] for w in weights], axis=0)
            for i in range(3)
        )
        rows = jnp.concatenate([ref[...] for ref in rows_refs], axis=0)
        grad = jnp.concatenate([ref[...] for ref in grad_refs], axis=0)
        act_a = mm_nt(rows, swish)
        act_u = mm_nt(rows, up)
        d_hidden = mm_nt(grad, down)
        sig = jax.nn.sigmoid(act_a)
        gate = act_a * sig
        hidden = gate * act_u
        d_a = d_hidden * act_u * sig * (1.0 + act_a * (1.0 - sig))
        d_u = d_hidden * gate
        d_all[...] = (mm(d_a.astype(BF16), swish) + mm(d_u.astype(BF16), up)).astype(BF16)
        y_all[...] = mm(hidden.astype(BF16), down).astype(BF16)
        fill = -hidden.shape[1] % 128
        for out, value in ((a_t, d_a), (u_t, d_u), (h_t, hidden)):
            if fill:
                value = jnp.concatenate([value, jnp.zeros((value.shape[0], fill), F32)], axis=1)
            out[...] = jnp.transpose(value)[: out.shape[0]].astype(BF16)

    for i in range(count):

        @pl.when(step == i)
        def _(i=i):
            part = slice(i * size, (i + 1) * size)
            at_ref[...] = a_t[:, part]
            ut_ref[...] = u_t[:, part]
            ht_ref[...] = h_t[:, part]
            y_ref[0] = y_all[part]
            d_ref[...] = d_all[part]


def ffn_step(members, seq, slot, rows, grads, weights, kept):
    count = len(rows)
    size, width = rows[0].shape
    total = seq * size
    features = sum(w.shape[0] for w in weights) // 3
    whole = pl.BlockSpec(memory_space=pltpu.VMEM)

    turned_spec = pl.BlockSpec((features, size), lambda s, member: (0, slot + s))
    turned = jax.ShapeDtypeStruct((features, total), BF16)
    first = 1 + 2 * count + len(weights)
    out = pl.pallas_call(
        partial(ffn_kernel, count, len(weights), len(kept)),
        grid_spec=pltpu.PrefetchScalarGridSpec(
            num_scalar_prefetch=1,
            grid=(count,),
            in_specs=[whole] * (2 * count + len(weights))
            + [pl.BlockSpec(memory_space=pl.ANY)] * len(kept),
            out_specs=[turned_spec] * 3
            + [
                pl.BlockSpec((1, size, width), lambda s, member: (member[s], 0, 0)),
                pl.BlockSpec((size, width), lambda s, member: (s, 0)),
            ],
            scratch_shapes=[pltpu.VMEM((features, count * size), BF16)] * 3
            + [pltpu.VMEM((count * size, width), BF16)] * 2,
        ),
        out_shape=[turned] * 3
        + [
            jax.ShapeDtypeStruct((seq, size, width), BF16),
            jax.ShapeDtypeStruct((count * size, width), BF16),
        ],
        input_output_aliases={first + i: i for i in range(len(kept))},
        compiler_params=pltpu.CompilerParams(
            dimension_semantics=("arbitrary",), vmem_limit_bytes=VMEM_ASKED
        ),
        cost_estimate=pl.CostEstimate(flops=1, bytes_accessed=1, transcendentals=0),
        name="ffn_step",
    )(members, *rows, *grads, *weights, *kept)
    return out[:-1], out[-1]


def ffn_grad_kernel(parts, count, at_ref, ut_ref, ht_ref, *refs):
    x = jnp.concatenate([ref[...] for ref in refs[:count]], axis=0)
    g = jnp.concatenate([ref[...] for ref in refs[count : 2 * count]], axis=0)
    padded = at_ref.shape[0] // parts
    for i, out in enumerate(refs[2 * count :]):
        own = slice(i * padded, (i + 1) * padded)
        out[:padded] = mm(at_ref[own], x).astype(BF16)
        out[padded : 2 * padded] = mm(ut_ref[own], x).astype(BF16)
        out[2 * padded :] = mm(ht_ref[own], g).astype(BF16)


def ffn_grads(parts, turned, rows, grads):
    size, width = rows[0].shape
    count = len(rows)
    features = turned[0].shape[0]
    wide = pl.BlockSpec((size, 256), lambda i: (0, i))
    whole = pl.BlockSpec((features, count * size), lambda i: (0, 0))
    each = 3 * features // parts
    return pl.pallas_call(
        partial(ffn_grad_kernel, parts, count),
        grid=(width // 256,),
        in_specs=[whole] * 3 + [wide] * (2 * count),
        out_specs=[pl.BlockSpec((each, 256), lambda i: (0, i))] * parts,
        out_shape=[jax.ShapeDtypeStruct((each, width), BF16)] * parts,
        compiler_params=pltpu.CompilerParams(
            dimension_semantics=("arbitrary",), vmem_limit_bytes=VMEM_ASKED
        ),
        cost_estimate=pl.CostEstimate(flops=1, bytes_accessed=1, transcendentals=0),
        name="ffn_grads",
    )(*turned, *rows, *grads)


def proj_grad_kernel(heads, head_dim, d_ref, x_ref, w_ref, gated_ref, *refs):
    count = len(refs) - heads - 4
    mix = refs[:count]
    outs, rate_ref, gain_ref = refs[count : count + heads], refs[-4], refs[-3]
    turned, gated_turned = refs[-2:]
    each = 3 * head_dim

    @pl.when(pl.program_id(0) == 0)
    def _():
        turned[...] = jnp.transpose(d_ref[...].astype(F32)).astype(BF16)
        gated_turned[...] = jnp.transpose(gated_ref[...].astype(F32)).astype(BF16)

    grad = mm(turned[...], x_ref[...])
    grad_out = mm(gated_turned[...], jnp.concatenate([ref[...] for ref in mix], axis=0))
    gain_ref[...] = jnp.broadcast_to(
        jnp.sum(grad * w_ref[...].astype(F32), axis=0, keepdims=True), gain_ref.shape
    )
    gate = heads * each + 128
    for h, out in enumerate(outs):
        own = slice(h * head_dim, (h + 1) * head_dim)
        out[:each] = grad[h * each : (h + 1) * each].astype(BF16)
        out[each : each + head_dim] = grad[gate + h * head_dim : gate + (h + 1) * head_dim].astype(
            BF16
        )
        out[each + head_dim :] = grad_out[own].astype(BF16)
    rate_ref[...] = grad[heads * each : heads * each + 8]


def proj_grads(d_x, normed, weight, gated, mix, heads, head_dim):
    total, packed = d_x.shape
    width = normed.shape[1]

    def wide(rows):
        return pl.BlockSpec((rows, 256), lambda i: (0, i))

    def whole(array):
        return pl.BlockSpec(array.shape, lambda i: (0, 0))

    return pl.pallas_call(
        partial(proj_grad_kernel, heads, head_dim),
        grid=(width // 256,),
        in_specs=[whole(d_x), wide(total), wide(packed), whole(gated)]
        + [wide(block.shape[0]) for block in mix],
        out_specs=[wide(5 * head_dim)] * heads + [wide(8)] * 2,
        out_shape=[jax.ShapeDtypeStruct((5 * head_dim, width), BF16)] * heads
        + [jax.ShapeDtypeStruct((8, width), F32)] * 2,
        scratch_shapes=[pltpu.VMEM((packed, total), BF16), pltpu.VMEM(gated.shape[::-1], BF16)],
        compiler_params=pltpu.CompilerParams(
            dimension_semantics=("arbitrary",), vmem_limit_bytes=VMEM_ASKED
        ),
        cost_estimate=pl.CostEstimate(flops=1, bytes_accessed=1, transcendentals=0),
        name="proj_grads",
    )(d_x, normed, weight, gated, *mix)


def project_kernel(count, parts, *refs):
    blocks = refs[:count]
    weights = refs[count : count + parts]
    rate_ref, bias_ref, gain_ref, normed_ref, x_ref, logit_ref = refs[count + parts :]
    size = blocks[0].shape[0]
    packed = x_ref.shape[1]
    for i in range(0, count, 2):

        @pl.when(pl.program_id(0) == i // 2)
        def _(i=i):
            rows = jnp.concatenate([ref[...] for ref in blocks[i : i + 2]], axis=0).astype(F32)
            inv = lax.rsqrt(jnp.mean(rows * rows, -1, keepdims=True) + EPS)
            normed = (rows * inv * gain_ref[...]).astype(BF16)
            normed_ref[...] = normed
            weight = jnp.concatenate([ref[...] for ref in weights] + [rate_ref[...]], axis=0)
            out = mm_nt(normed, weight)
            x_ref[...] = out[:, :packed].astype(BF16)
            logit_ref[...] = out[:, packed:] + bias_ref[...]


def project(blocks, weights, rate_rows, bias, gain):
    size, width = blocks[0].shape
    count = len(blocks)
    total = count * size
    packed = sum(w.shape[0] for w in weights)

    def rows(lanes):
        return pl.BlockSpec((2 * size, lanes), lambda i: (i, 0))

    return pl.pallas_call(
        partial(project_kernel, count, len(weights)),
        grid=(count // 2,),
        in_specs=[pl.BlockSpec(memory_space=pltpu.VMEM)] * (count + len(weights) + 3),
        out_specs=[rows(width), rows(packed), rows(128)],
        out_shape=[
            jax.ShapeDtypeStruct((total, width), BF16),
            jax.ShapeDtypeStruct((total, packed), BF16),
            jax.ShapeDtypeStruct((total, 128), F32),
        ],
        compiler_params=pltpu.CompilerParams(
            dimension_semantics=("arbitrary",), vmem_limit_bytes=VMEM_ASKED
        ),
        cost_estimate=pl.CostEstimate(flops=1, bytes_accessed=1, transcendentals=0),
        name="project",
    )(*blocks, *weights, rate_rows, bias, gain)


def trans_dot(left, right):
    return lax.dot_general(
        left, right, (((0,), (0,)), ((), ())), preferred_element_type=jnp.float32
    )


def after(value, *first):
    anywhere = pl.BlockSpec(memory_space=pl.ANY)
    return pl.pallas_call(
        lambda *refs: None,
        out_shape=jax.ShapeDtypeStruct(value.shape, value.dtype),
        in_specs=[anywhere] * (1 + len(first)),
        out_specs=anywhere,
        input_output_aliases={0: 0},
        name="after",
    )(value, *first)


def ring_pairs(size, step):
    order = list(range(0, size, 2)) + list(range(size - 1, 0, -2))
    return [(order[i], order[(i + step) % size]) for i in range(size)]


def ring_place(size, index):
    return jnp.where(index % 2 == 0, index // 2, size - (index + 1) // 2)


def ring_member(size, place):
    return jnp.where(place < size // 2, 2 * place, 2 * (size - place) - 1)


def slot_steps(size):
    steps = [0, -(size // 2)]
    for s in range(1, size // 2):
        steps += [-s, s]
    return steps


def by_slots(arrived):
    return [arrived[0], arrived[-1]] + list(arrived[1:-1])


def ring_step(blocks, s, size):
    ahead = lax.ppermute(blocks[0], "seq", ring_pairs(size, 1))
    if s == size // 2:
        return (ahead,)
    return ahead, lax.ppermute(blocks[-1], "seq", ring_pairs(size, -1))


def ring_gather(block, size, work=None, beside=None):
    arrived = [(block,)]
    others = list(beside or ())

    def do_work(s):
        if not work:
            return []
        return list(work(s, arrived[s], others[s]) if others else work(s, arrived[s]))

    for s in range(1, size // 2 + 1):
        done = do_work(s - 1)
        moved = ring_step(arrived[-1], s, size)
        done += moved[1:]
        if others and len(others) <= size // 2:
            others.append(ring_step(others[-1], len(others), size))
            done += others[-1]
        ahead = after(moved[0], *done) if done else moved[0]
        arrived.append((ahead,) + moved[1:])
    do_work(size // 2)
    return arrived


def ring_scatter(part, size, work=()):
    half = size // 2
    ahead, back = part(half).astype(BF16), part(1 - half).astype(BF16)
    for s in range(1, half + 1):
        done = work[s - 1](ahead) if s <= len(work) else []
        ahead = lax.ppermute(ahead, "seq", ring_pairs(size, 1))
        if s < half:
            back = lax.ppermute(back, "seq", ring_pairs(size, -1))
            done = list(done) + [back]
        if done:
            ahead = after(ahead, *done)
        if s < half:
            back = after(back, ahead)
        ahead = ahead.astype(F32)
        if s < half:
            ahead = (ahead + part(half - s)).astype(BF16)
            if s < half - 1:
                back = (back.astype(F32) + part(1 - half + s)).astype(BF16)
    return part(0).astype(F32) + ahead + back.astype(F32)


def pairwise_sum(value, axis, size):
    bit = 1
    while bit < size:
        value = value + lax.ppermute(value, axis, [(i, i ^ bit) for i in range(size)])
        bit *= 2
    return value


def swap(value, bit):
    return lax.ppermute(value, "grp", [(i, i ^ bit) for i in range(4)])


def near(index, k):
    return index ^ k if lax.axis_size("grp") == 4 else k


def start_gather(value):
    if lax.axis_size("grp") != 4:
        whole = lax.all_gather(value, "grp", axis=0)
        return [whole[k] for k in range(whole.shape[0])]
    return [value, swap(value, 1), swap(value, 2)]


def end_gather(parts):
    if lax.axis_size("grp") != 4:
        return parts
    return parts + [swap(parts[2], 1)]


def start_scatter(block):
    if lax.axis_size("grp") != 4:
        whole = jnp.stack([block(k) for k in range(lax.axis_size("grp"))]).astype(BF16)
        return lax.psum_scatter(whole, "grp", scatter_dimension=0, tiled=False)
    return swap(block(3).astype(BF16), 1)


def cross_scatter(block, corner):
    if lax.axis_size("grp") != 4:
        return corner
    return swap((corner.astype(F32) + block(2)).astype(BF16), 2)


def end_scatter(block, across):
    if lax.axis_size("grp") != 4:
        return across
    beside = swap(block(1).astype(BF16), 1).astype(F32)
    return (block(0) + beside + across.astype(F32)).astype(BF16)


def in_turn(blocks, order):
    picked = [lax.dynamic_index_in_dim(blocks, order[i], 0) for i in range(blocks.shape[0])]
    return jnp.concatenate(picked, axis=0)


class HeadPlan:
    def __init__(self, heads, seq, grp):
        self.seq, self.grp, self.heads = seq, grp, heads
        self.local = heads // seq
        self.mixed = (heads // grp) % seq == 0
        self.each = (heads // grp) // seq if self.mixed else 0

    def pick(self, item, seq_index, grp_index):
        rest = item.shape[1:]
        if self.mixed:
            item = item.reshape((self.grp, self.seq, self.each) + rest)
            item = lax.dynamic_index_in_dim(item, seq_index, 1, keepdims=False)
            return self.turn(item.reshape((self.local,) + rest), grp_index)
        return lax.dynamic_slice_in_dim(item, seq_index * self.local, self.local, 0)

    def turn(self, item, grp_index):
        if not self.mixed:
            return item
        item = item.reshape((self.grp, self.each) + item.shape[1:])
        parts = [
            lax.dynamic_index_in_dim(item, near(grp_index, k), 0, keepdims=False)
            for k in range(self.grp)
        ]
        return jnp.concatenate(parts, axis=0)

    def order(self, item):
        rest = item.shape[2:]
        if self.mixed:
            item = item.reshape((self.seq, self.grp, self.each) + rest)
            item = jnp.swapaxes(item, 0, 1)
        return item.reshape((self.heads,) + rest)


def exchange(block):
    return lax.all_to_all(block, "seq", 0, 0, tiled=True)


def cut_heads(plan, mats, turned, head_dim):
    count = len(mats)
    seq = plan.seq
    if plan.each == 1:
        return cut_features(seq, mats, turned)
    mats = [m.T if turn else m for m, turn in zip(mats, turned)]
    cols = mats[0].shape[1]
    if plan.mixed:
        block = jnp.stack([m.reshape(seq, plan.each, head_dim, cols) for m in mats], axis=2)
    else:
        block = lax.all_gather(jnp.stack(mats), "grp", axis=1, tiled=True)
        block = block.reshape(count, seq, plan.local, head_dim, cols).transpose(1, 2, 0, 3, 4)
    return block.reshape(seq, -1, cols)


def start_heads(plan, block):
    seq, _, cols = block.shape
    block = block.transpose(1, 0, 2).reshape(-1, seq * cols)
    return start_gather(block) if plan.mixed else [block]


def end_heads(plan, parts, count, head_dim):
    parts = end_gather(parts) if plan.mixed else parts
    size = count * head_dim
    return [part[i : i + size] for part in parts for i in range(0, part.shape[0], size)]


def heads_block(plan, grads):
    each = plan.each
    return lambda k: jnp.concatenate(grads[k * each : (k + 1) * each], axis=0)


def scatter_heads(plan, grads, block, turned):
    packed, width = grads[0].shape
    count = len(turned)
    seq = plan.seq
    cols = width // seq
    head_dim = packed // count
    if plan.mixed:
        each = plan.each
        block = exchange(block.reshape(-1, seq, cols).transpose(1, 0, 2))
        if each == 1:
            return join_features(block, seq * head_dim, turned)
        block = block.reshape(seq, each, count, head_dim, cols)
        block = block.transpose(2, 0, 1, 3, 4).reshape(count, -1, cols).astype(F32)
        return [part.T if turn else part for part, turn in zip(block, turned)]
    block = jnp.concatenate(grads, axis=0).astype(BF16)
    block = block.reshape(-1, seq, cols).transpose(1, 0, 2)
    block = exchange(block).reshape(seq, plan.local, count, head_dim, cols)
    block = block.transpose(2, 0, 1, 3, 4).reshape(count, -1, cols)
    block = lax.psum_scatter(block, "grp", scatter_dimension=1, tiled=True).astype(F32)
    return [part.T if turn else part for part, turn in zip(block, turned)]


def body(
    tokens,
    cotangent,
    lengths,
    prenorm_gain,
    w_query,
    w_key,
    w_value,
    w_gate,
    rate_weight,
    rate_bias,
    init_weight,
    init_bias,
    inner_gain,
    inner_bias,
    post_gain,
    post_bias,
    w_out,
    feedforward_norm_gain,
    w_swish,
    w_up,
    w_down,
):
    seq_index = lax.axis_index("seq")
    grp_index = lax.axis_index("grp")
    groups = lax.axis_size("grp")
    seq = lax.axis_size("seq")
    rows_tok = tokens.shape[1]
    width = tokens.shape[2]
    heads, head_dim, _ = init_weight.shape
    plan = HeadPlan(heads, seq, groups)
    local = plan.local
    features = local * head_dim
    stream = rows_tok * seq
    steps = slot_steps(seq)
    place = ring_place(seq, seq_index)
    member_of_slot = ring_member(seq, (place + jnp.array(steps, jnp.int32)) % seq)
    apart = (ring_place(seq, jnp.arange(seq, dtype=jnp.int32)) - place) % seq
    slot_of_member = jnp.where(apart > seq // 2, 2 * (seq - apart), 2 * apart + 1)
    slot_of_member = jnp.where(apart == 0, 0, jnp.where(apart == seq // 2, 1, slot_of_member))
    to_slots = (member_of_slot[:, None] == jnp.arange(seq)[None, :]).astype(F32)

    def in_slots(stat):
        cut = stat.reshape(-1, seq, rows_tok)
        out = jnp.einsum("sm,kmt->kst", to_slots, cut, precision=lax.Precision.HIGHEST)
        return out.reshape(-1, stream)

    def in_order(stat):
        cut = stat.reshape(-1, seq, rows_tok)
        out = jnp.einsum("sm,kst->kmt", to_slots, cut, precision=lax.Precision.HIGHEST)
        return out.reshape(-1, stream)

    def pick(item):
        return plan.pick(item, seq_index, grp_index)

    def by_distance(rows):
        return lambda k: lax.slice_in_dim(
            rows, at_slot(k) * rows_tok, (at_slot(k) + 1) * rows_tok, axis=0
        )

    def at_slot(k):
        return steps.index(k if k < seq // 2 else k - seq)

    own_lengths = lax.dynamic_index_in_dim(lengths, grp_index, 0, keepdims=False)
    ends = jnp.cumsum(own_lengths)
    starts = ends - own_lengths
    docs = jnp.concatenate([starts, ends[-1:]])

    proj_block = exchange(
        cut_heads(plan, (w_query, w_key, w_value), (True, True, True), head_dim)
    )
    padded = w_down.shape[0] // seq
    padded += -padded % MB
    rate_rows = jnp.pad(pick(rate_weight.T), ((0, 128 - local), (0, 0)))
    gb, init = chain_params(*(pick(i) for i in (init_weight, init_bias, inner_gain, inner_bias)))
    own = {}

    bias = jnp.pad(pick(rate_bias), (0, 128 - local))[None]

    def token_work(s, arrived):
        if s == 1:
            own["parts"] = start_heads(plan, after(proj_block, arrived[0]))
            return [gb, init, rate_rows, bias, docs, slot_of_member, member_of_slot]
        if s == seq // 2 - 2:
            mats = (w_swish.T, w_up.T, w_down)
            if plan.each == 1:
                turned = (True, False, False, False, False)
                own["rest"] = cut_features(seq, (w_gate, w_out) + mats, turned)
            else:
                side = cut_heads(plan, (w_gate, w_out), (True, False), head_dim)
                own["rest"] = jnp.concatenate(
                    [side, cut_features(seq, mats, (False,) * 3)], axis=1
                )
            return [own["rest"]]
        if s == seq // 2 - 1:
            own["parts"] = end_heads(plan, own["parts"], 3, head_dim)
            return own["parts"][-1:]
        return []

    token_steps = ring_gather(tokens[0], seq, token_work)
    normed, x3, logits = project(
        sum(by_slots(token_steps), ()), own["parts"], rate_rows, bias, prenorm_gain[None]
    )
    rest_block = exchange(after(own["rest"], token_steps[-1][0]))
    grad_own = cotangent[0]
    grad_steps = [(after(grad_own, rest_block),)]
    grad_steps.append(ring_step(grad_steps[0], 1, seq))

    inner, *kept = chain_forward(slot_of_member, docs, x3, logits, gb, init, rows_tok)
    side_rows = rest_block.shape[1] - 3 * padded
    side_block, ffn_block = rest_block[:, :side_rows], rest_block[:, side_rows:]

    sides = end_heads(plan, start_heads(plan, side_block), 2, head_dim)
    m_gate = jnp.concatenate([side[:head_dim] for side in sides], axis=0)
    m_out = jnp.concatenate([side[head_dim:] for side in sides], axis=0)
    gate_pre = mm_nt(normed, m_gate)
    ffn_block = ffn_block.transpose(1, 0, 2).reshape(3 * padded, width)
    ffn_parts = start_gather(ffn_block)

    sums = jnp.sum(kept[3][2:4].reshape(2, stream // MB, local, MB), axis=2).reshape(2, stream)
    sums = after(pairwise_sum(sums, "seq", seq), rest_block)
    sums = in_slots(sums) / width
    mean_o = sums[0][:, None]
    inv_o = lax.rsqrt(sums[1][:, None] - mean_o * mean_o + EPS)
    o_hat = (inner - mean_o) * inv_o
    post_g = pick(post_gain.reshape(heads, head_dim)).reshape(features)
    post_b = pick(post_bias.reshape(heads, head_dim)).reshape(features)
    post = o_hat * post_g + post_b
    gelu_val, gelu_pull = jax.vjp(jax.nn.gelu, gate_pre)
    gated = (gelu_val * post).astype(BF16)
    ffn = {}


    def ffn_corner(since):
        ffn["parts"] = end_gather(ffn_parts[:-1] + [after(ffn_parts[-1], since)])
        return ffn["parts"][-1:]

    mixing = ring_scatter(
        by_distance(after(mm(gated, m_out).astype(BF16), *grad_steps[1])),
        seq,
        [lambda since: [], lambda since: [], lambda since: [], ffn_corner],
    )
    own_rows = tokens[0].astype(F32)
    resid = own_rows + mixing
    inv_second = lax.rsqrt(jnp.mean(resid * resid, -1, keepdims=True) + EPS)
    unit_second = resid * inv_second
    ffn_in = (unit_second * feedforward_norm_gain).astype(BF16)

    got = {"kept": (), "rows": [], "grads": []}
    d_parts = {}

    def step_work(s, arrived, grads):
        slot = 2 * s if s < seq // 2 else 1
        members = lax.slice_in_dim(member_of_slot, slot, slot + len(arrived))
        got["kept"], d_in = ffn_step(
            members, seq, slot, arrived, grads, ffn["parts"], got["kept"]
        )
        got["rows"].append(arrived)
        got["grads"].append(grads)
        for i in range(len(arrived)):
            d_parts[steps[slot + i]] = d_in[i * rows_tok : (i + 1) * rows_tok]
        return [d_in]

    ring_gather(ffn_in, seq, step_work, grad_steps)
    kept_ffn = got["kept"]

    def ffn_work(since):
        first, *others = kept_ffn[:3]
        got["ffn"] = ffn_grads(
            groups,
            [after(first, since)] + others,
            sum(by_slots(got["rows"]), ()),
            sum(by_slots(got["grads"]), ()),
        )
        return got["ffn"][:1]

    def ffn_corner_work(since):
        got["corner"] = start_scatter(lambda k: after(got["ffn"][k], since))
        got["across"] = cross_scatter(ffn_grad, got["corner"])
        return [got["corner"]]

    def ffn_grad(k):
        return got["ffn"][k]

    d_ffn = ring_scatter(
        lambda k: d_parts[k if k < seq // 2 else k - seq], seq, [ffn_work, ffn_corner_work]
    )
    second_scaled = d_ffn * feedforward_norm_gain
    g_ffn_gain = jnp.sum(d_ffn * unit_second, 0)
    d_resid = grad_own.astype(F32) + inv_second * (
        second_scaled - unit_second * jnp.mean(second_scaled * unit_second, -1, keepdims=True)
    )

    def mix_work(s, arrived):
        if s == 0:
            late = [after(own["parts"][0], arrived[0])] + own["parts"][1:]
            got["w_all"] = jnp.concatenate(late + [rate_rows, m_gate], axis=0)
            return [got["w_all"]]
        if s == seq // 2 - 2:
            return [got["across"]]
        if s == seq // 2 - 1:
            summed = end_scatter(ffn_grad, after(got["across"], arrived[0]))
            got["summed"] = summed.reshape(3 * padded, seq, -1).transpose(1, 0, 2)
            return [got["summed"]]
        return []

    mix_steps = ring_gather(d_resid.astype(BF16), seq, mix_work)
    ffn_out = lax.psum_scatter(
        after(kept_ffn[3], mix_steps[seq // 2 - 2][0]), "seq", scatter_dimension=0, tiled=False
    )
    out_tokens = (resid + ffn_out.astype(F32)).astype(BF16)[None]
    d_gated = [mm_nt(jnp.concatenate(arrived, axis=0), m_out) for arrived in mix_steps]
    d_gated = jnp.concatenate(by_slots(d_gated), axis=0)
    d_post = d_gated * gelu_val
    d_gate_pre = gelu_pull(d_gated * post)[0].astype(BF16)
    g_post_gain = jnp.sum(d_post * o_hat, 0)
    g_post_bias = jnp.sum(d_post, 0)
    d_ohat = d_post * post_g
    sums = jnp.stack([jnp.sum(d_ohat, -1), jnp.sum(d_ohat * o_hat, -1)])
    sums = in_slots(pairwise_sum(in_order(sums), "seq", seq)) / width
    g_ffn = exchange(after(got["summed"], sums))
    d_inner = inv_o * (d_ohat - sums[0][:, None] - o_hat * sums[1][:, None])
    d_x, d_gb, d_init = chain_backward(
        slot_of_member, docs, x3, d_inner, d_gate_pre, logits, gb, init, kept, rows_tok
    )
    *head_rows_grads, g_rates, g_gain = proj_grads(
        d_x, normed, got["w_all"], gated, sum(by_slots(mix_steps), ()), local, head_dim
    )
    d_logits = d_x[:, 3 * features : 3 * features + local].astype(F32)
    parts = [item.reshape(local, -1) for item in chain_param_grads(d_gb, d_init, local)]
    parts += [item.reshape(local, head_dim) for item in (g_post_gain, g_post_bias)]
    parts += [g_rates[:local], jnp.sum(d_logits, 0)[:, None]]
    sizes = [item.shape[1] for item in parts]
    flat = jnp.concatenate(parts, axis=1)
    flat = plan.turn(jnp.pad(flat, ((0, 0), (0, -flat.shape[1] % 1024))), grp_index)
    count = flat.size
    flat = jnp.concatenate([flat.reshape(-1), g_gain[0] / prenorm_gain, g_ffn_gain])
    flat = pairwise_sum(flat.reshape(-1, 1024), "grp", groups)
    flat_all = lax.all_gather(flat, "seq", axis=0)
    d_x = after(d_x, g_gain, g_ffn)
    d_normed_part = mm(d_x, got["w_all"]).astype(BF16)

    def corner_work(since):
        if not plan.mixed:
            return [ffn_out]
        block = heads_block(plan, head_rows_grads)
        got["corner"] = start_scatter(block)
        got["across"] = cross_scatter(block, after(got["corner"], flat))
        return [got["corner"], ffn_out]

    def join_work(since):
        got["join"] = join_features(after(g_ffn, since), w_down.shape[0], (False,) * 3)
        return got["join"][:1]

    def across_work(since):
        return [got["across"]] if plan.mixed else []

    d_normed = ring_scatter(
        by_distance(d_normed_part), seq, [corner_work, join_work, across_work]
    )
    summed = end_scatter(heads_block(plan, head_rows_grads), got["across"]) if plan.mixed else None
    g_heads = scatter_heads(plan, head_rows_grads, summed, (True,) * 4 + (False,))
    own_inv = lax.rsqrt(jnp.mean(own_rows * own_rows, -1, keepdims=True) + EPS)
    own_unit = own_rows * own_inv
    first_scaled = d_normed * prenorm_gain
    grad_tokens = (
        d_resid
        + own_inv
        * (first_scaled - own_unit * jnp.mean(first_scaled * own_unit, -1, keepdims=True))
    )[None]

    flat = after(flat_all, d_normed).reshape(seq, -1)
    gains = jnp.sum(flat[:, count:], 0).reshape(2, width)
    flat = plan.order(flat[:, :count].reshape(seq, local, -1))
    small = []
    offset = 0
    for size in sizes:
        small.append(flat[:, offset : offset + size])
        offset += size
    g_ffn = got["join"]
    return (
        out_tokens,
        grad_tokens,
        gains[0],
        g_heads[0],
        g_heads[1],
        g_heads[2],
        g_heads[3],
        small[6].T,
        small[7][:, 0],
        small[0].reshape(heads, head_dim, head_dim),
        small[1],
        small[2],
        small[3],
        small[4].reshape(width),
        small[5].reshape(width),
        g_heads[4],
        gains[1],
        g_ffn[0].T,
        g_ffn[1].T,
        g_ffn[2],
    )


def solution(mesh):
    whole = P()
    rows = P("grp", "seq", None)
    wide = P("seq", "grp")
    tall = P("grp", "seq")
    return jax.shard_map(
        body,
        mesh=mesh,
        in_specs=(rows, rows, whole, whole, wide, wide, wide, wide)
        + (whole,) * 8
        + (tall, whole, wide, wide, tall),
        out_specs=(rows, rows, whole, wide, wide, wide, wide)
        + (whole,) * 8
        + (tall, whole, wide, wide, tall),
        check_vma=False,
    )
```

```python
from functools import partial

import jax
import jax.numpy as jnp
from jax import lax
from jax.experimental import pallas as pl
from jax.experimental.pallas import tpu as pltpu
from jax.sharding import PartitionSpec as P

MB = 16
EPS = 1e-06
F32 = jnp.float32
VMEM_ASKED = 58 * 1024 * 1024
BF16 = jnp.bfloat16


def mm(left, right):
    return jnp.dot(left, right, preferred_element_type=F32)


def mm_nt(left, right):
    return lax.dot_general(left, right, (((1,), (1,)), ((), ())), preferred_element_type=F32)


def split_two(value):
    high = value.astype(BF16)
    return high, (value - high.astype(F32)).astype(BF16)


def mean_rows(value):
    return jnp.mean(value, axis=0, keepdims=True)


def chunk_rows(value, heads, start, lanes, size):
    tokens = value.shape[0]
    cuts = [value[:, lanes * h + start : lanes * h + start + size] for h in range(heads)]
    parts = [cut[m * MB : (m + 1) * MB] for m in range(tokens // MB) for cut in cuts]
    return jnp.concatenate(parts, axis=0)


def head_rows(rows, heads, h):
    step = MB * heads
    parts = [rows[m * step + h * MB : m * step + (h + 1) * MB] for m in range(rows.shape[0] // step)]
    return jnp.concatenate(parts, axis=0)


def chunk_masks(info, heads, count):
    step = MB * heads
    row = lax.broadcasted_iota(jnp.int32, (count, count), 0)
    col = lax.broadcasted_iota(jnp.int32, (count, count), 1)
    columns = jnp.transpose(info)
    same = ((row % step) // MB == (col % step) // MB) & (columns[:, 1:2] == info[1:2, :])
    return row // step, col // step, row % MB, col % MB, same, columns


def chunk_info(docs_ref, logits, heads, head_dim, chunk):
    tokens = logits.shape[0]
    count = heads * tokens
    step = MB * heads
    docs = docs_ref.shape[0] - 1
    pieces = [logits[m * MB : (m + 1) * MB] for m in range(tokens // MB) for _ in range(heads)]
    spread = jnp.concatenate(pieces, axis=0)
    lane = lax.broadcasted_iota(jnp.int32, spread.shape, 1)
    own = (lax.broadcasted_iota(jnp.int32, spread.shape, 0) % step) // MB
    logit = jnp.sum(jnp.transpose(jnp.where(lane == own, spread, 0.0)), axis=0, keepdims=True)
    start = chunk * tokens
    col = lax.broadcasted_iota(jnp.int32, (1, count), 1)
    block_at = start + (col // step) * MB
    doc = jnp.zeros((1, count), jnp.int32)
    before = end = jnp.int32(0)
    for d in range(docs):
        doc = doc + (block_at >= docs_ref[d]).astype(jnp.int32)
        before = before + (docs_ref[d] < start).astype(jnp.int32)
        end = end + (docs_ref[d] < start + tokens).astype(jnp.int32)
    live = (block_at + col % MB < docs_ref[docs]).astype(F32)
    sig = jax.nn.sigmoid(logit)
    zero = jnp.zeros((1, count), F32)
    return jnp.concatenate(
        [
            sig / head_dim * live,
            doc.astype(F32),
            (doc > before).astype(F32),
            (doc == end).astype(F32),
            zero + (end > before).astype(F32),
            live * sig * (1.0 - sig) / head_dim,
            zero,
            zero,
        ],
        axis=0,
    )


def augment(rows, heads, head_dim, wide):
    count = rows.shape[0]
    near = lax.broadcasted_iota(jnp.int32, (head_dim, wide), 0)
    far = lax.broadcasted_iota(jnp.int32, (head_dim, wide), 1)
    tile = (far % head_dim == near).astype(BF16)
    lane = lax.broadcasted_iota(jnp.int32, (count, wide), 1)
    own = (lax.broadcasted_iota(jnp.int32, (count, wide), 0) % (MB * heads)) // MB
    return jnp.where(lane // head_dim == own, mm(rows, tile), 0.0)


def one_hot_heads(count, heads):
    lane = lax.broadcasted_iota(jnp.int32, (count, 128), 1)
    own = (lax.broadcasted_iota(jnp.int32, (count, 128), 0) % (MB * heads)) // MB
    return (lane == own).astype(BF16)


def forward_kernel(
    heads, idx_ref, docs_ref, x_ref, logit_ref, gb_ref, init_ref, out_ref, n_ref, r_ref, nb_ref, stat_ref, w_ref, state
):
    head_dim = gb_ref.shape[1]
    tokens = x_ref.shape[0]
    count = heads * tokens
    full = init_ref.shape[1]
    wide = full - 128

    @pl.when(pl.program_id(0) == 0)
    def _():
        state[...] = init_ref[...]

    carried = state[...]
    w_ref[0] = carried
    info = chunk_info(docs_ref, logit_ref[...], heads, head_dim, pl.program_id(0))
    x = x_ref[...]
    q_rows = chunk_rows(x, heads, 0, 3 * head_dim, head_dim)
    k_rows = chunk_rows(x, heads, head_dim, 3 * head_dim, head_dim)
    v_rows = chunk_rows(x, heads, 2 * head_dim, 3 * head_dim, head_dim)
    q_t = jnp.transpose(q_rows.astype(F32))
    target_t = jnp.transpose(v_rows.astype(F32) - k_rows.astype(F32))
    mb_row, mb_col, t_row, t_col, same, columns = chunk_masks(info, heads, count)
    gram = jnp.where(same & (mb_row < mb_col), mm_nt(k_rows, k_rows) + 1.0, 0.0).astype(BF16)
    cross = jnp.where(
        same & ((mb_row < mb_col) | ((mb_row == mb_col) & (t_row <= t_col))),
        mm_nt(k_rows, q_rows) + 1.0,
        0.0,
    ).astype(BF16)
    hot = one_hot_heads(count, heads)
    k_aug = jnp.concatenate([augment(k_rows, heads, head_dim, wide).astype(BF16), hot], axis=1)
    q_aug = jnp.concatenate([augment(q_rows, heads, head_dim, wide).astype(BF16), hot], axis=1)
    init = init_ref[...]
    stacked = jnp.concatenate(split_two(carried) + split_two(init), axis=0)
    fresh = info[2:3, :] > 0.5

    def through_state(rows):
        both = mm_nt(stacked, rows)
        return jnp.where(
            fresh,
            both[2 * head_dim : 3 * head_dim] + both[3 * head_dim :],
            both[:head_dim] + both[head_dim : 2 * head_dim],
        )

    z_start = through_state(k_aug)
    gain = gb_ref[0]
    shift = gb_ref[1]
    repeats = count // 128
    inner = 128 // (MB * heads)
    done = []
    for p in range(repeats):
        cols = slice(p * 128, (p + 1) * 128)
        z_base = z_start[:, cols]
        if p:
            z_base = z_base - mm(jnp.concatenate(done, axis=1), gram[: p * 128, cols])
        target = target_t[:, cols]
        rate = info[0:1, cols]
        z = z_base
        for step in range(inner):
            if step:
                z = z_base - mm(scaled.astype(BF16), gram[cols, cols])
            centred = z - mean_rows(z)
            inv = lax.rsqrt(mean_rows(centred * centred) + EPS)
            n = centred * inv
            err = (n * gain + shift - target) * gain
            scaled = (rate * inv) * (err - mean_rows(err) - n * mean_rows(err * n))
        done.append(scaled.astype(BF16))
        n_ref[:, cols] = n
        r_ref[:, cols] = scaled
        stat_ref[0:1, cols] = inv
    r_bf = jnp.concatenate(done, axis=1)
    z_bar = through_state(q_aug) - mm(r_bf, cross)
    centred = z_bar - mean_rows(z_bar)
    inv = lax.rsqrt(mean_rows(centred * centred) + EPS)
    nb = centred * inv
    nb_ref[...] = nb
    stat_ref[1:2, :] = inv
    wide_gain = jnp.concatenate([gain] * repeats, axis=1)
    wide_shift = jnp.concatenate([shift] * repeats, axis=1)
    out_t = q_t + nb * wide_gain + wide_shift
    stat_ref[2:3, :] = jnp.sum(out_t, axis=0, keepdims=True)
    stat_ref[3:4, :] = jnp.sum(out_t * out_t, axis=0, keepdims=True)
    out_rows = jnp.transpose(out_t)
    for h in range(heads):
        out_ref[:, h * head_dim : (h + 1) * head_dim] = head_rows(out_rows, heads, h)
    base = jnp.where(info[4:5, 0:1] > 0.5, init, carried)
    state[...] = base - mm((r_ref[...] * info[3:4, :]).astype(BF16), k_aug)


def backward_kernel(
    heads,
    idx_ref,
    docs_ref,
    x_ref,
    d_ref,
    gate_ref,
    logit_ref,
    gb_ref,
    init_ref,
    n_ref,
    r_ref,
    nb_ref,
    stat_ref,
    w_ref,
    dx_ref,
    dgb_ref,
    dinit_ref,
    state,
):
    head_dim = gb_ref.shape[1]
    tokens = x_ref.shape[0]
    count = heads * tokens
    full = init_ref.shape[1]
    wide = full - 128

    @pl.when(pl.program_id(0) == 0)
    def _():
        state[...] = jnp.zeros_like(state)
        dgb_ref[...] = jnp.zeros_like(dgb_ref)
        dinit_ref[...] = jnp.zeros_like(dinit_ref)

    d_end = state[...]
    carried = w_ref[0]
    init = init_ref[...]
    chunk = pl.num_programs(0) - 1 - pl.program_id(0)
    info = chunk_info(docs_ref, logit_ref[...], heads, head_dim, chunk)
    x = x_ref[...]
    q_rows = chunk_rows(x, heads, 0, 3 * head_dim, head_dim)
    k_rows = chunk_rows(x, heads, head_dim, 3 * head_dim, head_dim)
    v_rows = chunk_rows(x, heads, 2 * head_dim, 3 * head_dim, head_dim)
    d_rows = chunk_rows(d_ref[...], heads, 0, head_dim, head_dim)
    target_t = jnp.transpose(v_rows.astype(F32) - k_rows.astype(F32))
    d_t = jnp.transpose(d_rows)
    mb_row, mb_col, t_row, t_col, same, columns = chunk_masks(info, heads, count)
    earlier = same & (mb_row < mb_col)
    later = same & (mb_row > mb_col)
    up_to = same & ((mb_row < mb_col) | ((mb_row == mb_col) & (t_row <= t_col)))
    from_on = same & ((mb_row > mb_col) | ((mb_row == mb_col) & (t_row >= t_col)))
    gram = jnp.where(later, mm_nt(k_rows, k_rows) + 1.0, 0.0).astype(BF16)
    cross = jnp.where(from_on, mm_nt(q_rows, k_rows) + 1.0, 0.0).astype(BF16)
    hot = one_hot_heads(count, heads)
    k_aug = jnp.concatenate([augment(k_rows, heads, head_dim, wide).astype(BF16), hot], axis=1)
    q_aug = jnp.concatenate([augment(q_rows, heads, head_dim, wide).astype(BF16), hot], axis=1)
    gain = gb_ref[0]
    shift = gb_ref[1]
    repeats = count // 128
    inner = 128 // (MB * heads)
    wide_gain = jnp.concatenate([gain] * repeats, axis=1)
    nb = nb_ref[...]
    inv_b = stat_ref[1:2, :]
    d_nb = d_t * wide_gain
    d_zbar = inv_b * (d_nb - mean_rows(d_nb) - nb * mean_rows(d_nb * nb))
    scaled_t = r_ref[...]
    last = info[3:4, :]
    dr_base = -mm(d_zbar.astype(BF16), cross) - last * mm_nt(d_end.astype(BF16), k_aug)
    gain_sum = jnp.zeros((head_dim, 128), F32)
    shift_sum = jnp.zeros((head_dim, 128), F32)
    for p in range(repeats):
        cols = slice(p * 128, (p + 1) * 128)
        gain_sum = gain_sum + d_t[:, cols] * nb[:, cols]
        shift_sum = shift_sum + d_t[:, cols]
    done = []
    errs = []
    d_rates = []
    for p in reversed(range(repeats)):
        cols = slice(p * 128, (p + 1) * 128)
        base = dr_base[:, cols]
        if done:
            base = base - mm(jnp.concatenate(done, axis=1), gram[(p + 1) * 128 :, cols])
        n = n_ref[:, cols]
        inv = stat_ref[0:1, cols]
        rate = info[0:1, cols]
        miss = n * gain + shift - target_t[:, cols]
        err = miss * gain
        along = mean_rows(err * n)
        plain = inv * (err - mean_rows(err) - n * along)
        gain2 = gain * gain
        d_scaled = base
        for step in range(inner):
            if step:
                d_scaled = base - mm(d_z.astype(BF16), gram[cols, cols])
            g = rate * d_scaled
            g_n = mean_rows(g * n)
            d_err = inv * (g - mean_rows(g) - n * g_n)
            d_n = d_err * gain2 - inv * (g * along + err * g_n)
            d_z = inv * (d_n - mean_rows(d_n) - n * (mean_rows(d_n * n) + mean_rows(g * plain)))
        done.insert(0, d_z.astype(BF16))
        errs.insert(0, d_err * gain)
        d_rates.insert(0, jnp.sum(d_scaled * plain, axis=0, keepdims=True))
        gain_sum = gain_sum + d_err * (miss + gain * n)
        shift_sum = shift_sum + d_err * gain
    dgb_ref[0] += gain_sum
    dgb_ref[1] += shift_sum
    dz_bf = jnp.concatenate(done, axis=1)
    d_z = dz_bf.astype(F32)
    d_errg = jnp.concatenate(errs, axis=1)
    turned = jnp.transpose(jnp.concatenate([d_zbar, scaled_t, d_z, d_errg], axis=0))
    zb_rows = turned[:, :head_dim].astype(BF16)
    r_rows = turned[:, head_dim : 2 * head_dim].astype(BF16)
    z_rows = turned[:, 2 * head_dim : 3 * head_dim].astype(BF16)
    e_rows = turned[:, 3 * head_dim :]
    d_cross = jnp.where(from_on, -mm_nt(zb_rows, r_rows), 0.0).astype(BF16)
    d_cross_t = jnp.where(up_to, -mm_nt(r_rows, zb_rows), 0.0).astype(BF16)
    d_gram = (
        jnp.where(later, -mm_nt(z_rows, r_rows), 0.0)
        + jnp.where(earlier, -mm_nt(r_rows, z_rows), 0.0)
    ).astype(BF16)
    is_init = columns[:, 2:3] > 0.5
    is_last = columns[:, 3:4] > 0.5

    def stack_heads(weight):
        parts = [weight[:, h * head_dim : (h + 1) * head_dim] for h in range(heads)]
        pad = wide - heads * head_dim
        if pad:
            parts.append(jnp.zeros((pad, head_dim), F32))
        return jnp.concatenate(parts, axis=0).astype(BF16)

    w_both = jnp.concatenate([stack_heads(carried), stack_heads(init)], axis=0)
    d_stack = stack_heads(d_end)

    def by_state(rows):
        own = augment(rows, heads, head_dim, wide)
        return jnp.concatenate(
            [jnp.where(is_init, 0.0, own), jnp.where(is_init, own, 0.0)], axis=1
        ).astype(BF16)

    dq = d_rows + mm(d_cross, k_rows) + mm(by_state(zb_rows), w_both)
    r_own = jnp.where(is_last, augment(r_rows, heads, head_dim, wide), 0.0).astype(BF16)
    dk = (
        e_rows
        + mm(d_gram, k_rows)
        + mm(d_cross_t, q_rows)
        + mm(by_state(z_rows), w_both)
        - mm(r_own, d_stack)
    )
    packed = jnp.concatenate([dq.astype(BF16), dk.astype(BF16), (-e_rows).astype(BF16)], axis=1)
    each = 3 * head_dim
    d_logits = jnp.concatenate(d_rates, axis=1) * info[5:6, :]
    turned = jnp.transpose(jnp.concatenate([d_logits, jnp.zeros((7, count), F32)], axis=0))
    lane = lax.broadcasted_iota(jnp.int32, (tokens, 128), 1)
    logit_rows = jnp.zeros((tokens, 128), F32)
    for h in range(heads):
        dx_ref[:, h * each : (h + 1) * each] = head_rows(packed, heads, h)
        logit_rows = jnp.where(lane == h, head_rows(turned, heads, h)[:, 0:1], logit_rows)
    dx_ref[:, heads * each : heads * each + 128] = logit_rows.astype(BF16)
    dx_ref[:, heads * each + 128 :] = gate_ref[...]
    row_init = info[2:3, :] > 0.5
    zb_two = jnp.concatenate(
        [jnp.where(row_init, 0.0, d_zbar), jnp.where(row_init, d_zbar, 0.0)], axis=0
    ).astype(BF16)
    z_two = jnp.concatenate(
        [jnp.where(row_init, 0.0, d_z), jnp.where(row_init, d_z, 0.0)], axis=0
    ).astype(BF16)
    d_both = mm(zb_two, q_aug) + mm(z_two, k_aug)
    fresh = info[4:5, 0:1] > 0.5
    state[...] = d_both[:head_dim] + jnp.where(fresh, 0.0, d_end)
    dinit_ref[...] += d_both[head_dim:] + jnp.where(fresh, d_end, 0.0)


def chain_specs(heads, tokens, head_dim, full, at):
    count = heads * tokens
    return dict(
        x=pl.BlockSpec((tokens, heads * 3 * head_dim), lambda i, idx, docs: (idx[at(i)], 0)),
        dx=pl.BlockSpec((tokens, heads * 4 * head_dim + 128), lambda i, idx, docs: (idx[at(i)], 0)),
        rows=pl.BlockSpec((tokens, heads * head_dim), lambda i, idx, docs: (idx[at(i)], 0)),
        logit=pl.BlockSpec((tokens, 128), lambda i, idx, docs: (idx[at(i)], 0)),
        gb=pl.BlockSpec((2, head_dim, 128), lambda i, idx, docs: (0, 0, 0)),
        init=pl.BlockSpec((head_dim, full), lambda i, idx, docs: (0, 0)),
        tall=pl.BlockSpec((head_dim, count), lambda i, idx, docs: (0, at(i))),
        stat=pl.BlockSpec((8, count), lambda i, idx, docs: (0, at(i))),
        weight=pl.BlockSpec((1, head_dim, full), lambda i, idx, docs: (at(i), 0, 0)),
    )


def chain_forward(idx, docs, x3, logits, gb, init, tokens):
    total = x3.shape[0]
    head_dim = gb.shape[1]
    heads = x3.shape[1] // (3 * head_dim)
    chunks = total // tokens
    full = init.shape[1]
    s = chain_specs(heads, tokens, head_dim, full, lambda i: i)
    tall = jax.ShapeDtypeStruct((head_dim, heads * total), F32)
    return pl.pallas_call(
        partial(forward_kernel, heads),
        grid_spec=pltpu.PrefetchScalarGridSpec(
            num_scalar_prefetch=2,
            grid=(chunks,),
            in_specs=[s["x"], s["logit"], s["gb"], s["init"]],
            out_specs=[s["rows"], s["tall"], s["tall"], s["tall"], s["stat"], s["weight"]],
            scratch_shapes=[pltpu.VMEM((head_dim, full), F32)],
        ),
        out_shape=[
            jax.ShapeDtypeStruct((total, heads * head_dim), F32),
            tall,
            tall,
            tall,
            jax.ShapeDtypeStruct((8, heads * total), F32),
            jax.ShapeDtypeStruct((chunks, head_dim, full), F32),
        ],
        compiler_params=pltpu.CompilerParams(
            dimension_semantics=("arbitrary",), vmem_limit_bytes=VMEM_ASKED
        ),
        cost_estimate=pl.CostEstimate(flops=1, bytes_accessed=1, transcendentals=0),
        name="chain_forward",
    )(idx, docs, x3, logits, gb, init)


def chain_backward(idx, docs, x3, d_inner, d_gate, logits, gb, init, kept, tokens):
    total = x3.shape[0]
    head_dim = gb.shape[1]
    heads = x3.shape[1] // (3 * head_dim)
    chunks = total // tokens
    full = init.shape[1]
    s = chain_specs(heads, tokens, head_dim, full, lambda i: chunks - 1 - i)
    return pl.pallas_call(
        partial(backward_kernel, heads),
        grid_spec=pltpu.PrefetchScalarGridSpec(
            num_scalar_prefetch=2,
            grid=(chunks,),
            in_specs=[
                s["x"],
                s["rows"],
                s["rows"],
                s["logit"],
                s["gb"],
                s["init"],
                s["tall"],
                s["tall"],
                s["tall"],
                s["stat"],
                s["weight"],
            ],
            out_specs=[s["dx"], s["gb"], s["init"]],
            scratch_shapes=[pltpu.VMEM((head_dim, full), F32)],
        ),
        out_shape=[
            jax.ShapeDtypeStruct((total, heads * 4 * head_dim + 128), BF16),
            jax.ShapeDtypeStruct(gb.shape, F32),
            jax.ShapeDtypeStruct(init.shape, F32),
        ],
        compiler_params=pltpu.CompilerParams(
            dimension_semantics=("arbitrary",), vmem_limit_bytes=VMEM_ASKED
        ),
        cost_estimate=pl.CostEstimate(flops=1, bytes_accessed=1, transcendentals=0),
        name="chain_backward",
    )(idx, docs, x3, d_inner, d_gate, logits, gb, init, *kept)


def chain_params(init_weight, init_bias, inner_gain, inner_bias):
    heads, head_dim, _ = init_weight.shape
    reps = 128 // (MB * heads)

    def pattern(item):
        row = jnp.broadcast_to(item.T[:, None, :, None], (head_dim, reps, heads, MB))
        return row.reshape(head_dim, 128)

    gb = jnp.stack([pattern(inner_gain), pattern(inner_bias)])
    wide = max(128, heads * head_dim)
    w_t = jnp.transpose(init_weight, (2, 0, 1)).reshape(head_dim, heads * head_dim)
    init = jnp.concatenate(
        [
            jnp.pad(w_t, ((0, 0), (0, wide - heads * head_dim))),
            jnp.pad(init_bias.T, ((0, 0), (0, 128 - heads))),
        ],
        axis=1,
    )
    return gb, init


def chain_param_grads(dgb, dinit, heads):
    head_dim = dinit.shape[0]
    wide = dinit.shape[1] - 128
    d_w = dinit[:, : heads * head_dim].reshape(head_dim, heads, head_dim).transpose(1, 2, 0)
    d_b = dinit[:, wide : wide + heads].T
    both = jnp.sum(dgb.reshape(2, head_dim, -1, heads, MB), axis=(2, 4))
    return d_w, d_b, both[0].T, both[1].T


def cut_kernel(turned, shares, *refs):
    mats, out_ref, held = refs[: len(turned)], refs[-2], refs[-1]
    at = 0
    for mat, turn, share in zip(mats, turned, shares):
        padded = share + -share % MB
        value = mat[...].astype(F32)
        held[: value.shape[1] if turn else value.shape[0]] = jnp.transpose(value) if turn else value
        for s in range(out_ref.shape[0]):
            out_ref[s, at : at + share] = held[s * share : (s + 1) * share].astype(BF16)
            if padded > share:
                out_ref[s, at + share : at + padded] = jnp.zeros(
                    (padded - share, out_ref.shape[2]), BF16
                )
        at += padded


def cut_features(seq, mats, turned):
    features = [m.shape[1] if turn else m.shape[0] for m, turn in zip(mats, turned)]
    cols = mats[0].shape[0] if turned[0] else mats[0].shape[1]
    shares = [count // seq for count in features]
    rows = sum(share + -share % MB for share in shares)
    return pl.pallas_call(
        partial(cut_kernel, turned, shares),
        out_shape=jax.ShapeDtypeStruct((seq, rows, cols), BF16),
        scratch_shapes=[pltpu.VMEM((max(features), cols), F32)],
        compiler_params=pltpu.CompilerParams(vmem_limit_bytes=VMEM_ASKED),
        cost_estimate=pl.CostEstimate(flops=1, bytes_accessed=1, transcendentals=0),
        name="cut_features",
    )(*mats)


def join_kernel(turned, share, padded, in_ref, *refs):
    outs, held = refs[:-1], refs[-1]
    for i, out in enumerate(outs):
        for s in range(in_ref.shape[0]):
            held[s * share : (s + 1) * share] = in_ref[
                s, i * padded : i * padded + share
            ].astype(F32)
        out[...] = jnp.transpose(held[...]) if turned[i] else held[...]


def join_features(block, features, turned):
    seq, rows, cols = block.shape
    shapes = [(cols, features) if turn else (features, cols) for turn in turned]
    return pl.pallas_call(
        partial(join_kernel, turned, features // seq, rows // len(turned)),
        out_shape=[jax.ShapeDtypeStruct(shape, F32) for shape in shapes],
        scratch_shapes=[pltpu.VMEM((features, cols), F32)],
        compiler_params=pltpu.CompilerParams(vmem_limit_bytes=VMEM_ASKED),
        cost_estimate=pl.CostEstimate(flops=1, bytes_accessed=1, transcendentals=0),
        name="join_features",
    )(block)


def ffn_kernel(count, parts, kept, member_ref, *refs):
    rows_refs = refs[:count]
    grad_refs = refs[count : 2 * count]
    weights = refs[2 * count : 2 * count + parts]
    outs = refs[2 * count + parts + kept :]
    (at_ref, ut_ref, ht_ref, y_ref, d_ref, a_t, u_t, h_t, y_all, d_all) = outs
    step = pl.program_id(0)
    size = rows_refs[0].shape[0]

    @pl.when(step == 0)
    def _():
        padded = weights[0].shape[0] // 3
        swish, up, down = (
            jnp.concatenate([w[i * padded : (i + 1) * padded] for w in weights], axis=0)
            for i in range(3)
        )
        rows = jnp.concatenate([ref[...] for ref in rows_refs], axis=0)
        grad = jnp.concatenate([ref[...] for ref in grad_refs], axis=0)
        act_a = mm_nt(rows, swish)
        act_u = mm_nt(rows, up)
        d_hidden = mm_nt(grad, down)
        sig = jax.nn.sigmoid(act_a)
        gate = act_a * sig
        hidden = gate * act_u
        d_a = d_hidden * act_u * sig * (1.0 + act_a * (1.0 - sig))
        d_u = d_hidden * gate
        d_all[...] = (mm(d_a.astype(BF16), swish) + mm(d_u.astype(BF16), up)).astype(BF16)
        y_all[...] = mm(hidden.astype(BF16), down).astype(BF16)
        fill = -hidden.shape[1] % 128
        for out, value in ((a_t, d_a), (u_t, d_u), (h_t, hidden)):
            if fill:
                value = jnp.concatenate([value, jnp.zeros((value.shape[0], fill), F32)], axis=1)
            out[...] = jnp.transpose(value)[: out.shape[0]].astype(BF16)

    for i in range(count):

        @pl.when(step == i)
        def _(i=i):
            part = slice(i * size, (i + 1) * size)
            at_ref[...] = a_t[:, part]
            ut_ref[...] = u_t[:, part]
            ht_ref[...] = h_t[:, part]
            y_ref[0] = y_all[part]
            d_ref[...] = d_all[part]


def ffn_step(members, seq, slot, rows, grads, weights, kept):
    count = len(rows)
    size, width = rows[0].shape
    total = seq * size
    features = sum(w.shape[0] for w in weights) // 3
    whole = pl.BlockSpec(memory_space=pltpu.VMEM)

    turned_spec = pl.BlockSpec((features, size), lambda s, member: (0, slot + s))
    turned = jax.ShapeDtypeStruct((features, total), BF16)
    first = 1 + 2 * count + len(weights)
    out = pl.pallas_call(
        partial(ffn_kernel, count, len(weights), len(kept)),
        grid_spec=pltpu.PrefetchScalarGridSpec(
            num_scalar_prefetch=1,
            grid=(count,),
            in_specs=[whole] * (2 * count + len(weights))
            + [pl.BlockSpec(memory_space=pl.ANY)] * len(kept),
            out_specs=[turned_spec] * 3
            + [
                pl.BlockSpec((1, size, width), lambda s, member: (member[s], 0, 0)),
                pl.BlockSpec((size, width), lambda s, member: (s, 0)),
            ],
            scratch_shapes=[pltpu.VMEM((features, count * size), BF16)] * 3
            + [pltpu.VMEM((count * size, width), BF16)] * 2,
        ),
        out_shape=[turned] * 3
        + [
            jax.ShapeDtypeStruct((seq, size, width), BF16),
            jax.ShapeDtypeStruct((count * size, width), BF16),
        ],
        input_output_aliases={first + i: i for i in range(len(kept))},
        compiler_params=pltpu.CompilerParams(
            dimension_semantics=("arbitrary",), vmem_limit_bytes=VMEM_ASKED
        ),
        cost_estimate=pl.CostEstimate(flops=1, bytes_accessed=1, transcendentals=0),
        name="ffn_step",
    )(members, *rows, *grads, *weights, *kept)
    return out[:-1], out[-1]


def ffn_grad_kernel(parts, count, at_ref, ut_ref, ht_ref, *refs):
    x = jnp.concatenate([ref[...] for ref in refs[:count]], axis=0)
    g = jnp.concatenate([ref[...] for ref in refs[count : 2 * count]], axis=0)
    padded = at_ref.shape[0] // parts
    for i, out in enumerate(refs[2 * count :]):
        own = slice(i * padded, (i + 1) * padded)
        out[:padded] = mm(at_ref[own], x).astype(BF16)
        out[padded : 2 * padded] = mm(ut_ref[own], x).astype(BF16)
        out[2 * padded :] = mm(ht_ref[own], g).astype(BF16)


def ffn_grads(parts, turned, rows, grads):
    size, width = rows[0].shape
    count = len(rows)
    features = turned[0].shape[0]
    wide = pl.BlockSpec((size, 256), lambda i: (0, i))
    whole = pl.BlockSpec((features, count * size), lambda i: (0, 0))
    each = 3 * features // parts
    return pl.pallas_call(
        partial(ffn_grad_kernel, parts, count),
        grid=(width // 256,),
        in_specs=[whole] * 3 + [wide] * (2 * count),
        out_specs=[pl.BlockSpec((each, 256), lambda i: (0, i))] * parts,
        out_shape=[jax.ShapeDtypeStruct((each, width), BF16)] * parts,
        compiler_params=pltpu.CompilerParams(
            dimension_semantics=("arbitrary",), vmem_limit_bytes=VMEM_ASKED
        ),
        cost_estimate=pl.CostEstimate(flops=1, bytes_accessed=1, transcendentals=0),
        name="ffn_grads",
    )(*turned, *rows, *grads)


def proj_grad_kernel(heads, head_dim, d_ref, x_ref, w_ref, gated_ref, *refs):
    count = len(refs) - heads - 4
    mix = refs[:count]
    outs, rate_ref, gain_ref = refs[count : count + heads], refs[-4], refs[-3]
    turned, gated_turned = refs[-2:]
    each = 3 * head_dim

    @pl.when(pl.program_id(0) == 0)
    def _():
        turned[...] = jnp.transpose(d_ref[...].astype(F32)).astype(BF16)
        gated_turned[...] = jnp.transpose(gated_ref[...].astype(F32)).astype(BF16)

    grad = mm(turned[...], x_ref[...])
    grad_out = mm(gated_turned[...], jnp.concatenate([ref[...] for ref in mix], axis=0))
    gain_ref[...] = jnp.broadcast_to(
        jnp.sum(grad * w_ref[...].astype(F32), axis=0, keepdims=True), gain_ref.shape
    )
    gate = heads * each + 128
    for h, out in enumerate(outs):
        own = slice(h * head_dim, (h + 1) * head_dim)
        out[:each] = grad[h * each : (h + 1) * each].astype(BF16)
        out[each : each + head_dim] = grad[gate + h * head_dim : gate + (h + 1) * head_dim].astype(
            BF16
        )
        out[each + head_dim :] = grad_out[own].astype(BF16)
    rate_ref[...] = grad[heads * each : heads * each + 8]


def proj_grads(d_x, normed, weight, gated, mix, heads, head_dim):
    total, packed = d_x.shape
    width = normed.shape[1]

    def wide(rows):
        return pl.BlockSpec((rows, 256), lambda i: (0, i))

    def whole(array):
        return pl.BlockSpec(array.shape, lambda i: (0, 0))

    return pl.pallas_call(
        partial(proj_grad_kernel, heads, head_dim),
        grid=(width // 256,),
        in_specs=[whole(d_x), wide(total), wide(packed), whole(gated)]
        + [wide(block.shape[0]) for block in mix],
        out_specs=[wide(5 * head_dim)] * heads + [wide(8)] * 2,
        out_shape=[jax.ShapeDtypeStruct((5 * head_dim, width), BF16)] * heads
        + [jax.ShapeDtypeStruct((8, width), F32)] * 2,
        scratch_shapes=[pltpu.VMEM((packed, total), BF16), pltpu.VMEM(gated.shape[::-1], BF16)],
        compiler_params=pltpu.CompilerParams(
            dimension_semantics=("arbitrary",), vmem_limit_bytes=VMEM_ASKED
        ),
        cost_estimate=pl.CostEstimate(flops=1, bytes_accessed=1, transcendentals=0),
        name="proj_grads",
    )(d_x, normed, weight, gated, *mix)


def project_kernel(count, parts, *refs):
    blocks = refs[:count]
    weights = refs[count : count + parts]
    rate_ref, bias_ref, gain_ref, normed_ref, x_ref, logit_ref = refs[count + parts :]
    size = blocks[0].shape[0]
    packed = x_ref.shape[1]
    for i in range(0, count, 2):

        @pl.when(pl.program_id(0) == i // 2)
        def _(i=i):
            rows = jnp.concatenate([ref[...] for ref in blocks[i : i + 2]], axis=0).astype(F32)
            inv = lax.rsqrt(jnp.mean(rows * rows, -1, keepdims=True) + EPS)
            normed = (rows * inv * gain_ref[...]).astype(BF16)
            normed_ref[...] = normed
            weight = jnp.concatenate([ref[...] for ref in weights] + [rate_ref[...]], axis=0)
            out = mm_nt(normed, weight)
            x_ref[...] = out[:, :packed].astype(BF16)
            logit_ref[...] = out[:, packed:] + bias_ref[...]


def project(blocks, weights, rate_rows, bias, gain):
    size, width = blocks[0].shape
    count = len(blocks)
    total = count * size
    packed = sum(w.shape[0] for w in weights)

    def rows(lanes):
        return pl.BlockSpec((2 * size, lanes), lambda i: (i, 0))

    return pl.pallas_call(
        partial(project_kernel, count, len(weights)),
        grid=(count // 2,),
        in_specs=[pl.BlockSpec(memory_space=pltpu.VMEM)] * (count + len(weights) + 3),
        out_specs=[rows(width), rows(packed), rows(128)],
        out_shape=[
            jax.ShapeDtypeStruct((total, width), BF16),
            jax.ShapeDtypeStruct((total, packed), BF16),
            jax.ShapeDtypeStruct((total, 128), F32),
        ],
        compiler_params=pltpu.CompilerParams(
            dimension_semantics=("arbitrary",), vmem_limit_bytes=VMEM_ASKED
        ),
        cost_estimate=pl.CostEstimate(flops=1, bytes_accessed=1, transcendentals=0),
        name="project",
    )(*blocks, *weights, rate_rows, bias, gain)


def trans_dot(left, right):
    return lax.dot_general(
        left, right, (((0,), (0,)), ((), ())), preferred_element_type=jnp.float32
    )


def after(value, *first):
    anywhere = pl.BlockSpec(memory_space=pl.ANY)
    return pl.pallas_call(
        lambda *refs: None,
        out_shape=jax.ShapeDtypeStruct(value.shape, value.dtype),
        in_specs=[anywhere] * (1 + len(first)),
        out_specs=anywhere,
        input_output_aliases={0: 0},
        name="after",
    )(value, *first)


def ring_pairs(size, step):
    order = list(range(0, size, 2)) + list(range(size - 1, 0, -2))
    return [(order[i], order[(i + step) % size]) for i in range(size)]


def ring_place(size, index):
    return jnp.where(index % 2 == 0, index // 2, size - (index + 1) // 2)


def ring_member(size, place):
    return jnp.where(place < size // 2, 2 * place, 2 * (size - place) - 1)


def slot_steps(size):
    steps = [0, -(size // 2)]
    for s in range(1, size // 2):
        steps += [-s, s]
    return steps


def by_slots(arrived):
    return [arrived[0], arrived[-1]] + list(arrived[1:-1])


def ring_step(blocks, s, size):
    ahead = lax.ppermute(blocks[0], "seq", ring_pairs(size, 1))
    if s == size // 2:
        return (ahead,)
    return ahead, lax.ppermute(blocks[-1], "seq", ring_pairs(size, -1))


def ring_gather(block, size, work=None, beside=None):
    arrived = [(block,)]
    others = list(beside or ())

    def do_work(s):
        if not work:
            return []
        return list(work(s, arrived[s], others[s]) if others else work(s, arrived[s]))

    for s in range(1, size // 2 + 1):
        done = do_work(s - 1)
        moved = ring_step(arrived[-1], s, size)
        done += moved[1:]
        if others and len(others) <= size // 2:
            others.append(ring_step(others[-1], len(others), size))
            done += others[-1]
        ahead = after(moved[0], *done) if done else moved[0]
        arrived.append((ahead,) + moved[1:])
    do_work(size // 2)
    return arrived


def ring_scatter(part, size, work=()):
    half = size // 2
    ahead, back = part(half).astype(BF16), part(1 - half).astype(BF16)
    for s in range(1, half + 1):
        done = work[s - 1](ahead) if s <= len(work) else []
        ahead = lax.ppermute(ahead, "seq", ring_pairs(size, 1))
        if s < half:
            back = lax.ppermute(back, "seq", ring_pairs(size, -1))
            done = list(done) + [back]
        if done:
            ahead = after(ahead, *done)
        if s < half:
            back = after(back, ahead)
        ahead = ahead.astype(F32)
        if s < half:
            ahead = (ahead + part(half - s)).astype(BF16)
            if s < half - 1:
                back = (back.astype(F32) + part(1 - half + s)).astype(BF16)
    return part(0).astype(F32) + ahead + back.astype(F32)


def pairwise_sum(value, axis, size):
    bit = 1
    while bit < size:
        value = value + lax.ppermute(value, axis, [(i, i ^ bit) for i in range(size)])
        bit *= 2
    return value


def swap(value, bit):
    return lax.ppermute(value, "grp", [(i, i ^ bit) for i in range(4)])


def near(index, k):
    return index ^ k if lax.axis_size("grp") == 4 else k


def start_gather(value):
    if lax.axis_size("grp") != 4:
        whole = lax.all_gather(value, "grp", axis=0)
        return [whole[k] for k in range(whole.shape[0])]
    return [value, swap(value, 1), swap(value, 2)]


def end_gather(parts):
    if lax.axis_size("grp") != 4:
        return parts
    return parts + [swap(parts[2], 1)]


def start_scatter(block):
    if lax.axis_size("grp") != 4:
        whole = jnp.stack([block(k) for k in range(lax.axis_size("grp"))]).astype(BF16)
        return lax.psum_scatter(whole, "grp", scatter_dimension=0, tiled=False)
    return swap(block(3).astype(BF16), 1)


def cross_scatter(block, corner):
    if lax.axis_size("grp") != 4:
        return corner
    return swap((corner.astype(F32) + block(2)).astype(BF16), 2)


def end_scatter(block, across):
    if lax.axis_size("grp") != 4:
        return across
    beside = swap(block(1).astype(BF16), 1).astype(F32)
    return (block(0) + beside + across.astype(F32)).astype(BF16)


def in_turn(blocks, order):
    picked = [lax.dynamic_index_in_dim(blocks, order[i], 0) for i in range(blocks.shape[0])]
    return jnp.concatenate(picked, axis=0)


class HeadPlan:
    def __init__(self, heads, seq, grp):
        self.seq, self.grp, self.heads = seq, grp, heads
        self.local = heads // seq
        self.mixed = (heads // grp) % seq == 0
        self.each = (heads // grp) // seq if self.mixed else 0

    def pick(self, item, seq_index, grp_index):
        rest = item.shape[1:]
        if self.mixed:
            item = item.reshape((self.grp, self.seq, self.each) + rest)
            item = lax.dynamic_index_in_dim(item, seq_index, 1, keepdims=False)
            return self.turn(item.reshape((self.local,) + rest), grp_index)
        return lax.dynamic_slice_in_dim(item, seq_index * self.local, self.local, 0)

    def turn(self, item, grp_index):
        if not self.mixed:
            return item
        item = item.reshape((self.grp, self.each) + item.shape[1:])
        parts = [
            lax.dynamic_index_in_dim(item, near(grp_index, k), 0, keepdims=False)
            for k in range(self.grp)
        ]
        return jnp.concatenate(parts, axis=0)

    def order(self, item):
        rest = item.shape[2:]
        if self.mixed:
            item = item.reshape((self.seq, self.grp, self.each) + rest)
            item = jnp.swapaxes(item, 0, 1)
        return item.reshape((self.heads,) + rest)


def exchange(block):
    return lax.all_to_all(block, "seq", 0, 0, tiled=True)


def cut_heads(plan, mats, turned, head_dim):
    count = len(mats)
    seq = plan.seq
    if plan.each == 1:
        return cut_features(seq, mats, turned)
    mats = [m.T if turn else m for m, turn in zip(mats, turned)]
    cols = mats[0].shape[1]
    if plan.mixed:
        block = jnp.stack([m.reshape(seq, plan.each, head_dim, cols) for m in mats], axis=2)
    else:
        block = lax.all_gather(jnp.stack(mats), "grp", axis=1, tiled=True)
        block = block.reshape(count, seq, plan.local, head_dim, cols).transpose(1, 2, 0, 3, 4)
    return block.reshape(seq, -1, cols)


def start_heads(plan, block):
    seq, _, cols = block.shape
    block = block.transpose(1, 0, 2).reshape(-1, seq * cols)
    return start_gather(block) if plan.mixed else [block]


def end_heads(plan, parts, count, head_dim):
    parts = end_gather(parts) if plan.mixed else parts
    size = count * head_dim
    return [part[i : i + size] for part in parts for i in range(0, part.shape[0], size)]


def heads_block(plan, grads):
    each = plan.each
    return lambda k: jnp.concatenate(grads[k * each : (k + 1) * each], axis=0)


def scatter_heads(plan, grads, block, turned):
    packed, width = grads[0].shape
    count = len(turned)
    seq = plan.seq
    cols = width // seq
    head_dim = packed // count
    if plan.mixed:
        each = plan.each
        block = exchange(block.reshape(-1, seq, cols).transpose(1, 0, 2))
        if each == 1:
            return join_features(block, seq * head_dim, turned)
        block = block.reshape(seq, each, count, head_dim, cols)
        block = block.transpose(2, 0, 1, 3, 4).reshape(count, -1, cols).astype(F32)
        return [part.T if turn else part for part, turn in zip(block, turned)]
    block = jnp.concatenate(grads, axis=0).astype(BF16)
    block = block.reshape(-1, seq, cols).transpose(1, 0, 2)
    block = exchange(block).reshape(seq, plan.local, count, head_dim, cols)
    block = block.transpose(2, 0, 1, 3, 4).reshape(count, -1, cols)
    block = lax.psum_scatter(block, "grp", scatter_dimension=1, tiled=True).astype(F32)
    return [part.T if turn else part for part, turn in zip(block, turned)]


def body(
    tokens,
    cotangent,
    lengths,
    prenorm_gain,
    w_query,
    w_key,
    w_value,
    w_gate,
    rate_weight,
    rate_bias,
    init_weight,
    init_bias,
    inner_gain,
    inner_bias,
    post_gain,
    post_bias,
    w_out,
    feedforward_norm_gain,
    w_swish,
    w_up,
    w_down,
):
    seq_index = lax.axis_index("seq")
    grp_index = lax.axis_index("grp")
    groups = lax.axis_size("grp")
    seq = lax.axis_size("seq")
    rows_tok = tokens.shape[1]
    width = tokens.shape[2]
    heads, head_dim, _ = init_weight.shape
    plan = HeadPlan(heads, seq, groups)
    local = plan.local
    features = local * head_dim
    stream = rows_tok * seq
    steps = slot_steps(seq)
    place = ring_place(seq, seq_index)
    member_of_slot = ring_member(seq, (place + jnp.array(steps, jnp.int32)) % seq)
    apart = (ring_place(seq, jnp.arange(seq, dtype=jnp.int32)) - place) % seq
    slot_of_member = jnp.where(apart > seq // 2, 2 * (seq - apart), 2 * apart + 1)
    slot_of_member = jnp.where(apart == 0, 0, jnp.where(apart == seq // 2, 1, slot_of_member))
    to_slots = (member_of_slot[:, None] == jnp.arange(seq)[None, :]).astype(F32)

    def in_slots(stat):
        cut = stat.reshape(-1, seq, rows_tok)
        out = jnp.einsum("sm,kmt->kst", to_slots, cut, precision=lax.Precision.HIGHEST)
        return out.reshape(-1, stream)

    def in_order(stat):
        cut = stat.reshape(-1, seq, rows_tok)
        out = jnp.einsum("sm,kst->kmt", to_slots, cut, precision=lax.Precision.HIGHEST)
        return out.reshape(-1, stream)

    def pick(item):
        return plan.pick(item, seq_index, grp_index)

    def by_distance(rows):
        return lambda k: lax.slice_in_dim(
            rows, at_slot(k) * rows_tok, (at_slot(k) + 1) * rows_tok, axis=0
        )

    def at_slot(k):
        return steps.index(k if k < seq // 2 else k - seq)

    own_lengths = lax.dynamic_index_in_dim(lengths, grp_index, 0, keepdims=False)
    ends = jnp.cumsum(own_lengths)
    starts = ends - own_lengths
    docs = jnp.concatenate([starts, ends[-1:]])

    proj_block = exchange(
        cut_heads(plan, (w_query, w_key, w_value), (True, True, True), head_dim)
    )
    padded = w_down.shape[0] // seq
    padded += -padded % MB
    rate_rows = jnp.pad(pick(rate_weight.T), ((0, 128 - local), (0, 0)))
    gb, init = chain_params(*(pick(i) for i in (init_weight, init_bias, inner_gain, inner_bias)))
    own = {}

    bias = jnp.pad(pick(rate_bias), (0, 128 - local))[None]

    def token_work(s, arrived):
        if s == 1:
            own["parts"] = start_heads(plan, after(proj_block, arrived[0]))
            return [gb, init, rate_rows, bias, docs, slot_of_member, member_of_slot]
        if s == seq // 2 - 2:
            mats = (w_swish.T, w_up.T, w_down)
            if plan.each == 1:
                turned = (True, False, False, False, False)
                own["rest"] = cut_features(seq, (w_gate, w_out) + mats, turned)
            else:
                side = cut_heads(plan, (w_gate, w_out), (True, False), head_dim)
                own["rest"] = jnp.concatenate(
                    [side, cut_features(seq, mats, (False,) * 3)], axis=1
                )
            return [own["rest"]]
        if s == seq // 2 - 1:
            own["parts"] = end_heads(plan, own["parts"], 3, head_dim)
            return own["parts"][-1:]
        return []

    token_steps = ring_gather(tokens[0], seq, token_work)
    normed, x3, logits = project(
        sum(by_slots(token_steps), ()), own["parts"], rate_rows, bias, prenorm_gain[None]
    )
    rest_block = exchange(after(own["rest"], token_steps[-1][0]))
    grad_own = cotangent[0]
    grad_steps = [(after(grad_own, rest_block),)]
    grad_steps.append(ring_step(grad_steps[0], 1, seq))
    grad_steps.append(ring_step(grad_steps[1], 2, seq))

    inner, *kept = chain_forward(slot_of_member, docs, x3, logits, gb, init, rows_tok)
    side_rows = rest_block.shape[1] - 3 * padded
    side_block, ffn_block = rest_block[:, :side_rows], rest_block[:, side_rows:]

    sides = end_heads(plan, start_heads(plan, side_block), 2, head_dim)
    m_gate = jnp.concatenate([side[:head_dim] for side in sides], axis=0)
    m_out = jnp.concatenate([side[head_dim:] for side in sides], axis=0)
    gate_pre = mm_nt(normed, m_gate)
    ffn_block = ffn_block.transpose(1, 0, 2).reshape(3 * padded, width)
    ffn_parts = start_gather(ffn_block)

    sums = jnp.sum(kept[3][2:4].reshape(2, stream // MB, local, MB), axis=2).reshape(2, stream)
    sums = after(pairwise_sum(sums, "seq", seq), rest_block)
    sums = in_slots(sums) / width
    mean_o = sums[0][:, None]
    inv_o = lax.rsqrt(sums[1][:, None] - mean_o * mean_o + EPS)
    o_hat = (inner - mean_o) * inv_o
    post_g = pick(post_gain.reshape(heads, head_dim)).reshape(features)
    post_b = pick(post_bias.reshape(heads, head_dim)).reshape(features)
    post = o_hat * post_g + post_b
    gelu_val, gelu_pull = jax.vjp(jax.nn.gelu, gate_pre)
    gated = (gelu_val * post).astype(BF16)
    ffn = {}


    def ffn_corner(since):
        ffn["parts"] = end_gather(ffn_parts[:-1] + [after(ffn_parts[-1], since)])
        return ffn["parts"][-1:]

    mixing = ring_scatter(
        by_distance(after(mm(gated, m_out).astype(BF16), *grad_steps[1])),
        seq,
        [lambda since: [], lambda since: list(grad_steps[2]), lambda since: [], ffn_corner],
    )
    own_rows = tokens[0].astype(F32)
    resid = own_rows + mixing
    inv_second = lax.rsqrt(jnp.mean(resid * resid, -1, keepdims=True) + EPS)
    unit_second = resid * inv_second
    ffn_in = (unit_second * feedforward_norm_gain).astype(BF16)

    got = {"kept": (), "rows": [], "grads": []}
    d_parts = {}

    def step_work(s, arrived, grads):
        slot = 2 * s if s < seq // 2 else 1
        members = lax.slice_in_dim(member_of_slot, slot, slot + len(arrived))
        got["kept"], d_in = ffn_step(
            members, seq, slot, arrived, grads, ffn["parts"], got["kept"]
        )
        got["rows"].append(arrived)
        got["grads"].append(grads)
        for i in range(len(arrived)):
            d_parts[steps[slot + i]] = d_in[i * rows_tok : (i + 1) * rows_tok]
        return [d_in]

    ring_gather(ffn_in, seq, step_work, grad_steps)
    kept_ffn = got["kept"]

    def ffn_work(since):
        first, *others = kept_ffn[:3]
        got["ffn"] = ffn_grads(
            groups,
            [after(first, since)] + others,
            sum(by_slots(got["rows"]), ()),
            sum(by_slots(got["grads"]), ()),
        )
        return got["ffn"][:1]

    def ffn_corner_work(since):
        got["corner"] = start_scatter(lambda k: after(got["ffn"][k], since))
        got["across"] = cross_scatter(ffn_grad, got["corner"])
        return [got["corner"]]

    def ffn_grad(k):
        return got["ffn"][k]

    d_ffn = ring_scatter(
        lambda k: d_parts[k if k < seq // 2 else k - seq], seq, [ffn_work, ffn_corner_work]
    )
    second_scaled = d_ffn * feedforward_norm_gain
    g_ffn_gain = jnp.sum(d_ffn * unit_second, 0)
    d_resid = grad_own.astype(F32) + inv_second * (
        second_scaled - unit_second * jnp.mean(second_scaled * unit_second, -1, keepdims=True)
    )

    def mix_work(s, arrived):
        if s == 0:
            late = [after(own["parts"][0], arrived[0])] + own["parts"][1:]
            got["w_all"] = jnp.concatenate(late + [rate_rows, m_gate], axis=0)
            return [got["w_all"]]
        if s == seq // 2 - 2:
            return [got["across"]]
        if s == seq // 2 - 1:
            summed = end_scatter(ffn_grad, after(got["across"], arrived[0]))
            got["summed"] = summed.reshape(3 * padded, seq, -1).transpose(1, 0, 2)
            return [got["summed"]]
        return []

    mix_steps = ring_gather(d_resid.astype(BF16), seq, mix_work)
    ffn_out = lax.psum_scatter(
        after(kept_ffn[3], mix_steps[seq // 2 - 2][0]), "seq", scatter_dimension=0, tiled=False
    )
    out_tokens = (resid + ffn_out.astype(F32)).astype(BF16)[None]
    d_gated = [mm_nt(jnp.concatenate(arrived, axis=0), m_out) for arrived in mix_steps]
    d_gated = jnp.concatenate(by_slots(d_gated), axis=0)
    d_post = d_gated * gelu_val
    d_gate_pre = gelu_pull(d_gated * post)[0].astype(BF16)
    g_post_gain = jnp.sum(d_post * o_hat, 0)
    g_post_bias = jnp.sum(d_post, 0)
    d_ohat = d_post * post_g
    sums = jnp.stack([jnp.sum(d_ohat, -1), jnp.sum(d_ohat * o_hat, -1)])
    sums = in_slots(pairwise_sum(in_order(sums), "seq", seq)) / width
    g_ffn = exchange(after(got["summed"], sums))
    d_inner = inv_o * (d_ohat - sums[0][:, None] - o_hat * sums[1][:, None])
    d_x, d_gb, d_init = chain_backward(
        slot_of_member, docs, x3, d_inner, d_gate_pre, logits, gb, init, kept, rows_tok
    )
    *head_rows_grads, g_rates, g_gain = proj_grads(
        d_x, normed, got["w_all"], gated, sum(by_slots(mix_steps), ()), local, head_dim
    )
    d_logits = d_x[:, 3 * features : 3 * features + local].astype(F32)
    parts = [item.reshape(local, -1) for item in chain_param_grads(d_gb, d_init, local)]
    parts += [item.reshape(local, head_dim) for item in (g_post_gain, g_post_bias)]
    parts += [g_rates[:local], jnp.sum(d_logits, 0)[:, None]]
    sizes = [item.shape[1] for item in parts]
    flat = jnp.concatenate(parts, axis=1)
    flat = plan.turn(jnp.pad(flat, ((0, 0), (0, -flat.shape[1] % 1024))), grp_index)
    count = flat.size
    flat = jnp.concatenate([flat.reshape(-1), g_gain[0] / prenorm_gain, g_ffn_gain])
    flat = pairwise_sum(flat.reshape(-1, 1024), "grp", groups)
    flat_all = lax.all_gather(flat, "seq", axis=0)
    d_x = after(d_x, g_gain, g_ffn)
    d_normed_part = mm(d_x, got["w_all"]).astype(BF16)

    def corner_work(since):
        if not plan.mixed:
            return [ffn_out]
        block = heads_block(plan, head_rows_grads)
        got["corner"] = start_scatter(block)
        got["across"] = cross_scatter(block, after(got["corner"], flat))
        return [got["corner"], ffn_out]

    def join_work(since):
        got["join"] = join_features(after(g_ffn, since), w_down.shape[0], (False,) * 3)
        return got["join"][:1]

    def across_work(since):
        return [got["across"]] if plan.mixed else []

    d_normed = ring_scatter(
        by_distance(d_normed_part), seq, [corner_work, join_work, across_work]
    )
    summed = end_scatter(heads_block(plan, head_rows_grads), got["across"]) if plan.mixed else None
    g_heads = scatter_heads(plan, head_rows_grads, summed, (True,) * 4 + (False,))
    own_inv = lax.rsqrt(jnp.mean(own_rows * own_rows, -1, keepdims=True) + EPS)
    own_unit = own_rows * own_inv
    first_scaled = d_normed * prenorm_gain
    grad_tokens = (
        d_resid
        + own_inv
        * (first_scaled - own_unit * jnp.mean(first_scaled * own_unit, -1, keepdims=True))
    )[None]

    flat = after(flat_all, d_normed).reshape(seq, -1)
    gains = jnp.sum(flat[:, count:], 0).reshape(2, width)
    flat = plan.order(flat[:, :count].reshape(seq, local, -1))
    small = []
    offset = 0
    for size in sizes:
        small.append(flat[:, offset : offset + size])
        offset += size
    g_ffn = got["join"]
    return (
        out_tokens,
        grad_tokens,
        gains[0],
        g_heads[0],
        g_heads[1],
        g_heads[2],
        g_heads[3],
        small[6].T,
        small[7][:, 0],
        small[0].reshape(heads, head_dim, head_dim),
        small[1],
        small[2],
        small[3],
        small[4].reshape(width),
        small[5].reshape(width),
        g_heads[4],
        gains[1],
        g_ffn[0].T,
        g_ffn[1].T,
        g_ffn[2],
    )


def solution(mesh):
    whole = P()
    rows = P("grp", "seq", None)
    wide = P("seq", "grp")
    tall = P("grp", "seq")
    return jax.shard_map(
        body,
        mesh=mesh,
        in_specs=(rows, rows, whole, whole, wide, wide, wide, wide)
        + (whole,) * 8
        + (tall, whole, wide, wide, tall),
        out_specs=(rows, rows, whole, wide, wide, wide, wide)
        + (whole,) * 8
        + (tall, whole, wide, wide, tall),
        check_vma=False,
    )
```
